32 devices in a mesh: grp: 4 (over y, x), fsdp: 4 (over z), ctx: 2 (over core).
Axes of the slice: x: 2, y: 2, z: 4, core: 2. Of those that a mesh axis runs over, the one named last changes fastest.
Arguments:
- activations_in: bfloat16 [2, 16, 1024, 1152], P(None, ('grp', 'fsdp'), 'ctx'), may hold values from -6 to 6
- prefix_len: int32 [2, 16], P(None, ('grp', 'fsdp')), may hold values from 102 to 512
- attn_gain: bfloat16 [1152], P(('fsdp', 'ctx')), may hold values from 0.5 to 1.5
- query_weight: bfloat16 [1152, 1152], P(('fsdp', 'ctx')), may hold values from -0.1875 to 0.1875
- key_weight: bfloat16 [1152, 384], P(('fsdp', 'ctx')), may hold values from -0.1875 to 0.1875
- value_weight: bfloat16 [1152, 384], P(('fsdp', 'ctx')), may hold values from -0.1875 to 0.1875
- out_weight: bfloat16 [1152, 1152], P(('fsdp', 'ctx')), may hold values from -0.75 to 0.75
- ffn_gain: bfloat16 [1152], P(('fsdp', 'ctx')), may hold values from 0.5 to 1.5
- gate_weight: bfloat16 [1152, 3072], P(('fsdp', 'ctx')), may hold values from -0.1875 to 0.1875
- up_weight: bfloat16 [1152, 3072], P(('fsdp', 'ctx')), may hold values from -0.1875 to 0.1875
- down_weight: bfloat16 [3072, 1152], P(('fsdp', 'ctx')), may hold values from -0.109375 to 0.109375
- cotangent: bfloat16 [2, 16, 1024, 1152], P(None, ('grp', 'fsdp'), 'ctx'), may hold values from -6 to 6
Outputs:
- activations_out: bfloat16 [2, 16, 1024, 1152], P(None, ('grp', 'fsdp'), 'ctx')
- input_grad: bfloat16 [2, 16, 1024, 1152], P(None, ('grp', 'fsdp'), 'ctx')
- grad_attn_gain: float32 [1152], P(('fsdp', 'ctx'))
- grad_query_weight: float32 [1152, 1152], P(('fsdp', 'ctx'))
- grad_key_weight: float32 [1152, 384], P(('fsdp', 'ctx'))
- grad_value_weight: float32 [1152, 384], P(('fsdp', 'ctx'))
- grad_out_weight: float32 [1152, 1152], P(('fsdp', 'ctx'))
- grad_ffn_gain: float32 [1152], P(('fsdp', 'ctx'))
- grad_gate_weight: float32 [1152, 3072], P(('fsdp', 'ctx'))
- grad_up_weight: float32 [1152, 3072], P(('fsdp', 'ctx'))
- grad_down_weight: float32 [3072, 1152], P(('fsdp', 'ctx'))
The draws below stay inside these ranges and needn't reach their ends.
Inputs may be any that keep to these rules, and one draw needn't show every extreme that they name: prefix_len of a sequence is how many of its first positions every position of that sequence may attend to.
All inputs are finite; a program needn't handle non-finite values.
Results may differ from the reference program's by a relative error of at most 0.019.
Values may be sent and summed in bfloat16 or wider, within the bound.
A program may use at most 384 MiB of HBM per device.

```python
import math
import jax
import jax.numpy as jnp
from jax import lax

D = 1152
HEADS = 18
KV_HEADS = 6
HEAD = 64
FF = 3072
SEQ_LEN = 1024
MICRO = 2
SEQS = 16


def set_ends(values, stream_key, least, largest):
    shape = values.shape
    index_at = [jax.random.randint(jax.random.fold_in(stream_key, axis), (), 0, shape[axis]) for axis in range(len(shape))]
    values = values.at[tuple(index_at)].set(least)
    longest = shape.index(max(shape))
    index_at[longest] = (index_at[longest] + 1) % shape[longest]
    return values.at[tuple(index_at)].set(largest)


def with_spikes(entries, stream_key, source, target, blocks, factor):
    owner, partner = [(jnp.arange(entries.shape[position]) // (entries.shape[position] // blocks)).reshape([-1 if axis == position else 1 for axis in range(entries.ndim)]) for position in (source, target)]
    chosen = jax.random.permutation(stream_key, blocks)[partner]
    strong = (owner == chosen) | (owner == (partner + blocks // 2) % blocks)
    return jnp.where(strong, factor * entries, entries)


def level_of(stream_key, extent, shards, low, top_value):
    gain = 1.0
    for dim, shards_of in shards:
        steps = jax.random.uniform(jax.random.fold_in(jax.random.fold_in(stream_key, 6), dim), (shards_of,), jnp.float32, low / len(shards), top_value / len(shards))
        gain = gain * jnp.repeat(jnp.exp(steps), extent[dim] // shards_of).reshape((-1,) + (1,) * (len(extent) - 1 - dim))
    return gain


def normal_values(stream_key, extent, scale, limit, split=(), kind=jnp.bfloat16):
    loudness = level_of(stream_key, extent, split, -0.22, 0.18) if split else 1.0
    values = jax.random.normal(stream_key, extent, jnp.float32) * scale * loudness
    return jnp.minimum(jnp.maximum(values, -limit), limit).astype(kind)


def noise_with(stream_key, shape, deviation, bound, split, heavy, kind=jnp.bfloat16):
    values = deviation * jax.random.normal(stream_key, shape, jnp.float32)
    if split:
        values = values * level_of(stream_key, shape, split, -0.22, 0.18)
    return jnp.clip(with_spikes(values, jax.random.fold_in(stream_key, 3), *heavy), -bound, bound).astype(kind)


def setup_inputs(seed: int = 0) -> dict:
    key_of = jax.random.split(jax.random.key(seed), 13)
    return {
        "activations_in": normal_values(key_of[0], (MICRO, SEQS, SEQ_LEN, D), 1.0, 6.0, ((1, 16), (2, 2))),
        "prefix_len": set_ends(jax.random.randint(key_of[1], (MICRO, SEQS), SEQ_LEN // 10, SEQ_LEN // 2 + 1), jax.random.fold_in(key_of[1], 1), SEQ_LEN // 10, (SEQ_LEN // 2 + 1) - 1).astype(jnp.int32),
        "attn_gain": jnp.clip(1.0 + 0.1 * jax.random.normal(key_of[2], (D,), jnp.float32), 0.5, 1.5).astype(jnp.bfloat16),
        "query_weight": normal_values(key_of[3], (D, HEADS * HEAD), D ** -0.5, 0.1875, ((0, 8),)),
        "key_weight": normal_values(key_of[4], (D, KV_HEADS * HEAD), D ** -0.5, 0.1875, ((0, 8),)),
        "value_weight": normal_values(key_of[5], (D, KV_HEADS * HEAD), D ** -0.5, 0.1875, ((0, 8),)),
        "out_weight": normal_values(key_of[6], (HEADS * HEAD, D), (D // 16) ** -0.5, 0.75, ((0, 8),)),
        "ffn_gain": jnp.clip(1.0 + 0.1 * jax.random.normal(key_of[7], (D,), jnp.float32), 0.5, 1.5).astype(jnp.bfloat16),
        "gate_weight": normal_values(key_of[8], (D, FF), D ** -0.5, 0.1875, ((0, 8),)),
        "up_weight": normal_values(key_of[9], (D, FF), D ** -0.5, 0.1875, ((0, 8),)),
        "down_weight": normal_values(key_of[10], (FF, D), FF ** -0.5, 0.109375, ((0, 8),)),
        "cotangent": noise_with(key_of[11], (MICRO, SEQS, SEQ_LEN, D), 1.0, 6.0, ((1, 16), (2, 2)), (2, 3, 2, 2.0)),
    }


precise = lax.Precision.HIGHEST
epsilon = 1e-05

@jax.custom_vjp
def low(v):
    return lax.optimization_barrier(v.astype(jnp.bfloat16)).astype(jnp.float32)

@jax.custom_vjp
def low_back(v):
    return v

def low_keep(v):
    return (low(v), None)

def low_pass(kept, grad):
    return (grad,)

def back_keep(v):
    return (v, None)

def back_low(kept, grad):
    return (low(grad),)
low.defvjp(low_keep, low_pass)
low_back.defvjp(back_keep, back_low)

def rotary_tables(length):
    halfway = HEAD // 2
    frequency = 10000.0 ** (-jnp.arange(halfway, dtype=jnp.float32) * 2.0 / HEAD)
    angles = jnp.arange(length, dtype=jnp.float32)[:, None] * frequency[None, :]
    return (jnp.cos(angles)[:, None, :], jnp.sin(angles)[:, None, :])

def rotate(values, cosine, sine):
    halfway = values.shape[-1] // 2
    first = values[..., :halfway]
    second = values[..., halfway:]
    return jnp.concatenate([first * cosine - second * sine, second * cosine + first * sine], -1)

def attend_one(item):
    query, keys, values, prefix = item
    length = query.shape[0]
    groups = HEADS // KV_HEADS
    query = query.reshape(length, KV_HEADS, groups, HEAD)
    scores = jnp.einsum('qhgd,khd->hgqk', query, keys, precision=precise) / math.sqrt(HEAD)
    scores = low_back(scores)
    places = jnp.arange(length, dtype=jnp.int32)
    visible = (places[None, :] <= places[:, None]) | (places[None, :] < prefix)
    scores = jnp.where(visible, scores, -1e+30)
    probs = low(jax.nn.softmax(scores, axis=-1))
    mixed = jnp.einsum('hgqk,khd->qhgd', probs, values, precision=precise)
    return mixed.reshape(length, HEADS * HEAD)

def layer(inputs, prefix, attn_gain, query_weight, key_weight, value_weight, out_weight, ffn_gain, gate_weight, up_weight, down_weight):
    count, length, width = inputs.shape
    cosine, sine = rotary_tables(length)
    normed_one = inputs * lax.rsqrt(lax.optimization_barrier(jnp.mean(inputs * inputs, -1, keepdims=True)) + epsilon)
    first_in = low(normed_one * attn_gain)
    query = low_back(jnp.dot(first_in, query_weight, precision=precise))
    keys = low_back(jnp.dot(first_in, key_weight, precision=precise))
    values = low(low_back(jnp.dot(first_in, value_weight, precision=precise)))
    query = low(rotate(query.reshape(count, length, HEADS, HEAD), cosine, sine))
    keys = low(rotate(keys.reshape(count, length, KV_HEADS, HEAD), cosine, sine))
    values = values.reshape(count, length, KV_HEADS, HEAD)
    mixed = lax.map(jax.checkpoint(attend_one), (query, keys, values, prefix))
    mixed = low(low_back(mixed))
    middle = inputs + low_back(jnp.dot(mixed, out_weight, precision=precise))
    normed_two = middle * lax.rsqrt(lax.optimization_barrier(jnp.mean(middle * middle, -1, keepdims=True)) + epsilon)
    second_in = low(normed_two * ffn_gain)
    gate = low_back(jnp.dot(second_in, gate_weight, precision=precise))
    upward = low_back(jnp.dot(second_in, up_weight, precision=precise))
    hidden = low(jax.nn.silu(gate) * upward)
    return middle + low_back(jnp.dot(hidden, down_weight, precision=precise))

def reference(activations_in, prefix_len, attn_gain, query_weight, key_weight, value_weight, out_weight, ffn_gain, gate_weight, up_weight, down_weight, cotangent):
    total = MICRO * SEQS
    group_size = math.gcd(total, 4)
    blocks = total // group_size
    inputs = activations_in.astype(jnp.float32).reshape(blocks, group_size, SEQ_LEN, D)
    prefixes = prefix_len.reshape(blocks, group_size).astype(jnp.int32)
    cotangents = cotangent.astype(jnp.float32).reshape(blocks, group_size, SEQ_LEN, D)
    weights = tuple((w.astype(jnp.float32) for w in (attn_gain, query_weight, key_weight, value_weight, out_weight, ffn_gain, gate_weight, up_weight, down_weight)))

    def one_block(carry, item):
        block_in, block_prefix, block_cot = item

        def forward(inputs_now, *params):
            return layer(inputs_now, block_prefix, *params)
        result, pullback = jax.vjp(forward, block_in, *weights)
        grads = pullback(block_cot)
        carry = tuple((c + g for c, g in zip(carry, grads[1:])))
        return (carry, (result.astype(jnp.bfloat16), grads[0].astype(jnp.bfloat16)))
    zeros = tuple((jnp.zeros_like(w) for w in weights))
    totals, (outputs, input_grads) = lax.scan(one_block, zeros, (inputs, prefixes, cotangents))
    outputs = outputs.reshape(MICRO, SEQS, SEQ_LEN, D)
    input_grads = input_grads.reshape(MICRO, SEQS, SEQ_LEN, D)
    return (outputs, input_grads, totals[0], totals[1], totals[2], totals[3], totals[4], totals[5], totals[6], totals[7], totals[8])
```

```python
import functools
import math

import jax
import jax.numpy as jnp
import numpy as np
from jax import lax
from jax.experimental import pallas as pl
from jax.experimental.pallas import tpu as pltpu
from jax.sharding import PartitionSpec as P

HEADS = 18
KV_HEADS = 6
HEAD = 64


epsilon = 1e-05


def shortened(array):

    def short(part):
        return part.astype(jnp.bfloat16) if part.dtype == jnp.float32 else part

    return jax.tree.map(short, array)


def rotary_tables(positions):
    halfway = HEAD // 2
    frequency = 10000.0 ** (-jnp.arange(halfway, dtype=jnp.float32) * 2.0 / HEAD)
    angles = positions.astype(jnp.float32)[:, None] * frequency[None, :]
    return (jnp.cos(angles)[:, None, :], jnp.sin(angles)[:, None, :])


def rotate(values, cosine, sine):
    halfway = values.shape[-1] // 2
    first = values[..., :halfway]
    second = values[..., halfway:]
    return jnp.concatenate([first * cosine - second * sine, second * cosine + first * sine], -1)


def rotate_back(values, cosine, sine):
    halfway = values.shape[-1] // 2
    first = values[..., :halfway]
    second = values[..., halfway:]
    return jnp.concatenate([first * cosine + second * sine, second * cosine - first * sine], -1)


def norm_back(grad_normed, normed, inverse):
    return inverse * (grad_normed - normed * jnp.mean(grad_normed * normed, -1, keepdims=True))


def flatten_all(grads):
    return tuple((g.reshape(-1) for g in grads))


def local(
    activations_in,
    prefix_len,
    attn_gain,
    query_weight,
    key_weight,
    value_weight,
    out_weight,
    ffn_gain,
    gate_weight,
    up_weight,
    down_weight,
    cotangent,
):
    micro, seq_count, span, width = activations_in.shape
    rows = seq_count * span
    length = span * lax.axis_size("ctx")
    groups = HEADS // KV_HEADS
    scale = 1.0 / math.sqrt(HEAD)
    shards = (
        attn_gain,
        query_weight,
        key_weight,
        value_weight,
        out_weight,
        ffn_gain,
        gate_weight,
        up_weight,
        down_weight,
    )
    offset = lax.axis_index("ctx") * span
    query_pos = offset + jnp.arange(span, dtype=jnp.int32)
    key_pos = jnp.arange(length, dtype=jnp.int32)
    cosine, sine = rotary_tables(jnp.tile(query_pos, seq_count))

    def visibility(prefix):
        return (key_pos[None, :] <= query_pos[:, None]) | (key_pos[None, :] < prefix)

    def attend(item):
        query, keys, values, prefix = item
        scores = (
            jnp.einsum("qhgd,khd->hgqk", query, keys, preferred_element_type=jnp.float32) * scale
        )
        scores = jnp.where(visibility(prefix), scores, -1e30)
        peak = jnp.max(scores, -1, keepdims=True)
        weights = jnp.exp(scores - peak)
        totals = jnp.sum(weights, -1, keepdims=True)
        probs = (weights / totals).astype(jnp.bfloat16)
        mixed = jnp.einsum("hgqk,khd->qhgd", probs, values, preferred_element_type=jnp.float32)
        return (mixed.reshape(span, HEADS * HEAD), (peak + jnp.log(totals))[..., 0])

    def attend_back(item):
        query, keys, values, prefix, log_total, grad_mixed = item
        scores = (
            jnp.einsum("qhgd,khd->hgqk", query, keys, preferred_element_type=jnp.float32) * scale
        )
        probs = jnp.where(visibility(prefix), jnp.exp(scores - log_total[..., None]), 0.0)
        grad_probs = jnp.einsum(
            "qhgd,khd->hgqk", grad_mixed, values, preferred_element_type=jnp.float32
        )
        grad_scores = (
            probs * (grad_probs - jnp.sum(probs * grad_probs, -1, keepdims=True))
        ).astype(jnp.bfloat16)
        grad_query = (
            jnp.einsum("hgqk,khd->qhgd", grad_scores, keys, preferred_element_type=jnp.float32)
            * scale
        )
        grad_keys = (
            jnp.einsum("hgqk,qhgd->khd", grad_scores, query, preferred_element_type=jnp.float32)
            * scale
        )
        grad_values = jnp.einsum(
            "hgqk,qhgd->khd",
            probs.astype(jnp.bfloat16),
            grad_mixed,
            preferred_element_type=jnp.float32,
        )
        return (
            grad_query.reshape(span, HEADS * HEAD),
            grad_keys.reshape(length, KV_HEADS * HEAD),
            grad_values.reshape(length, KV_HEADS * HEAD),
        )

    outputs = []
    input_grads = []
    collected = None
    for index in range(micro):
        full = (
            lax.all_gather(shards[0], ("fsdp", "ctx"), axis=0, tiled=True),
            lax.all_gather(shards[1], ("fsdp", "ctx"), axis=0, tiled=True),
            lax.all_gather(shards[2], ("fsdp", "ctx"), axis=0, tiled=True),
            lax.all_gather(shards[3], ("fsdp", "ctx"), axis=0, tiled=True),
            lax.all_gather(shards[4], ("fsdp", "ctx"), axis=0, tiled=True),
            lax.all_gather(shards[5], ("fsdp", "ctx"), axis=0, tiled=True),
            lax.all_gather(shards[6], ("fsdp", "ctx"), axis=0, tiled=True),
            lax.all_gather(shards[7], ("fsdp", "ctx"), axis=0, tiled=True),
            lax.all_gather(shards[8], ("fsdp", "ctx"), axis=0, tiled=True),
        )
        gain_attn, w_query, w_key, w_value, w_out, gain_ffn, w_gate, w_up, w_down = full
        inputs = activations_in[index].reshape(rows, width).astype(jnp.float32)
        inverse_one = lax.rsqrt(jnp.mean(inputs * inputs, -1, keepdims=True) + epsilon)
        normed_one = inputs * inverse_one
        first_in = (normed_one * gain_attn).astype(jnp.bfloat16)
        query_lin = jnp.dot(first_in, w_query, preferred_element_type=jnp.float32)
        key_lin = jnp.dot(first_in, w_key, preferred_element_type=jnp.float32)
        value_lin = jnp.dot(first_in, w_value, preferred_element_type=jnp.float32)
        query_rot = rotate(query_lin.reshape(rows, HEADS, HEAD), cosine, sine).astype(jnp.bfloat16)
        key_rot = rotate(key_lin.reshape(rows, KV_HEADS, HEAD), cosine, sine).astype(jnp.bfloat16)
        key_rot = key_rot.reshape(seq_count, span, KV_HEADS * HEAD)
        value_low = value_lin.astype(jnp.bfloat16).reshape(seq_count, span, KV_HEADS * HEAD)
        key_all, value_all = (
            lax.all_gather(key_rot, "ctx", axis=1, tiled=True),
            lax.all_gather(value_low, "ctx", axis=1, tiled=True),
        )
        query_split = query_rot.reshape(seq_count, span, KV_HEADS, groups, HEAD)
        key_split = key_all.reshape(seq_count, length, KV_HEADS, HEAD)
        value_split = value_all.reshape(seq_count, length, KV_HEADS, HEAD)
        mixed_all, log_totals = lax.map(
            attend, (query_split, key_split, value_split, prefix_len[index])
        )
        attn_low = mixed_all.reshape(rows, HEADS * HEAD).astype(jnp.bfloat16)
        middle = inputs + jnp.dot(attn_low, w_out, preferred_element_type=jnp.float32)
        inverse_two = lax.rsqrt(jnp.mean(middle * middle, -1, keepdims=True) + epsilon)
        normed_two = middle * inverse_two
        second_in = (normed_two * gain_ffn).astype(jnp.bfloat16)
        gate = jnp.dot(second_in, w_gate, preferred_element_type=jnp.float32)
        upward = jnp.dot(second_in, w_up, preferred_element_type=jnp.float32)
        hidden = (jax.nn.silu(gate) * upward).astype(jnp.bfloat16)
        result = middle + jnp.dot(hidden, w_down, preferred_element_type=jnp.float32)
        outputs.append(result.astype(jnp.bfloat16).reshape(seq_count, span, width))
        back = (
            lax.all_gather(shards[0], ("fsdp", "ctx"), axis=0, tiled=True),
            lax.all_gather(shards[1], ("fsdp", "ctx"), axis=0, tiled=True),
            lax.all_gather(shards[2], ("fsdp", "ctx"), axis=0, tiled=True),
            lax.all_gather(shards[3], ("fsdp", "ctx"), axis=0, tiled=True),
            lax.all_gather(shards[4], ("fsdp", "ctx"), axis=0, tiled=True),
            lax.all_gather(shards[5], ("fsdp", "ctx"), axis=0, tiled=True),
            lax.all_gather(shards[6], ("fsdp", "ctx"), axis=0, tiled=True),
            lax.all_gather(shards[7], ("fsdp", "ctx"), axis=0, tiled=True),
            lax.all_gather(shards[8], ("fsdp", "ctx"), axis=0, tiled=True),
        )
        gain_attn, w_query, w_key, w_value, w_out, gain_ffn, w_gate, w_up, w_down = back
        grad_y = cotangent[index].reshape(rows, width).astype(jnp.float32)
        grad_y_low = grad_y.astype(jnp.bfloat16)
        grad_wdown = jnp.einsum("rf,rd->fd", hidden, grad_y_low, preferred_element_type=jnp.float32)
        grad_hidden = jnp.einsum(
            "rd,fd->rf", grad_y_low, w_down, preferred_element_type=jnp.float32
        )
        sigma = jax.nn.sigmoid(gate)
        grad_up_low = (grad_hidden * gate * sigma).astype(jnp.bfloat16)
        grad_gate_low = (grad_hidden * upward * sigma * (1.0 + gate * (1.0 - sigma))).astype(
            jnp.bfloat16
        )
        grad_wgate = jnp.einsum(
            "rd,rf->df", second_in, grad_gate_low, preferred_element_type=jnp.float32
        )
        grad_wup = jnp.einsum(
            "rd,rf->df", second_in, grad_up_low, preferred_element_type=jnp.float32
        )
        grad_second = jnp.einsum(
            "rf,df->rd", grad_gate_low, w_gate, preferred_element_type=jnp.float32
        ) + jnp.einsum("rf,df->rd", grad_up_low, w_up, preferred_element_type=jnp.float32)
        grad_gain_ffn = jnp.sum(grad_second * normed_two, 0)
        grad_middle = grad_y + norm_back(grad_second * gain_ffn, normed_two, inverse_two)
        grad_branch_low = grad_middle.astype(jnp.bfloat16)
        grad_wout = jnp.einsum(
            "ra,rd->ad", attn_low, grad_branch_low, preferred_element_type=jnp.float32
        )
        grad_attn_low = jnp.einsum(
            "rd,ad->ra", grad_branch_low, w_out, preferred_element_type=jnp.float32
        ).astype(jnp.bfloat16)
        grad_mixed = grad_attn_low.reshape(seq_count, span, KV_HEADS, groups, HEAD)
        grad_query_rot, grad_key_part, grad_value_part = lax.map(
            attend_back,
            (query_split, key_split, value_split, prefix_len[index], log_totals, grad_mixed),
        )
        grad_key_own, grad_value_own = (
            lax.psum_scatter(
                grad_key_part.astype(jnp.bfloat16), "ctx", scatter_dimension=1, tiled=True
            ).astype(jnp.float32),
            lax.psum_scatter(
                grad_value_part.astype(jnp.bfloat16), "ctx", scatter_dimension=1, tiled=True
            ).astype(jnp.float32),
        )
        grad_query = rotate_back(grad_query_rot.reshape(rows, HEADS, HEAD), cosine, sine)
        grad_query = grad_query.reshape(rows, HEADS * HEAD).astype(jnp.bfloat16)
        grad_key = rotate_back(grad_key_own.reshape(rows, KV_HEADS, HEAD), cosine, sine)
        grad_key = grad_key.reshape(rows, KV_HEADS * HEAD).astype(jnp.bfloat16)
        grad_value = grad_value_own.reshape(rows, KV_HEADS * HEAD).astype(jnp.bfloat16)
        grad_wquery = jnp.einsum(
            "rd,rq->dq", first_in, grad_query, preferred_element_type=jnp.float32
        )
        grad_wkey = jnp.einsum("rd,rq->dq", first_in, grad_key, preferred_element_type=jnp.float32)
        grad_wvalue = jnp.einsum(
            "rd,rq->dq", first_in, grad_value, preferred_element_type=jnp.float32
        )
        grad_first = (
            jnp.einsum("rq,dq->rd", grad_query, w_query, preferred_element_type=jnp.float32)
            + jnp.einsum("rq,dq->rd", grad_key, w_key, preferred_element_type=jnp.float32)
            + jnp.einsum("rq,dq->rd", grad_value, w_value, preferred_element_type=jnp.float32)
        )
        grad_gain_attn = jnp.sum(grad_first * normed_one, 0)
        grad_inputs = grad_middle + norm_back(grad_first * gain_attn, normed_one, inverse_one)
        input_grads.append(grad_inputs.astype(jnp.bfloat16).reshape(seq_count, span, width))
        grads = flatten_all(
            (
                grad_gain_attn,
                grad_wquery,
                grad_wkey,
                grad_wvalue,
                grad_wout,
                grad_gain_ffn,
                grad_wgate,
                grad_wup,
                grad_wdown,
            )
        )
        pieces = lax.psum_scatter(grads, ("fsdp", "ctx"), scatter_dimension=0, tiled=True)
        if index == 0:
            collected = pieces
        else:
            collected = tuple((a + b for a, b in zip(collected, pieces)))
    summed = jax.tree.map(
        lambda part: part.astype(jnp.float32), lax.psum(shortened(collected), "grp")
    )
    shaped = tuple((s.reshape(w.shape) for s, w in zip(summed, shards)))
    return (
        jnp.stack(outputs, 0),
        jnp.stack(input_grads, 0),
        shaped[0],
        shaped[1],
        shaped[2],
        shaped[3],
        shaped[4],
        shaped[5],
        shaped[6],
        shaped[7],
        shaped[8],
    )


GATHER_ORDER = ('f0', 's0', 'f1', 't0', 's1', 'f2', 't1', 's2', 'f3', 't2', 's3', 't3', 'l0', 'l1', 'l2', 'l3')
MESH = pl.DeviceIdType.MESH

def where_am_i():
    return lax.axis_index("grp"), lax.axis_index("fsdp"), lax.axis_index("ctx")

def remote(src, dst, send, recv, grp, fsdp, ctx):
    return pltpu.make_async_remote_copy(src_ref=src, dst_ref=dst, send_sem=send, recv_sem=recv,
        device_id={"grp": grp, "fsdp": fsdp, "ctx": ctx}, device_id_type=MESH)

def greet(partners):
    barrier = pltpu.get_barrier_semaphore()
    for grp, fsdp, ctx in partners:
        pl.semaphore_signal(barrier, inc=1, device_id={"grp": grp, "fsdp": fsdp, "ctx": ctx}, device_id_type=MESH)
    pl.semaphore_wait(barrier, len(partners))


class Column:
    def __init__(self, shard, out):
        self.shard, self.out = shard, out
        self.rows = shard.shape[0]
        self.block = out.shape[1] // 4
    def mine(self, quarter, core):
        return self.shard.at[:, pl.ds(pl.multiple_of((2 * quarter + core) * self.block, 128), self.block)]
    def place(self, plane, core, quarter):
        start = pl.multiple_of((2 * plane + core) * self.rows, 16)
        return self.out.at[pl.ds(start, self.rows), pl.ds(pl.multiple_of(quarter * self.block, 128), self.block)]
    def whole(self, plane, quarter):
        start = pl.multiple_of(2 * plane * self.rows, 16)
        return self.out.at[pl.ds(start, 2 * self.rows), pl.ds(pl.multiple_of(quarter * self.block, 128), self.block)]
    def half(self, plane, quarter, which):
        return self.place(plane, which, quarter)


class Row:
    def __init__(self, shard, out):
        self.shard, self.out = shard, out
        self.rows = shard.shape[0]
        self.block = self.rows // 4
    def mine(self, quarter):
        return self.shard.at[pl.ds(pl.multiple_of(quarter * self.block, 16), self.block), :]
    def whole(self, plane, quarter):
        return self.out.at[pl.ds(pl.multiple_of(plane * self.rows + quarter * self.block, 16), self.block), :]
    def half(self, plane, quarter, which):
        size = self.block // 2
        return self.out.at[pl.ds(pl.multiple_of(plane * self.rows + quarter * self.block + which * size, 16), size), :]


def gather_kernel(order, *refs):
    p_sh, g_sh, u_sh, d_sh, p_out, g_out, u_out, d_out, loc, near_s, near_r, z_s, z_r, xy_s, xy_r, fw_s, fw_r = refs
    grp, plane, core = where_am_i()
    side = grp + 1 - 2 * lax.rem(grp, 2)
    up = lax.rem(grp + 2, 4)
    planes = [lax.rem(plane + s, 4) for s in (1, 2, 3)]
    origins = [lax.rem(plane + 4 - s, 4) for s in (1, 2, 3)]
    partners = [(grp, z, c) for z in planes for c in (core, 1 - core)]
    partners += [(grp, plane, 1 - core), (side, plane, core), (up, plane, core)]
    greet(partners)
    units = [Column(p_sh, p_out), Column(g_sh, g_out), Column(u_sh, u_out), Row(d_sh, d_out)]
    tail = []

    def first(n):
        u = units[n]
        if isinstance(u, Column):
            for i, z in enumerate(planes):
                for j, c in enumerate((core, 1 - core)):
                    d = remote(u.mine(grp, c), u.place(plane, core, grp), z_s.at[n, i, j], z_r.at[n, i, j], grp, z, c)
                    d.start(); tail.append(d.wait_send)
            for q in range(4):
                d = remote(u.mine(q, 1 - core), u.place(plane, core, q), near_s.at[n, q], near_r.at[n, q], grp, plane, 1 - core)
                d.start(); tail.append(d.wait_send)
                d = pltpu.make_async_copy(u.mine(q, core), u.place(plane, core, q), loc.at[n, q])
                d.start(); tail.append(d.wait)
        else:
            for i, z in enumerate(planes):
                d = remote(u.mine(grp), u.whole(plane, grp), z_s.at[n, i, 0], z_r.at[n, i, 0], grp, z, core)
                d.start(); tail.append(d.wait_send)
            d = pltpu.make_async_copy(u.shard, u.out.at[pl.ds(pl.multiple_of(plane * u.rows, 16), u.rows), :], loc.at[n, 0])
            d.start(); tail.append(d.wait)

    def second(n):
        u = units[n]
        for i, z in enumerate(origins):
            if isinstance(u, Column):
                for j, c in enumerate((core, 1 - core)):
                    here = u.place(z, c, grp)
                    remote(here, here, z_s.at[n, i, j], z_r.at[n, i, j], grp, z, c).wait_recv()
            else:
                here = u.whole(z, grp)
                remote(here, here, z_s.at[n, i, 0], z_r.at[n, i, 0], grp, z, core).wait_recv()
            here = u.whole(z, grp)
            for j, to in enumerate((side, up)):
                d = remote(here, here, xy_s.at[n, i, j], xy_r.at[n, i, j], to, plane, core)
                d.start(); tail.append(d.wait_send)

    def third(n):
        u = units[n]
        for i, z in enumerate(origins):
            for j, (frm, to) in enumerate(((side, up), (up, side))):
                here = u.whole(z, frm)
                remote(here, here, xy_s.at[n, i, j], xy_r.at[n, i, j], frm, plane, core).wait_recv()
                part = u.half(z, frm, j)
                d = remote(part, part, fw_s.at[n, i, j], fw_r.at[n, i, j], to, plane, core)
                d.start(); tail.append(d.wait_send)

    def last(n):
        u = units[n]
        far = 3 - grp
        for i, z in enumerate(origins):
            for j, frm in enumerate((up, side)):
                part = u.half(z, far, j)
                remote(part, part, fw_s.at[n, i, j], fw_r.at[n, i, j], frm, plane, core).wait_recv()
        if isinstance(u, Column):
            for q in range(4):
                here = u.place(plane, 1 - core, q)
                remote(here, here, near_s.at[n, q], near_r.at[n, q], grp, plane, 1 - core).wait_recv()

    ops = {'f': first, 's': second, 't': third, 'l': last}
    for word in order: ops[word[0]](int(word[1]))
    for w in tail: w()


def gather(p, g, u, d):
    out = lambda a, b: jax.ShapeDtypeStruct((a, b), jnp.bfloat16)
    rows, cols = p.shape[0] * 8, p.shape[1] // 2
    any_ = pl.BlockSpec(memory_space=pl.ANY)
    dma = pltpu.SemaphoreType.DMA
    return pl.pallas_call(functools.partial(gather_kernel, GATHER_ORDER),
        out_shape=(out(rows, cols),) * 3 + (out(d.shape[0] * 4, d.shape[1]),),
        in_specs=[any_] * 4, out_specs=(any_,) * 4,
        scratch_shapes=[dma((4, 4)), dma((4, 4)), dma((4, 4)), dma((4, 3, 2)), dma((4, 3, 2)), dma((4, 3, 2)), dma((4, 3, 2)), dma((4, 3, 2)), dma((4, 3, 2))],
        compiler_params=pltpu.CompilerParams(collective_id=0, has_side_effects=True),
        name="gather_weights",
    )(p, g, u, d)


REDUCE_ORDER = ('a0', 'a1', 'b0', 'a2', 'b1', 'c0', 'a3', 'b2', 'c1', 'd0', 'b3', 'c2', 'd1', 'e0', 'c3', 'd2', 'e1', 'd3', 'e2', 'e3')

def reduce_kernel(order, *refs):
    grads, outs = refs[:4], refs[4:8]
    accs, recvs, seconds, thirds, fins = refs[8:12], refs[12:16], refs[16:20], refs[20:24], refs[24:28]
    load, s1, r1, s2, r2, s3, r3, s4, r4 = refs[28:]
    grp, plane, core = where_am_i()
    gx, gy = lax.rem(grp, 2), grp // 2
    side, up = grp + 1 - 2 * gx, lax.rem(grp + 2, 4)
    planes = [lax.rem(plane + s, 4) for s in (1, 2, 3)]
    origins = [lax.rem(plane + 4 - s, 4) for s in (1, 2, 3)]
    others = [lax.rem(grp + s, 4) for s in (1, 2, 3)]
    sources = [lax.rem(grp + 4 - s, 4) for s in (1, 2, 3)]
    partners = [(grp, z, core) for z in planes] + [(g, plane, c) for g in others for c in (core, 1 - core)] + [(grp, plane, 1 - core)]
    greet(partners)
    tail = []

    def half(n, z, q, h):
        ref = grads[n]
        if n < 3:
            rows, cols = ref.shape[0] // 8, ref.shape[1] // 4
            return ref.at[pl.ds((2 * z + h) * rows, rows), pl.ds(pl.multiple_of(q * cols, 128), cols)]
        rows = ref.shape[0] // 32
        return ref.at[pl.ds(pl.multiple_of(((4 * z + q) * 2 + h) * rows, 16), rows), :]

    def quarter(path, i, own):
        if path == 0:
            return 2 * i + (gx if own else 1 - gx)
        return 2 * (gy if own else 1 - gy) + i

    first_to, second_to = (side, up), (up, side)
    keep = (gy, gx)

    def a(n):
        for z in range(4):
            for path in range(2):
                for i in range(2):
                    d = pltpu.make_async_copy(half(n, z, quarter(path, i, True), path), accs[n].at[path, z, i], load.at[n, path, z, i])
                    d.start()
                    d = remote(half(n, z, quarter(path, i, False), path), recvs[n].at[path, z, i], s1.at[n, path, z, i], r1.at[n, path, z, i], first_to[path], plane, core)
                    d.start(); tail.append(d.wait_send)

    def b(n):
        for z in range(4):
            for path in range(2):
                for i in range(2):
                    here = accs[n].at[path, z, i]
                    pltpu.make_async_copy(half(n, z, quarter(path, i, True), path), here, load.at[n, path, z, i]).wait()
                    got = recvs[n].at[path, z, i]
                    remote(got, got, s1.at[n, path, z, i], r1.at[n, path, z, i], first_to[path], plane, core).wait_recv()
                    here[...] = (here[...].astype(jnp.float32) + got[...].astype(jnp.float32)).astype(jnp.bfloat16)
                d = remote(accs[n].at[path, z, 1 - keep[path]], seconds[n].at[path, z], s2.at[n, path, z], r2.at[n, path, z], second_to[path], plane, core)
                d.start(); tail.append(d.wait_send)

    def c(n):
        for z in range(4):
            for path in range(2):
                got = seconds[n].at[path, z]
                remote(got, got, s2.at[n, path, z], r2.at[n, path, z], second_to[path], plane, core).wait_recv()
                here = accs[n].at[path, z, keep[path]]
                fins[n][z, path] = (here[...].astype(jnp.float32) + got[...].astype(jnp.float32)).astype(jnp.bfloat16)
        for i, z in enumerate(planes):
            d = remote(fins[n].at[z], thirds[n].at[i], s3.at[n, i], r3.at[n, i], grp, z, core)
            d.start(); tail.append(d.wait_send)

    def sent(n, which, to, c_to, i, j):
        if n < 3:
            rows, cols = outs[n].shape[0], outs[n].shape[1] // 8
            dst = outs[n].at[:, pl.ds(pl.multiple_of((2 * which + c_to[1]) * cols, 128), cols)]
            src = fins[n].at[plane, c_to[0]]
            return src, dst
        rows = outs[n].shape[0] // 8
        dst = outs[n].at[pl.ds(pl.multiple_of((2 * which + j) * rows, 16), rows), :]
        return fins[n].at[plane, j], dst

    def d_(n):
        for i, z in enumerate(origins):
            got = thirds[n].at[i]
            remote(got, got, s3.at[n, i], r3.at[n, i], grp, z, core).wait_recv()
        for j in range(2):
            total = fins[n][plane, j].astype(jnp.float32)
            for i in range(3):
                total += thirds[n][i, j].astype(jnp.float32)
            fins[n][plane, j] = total.astype(jnp.bfloat16)
        for j in range(2):
            target = (core if j == 0 else 1 - core) if n < 3 else core
            src, dst = sent(n, grp, None, (target, core), None, j)
            if n < 3 and j == 1:
                d = remote(src, dst, s4.at[n, 3, j], r4.at[n, 3, j], grp, plane, target)
                d.start(); tail.append(d.wait_send)
            else:
                d = pltpu.make_async_copy(src, dst, s4.at[n, 3, j])
                d.start(); tail.append(d.wait)
            for i, g in enumerate(others):
                d = remote(src, dst, s4.at[n, i, j], r4.at[n, i, j], g, plane, target)
                d.start(); tail.append(d.wait_send)

    def e(n):
        for j in range(2):
            origin = (core if j == 0 else 1 - core) if n < 3 else core
            for i, g in enumerate(sources):
                _, dst = sent(n, g, None, (core, origin), None, j)
                remote(dst, dst, s4.at[n, i, j], r4.at[n, i, j], g, plane, origin).wait_recv()
            if n < 3 and j == 1:
                _, dst = sent(n, grp, None, (core, origin), None, j)
                remote(dst, dst, s4.at[n, 3, j], r4.at[n, 3, j], grp, plane, origin).wait_recv()

    ops = {"a": a, "b": b, "c": c, "d": d_, "e": e}
    for word in order:
        ops[word[0]](int(word[1]))
    for w in tail:
        w()


def reduce_grads(*grads):
    any_ = pl.BlockSpec(memory_space=pl.ANY)
    dma = pltpu.SemaphoreType.DMA
    halves = [(x.shape[0] // 8, x.shape[1] // 4) for x in grads[:3]] + [(grads[3].shape[0] // 32, grads[3].shape[1])]
    def buf(*lead):
        return [pltpu.VMEM(lead + h, jnp.bfloat16) for h in halves]
    out = [jax.ShapeDtypeStruct((x.shape[0] // 8, x.shape[1] * 2), jnp.bfloat16) for x in grads[:3]] + [jax.ShapeDtypeStruct((grads[3].shape[0] // 4, grads[3].shape[1]), jnp.bfloat16)]
    return pl.pallas_call(functools.partial(reduce_kernel, REDUCE_ORDER),
        out_shape=tuple(out), in_specs=[any_] * 4, out_specs=(any_,) * 4,
        scratch_shapes=buf(2, 4, 2) + buf(2, 4, 2) + buf(2, 4) + buf(3, 2) + buf(4, 2) + [
            dma((4, 2, 4, 2)), dma((4, 2, 4, 2)), dma((4, 2, 4, 2)), dma((4, 2, 4)), dma((4, 2, 4)), dma((4, 3)), dma((4, 3)), dma((4, 4, 2)), dma((4, 4, 2))],
        compiler_params=pltpu.CompilerParams(collective_id=1, has_side_effects=True, vmem_limit_bytes=48 * 2**20),
        name="reduce_grads",
    )(*grads)


BLOCK = 256
TO_LOG2 = math.log2(math.e) / math.sqrt(HEAD)
F32, BF16 = jnp.float32, jnp.bfloat16
NN = (((1,), (0,)), ((), ()))
NT = (((1,), (1,)), ((), ()))
TN = (((0,), (0,)), ((), ()))


def dot(a, b, dims=NN):
    return lax.dot_general(a, b, dims, preferred_element_type=F32)


def turned(rows, cosine, sine, sign):
    a, b = rows[: HEAD // 2], rows[HEAD // 2 :]
    return jnp.concatenate([a * cosine - sign * b * sine, b * cosine + sign * a * sine], 0)


def project_kernel(heads, kv_heads, x_ref, w_ref, cos_ref, sin_ref, n_ref, qt_ref, kvt_ref, kv_ref):
    x = x_ref[...].astype(F32)
    inverse = lax.rsqrt(jnp.mean(x * x, -1, keepdims=True) + epsilon)
    normed = (x * inverse).astype(BF16)
    n_ref[...] = normed
    flat = dot(normed, w_ref[:, : (heads + 2 * kv_heads) * HEAD])
    across = flat.T
    cosine, sine = cos_ref[...], sin_ref[...]
    for h in range(heads):
        rows = turned(across[h * HEAD : (h + 1) * HEAD], cosine, sine, 1.0)
        qt_ref[h * HEAD : (h + 1) * HEAD, :] = (rows * TO_LOG2).astype(BF16)
    base = heads * HEAD
    keys = jnp.concatenate([turned(across[base + h * HEAD : base + (h + 1) * HEAD], cosine, sine, 1.0) for h in range(kv_heads)], 0)
    kv_width = kv_heads * HEAD
    values = across[base + kv_width : base + 2 * kv_width]
    kvt_ref[:kv_width, :] = keys.astype(BF16)
    kvt_ref[kv_width:, :] = values.astype(BF16)
    kv_ref[:, :kv_width] = keys.T.astype(BF16)
    kv_ref[:, kv_width:] = flat[:, base + kv_width : base + 2 * kv_width].astype(BF16)


def project(x, weight, cosine, sine, heads, kv_heads, length):
    tokens, width = x.shape
    cols = (heads + 2 * kv_heads) * HEAD
    per = length // BLOCK
    return pl.pallas_call(
        functools.partial(project_kernel, heads, kv_heads),
        grid=(tokens // BLOCK,),
        in_specs=[
            pl.BlockSpec((BLOCK, width), lambda i: (i, 0)),
            pl.BlockSpec((width, -(-cols // 128) * 128), lambda i: (0, 0)),
            pl.BlockSpec((HEAD // 2, BLOCK), lambda i: (0, lax.rem(i, per))),
            pl.BlockSpec((HEAD // 2, BLOCK), lambda i: (0, lax.rem(i, per))),
        ],
        out_specs=(
            pl.BlockSpec((BLOCK, width), lambda i: (i, 0)),
            pl.BlockSpec((heads * HEAD, BLOCK), lambda i: (0, i)),
            pl.BlockSpec((2 * kv_heads * HEAD, BLOCK), lambda i: (0, i)),
            pl.BlockSpec((BLOCK, 2 * kv_heads * HEAD), lambda i: (i, 0)),
        ),
        out_shape=(
            jax.ShapeDtypeStruct((tokens, width), BF16),
            jax.ShapeDtypeStruct((heads * HEAD, tokens), BF16),
            jax.ShapeDtypeStruct((2 * kv_heads * HEAD, tokens), BF16),
            jax.ShapeDtypeStruct((tokens, 2 * kv_heads * HEAD), BF16),
        ),
        compiler_params=pltpu.CompilerParams(vmem_limit_bytes=48 * 2**20),
        cost_estimate=pl.CostEstimate(flops=2 * tokens * width * cols, bytes_accessed=4 * tokens * (width + cols), transcendentals=0),
        name="project",
    )(x, weight, cosine, sine)


def masked(scores, prefix, first, block):
    key = first + lax.broadcasted_iota(jnp.int32, scores.shape, 0)
    query = block * BLOCK + lax.broadcasted_iota(jnp.int32, scores.shape, 1)
    return jnp.where((key <= query) | (key < prefix), scores, -1e30)


def reach(block):
    return max(2, block + 1) * BLOCK


def scores_of(keys, query, prefix, block):
    clear = block * BLOCK
    edge = masked(dot(keys[clear:], query), prefix, clear, block)
    if not clear:
        return edge
    return jnp.concatenate([dot(keys[:clear], query), edge], 0)


def attend_kernel(heads, kv_heads, blocks, prefix_ref, qt_ref, kv_ref, vt_ref, wo_ref, ot_ref, lse_ref, part_ref):
    prefix = prefix_ref[pl.program_id(0)]
    groups = heads // kv_heads

    def run(block):
        n = reach(block)
        for kh in range(kv_heads):
            keys = kv_ref[:n, kh * HEAD : (kh + 1) * HEAD]
            vt = vt_ref[kh * HEAD : (kh + 1) * HEAD, :n]
            for h in range(kh * groups, (kh + 1) * groups):
                scores = scores_of(keys, qt_ref[h * HEAD : (h + 1) * HEAD, :], prefix, block)
                peak = jnp.max(scores, 0, keepdims=True)
                weights = jnp.exp2(scores - peak)
                total = jnp.sum(weights, 0, keepdims=True)
                mixed = dot(vt, weights.astype(BF16)) / total
                ot_ref[h * HEAD : (h + 1) * HEAD, :] = mixed.astype(BF16)
                lse_ref[h : h + 1, :] = peak + jnp.log2(total)

    for block in range(blocks):
        pl.when(pl.program_id(1) == block)(functools.partial(run, block))
    part_ref[...] = dot(ot_ref[...], wo_ref[...], TN).astype(BF16)


def attend(prefix, qt, kv, kvt, wo, heads, kv_heads, length):
    tokens = qt.shape[1]
    width = wo.shape[1]
    count, blocks = tokens // length, length // BLOCK
    kv_width = kv_heads * HEAD
    cells = count * heads * sum(reach(b) for b in range(blocks)) * BLOCK
    return pl.pallas_call(
        functools.partial(attend_kernel, heads, kv_heads, blocks),
        grid=(count, blocks),
        in_specs=[
            pl.BlockSpec(memory_space=pltpu.SMEM),
            pl.BlockSpec((heads * HEAD, BLOCK), lambda s, i: (0, s * blocks + i)),
            pl.BlockSpec((length, 2 * kv_width), lambda s, i: (s, 0)),
            pl.BlockSpec((kv_width, length), lambda s, i: (1, s)),
            pl.BlockSpec((heads * HEAD, width), lambda s, i: (0, 0)),
        ],
        out_specs=(
            pl.BlockSpec((heads * HEAD, BLOCK), lambda s, i: (0, s * blocks + i)),
            pl.BlockSpec((heads, BLOCK), lambda s, i: (0, s * blocks + i)),
            pl.BlockSpec((BLOCK, width), lambda s, i: (s * blocks + i, 0)),
        ),
        out_shape=(
            jax.ShapeDtypeStruct((heads * HEAD, tokens), BF16),
            jax.ShapeDtypeStruct((heads, tokens), F32),
            jax.ShapeDtypeStruct((tokens, width), BF16),
        ),
        compiler_params=pltpu.CompilerParams(vmem_limit_bytes=48 * 2**20),
        cost_estimate=pl.CostEstimate(flops=4 * cells * 256, bytes_accessed=8 * tokens * width, transcendentals=cells),
        name="attend",
    )(prefix, qt, kv, kvt, wo)


def attend_back_kernel(heads, kv_heads, blocks, prefix_ref, qt_ref, kv_ref, kt_ref, ot_ref, lse_ref, dx_ref, wo_ref,
                       cos_ref, sin_ref, cos_all, sin_all, dqt_ref, dkvt_ref, dot_ref, dk_ref, dv_ref):
    prefix = prefix_ref[pl.program_id(0)]
    groups = heads // kv_heads
    kv_width = kv_heads * HEAD
    at = pl.program_id(1)
    dot_ref[...] = dot(wo_ref[...], dx_ref[...], NT).astype(BF16)

    @pl.when(at == 0)
    def _():
        dk_ref[...] = jnp.zeros_like(dk_ref)
        dv_ref[...] = jnp.zeros_like(dv_ref)

    def run(block):
        n = reach(block)
        for kh in range(kv_heads):
            keys = kv_ref[:n, kh * HEAD : (kh + 1) * HEAD]
            values = kv_ref[:n, kv_width + kh * HEAD : kv_width + (kh + 1) * HEAD]
            kt = kt_ref[kh * HEAD : (kh + 1) * HEAD, :n]
            for h in range(kh * groups, (kh + 1) * groups):
                own = slice(h * HEAD, (h + 1) * HEAD)
                query, grad = qt_ref[own, :], dot_ref[own, :]
                delta = jnp.sum(grad.astype(F32) * ot_ref[own, :].astype(F32), 0, keepdims=True)
                scores = scores_of(keys, query, prefix, block)
                probs = jnp.exp2(scores - lse_ref[h : h + 1, :])
                grad_probs = dot(values, grad)
                grad_scores = (probs * (grad_probs - delta)).astype(BF16)
                dv_ref[kh, :n, :] += dot(probs.astype(BF16), grad, NT)
                dk_ref[kh, :n, :] += dot(grad_scores, query, NT)
                grad_query = dot(kt, grad_scores)
                dqt_ref[own, :] = (turned(grad_query, cos_ref[...], sin_ref[...], -1.0) * (1.0 / math.sqrt(HEAD))).astype(BF16)

    for block in range(blocks):
        pl.when(at == block)(functools.partial(run, block))

    @pl.when(at == blocks - 1)
    def _():
        for kh in range(kv_heads):
            rows = turned(dk_ref[kh].T, cos_all[...], sin_all[...], -1.0) * math.log(2.0)
            dkvt_ref[kh * HEAD : (kh + 1) * HEAD, :] = rows.astype(BF16)
            dkvt_ref[kv_width + kh * HEAD : kv_width + (kh + 1) * HEAD, :] = dv_ref[kh].T.astype(BF16)


def attend_back(prefix, qt, kv, kvt, ot, lse, dx, wo, cosine, sine, heads, kv_heads, length):
    tokens = qt.shape[1]
    width = wo.shape[1]
    count, blocks = tokens // length, length // BLOCK
    kv_width = kv_heads * HEAD
    cells = count * heads * sum(reach(b) for b in range(blocks)) * BLOCK
    tile = pl.BlockSpec((heads * HEAD, BLOCK), lambda s, i: (0, s * blocks + i))
    table = pl.BlockSpec((HEAD // 2, BLOCK), lambda s, i: (0, i))
    whole = pl.BlockSpec((HEAD // 2, length), lambda s, i: (0, 0))
    return pl.pallas_call(
        functools.partial(attend_back_kernel, heads, kv_heads, blocks),
        grid=(count, blocks),
        in_specs=[
            pl.BlockSpec(memory_space=pltpu.SMEM),
            tile,
            pl.BlockSpec((length, 2 * kv_width), lambda s, i: (s, 0)),
            pl.BlockSpec((kv_width, length), lambda s, i: (0, s)),
            tile,
            pl.BlockSpec((heads, BLOCK), lambda s, i: (0, s * blocks + i)),
            pl.BlockSpec((BLOCK, width), lambda s, i: (s * blocks + i, 0)),
            pl.BlockSpec((heads * HEAD, width), lambda s, i: (0, 0)),
            table, table, whole, whole,
        ],
        out_specs=(tile, pl.BlockSpec((2 * kv_width, length), lambda s, i: (0, s))),
        out_shape=(
            jax.ShapeDtypeStruct((heads * HEAD, tokens), BF16),
            jax.ShapeDtypeStruct((2 * kv_width, tokens), BF16),
        ),
        scratch_shapes=[
            pltpu.VMEM((heads * HEAD, BLOCK), BF16),
            pltpu.VMEM((kv_heads, length, HEAD), F32),
            pltpu.VMEM((kv_heads, length, HEAD), F32),
        ],
        compiler_params=pltpu.CompilerParams(vmem_limit_bytes=48 * 2**20),
        cost_estimate=pl.CostEstimate(flops=10 * cells * 256, bytes_accessed=12 * tokens * width, transcendentals=cells),
        name="attend_back",
    )(prefix, qt, kv, kvt, ot, lse, dx, wo, cosine, sine, cosine, sine)


SWAP = [(0, 1), (1, 0)]


def trade(mine):
    return lax.ppermute(mine, "ctx", SWAP)


def ordered(core, mine, other, axis):
    return jnp.concatenate([jnp.where(core == 0, mine, other), jnp.where(core == 0, other, mine)], axis)


def part_of(array, which, axis):
    size = array.shape[axis] // 2
    return lax.dynamic_slice_in_dim(array, which * size, size, axis)


def tables(length):
    frequency = np.float32(10000.0) ** (-np.arange(HEAD // 2, dtype=np.float32) * np.float32(2.0) / np.float32(HEAD))
    angles = frequency[:, None] * np.arange(length, dtype=np.float32)[None, :]
    return jnp.asarray(np.cos(angles)), jnp.asarray(np.sin(angles))


def paired(
    activations_in,
    prefix_len,
    attn_gain,
    query_weight,
    key_weight,
    value_weight,
    out_weight,
    ffn_gain,
    gate_weight,
    up_weight,
    down_weight,
    cotangent,
):
    micro, seq_count, span, width = activations_in.shape
    count, length = micro * seq_count, 2 * span
    core = lax.axis_index("ctx")
    heads, kv_heads = HEADS // 2, KV_HEADS // 2
    q_cols, kv_cols = heads * HEAD, kv_heads * HEAD
    shard = attn_gain.shape[0]

    own_x = activations_in.reshape(count, span, width)
    own_dy = cotangent.reshape(count, span, width)

    def whole(mine):
        return ordered(core, mine, trade(mine), 1).reshape(count * length, width)

    def summed(part):
        part = part.reshape(count, length, width)
        theirs = trade(part_of(part, 1 - core, 1))
        return part_of(part, core, 1).astype(F32) + theirs.astype(F32)

    gain_attn = attn_gain.astype(F32)[:, None]
    gain_ffn = ffn_gain.astype(F32)[:, None]
    qkv = [w.astype(F32) for w in (query_weight, key_weight, value_weight)]
    first = [(w * gain_attn).astype(BF16).reshape(shard, 2, -1) for w in qkv]
    pack = jnp.concatenate(first + [out_weight.reshape(shard, 2, -1)], -1)
    pack = pack.reshape(shard, 2, 4, -1).swapaxes(1, 2).reshape(shard, -1)
    w_pack, w_gate, w_up, w_down = gather(
        pack, (gate_weight * gain_ffn).astype(BF16), (up_weight * gain_ffn).astype(BF16), down_weight
    )
    w_out_cols = w_pack[:, q_cols + 2 * kv_cols :]
    w_out = ordered(core, part_of(w_out_cols, core, 0), trade(part_of(w_out_cols, 1 - core, 0)), 1)

    cosine, sine = tables(length)
    prefix = prefix_len.reshape(count)
    full_x, full_dy = whole(own_x), whole(own_dy)
    normed_one, qt, kvt, kv = project(full_x, w_pack, cosine, sine, heads, kv_heads, length)
    ot, lse, part = attend(prefix, qt, kv, kvt, w_out, heads, kv_heads, length)
    middle = own_x.astype(F32) + summed(part)
    inverse_two = lax.rsqrt(jnp.mean(middle * middle, -1, keepdims=True) + epsilon)
    normed_two = middle * inverse_two
    full_two = whole(normed_two.astype(BF16))
    gate = dot(full_two, w_gate)
    upward = dot(full_two, w_up)
    hidden = (jax.nn.silu(gate) * upward).astype(BF16)
    result = middle + summed(dot(hidden, w_down).astype(BF16))

    gate, upward = gate.astype(BF16).astype(F32), upward.astype(BF16).astype(F32)
    grad_down = dot(hidden, full_dy, TN).astype(BF16)
    grad_hidden = dot(full_dy, w_down, NT)
    sigma = jax.nn.sigmoid(gate)
    d_up = (grad_hidden * gate * sigma).astype(BF16)
    d_gate = (grad_hidden * upward * sigma * (1.0 + gate * (1.0 - sigma))).astype(BF16)
    grad_gate = dot(full_two, d_gate, TN).astype(BF16)
    grad_up = dot(full_two, d_up, TN).astype(BF16)
    grad_two = summed((dot(d_gate, w_gate, NT) + dot(d_up, w_up, NT)).astype(BF16))
    grad_middle = own_dy.astype(F32) + norm_back(grad_two, normed_two, inverse_two)
    full_dx = whole(grad_middle.astype(BF16))
    grad_out_rows = dot(ot, full_dx).astype(BF16)
    dqt, dkvt = attend_back(prefix, qt, kv, kvt, ot, lse, full_dx, w_out, cosine, sine, heads, kv_heads, length)
    dt = jnp.concatenate([dqt, dkvt], 0)
    grad_qkv = dot(normed_one, dt, (((0,), (1,)), ((), ()))).astype(BF16)
    grad_one = summed(dot(dt, w_pack[:, : q_cols + 2 * kv_cols], (((0,), (1,)), ((), ()))).astype(BF16))
    x = own_x.astype(F32)
    inverse_one = lax.rsqrt(jnp.mean(x * x, -1, keepdims=True) + epsilon)
    grad_inputs = grad_middle + norm_back(grad_one, x * inverse_one, inverse_one)

    grad_out_cols = ordered(core, part_of(grad_out_rows, core, 1), trade(part_of(grad_out_rows, 1 - core, 1)), 0)
    grad_pack = jnp.concatenate([grad_qkv, grad_out_cols], 1)
    r_pack, r_gate, r_up, r_down = (g.astype(F32) for g in reduce_grads(grad_pack, grad_gate, grad_up, grad_down))
    r_pack = r_pack.reshape(shard, 4, 2, -1).swapaxes(1, 2).reshape(shard, 2, -1)
    r_q, r_k, r_v, r_out = (
        piece.reshape(shard, -1)
        for piece in jnp.split(r_pack, [q_cols, q_cols + kv_cols, q_cols + 2 * kv_cols], axis=2)
    )
    grad_gain_attn = sum(jnp.sum(w * r, -1) for w, r in zip(qkv, (r_q, r_k, r_v)))
    grad_gain_ffn = jnp.sum(gate_weight * r_gate, -1) + jnp.sum(up_weight * r_up, -1)
    shape = activations_in.shape
    return (
        result.astype(BF16).reshape(shape),
        grad_inputs.astype(BF16).reshape(shape),
        grad_gain_attn,
        r_q * gain_attn,
        r_k * gain_attn,
        r_v * gain_attn,
        r_out,
        grad_gain_ffn,
        r_gate * gain_ffn,
        r_up * gain_ffn,
        r_down,
    )


def solution(mesh):
    small = dict(mesh.shape) == {"grp": 4, "fsdp": 4, "ctx": 2}

    return jax.shard_map(
        paired if small else local,
        mesh=mesh,
        in_specs=(
            P(None, ("grp", "fsdp"), "ctx", None),
            P(None, ("grp", "fsdp")),
            P(("fsdp", "ctx")),
            P(("fsdp", "ctx"), None),
            P(("fsdp", "ctx"), None),
            P(("fsdp", "ctx"), None),
            P(("fsdp", "ctx"), None),
            P(("fsdp", "ctx")),
            P(("fsdp", "ctx"), None),
            P(("fsdp", "ctx"), None),
            P(("fsdp", "ctx"), None),
            P(None, ("grp", "fsdp"), "ctx", None),
        ),
        out_specs=(
            P(None, ("grp", "fsdp"), "ctx", None),
            P(None, ("grp", "fsdp"), "ctx", None),
            P(("fsdp", "ctx")),
            P(("fsdp", "ctx"), None),
            P(("fsdp", "ctx"), None),
            P(("fsdp", "ctx"), None),
            P(("fsdp", "ctx"), None),
            P(("fsdp", "ctx")),
            P(("fsdp", "ctx"), None),
            P(("fsdp", "ctx"), None),
            P(("fsdp", "ctx"), None),
        ),
        check_vma=False,
    )
```

```python
import functools
import math

import jax
import jax.numpy as jnp
import numpy as np
from jax import lax
from jax.experimental import pallas as pl
from jax.experimental.pallas import tpu as pltpu
from jax.sharding import PartitionSpec as P

HEADS = 18
KV_HEADS = 6
HEAD = 64


epsilon = 1e-05


def shortened(array):

    def short(part):
        return part.astype(jnp.bfloat16) if part.dtype == jnp.float32 else part

    return jax.tree.map(short, array)


def rotary_tables(positions):
    halfway = HEAD // 2
    frequency = 10000.0 ** (-jnp.arange(halfway, dtype=jnp.float32) * 2.0 / HEAD)
    angles = positions.astype(jnp.float32)[:, None] * frequency[None, :]
    return (jnp.cos(angles)[:, None, :], jnp.sin(angles)[:, None, :])


def rotate(values, cosine, sine):
    halfway = values.shape[-1] // 2
    first = values[..., :halfway]
    second = values[..., halfway:]
    return jnp.concatenate([first * cosine - second * sine, second * cosine + first * sine], -1)


def rotate_back(values, cosine, sine):
    halfway = values.shape[-1] // 2
    first = values[..., :halfway]
    second = values[..., halfway:]
    return jnp.concatenate([first * cosine + second * sine, second * cosine - first * sine], -1)


def norm_back(grad_normed, normed, inverse):
    return inverse * (grad_normed - normed * jnp.mean(grad_normed * normed, -1, keepdims=True))


def flatten_all(grads):
    return tuple((g.reshape(-1) for g in grads))


def local(
    activations_in,
    prefix_len,
    attn_gain,
    query_weight,
    key_weight,
    value_weight,
    out_weight,
    ffn_gain,
    gate_weight,
    up_weight,
    down_weight,
    cotangent,
):
    micro, seq_count, span, width = activations_in.shape
    rows = seq_count * span
    length = span * lax.axis_size("ctx")
    groups = HEADS // KV_HEADS
    scale = 1.0 / math.sqrt(HEAD)
    shards = (
        attn_gain,
        query_weight,
        key_weight,
        value_weight,
        out_weight,
        ffn_gain,
        gate_weight,
        up_weight,
        down_weight,
    )
    offset = lax.axis_index("ctx") * span
    query_pos = offset + jnp.arange(span, dtype=jnp.int32)
    key_pos = jnp.arange(length, dtype=jnp.int32)
    cosine, sine = rotary_tables(jnp.tile(query_pos, seq_count))

    def visibility(prefix):
        return (key_pos[None, :] <= query_pos[:, None]) | (key_pos[None, :] < prefix)

    def attend(item):
        query, keys, values, prefix = item
        scores = (
            jnp.einsum("qhgd,khd->hgqk", query, keys, preferred_element_type=jnp.float32) * scale
        )
        scores = jnp.where(visibility(prefix), scores, -1e30)
        peak = jnp.max(scores, -1, keepdims=True)
        weights = jnp.exp(scores - peak)
        totals = jnp.sum(weights, -1, keepdims=True)
        probs = (weights / totals).astype(jnp.bfloat16)
        mixed = jnp.einsum("hgqk,khd->qhgd", probs, values, preferred_element_type=jnp.float32)
        return (mixed.reshape(span, HEADS * HEAD), (peak + jnp.log(totals))[..., 0])

    def attend_back(item):
        query, keys, values, prefix, log_total, grad_mixed = item
        scores = (
            jnp.einsum("qhgd,khd->hgqk", query, keys, preferred_element_type=jnp.float32) * scale
        )
        probs = jnp.where(visibility(prefix), jnp.exp(scores - log_total[..., None]), 0.0)
        grad_probs = jnp.einsum(
            "qhgd,khd->hgqk", grad_mixed, values, preferred_element_type=jnp.float32
        )
        grad_scores = (
            probs * (grad_probs - jnp.sum(probs * grad_probs, -1, keepdims=True))
        ).astype(jnp.bfloat16)
        grad_query = (
            jnp.einsum("hgqk,khd->qhgd", grad_scores, keys, preferred_element_type=jnp.float32)
            * scale
        )
        grad_keys = (
            jnp.einsum("hgqk,qhgd->khd", grad_scores, query, preferred_element_type=jnp.float32)
            * scale
        )
        grad_values = jnp.einsum(
            "hgqk,qhgd->khd",
            probs.astype(jnp.bfloat16),
            grad_mixed,
            preferred_element_type=jnp.float32,
        )
        return (
            grad_query.reshape(span, HEADS * HEAD),
            grad_keys.reshape(length, KV_HEADS * HEAD),
            grad_values.reshape(length, KV_HEADS * HEAD),
        )

    outputs = []
    input_grads = []
    collected = None
    for index in range(micro):
        full = (
            lax.all_gather(shards[0], ("fsdp", "ctx"), axis=0, tiled=True),
            lax.all_gather(shards[1], ("fsdp", "ctx"), axis=0, tiled=True),
            lax.all_gather(shards[2], ("fsdp", "ctx"), axis=0, tiled=True),
            lax.all_gather(shards[3], ("fsdp", "ctx"), axis=0, tiled=True),
            lax.all_gather(shards[4], ("fsdp", "ctx"), axis=0, tiled=True),
            lax.all_gather(shards[5], ("fsdp", "ctx"), axis=0, tiled=True),
            lax.all_gather(shards[6], ("fsdp", "ctx"), axis=0, tiled=True),
            lax.all_gather(shards[7], ("fsdp", "ctx"), axis=0, tiled=True),
            lax.all_gather(shards[8], ("fsdp", "ctx"), axis=0, tiled=True),
        )
        gain_attn, w_query, w_key, w_value, w_out, gain_ffn, w_gate, w_up, w_down = full
        inputs = activations_in[index].reshape(rows, width).astype(jnp.float32)
        inverse_one = lax.rsqrt(jnp.mean(inputs * inputs, -1, keepdims=True) + epsilon)
        normed_one = inputs * inverse_one
        first_in = (normed_one * gain_attn).astype(jnp.bfloat16)
        query_lin = jnp.dot(first_in, w_query, preferred_element_type=jnp.float32)
        key_lin = jnp.dot(first_in, w_key, preferred_element_type=jnp.float32)
        value_lin = jnp.dot(first_in, w_value, preferred_element_type=jnp.float32)
        query_rot = rotate(query_lin.reshape(rows, HEADS, HEAD), cosine, sine).astype(jnp.bfloat16)
        key_rot = rotate(key_lin.reshape(rows, KV_HEADS, HEAD), cosine, sine).astype(jnp.bfloat16)
        key_rot = key_rot.reshape(seq_count, span, KV_HEADS * HEAD)
        value_low = value_lin.astype(jnp.bfloat16).reshape(seq_count, span, KV_HEADS * HEAD)
        key_all, value_all = (
            lax.all_gather(key_rot, "ctx", axis=1, tiled=True),
            lax.all_gather(value_low, "ctx", axis=1, tiled=True),
        )
        query_split = query_rot.reshape(seq_count, span, KV_HEADS, groups, HEAD)
        key_split = key_all.reshape(seq_count, length, KV_HEADS, HEAD)
        value_split = value_all.reshape(seq_count, length, KV_HEADS, HEAD)
        mixed_all, log_totals = lax.map(
            attend, (query_split, key_split, value_split, prefix_len[index])
        )
        attn_low = mixed_all.reshape(rows, HEADS * HEAD).astype(jnp.bfloat16)
        middle = inputs + jnp.dot(attn_low, w_out, preferred_element_type=jnp.float32)
        inverse_two = lax.rsqrt(jnp.mean(middle * middle, -1, keepdims=True) + epsilon)
        normed_two = middle * inverse_two
        second_in = (normed_two * gain_ffn).astype(jnp.bfloat16)
        gate = jnp.dot(second_in, w_gate, preferred_element_type=jnp.float32)
        upward = jnp.dot(second_in, w_up, preferred_element_type=jnp.float32)
        hidden = (jax.nn.silu(gate) * upward).astype(jnp.bfloat16)
        result = middle + jnp.dot(hidden, w_down, preferred_element_type=jnp.float32)
        outputs.append(result.astype(jnp.bfloat16).reshape(seq_count, span, width))
        back = (
            lax.all_gather(shards[0], ("fsdp", "ctx"), axis=0, tiled=True),
            lax.all_gather(shards[1], ("fsdp", "ctx"), axis=0, tiled=True),
            lax.all_gather(shards[2], ("fsdp", "ctx"), axis=0, tiled=True),
            lax.all_gather(shards[3], ("fsdp", "ctx"), axis=0, tiled=True),
            lax.all_gather(shards[4], ("fsdp", "ctx"), axis=0, tiled=True),
            lax.all_gather(shards[5], ("fsdp", "ctx"), axis=0, tiled=True),
            lax.all_gather(shards[6], ("fsdp", "ctx"), axis=0, tiled=True),
            lax.all_gather(shards[7], ("fsdp", "ctx"), axis=0, tiled=True),
            lax.all_gather(shards[8], ("fsdp", "ctx"), axis=0, tiled=True),
        )
        gain_attn, w_query, w_key, w_value, w_out, gain_ffn, w_gate, w_up, w_down = back
        grad_y = cotangent[index].reshape(rows, width).astype(jnp.float32)
        grad_y_low = grad_y.astype(jnp.bfloat16)
        grad_wdown = jnp.einsum("rf,rd->fd", hidden, grad_y_low, preferred_element_type=jnp.float32)
        grad_hidden = jnp.einsum(
            "rd,fd->rf", grad_y_low, w_down, preferred_element_type=jnp.float32
        )
        sigma = jax.nn.sigmoid(gate)
        grad_up_low = (grad_hidden * gate * sigma).astype(jnp.bfloat16)
        grad_gate_low = (grad_hidden * upward * sigma * (1.0 + gate * (1.0 - sigma))).astype(
            jnp.bfloat16
        )
        grad_wgate = jnp.einsum(
            "rd,rf->df", second_in, grad_gate_low, preferred_element_type=jnp.float32
        )
        grad_wup = jnp.einsum(
            "rd,rf->df", second_in, grad_up_low, preferred_element_type=jnp.float32
        )
        grad_second = jnp.einsum(
            "rf,df->rd", grad_gate_low, w_gate, preferred_element_type=jnp.float32
        ) + jnp.einsum("rf,df->rd", grad_up_low, w_up, preferred_element_type=jnp.float32)
        grad_gain_ffn = jnp.sum(grad_second * normed_two, 0)
        grad_middle = grad_y + norm_back(grad_second * gain_ffn, normed_two, inverse_two)
        grad_branch_low = grad_middle.astype(jnp.bfloat16)
        grad_wout = jnp.einsum(
            "ra,rd->ad", attn_low, grad_branch_low, preferred_element_type=jnp.float32
        )
        grad_attn_low = jnp.einsum(
            "rd,ad->ra", grad_branch_low, w_out, preferred_element_type=jnp.float32
        ).astype(jnp.bfloat16)
        grad_mixed = grad_attn_low.reshape(seq_count, span, KV_HEADS, groups, HEAD)
        grad_query_rot, grad_key_part, grad_value_part = lax.map(
            attend_back,
            (query_split, key_split, value_split, prefix_len[index], log_totals, grad_mixed),
        )
        grad_key_own, grad_value_own = (
            lax.psum_scatter(
                grad_key_part.astype(jnp.bfloat16), "ctx", scatter_dimension=1, tiled=True
            ).astype(jnp.float32),
            lax.psum_scatter(
                grad_value_part.astype(jnp.bfloat16), "ctx", scatter_dimension=1, tiled=True
            ).astype(jnp.float32),
        )
        grad_query = rotate_back(grad_query_rot.reshape(rows, HEADS, HEAD), cosine, sine)
        grad_query = grad_query.reshape(rows, HEADS * HEAD).astype(jnp.bfloat16)
        grad_key = rotate_back(grad_key_own.reshape(rows, KV_HEADS, HEAD), cosine, sine)
        grad_key = grad_key.reshape(rows, KV_HEADS * HEAD).astype(jnp.bfloat16)
        grad_value = grad_value_own.reshape(rows, KV_HEADS * HEAD).astype(jnp.bfloat16)
        grad_wquery = jnp.einsum(
            "rd,rq->dq", first_in, grad_query, preferred_element_type=jnp.float32
        )
        grad_wkey = jnp.einsum("rd,rq->dq", first_in, grad_key, preferred_element_type=jnp.float32)
        grad_wvalue = jnp.einsum(
            "rd,rq->dq", first_in, grad_value, preferred_element_type=jnp.float32
        )
        grad_first = (
            jnp.einsum("rq,dq->rd", grad_query, w_query, preferred_element_type=jnp.float32)
            + jnp.einsum("rq,dq->rd", grad_key, w_key, preferred_element_type=jnp.float32)
            + jnp.einsum("rq,dq->rd", grad_value, w_value, preferred_element_type=jnp.float32)
        )
        grad_gain_attn = jnp.sum(grad_first * normed_one, 0)
        grad_inputs = grad_middle + norm_back(grad_first * gain_attn, normed_one, inverse_one)
        input_grads.append(grad_inputs.astype(jnp.bfloat16).reshape(seq_count, span, width))
        grads = flatten_all(
            (
                grad_gain_attn,
                grad_wquery,
                grad_wkey,
                grad_wvalue,
                grad_wout,
                grad_gain_ffn,
                grad_wgate,
                grad_wup,
                grad_wdown,
            )
        )
        pieces = lax.psum_scatter(grads, ("fsdp", "ctx"), scatter_dimension=0, tiled=True)
        if index == 0:
            collected = pieces
        else:
            collected = tuple((a + b for a, b in zip(collected, pieces)))
    summed = jax.tree.map(
        lambda part: part.astype(jnp.float32), lax.psum(shortened(collected), "grp")
    )
    shaped = tuple((s.reshape(w.shape) for s, w in zip(summed, shards)))
    return (
        jnp.stack(outputs, 0),
        jnp.stack(input_grads, 0),
        shaped[0],
        shaped[1],
        shaped[2],
        shaped[3],
        shaped[4],
        shaped[5],
        shaped[6],
        shaped[7],
        shaped[8],
    )


BLOCK = 256
TO_LOG2 = math.log2(math.e) / math.sqrt(HEAD)
F32, BF16 = jnp.float32, jnp.bfloat16
NN = (((1,), (0,)), ((), ()))
NT = (((1,), (1,)), ((), ()))
TN = (((0,), (0,)), ((), ()))


def dot(a, b, dims=NN):
    return lax.dot_general(a, b, dims, preferred_element_type=F32)


def turned(rows, cosine, sine, sign):
    a, b = rows[: HEAD // 2], rows[HEAD // 2 :]
    return jnp.concatenate([a * cosine - sign * b * sine, b * cosine + sign * a * sine], 0)


def masked(scores, prefix, first, block):
    key = first + lax.broadcasted_iota(jnp.int32, scores.shape, 0)
    query = block * BLOCK + lax.broadcasted_iota(jnp.int32, scores.shape, 1)
    return jnp.where((key <= query) | (key < prefix), scores, -1e30)


def reach(block):
    return max(2, block + 1) * BLOCK


def scores_of(keys, query, prefix, block):
    clear = block * BLOCK
    edge = masked(dot(keys[clear:], query), prefix, clear, block)
    if not clear:
        return edge
    return jnp.concatenate([dot(keys[:clear], query), edge], 0)


def attend_back_kernel(heads, kv_heads, blocks, prefix_ref, qt_ref, kv_ref, kt_ref, ot_ref, lse_ref, dx_ref, wo_ref,
                       cos_ref, sin_ref, cos_all, sin_all, dqt_ref, dkvt_ref, dot_ref, dk_ref, dv_ref):
    prefix = prefix_ref[pl.program_id(0)]
    groups = heads // kv_heads
    kv_width = kv_heads * HEAD
    at = pl.program_id(1)
    dot_ref[...] = dot(wo_ref[...], dx_ref[...], NT).astype(BF16)

    @pl.when(at == 0)
    def _():
        dk_ref[...] = jnp.zeros_like(dk_ref)
        dv_ref[...] = jnp.zeros_like(dv_ref)

    def run(block):
        n = reach(block)
        for kh in range(kv_heads):
            keys = kv_ref[:n, kh * HEAD : (kh + 1) * HEAD]
            values = kv_ref[:n, kv_width + kh * HEAD : kv_width + (kh + 1) * HEAD]
            kt = kt_ref[kh * HEAD : (kh + 1) * HEAD, :n]
            for h in range(kh * groups, (kh + 1) * groups):
                own = slice(h * HEAD, (h + 1) * HEAD)
                query, grad = qt_ref[own, :], dot_ref[own, :]
                delta = jnp.sum(grad.astype(F32) * ot_ref[own, :].astype(F32), 0, keepdims=True)
                scores = scores_of(keys, query, prefix, block)
                probs = jnp.exp2(scores - lse_ref[h : h + 1, :])
                grad_probs = dot(values, grad)
                grad_scores = (probs * (grad_probs - delta)).astype(BF16)
                dv_ref[kh, :n, :] += dot(probs.astype(BF16), grad, NT)
                dk_ref[kh, :n, :] += dot(grad_scores, query, NT)
                grad_query = dot(kt, grad_scores)
                dqt_ref[own, :] = (turned(grad_query, cos_ref[...], sin_ref[...], -1.0) * (1.0 / math.sqrt(HEAD))).astype(BF16)

    for block in range(blocks):
        pl.when(at == block)(functools.partial(run, block))

    @pl.when(at == blocks - 1)
    def _():
        for kh in range(kv_heads):
            rows = turned(dk_ref[kh].T, cos_all[...], sin_all[...], -1.0) * math.log(2.0)
            dkvt_ref[kh * HEAD : (kh + 1) * HEAD, :] = rows.astype(BF16)
            dkvt_ref[kv_width + kh * HEAD : kv_width + (kh + 1) * HEAD, :] = dv_ref[kh].T.astype(BF16)


def attend_back(prefix, qt, kv, kvt, ot, lse, dx, wo, cosine, sine, heads, kv_heads, length):
    tokens = qt.shape[1]
    width = wo.shape[1]
    count, blocks = tokens // length, length // BLOCK
    kv_width = kv_heads * HEAD
    cells = count * heads * sum(reach(b) for b in range(blocks)) * BLOCK
    tile = pl.BlockSpec((heads * HEAD, BLOCK), lambda s, i: (0, s * blocks + i))
    table = pl.BlockSpec((HEAD // 2, BLOCK), lambda s, i: (0, i))
    whole = pl.BlockSpec((HEAD // 2, length), lambda s, i: (0, 0))
    return pl.pallas_call(
        functools.partial(attend_back_kernel, heads, kv_heads, blocks),
        grid=(count, blocks),
        in_specs=[
            pl.BlockSpec(memory_space=pltpu.SMEM),
            tile,
            pl.BlockSpec((length, 2 * kv_width), lambda s, i: (s, 0)),
            pl.BlockSpec((kv_width, length), lambda s, i: (0, s)),
            tile,
            pl.BlockSpec((heads, BLOCK), lambda s, i: (0, s * blocks + i)),
            pl.BlockSpec((BLOCK, width), lambda s, i: (s * blocks + i, 0)),
            pl.BlockSpec((heads * HEAD, width), lambda s, i: (0, 0)),
            table, table, whole, whole,
        ],
        out_specs=(tile, pl.BlockSpec((2 * kv_width, length), lambda s, i: (0, s))),
        out_shape=(
            jax.ShapeDtypeStruct((heads * HEAD, tokens), BF16),
            jax.ShapeDtypeStruct((2 * kv_width, tokens), BF16),
        ),
        scratch_shapes=[
            pltpu.VMEM((heads * HEAD, BLOCK), BF16),
            pltpu.VMEM((kv_heads, length, HEAD), F32),
            pltpu.VMEM((kv_heads, length, HEAD), F32),
        ],
        compiler_params=pltpu.CompilerParams(vmem_limit_bytes=48 * 2**20),
        cost_estimate=pl.CostEstimate(flops=10 * cells * 256, bytes_accessed=12 * tokens * width, transcendentals=cells),
        name="attend_back",
    )(prefix, qt, kv, kvt, ot, lse, dx, wo, cosine, sine, cosine, sine)


MESH = pl.DeviceIdType.MESH
DMA = pltpu.SemaphoreType.DMA
ANY = pl.BlockSpec(memory_space=pl.ANY)
VMEM = pl.BlockSpec(memory_space=pltpu.VMEM)


def where_am_i():
    return lax.axis_index("grp"), lax.axis_index("fsdp"), lax.axis_index("ctx")


def remote(src, dst, send, recv, grp, fsdp, ctx):
    return pltpu.make_async_remote_copy(
        src_ref=src,
        dst_ref=dst,
        send_sem=send,
        recv_sem=recv,
        device_id={"grp": grp, "fsdp": fsdp, "ctx": ctx},
        device_id_type=MESH,
    )


def greet(partners):
    barrier = pltpu.get_barrier_semaphore()
    for grp, fsdp, ctx in partners:
        pl.semaphore_signal(
            barrier, inc=1, device_id={"grp": grp, "fsdp": fsdp, "ctx": ctx}, device_id_type=MESH
        )
    pl.semaphore_wait(barrier, len(partners))


class Columns:
    split = True

    def __init__(self, core, shard, out):
        self.core, self.shard, self.out = core, shard, out
        self.rows, self.cols = shard.shape[0], out.shape[1] // 4

    def mine(self, j, quarter):
        to = self.core if j == 0 else 1 - self.core
        return self.shard.at[:, pl.ds(pl.multiple_of((2 * quarter + to) * self.cols, 128), self.cols)]

    def block(self, plane, j, quarter):
        owner = self.core if j == 0 else 1 - self.core
        start = pl.multiple_of((2 * plane + owner) * self.rows, 16)
        return self.out.at[pl.ds(start, self.rows), pl.ds(pl.multiple_of(quarter * self.cols, 128), self.cols)]


class Rows:
    split = False

    def __init__(self, core, shard, out):
        self.core, self.shard, self.out = core, shard, out
        self.rows = shard.shape[0] // 8

    def mine(self, j, quarter):
        return self.shard.at[pl.ds(pl.multiple_of((2 * quarter + j) * self.rows, 16), self.rows), :]

    def block(self, plane, j, quarter):
        start = pl.multiple_of((8 * plane + 2 * quarter + j) * self.rows, 16)
        return self.out.at[pl.ds(start, self.rows), :]

    def own(self, plane):
        return self.out.at[pl.ds(pl.multiple_of(plane * 8 * self.rows, 16), 8 * self.rows), :]


class Gather:
    @staticmethod
    def semaphores(count):
        return [DMA((count, 4)), DMA((count, 4)), DMA((count, 4))] + [DMA((count, 3, 2))] * 2 + [DMA((count, 3, 2, 2))] * 2 + [DMA((count, 3, 2))] * 2

    def __init__(self, units, sems):
        self.units, self.sems = units, sems
        self.grp, self.plane, self.core = where_am_i()
        self.side = self.grp + 1 - 2 * lax.rem(self.grp, 2)
        self.up = lax.rem(self.grp + 2, 4)
        self.planes = [lax.rem(self.plane + s, 4) for s in (1, 2, 3)]
        self.origins = [lax.rem(self.plane + 4 - s, 4) for s in (1, 2, 3)]
        self.left = []

    def partners(self):
        grp, plane, core = self.grp, self.plane, self.core
        found = [(grp, z, c) for z in self.planes for c in (core, 1 - core)]
        return found + [(grp, plane, 1 - core), (self.side, plane, core), (self.up, plane, core)]

    def other(self, j):
        return self.core if j == 0 else 1 - self.core

    def send(self, src, dst, send, recv, grp, plane, core):
        copy = remote(src, dst, send, recv, grp, plane, core)
        copy.start()
        self.left.append(copy.wait_send)

    def got(self, here, send, recv):
        remote(here, here, send, recv, self.side, self.plane, self.core).wait_recv()

    def first(self, n):
        u = self.units[n]
        loc, near_s, near_r, z_s, z_r = self.sems[:5]
        for i, z in enumerate(self.planes):
            for j in range(2):
                if u.split:
                    dst = u.block(self.plane, 0, self.grp)
                    self.send(u.mine(j, self.grp), dst, z_s.at[n, i, j], z_r.at[n, i, j], self.grp, z, self.other(j))
                else:
                    dst = u.block(self.plane, j, self.grp)
                    self.send(u.mine(j, self.grp), dst, z_s.at[n, i, j], z_r.at[n, i, j], self.grp, z, self.core)
        if u.split:
            for q in range(4):
                dst = u.block(self.plane, 0, q)
                self.send(u.mine(1, q), dst, near_s.at[n, q], near_r.at[n, q], self.grp, self.plane, 1 - self.core)
                copy = pltpu.make_async_copy(u.mine(0, q), dst, loc.at[n, q])
                copy.start()
                self.left.append(copy.wait)
        else:
            copy = pltpu.make_async_copy(u.shard, u.own(self.plane), loc.at[n, 0])
            copy.start()
            self.left.append(copy.wait)

    def first_in(self, n):
        u = self.units[n]
        for i, z in enumerate(self.origins):
            for j in range(2):
                self.got(u.block(z, j, self.grp), self.sems[3].at[n, i, j], self.sems[4].at[n, i, j])

    def near_in(self, n):
        u = self.units[n]
        if u.split:
            for q in range(4):
                self.got(u.block(self.plane, 1, q), self.sems[1].at[n, q], self.sems[2].at[n, q])

    def second(self, n, here=False):
        u = self.units[n]
        z_s, z_r, xy_s, xy_r = self.sems[3:7]
        for i, z in enumerate(self.origins):
            for j in range(2):
                block = u.block(z, j, self.grp)
                if not here:
                    self.got(block, z_s.at[n, i, j], z_r.at[n, i, j])
                for t, to in enumerate((self.side, self.up)):
                    self.send(block, block, xy_s.at[n, i, j, t], xy_r.at[n, i, j, t], to, self.plane, self.core)

    def third(self, n):
        u = self.units[n]
        xy_s, xy_r, fw_s, fw_r = self.sems[5:9]
        for i, z in enumerate(self.origins):
            for t, (origin, to) in enumerate(((self.side, self.up), (self.up, self.side))):
                block = u.block(z, t, origin)
                self.got(block, xy_s.at[n, i, t, t], xy_r.at[n, i, t, t])
                self.send(block, block, fw_s.at[n, i, t], fw_r.at[n, i, t], to, self.plane, self.core)

    def last(self, n):
        u = self.units[n]
        xy_s, xy_r, fw_s, fw_r = self.sems[5:9]
        for i, z in enumerate(self.origins):
            for t, origin in enumerate((self.side, self.up)):
                self.got(u.block(z, 1 - t, origin), xy_s.at[n, i, 1 - t, t], xy_r.at[n, i, 1 - t, t])
            for t in range(2):
                self.got(u.block(z, t, 3 - self.grp), fw_s.at[n, i, t], fw_r.at[n, i, t])

    def sent_all(self, firsts, rest):
        loc, near_s, near_r, z_s, z_r, xy_s, xy_r, fw_s, fw_r = self.sems

        def out(block, send, recv):
            remote(block, block, send, recv, self.side, self.plane, self.core).wait_send()

        for n in firsts:
            u = self.units[n]
            for i in range(3):
                for j in range(2):
                    out(u.block(self.plane, j, self.grp), z_s.at[n, i, j], z_r.at[n, i, j])
            if u.split:
                for q in range(4):
                    out(u.block(self.plane, 0, q), near_s.at[n, q], near_r.at[n, q])
                    pltpu.make_async_copy(u.mine(0, q), u.block(self.plane, 0, q), loc.at[n, q]).wait()
            else:
                pltpu.make_async_copy(u.shard, u.own(self.plane), loc.at[n, 0]).wait()
        for n in rest:
            u = self.units[n]
            for i, z in enumerate(self.origins):
                for j in range(2):
                    for t in range(2):
                        out(u.block(z, j, self.grp), xy_s.at[n, i, j, t], xy_r.at[n, i, j, t])
                for t, origin in enumerate((self.side, self.up)):
                    out(u.block(z, t, origin), fw_s.at[n, i, t], fw_r.at[n, i, t])

    def drain(self):
        for wait in self.left:
            wait()
        self.left = []


def start_kernel(heads, kv_heads, x_ref, dy_ref, wq_ref, wk_ref, wv_ref, wo_ref, gate_ref, ga_ref, gf_ref,
                 pack_out, gate_out, x_out, dy_out, pack, gate, trade_s, trade_r, own_s, *sems):
    _, _, core = where_am_i()
    q_cols, kv_cols, span = heads * HEAD, kv_heads * HEAD, x_ref.shape[1]
    cols = pack.shape[1] // 8
    gain = ga_ref[...].astype(F32)
    for k in range(2):
        parts = [(wq_ref[:, k * q_cols : (k + 1) * q_cols].astype(F32) * gain).astype(BF16)]
        parts += [(w[:, k * kv_cols : (k + 1) * kv_cols].astype(F32) * gain).astype(BF16) for w in (wk_ref, wv_ref)]
        row = jnp.concatenate(parts + [wo_ref[:, k * q_cols : (k + 1) * q_cols]], 1)
        for q in range(4):
            pack[:, (2 * q + k) * cols : (2 * q + k + 1) * cols] = row[:, q * cols : (q + 1) * cols]
    gather = Gather([Columns(core, pack, pack_out), Columns(core, gate, gate_out)], sems)
    greet(gather.partners())
    gather.first(0)
    gate[...] = (gate_ref[...].astype(F32) * gf_ref[...].astype(F32)).astype(BF16)
    waits = []

    def trade(ref, out, which):
        for s in range(ref.shape[0]):
            def rows(owner):
                return out.at[pl.ds(pl.multiple_of((2 * s + owner) * span, 16), span), :]
            copy = remote(ref.at[s], rows(core), trade_s.at[which, s], trade_r.at[which, s], gather.grp, gather.plane, 1 - core)
            copy.start()
            gather.left.append(copy.wait_send)
            copy = pltpu.make_async_copy(ref.at[s], rows(core), own_s.at[which, s])
            copy.start()
            gather.left.append(copy.wait)
            waits.append((rows(1 - core), trade_s.at[which, s], trade_r.at[which, s]))

    trade(x_ref, x_out, 0)
    gather.second(0)
    gather.first(1)
    trade(dy_ref, dy_out, 1)
    gather.third(0)
    gather.last(0)
    gather.near_in(0)
    gather.near_in(1)
    for wait in waits:
        gather.got(*wait)
    gather.first_in(1)
    gather.drain()


def start(x, dy, wq, wk, wv, wo, gate, gain_attn, gain_ffn, heads, kv_heads):
    count, span, width = x.shape
    shard, hidden = gate.shape
    cols = 2 * (heads + kv_heads) * HEAD
    shape = jax.ShapeDtypeStruct
    return pl.pallas_call(
        functools.partial(start_kernel, heads, kv_heads),
        in_specs=[VMEM] * 9,
        out_specs=(ANY,) * 4,
        out_shape=(
            shape((8 * shard, cols), BF16),
            shape((8 * shard, hidden // 2), BF16),
            shape((2 * count * span, width), BF16),
            shape((2 * count * span, width), BF16),
        ),
        scratch_shapes=[pltpu.VMEM((shard, 2 * cols), BF16), pltpu.VMEM((shard, hidden), BF16)]
        + [DMA((2, count))] * 3
        + Gather.semaphores(2),
        compiler_params=pltpu.CompilerParams(collective_id=0, has_side_effects=True, vmem_limit_bytes=48 * 2**20),
        name="start",
    )(x, dy, wq, wk, wv, wo, gate, gain_attn, gain_ffn)


def front_kernel(heads, kv_heads, blocks, prefix_ref, x_ref, own_ref, w_ref, up_ref, gf_ref, cos_ref, sin_ref, gate_in, down_ref,
                 n_ref, qt_ref, kvt_ref, kv_ref, ot_ref, lse_ref, wo_ref, x1_ref, two_out, gate_out, up_out, down_out,
                 up_s, wo_send, wo_recv, part_mine, part_send, part_recv, two_mine,
                 wo_sem, part_sem, two_sem, own_sem, *sems):
    step = pl.program_id(0)
    grp, plane, core = where_am_i()
    count = prefix_ref.shape[0]
    tiles = count * blocks
    groups = heads // kv_heads
    q_cols, kv_cols = heads * HEAD, kv_heads * HEAD
    width = x_ref.shape[1]
    half = blocks // 2
    gather = Gather([Columns(core, up_s, gate_out), Columns(core, up_s, up_out), Rows(core, down_ref, down_out)], sems)

    def at(when):
        return pl.when(step == when)

    def out_weight(owner):
        return w_ref[pl.ds(pl.multiple_of(owner * q_cols, 16), q_cols), q_cols + 2 * kv_cols :]

    def wo_copy():
        return remote(wo_send, wo_recv, wo_sem.at[0], wo_sem.at[1], grp, plane, 1 - core)

    @at(0)
    def _():
        greet(gather.partners())
        gather.second(0, here=True)
        wo_send[...] = out_weight(1 - core)
        wo_copy().start()
        up_s[...] = (up_ref[...].astype(F32) * gf_ref[...].astype(F32)).astype(BF16)
        gather.first(1)

    @at(tiles - 1)
    def _():
        wo_copy().wait()
        mine, other = out_weight(core), wo_recv[...]
        wo_ref[...] = jnp.concatenate([jnp.where(core == 0, mine, other), jnp.where(core == 0, other, mine)], 1)

    @at(tiles)
    def _():
        gather.first(2)
        gather.third(0)

    @at(tiles + 1)
    def _():
        gather.second(1)

    @at(tiles + 3)
    def _():
        gather.third(1)

    @at(tiles + 4)
    def _():
        gather.second(2)

    @at(tiles + 6)
    def _():
        gather.third(2)

    @pl.when(step < tiles)
    def _():
        x = x_ref[...].astype(F32)
        normed = (x * lax.rsqrt(jnp.mean(x * x, -1, keepdims=True) + epsilon)).astype(BF16)
        n_ref[...] = normed
        flat = dot(normed, w_ref[:, : q_cols + 2 * kv_cols])
        across = flat.T
        tokens = pl.ds(pl.multiple_of(step * BLOCK, BLOCK), BLOCK)
        here = pl.ds(pl.multiple_of(lax.rem(step, blocks) * BLOCK, BLOCK), BLOCK)
        cosine, sine = cos_ref[:, here], sin_ref[:, here]
        for h in range(heads):
            rows = turned(across[h * HEAD : (h + 1) * HEAD], cosine, sine, 1.0)
            qt_ref[h * HEAD : (h + 1) * HEAD, tokens] = (rows * TO_LOG2).astype(BF16)
        keys = [across[q_cols + h * HEAD : q_cols + (h + 1) * HEAD] for h in range(kv_heads)]
        keys = jnp.concatenate([turned(rows, cosine, sine, 1.0) for rows in keys], 0)
        kvt_ref[:kv_cols, tokens] = keys.astype(BF16)
        kvt_ref[kv_cols:, tokens] = across[q_cols + kv_cols :].astype(BF16)
        kv_ref[tokens, :kv_cols] = keys.T.astype(BF16)
        kv_ref[tokens, kv_cols:] = flat[:, q_cols + kv_cols :].astype(BF16)

    def rows_of(tile, owner):
        start = (tile // half) * blocks + owner * half + lax.rem(tile, half)
        return two_out.at[pl.ds(pl.multiple_of(start * BLOCK, BLOCK), BLOCK), :]

    def part_copy(slot):
        return remote(part_send.at[slot], part_recv.at[slot], part_sem.at[0, slot], part_sem.at[1, slot], grp, plane, 1 - core)

    def two_copy(slot):
        there = rows_of(slot, core)
        return remote(two_mine.at[slot], there, two_sem.at[0, slot], two_sem.at[1, slot], grp, plane, 1 - core)

    def two_keep(slot):
        return pltpu.make_async_copy(two_mine.at[slot], rows_of(slot, core), own_sem.at[slot])

    def finish(turn):
        block, s = lax.rem(turn, blocks), turn // blocks
        slot = s * half + lax.rem(block, half)

        @pl.when(block // half == core)
        def _():
            part_copy(slot).wait_recv()
            rows = pl.ds(pl.multiple_of(slot * BLOCK, BLOCK), BLOCK)
            middle = own_ref[rows, :].astype(F32) + part_mine[slot].astype(F32) + part_recv[slot].astype(F32)
            x1_ref[rows, :] = middle
            normed = middle * lax.rsqrt(jnp.mean(middle * middle, -1, keepdims=True) + epsilon)
            two_mine[slot] = normed.astype(BF16)
            two_copy(slot).start()
            two_keep(slot).start()

    def run(block):
        n = reach(block)
        turn = step - tiles
        s = turn // blocks
        prefix = prefix_ref[s]
        base = pl.multiple_of(s * blocks * BLOCK, BLOCK)
        tokens = pl.ds(pl.multiple_of(turn * BLOCK, BLOCK), BLOCK)
        for kh in range(kv_heads):
            keys = kv_ref[pl.ds(base, n), kh * HEAD : (kh + 1) * HEAD]
            vt = kvt_ref[kv_cols + kh * HEAD : kv_cols + (kh + 1) * HEAD, pl.ds(base, n)]
            for h in range(kh * groups, (kh + 1) * groups):
                scores = scores_of(keys, qt_ref[h * HEAD : (h + 1) * HEAD, tokens], prefix, block)
                peak = jnp.max(scores, 0, keepdims=True)
                weights = jnp.exp2(scores - peak)
                total = jnp.sum(weights, 0, keepdims=True)
                mixed = dot(vt, weights.astype(BF16)) / total
                ot_ref[h * HEAD : (h + 1) * HEAD, tokens] = mixed.astype(BF16)
                lse_ref[h : h + 1, tokens] = peak + jnp.log2(total)
        part = dot(ot_ref[:, tokens], wo_ref[...], TN).astype(BF16)
        slot = s * half + block % half

        @pl.when(core == block // half)
        def _():
            part_mine[slot] = part

        @pl.when(core != block // half)
        def _():
            part_send[slot] = part
            part_copy(slot).start()

    @pl.when(step > tiles)
    def _():
        finish(step - tiles - 1)

    for block in range(blocks):
        pl.when((step >= tiles) & (lax.rem(step, blocks) == block))(functools.partial(run, block))

    @at(2 * tiles - 1)
    def _():
        finish(step - tiles)
        for n in range(3):
            gather.last(n)
        gather.near_in(1)
        for slot in range(count * half):
            part_copy(slot).wait_send()
            two_copy(slot).wait_send()
            two_keep(slot).wait()
            there = rows_of(slot, 1 - core)
            remote(there, there, two_sem.at[0, slot], two_sem.at[1, slot], grp, plane, 1 - core).wait_recv()
        gather.sent_all((1, 2), (0, 1, 2))


def front(prefix, x, own, pack, gate_part, up, down, gain_ffn, cosine, sine, heads, kv_heads, length):
    tokens, width = x.shape
    count, blocks = tokens // length, length // BLOCK
    tiles = tokens // BLOCK
    slots = tiles // 2
    q_cols, kv_cols = heads * HEAD, kv_heads * HEAD
    shape = jax.ShapeDtypeStruct
    once = pl.Buffered(1)

    def fixed(*dims):
        return pl.BlockSpec(dims, lambda i: (0,) * len(dims), pipeline_mode=once)

    tile = pl.BlockSpec((BLOCK, width), lambda i: (jnp.minimum(i, tiles - 1), 0))
    return pl.pallas_call(
        functools.partial(front_kernel, heads, kv_heads, blocks),
        grid=(2 * tiles,),
        in_specs=[
            pl.BlockSpec(memory_space=pltpu.SMEM),
            tile,
            fixed(tokens // 2, width),
            fixed(*pack.shape),
            fixed(*up.shape),
            fixed(*gain_ffn.shape),
            fixed(*cosine.shape),
            fixed(*sine.shape),
            ANY,
            fixed(*down.shape),
        ],
        out_specs=(
            tile,
            fixed(q_cols, tokens),
            fixed(2 * kv_cols, tokens),
            fixed(tokens, 2 * kv_cols),
            fixed(q_cols, tokens),
            fixed(heads, tokens),
            fixed(q_cols, width),
            fixed(tokens // 2, width),
            ANY, ANY, ANY, ANY,
        ),
        out_shape=(
            shape((tokens, width), BF16),
            shape((q_cols, tokens), BF16),
            shape((2 * kv_cols, tokens), BF16),
            shape((tokens, 2 * kv_cols), BF16),
            shape((q_cols, tokens), BF16),
            shape((heads, tokens), F32),
            shape((q_cols, width), BF16),
            shape((tokens // 2, width), F32),
            shape((tokens, width), BF16),
            shape(gate_part.shape, BF16),
            shape(gate_part.shape, BF16),
            shape((4 * down.shape[0], width), BF16),
        ),
        input_output_aliases={8: 9},
        scratch_shapes=[
            pltpu.VMEM(up.shape, BF16),
            pltpu.VMEM((q_cols, q_cols), BF16),
            pltpu.VMEM((q_cols, q_cols), BF16),
        ]
        + [pltpu.VMEM((slots, BLOCK, width), BF16)] * 4
        + [DMA((2,)), DMA((2, slots)), DMA((2, slots)), DMA((slots,))]
        + Gather.semaphores(3),
        compiler_params=pltpu.CompilerParams(collective_id=1, has_side_effects=True, vmem_limit_bytes=60 * 2**20),
        cost_estimate=pl.CostEstimate(flops=2 * tokens * width * 1536, bytes_accessed=16 * tokens * width, transcendentals=0),
        name="front",
    )(prefix, x, own, pack, up, gain_ffn, cosine, sine, gate_part, down)


def feed_kernel(n_ref, gate_ref, up_ref, down_ref, hidden_ref, by_up_ref, by_gate_ref, part_ref):
    n = n_ref[...]
    gate = dot(n, gate_ref[...])
    upward = dot(n, up_ref[...])
    sigma = 1.0 / (1.0 + jnp.exp(-gate))
    silu = gate * sigma
    hidden = (silu * upward).astype(BF16)
    hidden_ref[...] = hidden
    by_up_ref[...] = silu.astype(BF16)
    by_gate_ref[...] = (upward * sigma * (1.0 + gate - silu)).astype(BF16)
    part_ref[...] = dot(hidden, down_ref[...]).astype(BF16)


def feed(n, gate, up, down):
    tokens, width = n.shape
    units = gate.shape[1]
    shape = jax.ShapeDtypeStruct
    once = pl.Buffered(1)
    tile = lambda cols: pl.BlockSpec((BLOCK, cols), lambda i: (i, 0))
    fixed = lambda a: pl.BlockSpec(a.shape, lambda i: (0, 0), pipeline_mode=once)
    return pl.pallas_call(
        feed_kernel,
        grid=(tokens // BLOCK,),
        in_specs=[tile(width), fixed(gate), fixed(up), fixed(down)],
        out_specs=(tile(units), tile(units), tile(units), tile(width)),
        out_shape=(shape((tokens, units), BF16),) * 3 + (shape((tokens, width), BF16),),
        compiler_params=pltpu.CompilerParams(vmem_limit_bytes=48 * 2**20),
        cost_estimate=pl.CostEstimate(flops=6 * tokens * width * units, bytes_accessed=2 * tokens * (3 * units + 2 * width), transcendentals=tokens * units),
        name="feed",
    )(n, gate, up, down)


def feed_back_kernel(dy_ref, gate_ref, up_ref, down_ref, by_up_ref, by_gate_ref, d_gate_ref, d_up_ref, part_ref):
    grad = dot(dy_ref[...], down_ref[...], NT)
    d_up = (grad * by_up_ref[...].astype(F32)).astype(BF16)
    d_gate = (grad * by_gate_ref[...].astype(F32)).astype(BF16)
    d_up_ref[...] = d_up
    d_gate_ref[...] = d_gate
    part_ref[...] = (dot(d_gate, gate_ref[...], NT) + dot(d_up, up_ref[...], NT)).astype(BF16)


def feed_back(dy, gate, up, down, by_up, by_gate):
    tokens, width = dy.shape
    units = gate.shape[1]
    shape = jax.ShapeDtypeStruct
    once = pl.Buffered(1)
    tile = lambda cols: pl.BlockSpec((BLOCK, cols), lambda i: (i, 0))
    fixed = lambda a: pl.BlockSpec(a.shape, lambda i: (0, 0), pipeline_mode=once)
    return pl.pallas_call(
        feed_back_kernel,
        grid=(tokens // BLOCK,),
        in_specs=[tile(width), fixed(gate), fixed(up), fixed(down), tile(units), tile(units)],
        out_specs=(tile(units), tile(units), tile(width)),
        out_shape=(shape((tokens, units), BF16),) * 2 + (shape((tokens, width), BF16),),
        compiler_params=pltpu.CompilerParams(vmem_limit_bytes=48 * 2**20),
        cost_estimate=pl.CostEstimate(flops=6 * tokens * width * units, bytes_accessed=2 * tokens * (4 * units + 2 * width), transcendentals=0),
        name="feed_back",
    )(dy, gate, up, down, by_up, by_gate)


def finish_kernel(heads, kv_heads, pack_ref, gate_ref, up_ref, down_ref, wq_ref, wk_ref, wv_ref, wg_ref, wu_ref, ga_ref, gf_ref,
                  q_out, k_out, v_out, o_out, gate_out, up_out, down_out, ga_out, gf_out):
    q_cols, kv_cols = heads * HEAD, kv_heads * HEAD
    cols = pack_ref.shape[1] // 8
    gain = ga_ref[...].astype(F32)
    total = jnp.zeros(gain.shape, F32)
    for k in range(2):
        row = jnp.concatenate([pack_ref[:, (2 * q + k) * cols : (2 * q + k + 1) * cols].astype(F32) for q in range(4)], 1)
        at = 0
        for w, out, size in ((wq_ref, q_out, q_cols), (wk_ref, k_out, kv_cols), (wv_ref, v_out, kv_cols)):
            part, here = row[:, at : at + size], slice(k * size, (k + 1) * size)
            total += jnp.sum(part * w[:, here].astype(F32), -1, keepdims=True)
            out[:, here] = part * gain
            at += size
        o_out[:, k * q_cols : (k + 1) * q_cols] = row[:, at:]
    ga_out[...] = total
    gain = gf_ref[...].astype(F32)
    total = jnp.zeros(gain.shape, F32)
    for ref, w, out in ((gate_ref, wg_ref, gate_out), (up_ref, wu_ref, up_out)):
        part = ref[...].astype(F32)
        total += jnp.sum(part * w[...].astype(F32), -1, keepdims=True)
        out[...] = part * gain
    gf_out[...] = total
    down_out[...] = down_ref[...].astype(F32)


def finish(pack, gate, up, down, wq, wk, wv, wo, wg, wu, ga, gf, heads, kv_heads):
    shape = lambda a: jax.ShapeDtypeStruct(a.shape, F32)
    whole = pl.BlockSpec(memory_space=pltpu.VMEM)
    return pl.pallas_call(
        functools.partial(finish_kernel, heads, kv_heads),
        in_specs=[whole] * 11,
        out_specs=(whole,) * 9,
        out_shape=(shape(wq), shape(wk), shape(wv), shape(wo), shape(wg), shape(wu), shape(down), shape(ga), shape(gf)),
        compiler_params=pltpu.CompilerParams(vmem_limit_bytes=48 * 2**20),
        name="finish",
    )(pack, gate, up, down, wq, wk, wv, wg, wu, ga, gf)


REDUCE_ORDER = ('a0', 'a1', 'b0', 'a2', 'b1', 'c0', 'a3', 'b2', 'c1', 'd0', 'b3', 'c2', 'd1', 'e0', 'c3', 'd2', 'e1', 'd3', 'e2', 'e3')

def reduce_kernel(order, *refs):
    grads, outs = refs[:4], refs[4:8]
    accs, recvs, seconds, thirds, fins = refs[8:12], refs[12:16], refs[16:20], refs[20:24], refs[24:28]
    load, s1, r1, s2, r2, s3, r3, s4, r4 = refs[28:]
    grp, plane, core = where_am_i()
    gx, gy = lax.rem(grp, 2), grp // 2
    side, up = grp + 1 - 2 * gx, lax.rem(grp + 2, 4)
    planes = [lax.rem(plane + s, 4) for s in (1, 2, 3)]
    origins = [lax.rem(plane + 4 - s, 4) for s in (1, 2, 3)]
    others = [lax.rem(grp + s, 4) for s in (1, 2, 3)]
    sources = [lax.rem(grp + 4 - s, 4) for s in (1, 2, 3)]
    partners = [(grp, z, core) for z in planes] + [(g, plane, c) for g in others for c in (core, 1 - core)] + [(grp, plane, 1 - core)]
    greet(partners)
    tail = []

    def half(n, z, q, h):
        ref = grads[n]
        if n < 3:
            rows, cols = ref.shape[0] // 8, ref.shape[1] // 4
            return ref.at[pl.ds((2 * z + h) * rows, rows), pl.ds(pl.multiple_of(q * cols, 128), cols)]
        rows = ref.shape[0] // 32
        return ref.at[pl.ds(pl.multiple_of(((4 * z + q) * 2 + h) * rows, 16), rows), :]

    def quarter(path, i, own):
        if path == 0:
            return 2 * i + (gx if own else 1 - gx)
        return 2 * (gy if own else 1 - gy) + i

    first_to, second_to = (side, up), (up, side)
    keep = (gy, gx)

    def a(n):
        for z in range(4):
            for path in range(2):
                for i in range(2):
                    d = pltpu.make_async_copy(half(n, z, quarter(path, i, True), path), accs[n].at[path, z, i], load.at[n, path, z, i])
                    d.start()
                    d = remote(half(n, z, quarter(path, i, False), path), recvs[n].at[path, z, i], s1.at[n, path, z, i], r1.at[n, path, z, i], first_to[path], plane, core)
                    d.start(); tail.append(d.wait_send)

    def b(n):
        for z in range(4):
            for path in range(2):
                for i in range(2):
                    here = accs[n].at[path, z, i]
                    pltpu.make_async_copy(half(n, z, quarter(path, i, True), path), here, load.at[n, path, z, i]).wait()
                    got = recvs[n].at[path, z, i]
                    remote(got, got, s1.at[n, path, z, i], r1.at[n, path, z, i], first_to[path], plane, core).wait_recv()
                    here[...] = (here[...].astype(jnp.float32) + got[...].astype(jnp.float32)).astype(jnp.bfloat16)
                d = remote(accs[n].at[path, z, 1 - keep[path]], seconds[n].at[path, z], s2.at[n, path, z], r2.at[n, path, z], second_to[path], plane, core)
                d.start(); tail.append(d.wait_send)

    def c(n):
        for z in range(4):
            for path in range(2):
                got = seconds[n].at[path, z]
                remote(got, got, s2.at[n, path, z], r2.at[n, path, z], second_to[path], plane, core).wait_recv()
                here = accs[n].at[path, z, keep[path]]
                fins[n][z, path] = (here[...].astype(jnp.float32) + got[...].astype(jnp.float32)).astype(jnp.bfloat16)
        for i, z in enumerate(planes):
            d = remote(fins[n].at[z], thirds[n].at[i], s3.at[n, i], r3.at[n, i], grp, z, core)
            d.start(); tail.append(d.wait_send)

    def sent(n, which, to, c_to, i, j):
        if n < 3:
            rows, cols = outs[n].shape[0], outs[n].shape[1] // 8
            dst = outs[n].at[:, pl.ds(pl.multiple_of((2 * which + c_to[1]) * cols, 128), cols)]
            src = fins[n].at[plane, c_to[0]]
            return src, dst
        rows = outs[n].shape[0] // 8
        dst = outs[n].at[pl.ds(pl.multiple_of((2 * which + j) * rows, 16), rows), :]
        return fins[n].at[plane, j], dst

    def d_(n):
        for i, z in enumerate(origins):
            got = thirds[n].at[i]
            remote(got, got, s3.at[n, i], r3.at[n, i], grp, z, core).wait_recv()
        for j in range(2):
            total = fins[n][plane, j].astype(jnp.float32)
            for i in range(3):
                total += thirds[n][i, j].astype(jnp.float32)
            fins[n][plane, j] = total.astype(jnp.bfloat16)
        for j in range(2):
            target = (core if j == 0 else 1 - core) if n < 3 else core
            src, dst = sent(n, grp, None, (target, core), None, j)
            if n < 3 and j == 1:
                d = remote(src, dst, s4.at[n, 3, j], r4.at[n, 3, j], grp, plane, target)
                d.start(); tail.append(d.wait_send)
            else:
                d = pltpu.make_async_copy(src, dst, s4.at[n, 3, j])
                d.start(); tail.append(d.wait)
            for i, g in enumerate(others):
                d = remote(src, dst, s4.at[n, i, j], r4.at[n, i, j], g, plane, target)
                d.start(); tail.append(d.wait_send)

    def e(n):
        for j in range(2):
            origin = (core if j == 0 else 1 - core) if n < 3 else core
            for i, g in enumerate(sources):
                _, dst = sent(n, g, None, (core, origin), None, j)
                remote(dst, dst, s4.at[n, i, j], r4.at[n, i, j], g, plane, origin).wait_recv()
            if n < 3 and j == 1:
                _, dst = sent(n, grp, None, (core, origin), None, j)
                remote(dst, dst, s4.at[n, 3, j], r4.at[n, 3, j], grp, plane, origin).wait_recv()

    ops = {"a": a, "b": b, "c": c, "d": d_, "e": e}
    for word in order:
        ops[word[0]](int(word[1]))
    for w in tail:
        w()


def reduce_grads(*grads):
    any_ = pl.BlockSpec(memory_space=pl.ANY)
    dma = pltpu.SemaphoreType.DMA
    halves = [(x.shape[0] // 8, x.shape[1] // 4) for x in grads[:3]] + [(grads[3].shape[0] // 32, grads[3].shape[1])]
    def buf(*lead):
        return [pltpu.VMEM(lead + h, jnp.bfloat16) for h in halves]
    out = [jax.ShapeDtypeStruct((x.shape[0] // 8, x.shape[1] * 2), jnp.bfloat16) for x in grads[:3]] + [jax.ShapeDtypeStruct((grads[3].shape[0] // 4, grads[3].shape[1]), jnp.bfloat16)]
    return pl.pallas_call(functools.partial(reduce_kernel, REDUCE_ORDER),
        out_shape=tuple(out), in_specs=[any_] * 4, out_specs=(any_,) * 4,
        scratch_shapes=buf(2, 4, 2) + buf(2, 4, 2) + buf(2, 4) + buf(3, 2) + buf(4, 2) + [
            dma((4, 2, 4, 2)), dma((4, 2, 4, 2)), dma((4, 2, 4, 2)), dma((4, 2, 4)), dma((4, 2, 4)), dma((4, 3)), dma((4, 3)), dma((4, 4, 2)), dma((4, 4, 2))],
        compiler_params=pltpu.CompilerParams(collective_id=2, has_side_effects=True, vmem_limit_bytes=48 * 2**20),
        name="reduce_grads",
    )(*grads)


SWAP = [(0, 1), (1, 0)]


def trade(mine):
    return lax.ppermute(mine, "ctx", SWAP)


def ordered(core, mine, other, axis):
    return jnp.concatenate([jnp.where(core == 0, mine, other), jnp.where(core == 0, other, mine)], axis)


def part_of(array, which, axis):
    size = array.shape[axis] // 2
    return lax.dynamic_slice_in_dim(array, which * size, size, axis)


def tables(length):
    frequency = np.float32(10000.0) ** (-np.arange(HEAD // 2, dtype=np.float32) * np.float32(2.0) / np.float32(HEAD))
    angles = frequency[:, None] * np.arange(length, dtype=np.float32)[None, :]
    return jnp.asarray(np.cos(angles)), jnp.asarray(np.sin(angles))


def paired(
    activations_in,
    prefix_len,
    attn_gain,
    query_weight,
    key_weight,
    value_weight,
    out_weight,
    ffn_gain,
    gate_weight,
    up_weight,
    down_weight,
    cotangent,
):
    micro, seq_count, span, width = activations_in.shape
    count, length = micro * seq_count, 2 * span
    core = lax.axis_index("ctx")
    heads, kv_heads = HEADS // 2, KV_HEADS // 2
    q_cols, kv_cols = heads * HEAD, kv_heads * HEAD
    shard = attn_gain.shape[0]

    own_x = activations_in.reshape(count, span, width)
    own_dy = cotangent.reshape(count, span, width)

    def whole(mine):
        return ordered(core, mine, trade(mine), 1).reshape(count * length, width)

    def summed(part):
        part = part.reshape(count, length, width)
        theirs = trade(part_of(part, 1 - core, 1))
        return part_of(part, core, 1).astype(F32) + theirs.astype(F32)

    gain_attn, gain_ffn = attn_gain[:, None], ffn_gain[:, None]
    pack, gate_part, full_x, full_dy = start(
        own_x, own_dy, query_weight, key_weight, value_weight, out_weight, gate_weight, gain_attn, gain_ffn, heads, kv_heads
    )
    cosine, sine = tables(length)
    prefix = prefix_len.reshape(count)
    normed_one, qt, kvt, kv, ot, lse, w_out, middle, full_two, w_gate, w_up, w_down = front(
        prefix, full_x, own_x.reshape(count * span, width), pack, gate_part, up_weight, down_weight, gain_ffn, cosine, sine,
        heads, kv_heads, length,
    )
    middle = middle.reshape(count, span, width)
    inverse_two = lax.rsqrt(jnp.mean(middle * middle, -1, keepdims=True) + epsilon)
    normed_two = middle * inverse_two
    hidden, by_up, by_gate, part = feed(full_two, w_gate, w_up, w_down)
    result = middle + summed(part)
    d_gate, d_up, part = feed_back(full_dy, w_gate, w_up, w_down, by_up, by_gate)
    grad_two = summed(part)
    grad_down = dot(hidden, full_dy, TN).astype(BF16)
    grad_gate = dot(full_two, d_gate, TN).astype(BF16)
    grad_up = dot(full_two, d_up, TN).astype(BF16)
    grad_middle = own_dy.astype(F32) + norm_back(grad_two, normed_two, inverse_two)
    full_dx = whole(grad_middle.astype(BF16))
    grad_out_rows = dot(ot, full_dx).astype(BF16)
    dqt, dkvt = attend_back(prefix, qt, kv, kvt, ot, lse, full_dx, w_out, cosine, sine, heads, kv_heads, length)
    dt = jnp.concatenate([dqt, dkvt], 0)
    grad_qkv = dot(normed_one, dt, (((0,), (1,)), ((), ()))).astype(BF16)
    grad_one = summed(dot(dt, pack[:, : q_cols + 2 * kv_cols], (((0,), (1,)), ((), ()))).astype(BF16))
    x = own_x.astype(F32)
    inverse_one = lax.rsqrt(jnp.mean(x * x, -1, keepdims=True) + epsilon)
    grad_inputs = grad_middle + norm_back(grad_one, x * inverse_one, inverse_one)

    grad_out_cols = ordered(core, part_of(grad_out_rows, core, 1), trade(part_of(grad_out_rows, 1 - core, 1)), 0)
    grad_pack = jnp.concatenate([grad_qkv, grad_out_cols], 1)
    r_pack, r_gate, r_up, r_down = reduce_grads(grad_pack, grad_gate, grad_up, grad_down)
    g_q, g_k, g_v, g_o, g_gate, g_up, g_down, g_ga, g_gf = finish(
        r_pack, r_gate, r_up, r_down, query_weight, key_weight, value_weight, out_weight, gate_weight, up_weight, gain_attn, gain_ffn,
        heads, kv_heads,
    )
    shape = activations_in.shape
    return (
        result.astype(BF16).reshape(shape),
        grad_inputs.astype(BF16).reshape(shape),
        g_ga[:, 0],
        g_q,
        g_k,
        g_v,
        g_o,
        g_gf[:, 0],
        g_gate,
        g_up,
        g_down,
    )


def solution(mesh):
    small = dict(mesh.shape) == {"grp": 4, "fsdp": 4, "ctx": 2}

    return jax.shard_map(
        paired if small else local,
        mesh=mesh,
        in_specs=(
            P(None, ("grp", "fsdp"), "ctx", None),
            P(None, ("grp", "fsdp")),
            P(("fsdp", "ctx")),
            P(("fsdp", "ctx"), None),
            P(("fsdp", "ctx"), None),
            P(("fsdp", "ctx"), None),
            P(("fsdp", "ctx"), None),
            P(("fsdp", "ctx")),
            P(("fsdp", "ctx"), None),
            P(("fsdp", "ctx"), None),
            P(("fsdp", "ctx"), None),
            P(None, ("grp", "fsdp"), "ctx", None),
        ),
        out_specs=(
            P(None, ("grp", "fsdp"), "ctx", None),
            P(None, ("grp", "fsdp"), "ctx", None),
            P(("fsdp", "ctx")),
            P(("fsdp", "ctx"), None),
            P(("fsdp", "ctx"), None),
            P(("fsdp", "ctx"), None),
            P(("fsdp", "ctx"), None),
            P(("fsdp", "ctx")),
            P(("fsdp", "ctx"), None),
            P(("fsdp", "ctx"), None),
            P(("fsdp", "ctx"), None),
        ),
        check_vma=False,
    )
```

```python
import functools
import math

import jax
import jax.numpy as jnp
import numpy as np
from jax import lax
from jax.experimental import pallas as pl
from jax.experimental.pallas import tpu as pltpu
from jax.sharding import PartitionSpec as P

HEADS = 18
KV_HEADS = 6
HEAD = 64


epsilon = 1e-05


def shortened(array):

    def short(part):
        return part.astype(jnp.bfloat16) if part.dtype == jnp.float32 else part

    return jax.tree.map(short, array)


def rotary_tables(positions):
    halfway = HEAD // 2
    frequency = 10000.0 ** (-jnp.arange(halfway, dtype=jnp.float32) * 2.0 / HEAD)
    angles = positions.astype(jnp.float32)[:, None] * frequency[None, :]
    return (jnp.cos(angles)[:, None, :], jnp.sin(angles)[:, None, :])


def rotate(values, cosine, sine):
    halfway = values.shape[-1] // 2
    first = values[..., :halfway]
    second = values[..., halfway:]
    return jnp.concatenate([first * cosine - second * sine, second * cosine + first * sine], -1)


def rotate_back(values, cosine, sine):
    halfway = values.shape[-1] // 2
    first = values[..., :halfway]
    second = values[..., halfway:]
    return jnp.concatenate([first * cosine + second * sine, second * cosine - first * sine], -1)


def norm_back(grad_normed, normed, inverse):
    return inverse * (grad_normed - normed * jnp.mean(grad_normed * normed, -1, keepdims=True))


def flatten_all(grads):
    return tuple((g.reshape(-1) for g in grads))


def local(
    activations_in,
    prefix_len,
    attn_gain,
    query_weight,
    key_weight,
    value_weight,
    out_weight,
    ffn_gain,
    gate_weight,
    up_weight,
    down_weight,
    cotangent,
):
    micro, seq_count, span, width = activations_in.shape
    rows = seq_count * span
    length = span * lax.axis_size("ctx")
    groups = HEADS // KV_HEADS
    scale = 1.0 / math.sqrt(HEAD)
    shards = (
        attn_gain,
        query_weight,
        key_weight,
        value_weight,
        out_weight,
        ffn_gain,
        gate_weight,
        up_weight,
        down_weight,
    )
    offset = lax.axis_index("ctx") * span
    query_pos = offset + jnp.arange(span, dtype=jnp.int32)
    key_pos = jnp.arange(length, dtype=jnp.int32)
    cosine, sine = rotary_tables(jnp.tile(query_pos, seq_count))

    def visibility(prefix):
        return (key_pos[None, :] <= query_pos[:, None]) | (key_pos[None, :] < prefix)

    def attend(item):
        query, keys, values, prefix = item
        scores = (
            jnp.einsum("qhgd,khd->hgqk", query, keys, preferred_element_type=jnp.float32) * scale
        )
        scores = jnp.where(visibility(prefix), scores, -1e30)
        peak = jnp.max(scores, -1, keepdims=True)
        weights = jnp.exp(scores - peak)
        totals = jnp.sum(weights, -1, keepdims=True)
        probs = (weights / totals).astype(jnp.bfloat16)
        mixed = jnp.einsum("hgqk,khd->qhgd", probs, values, preferred_element_type=jnp.float32)
        return (mixed.reshape(span, HEADS * HEAD), (peak + jnp.log(totals))[..., 0])

    def attend_back(item):
        query, keys, values, prefix, log_total, grad_mixed = item
        scores = (
            jnp.einsum("qhgd,khd->hgqk", query, keys, preferred_element_type=jnp.float32) * scale
        )
        probs = jnp.where(visibility(prefix), jnp.exp(scores - log_total[..., None]), 0.0)
        grad_probs = jnp.einsum(
            "qhgd,khd->hgqk", grad_mixed, values, preferred_element_type=jnp.float32
        )
        grad_scores = (
            probs * (grad_probs - jnp.sum(probs * grad_probs, -1, keepdims=True))
        ).astype(jnp.bfloat16)
        grad_query = (
            jnp.einsum("hgqk,khd->qhgd", grad_scores, keys, preferred_element_type=jnp.float32)
            * scale
        )
        grad_keys = (
            jnp.einsum("hgqk,qhgd->khd", grad_scores, query, preferred_element_type=jnp.float32)
            * scale
        )
        grad_values = jnp.einsum(
            "hgqk,qhgd->khd",
            probs.astype(jnp.bfloat16),
            grad_mixed,
            preferred_element_type=jnp.float32,
        )
        return (
            grad_query.reshape(span, HEADS * HEAD),
            grad_keys.reshape(length, KV_HEADS * HEAD),
            grad_values.reshape(length, KV_HEADS * HEAD),
        )

    outputs = []
    input_grads = []
    collected = None
    for index in range(micro):
        full = (
            lax.all_gather(shards[0], ("fsdp", "ctx"), axis=0, tiled=True),
            lax.all_gather(shards[1], ("fsdp", "ctx"), axis=0, tiled=True),
            lax.all_gather(shards[2], ("fsdp", "ctx"), axis=0, tiled=True),
            lax.all_gather(shards[3], ("fsdp", "ctx"), axis=0, tiled=True),
            lax.all_gather(shards[4], ("fsdp", "ctx"), axis=0, tiled=True),
            lax.all_gather(shards[5], ("fsdp", "ctx"), axis=0, tiled=True),
            lax.all_gather(shards[6], ("fsdp", "ctx"), axis=0, tiled=True),
            lax.all_gather(shards[7], ("fsdp", "ctx"), axis=0, tiled=True),
            lax.all_gather(shards[8], ("fsdp", "ctx"), axis=0, tiled=True),
        )
        gain_attn, w_query, w_key, w_value, w_out, gain_ffn, w_gate, w_up, w_down = full
        inputs = activations_in[index].reshape(rows, width).astype(jnp.float32)
        inverse_one = lax.rsqrt(jnp.mean(inputs * inputs, -1, keepdims=True) + epsilon)
        normed_one = inputs * inverse_one
        first_in = (normed_one * gain_attn).astype(jnp.bfloat16)
        query_lin = jnp.dot(first_in, w_query, preferred_element_type=jnp.float32)
        key_lin = jnp.dot(first_in, w_key, preferred_element_type=jnp.float32)
        value_lin = jnp.dot(first_in, w_value, preferred_element_type=jnp.float32)
        query_rot = rotate(query_lin.reshape(rows, HEADS, HEAD), cosine, sine).astype(jnp.bfloat16)
        key_rot = rotate(key_lin.reshape(rows, KV_HEADS, HEAD), cosine, sine).astype(jnp.bfloat16)
        key_rot = key_rot.reshape(seq_count, span, KV_HEADS * HEAD)
        value_low = value_lin.astype(jnp.bfloat16).reshape(seq_count, span, KV_HEADS * HEAD)
        key_all, value_all = (
            lax.all_gather(key_rot, "ctx", axis=1, tiled=True),
            lax.all_gather(value_low, "ctx", axis=1, tiled=True),
        )
        query_split = query_rot.reshape(seq_count, span, KV_HEADS, groups, HEAD)
        key_split = key_all.reshape(seq_count, length, KV_HEADS, HEAD)
        value_split = value_all.reshape(seq_count, length, KV_HEADS, HEAD)
        mixed_all, log_totals = lax.map(
            attend, (query_split, key_split, value_split, prefix_len[index])
        )
        attn_low = mixed_all.reshape(rows, HEADS * HEAD).astype(jnp.bfloat16)
        middle = inputs + jnp.dot(attn_low, w_out, preferred_element_type=jnp.float32)
        inverse_two = lax.rsqrt(jnp.mean(middle * middle, -1, keepdims=True) + epsilon)
        normed_two = middle * inverse_two
        second_in = (normed_two * gain_ffn).astype(jnp.bfloat16)
        gate = jnp.dot(second_in, w_gate, preferred_element_type=jnp.float32)
        upward = jnp.dot(second_in, w_up, preferred_element_type=jnp.float32)
        hidden = (jax.nn.silu(gate) * upward).astype(jnp.bfloat16)
        result = middle + jnp.dot(hidden, w_down, preferred_element_type=jnp.float32)
        outputs.append(result.astype(jnp.bfloat16).reshape(seq_count, span, width))
        back = (
            lax.all_gather(shards[0], ("fsdp", "ctx"), axis=0, tiled=True),
            lax.all_gather(shards[1], ("fsdp", "ctx"), axis=0, tiled=True),
            lax.all_gather(shards[2], ("fsdp", "ctx"), axis=0, tiled=True),
            lax.all_gather(shards[3], ("fsdp", "ctx"), axis=0, tiled=True),
            lax.all_gather(shards[4], ("fsdp", "ctx"), axis=0, tiled=True),
            lax.all_gather(shards[5], ("fsdp", "ctx"), axis=0, tiled=True),
            lax.all_gather(shards[6], ("fsdp", "ctx"), axis=0, tiled=True),
            lax.all_gather(shards[7], ("fsdp", "ctx"), axis=0, tiled=True),
            lax.all_gather(shards[8], ("fsdp", "ctx"), axis=0, tiled=True),
        )
        gain_attn, w_query, w_key, w_value, w_out, gain_ffn, w_gate, w_up, w_down = back
        grad_y = cotangent[index].reshape(rows, width).astype(jnp.float32)
        grad_y_low = grad_y.astype(jnp.bfloat16)
        grad_wdown = jnp.einsum("rf,rd->fd", hidden, grad_y_low, preferred_element_type=jnp.float32)
        grad_hidden = jnp.einsum(
            "rd,fd->rf", grad_y_low, w_down, preferred_element_type=jnp.float32
        )
        sigma = jax.nn.sigmoid(gate)
        grad_up_low = (grad_hidden * gate * sigma).astype(jnp.bfloat16)
        grad_gate_low = (grad_hidden * upward * sigma * (1.0 + gate * (1.0 - sigma))).astype(
            jnp.bfloat16
        )
        grad_wgate = jnp.einsum(
            "rd,rf->df", second_in, grad_gate_low, preferred_element_type=jnp.float32
        )
        grad_wup = jnp.einsum(
            "rd,rf->df", second_in, grad_up_low, preferred_element_type=jnp.float32
        )
        grad_second = jnp.einsum(
            "rf,df->rd", grad_gate_low, w_gate, preferred_element_type=jnp.float32
        ) + jnp.einsum("rf,df->rd", grad_up_low, w_up, preferred_element_type=jnp.float32)
        grad_gain_ffn = jnp.sum(grad_second * normed_two, 0)
        grad_middle = grad_y + norm_back(grad_second * gain_ffn, normed_two, inverse_two)
        grad_branch_low = grad_middle.astype(jnp.bfloat16)
        grad_wout = jnp.einsum(
            "ra,rd->ad", attn_low, grad_branch_low, preferred_element_type=jnp.float32
        )
        grad_attn_low = jnp.einsum(
            "rd,ad->ra", grad_branch_low, w_out, preferred_element_type=jnp.float32
        ).astype(jnp.bfloat16)
        grad_mixed = grad_attn_low.reshape(seq_count, span, KV_HEADS, groups, HEAD)
        grad_query_rot, grad_key_part, grad_value_part = lax.map(
            attend_back,
            (query_split, key_split, value_split, prefix_len[index], log_totals, grad_mixed),
        )
        grad_key_own, grad_value_own = (
            lax.psum_scatter(
                grad_key_part.astype(jnp.bfloat16), "ctx", scatter_dimension=1, tiled=True
            ).astype(jnp.float32),
            lax.psum_scatter(
                grad_value_part.astype(jnp.bfloat16), "ctx", scatter_dimension=1, tiled=True
            ).astype(jnp.float32),
        )
        grad_query = rotate_back(grad_query_rot.reshape(rows, HEADS, HEAD), cosine, sine)
        grad_query = grad_query.reshape(rows, HEADS * HEAD).astype(jnp.bfloat16)
        grad_key = rotate_back(grad_key_own.reshape(rows, KV_HEADS, HEAD), cosine, sine)
        grad_key = grad_key.reshape(rows, KV_HEADS * HEAD).astype(jnp.bfloat16)
        grad_value = grad_value_own.reshape(rows, KV_HEADS * HEAD).astype(jnp.bfloat16)
        grad_wquery = jnp.einsum(
            "rd,rq->dq", first_in, grad_query, preferred_element_type=jnp.float32
        )
        grad_wkey = jnp.einsum("rd,rq->dq", first_in, grad_key, preferred_element_type=jnp.float32)
        grad_wvalue = jnp.einsum(
            "rd,rq->dq", first_in, grad_value, preferred_element_type=jnp.float32
        )
        grad_first = (
            jnp.einsum("rq,dq->rd", grad_query, w_query, preferred_element_type=jnp.float32)
            + jnp.einsum("rq,dq->rd", grad_key, w_key, preferred_element_type=jnp.float32)
            + jnp.einsum("rq,dq->rd", grad_value, w_value, preferred_element_type=jnp.float32)
        )
        grad_gain_attn = jnp.sum(grad_first * normed_one, 0)
        grad_inputs = grad_middle + norm_back(grad_first * gain_attn, normed_one, inverse_one)
        input_grads.append(grad_inputs.astype(jnp.bfloat16).reshape(seq_count, span, width))
        grads = flatten_all(
            (
                grad_gain_attn,
                grad_wquery,
                grad_wkey,
                grad_wvalue,
                grad_wout,
                grad_gain_ffn,
                grad_wgate,
                grad_wup,
                grad_wdown,
            )
        )
        pieces = lax.psum_scatter(grads, ("fsdp", "ctx"), scatter_dimension=0, tiled=True)
        if index == 0:
            collected = pieces
        else:
            collected = tuple((a + b for a, b in zip(collected, pieces)))
    summed = jax.tree.map(
        lambda part: part.astype(jnp.float32), lax.psum(shortened(collected), "grp")
    )
    shaped = tuple((s.reshape(w.shape) for s, w in zip(summed, shards)))
    return (
        jnp.stack(outputs, 0),
        jnp.stack(input_grads, 0),
        shaped[0],
        shaped[1],
        shaped[2],
        shaped[3],
        shaped[4],
        shaped[5],
        shaped[6],
        shaped[7],
        shaped[8],
    )


BLOCK = 256
TO_LOG2 = math.log2(math.e) / math.sqrt(HEAD)
F32, BF16 = jnp.float32, jnp.bfloat16
NN = (((1,), (0,)), ((), ()))
NT = (((1,), (1,)), ((), ()))
TN = (((0,), (0,)), ((), ()))


def dot(a, b, dims=NN):
    return lax.dot_general(a, b, dims, preferred_element_type=F32)


def turned(rows, cosine, sine, sign):
    a, b = rows[: HEAD // 2], rows[HEAD // 2 :]
    return jnp.concatenate([a * cosine - sign * b * sine, b * cosine + sign * a * sine], 0)


def masked(scores, prefix, first, block):
    key = first + lax.broadcasted_iota(jnp.int32, scores.shape, 0)
    query = block * BLOCK + lax.broadcasted_iota(jnp.int32, scores.shape, 1)
    return jnp.where((key <= query) | (key < prefix), scores, -1e30)


def reach(block):
    return max(2, block + 1) * BLOCK


def scores_of(keys, query, prefix, block):
    clear = block * BLOCK
    edge = masked(dot(keys[clear:], query), prefix, clear, block)
    if not clear:
        return edge
    return jnp.concatenate([dot(keys[:clear], query), edge], 0)


MESH = pl.DeviceIdType.MESH
DMA = pltpu.SemaphoreType.DMA
ANY = pl.BlockSpec(memory_space=pl.ANY)
VMEM = pl.BlockSpec(memory_space=pltpu.VMEM)


def where_am_i():
    return lax.axis_index("grp"), lax.axis_index("fsdp"), lax.axis_index("ctx")


def remote(src, dst, send, recv, grp, fsdp, ctx):
    return pltpu.make_async_remote_copy(
        src_ref=src,
        dst_ref=dst,
        send_sem=send,
        recv_sem=recv,
        device_id={"grp": grp, "fsdp": fsdp, "ctx": ctx},
        device_id_type=MESH,
    )


def greet(partners):
    barrier = pltpu.get_barrier_semaphore()
    for grp, fsdp, ctx in partners:
        pl.semaphore_signal(
            barrier, inc=1, device_id={"grp": grp, "fsdp": fsdp, "ctx": ctx}, device_id_type=MESH
        )
    pl.semaphore_wait(barrier, len(partners))


class Columns:
    split = True

    def __init__(self, core, shard, out):
        self.core, self.shard, self.out = core, shard, out
        self.rows, self.cols = shard.shape[0], out.shape[1] // 4

    def mine(self, j, quarter):
        to = self.core if j == 0 else 1 - self.core
        return self.shard.at[:, pl.ds(pl.multiple_of((2 * quarter + to) * self.cols, 128), self.cols)]

    def block(self, plane, j, quarter):
        owner = self.core if j == 0 else 1 - self.core
        start = pl.multiple_of((2 * plane + owner) * self.rows, 16)
        return self.out.at[pl.ds(start, self.rows), pl.ds(pl.multiple_of(quarter * self.cols, 128), self.cols)]


class Rows:
    split = False

    def __init__(self, core, shard, out):
        self.core, self.shard, self.out = core, shard, out
        self.rows = shard.shape[0] // 8

    def mine(self, j, quarter):
        return self.shard.at[pl.ds(pl.multiple_of((2 * quarter + j) * self.rows, 16), self.rows), :]

    def block(self, plane, j, quarter):
        start = pl.multiple_of((8 * plane + 2 * quarter + j) * self.rows, 16)
        return self.out.at[pl.ds(start, self.rows), :]

    def own(self, plane):
        return self.out.at[pl.ds(pl.multiple_of(plane * 8 * self.rows, 16), 8 * self.rows), :]


class Gather:
    @staticmethod
    def semaphores(count):
        return [DMA((count, 4)), DMA((count, 4)), DMA((count, 4))] + [DMA((count, 3, 2))] * 2 + [DMA((count, 3, 2, 2))] * 2 + [DMA((count, 3, 2))] * 2

    def __init__(self, units, sems):
        self.units, self.sems = units, sems
        self.grp, self.plane, self.core = where_am_i()
        self.side = self.grp + 1 - 2 * lax.rem(self.grp, 2)
        self.up = lax.rem(self.grp + 2, 4)
        self.planes = [lax.rem(self.plane + s, 4) for s in (1, 2, 3)]
        self.origins = [lax.rem(self.plane + 4 - s, 4) for s in (1, 2, 3)]
        self.left = []

    def partners(self):
        grp, plane, core = self.grp, self.plane, self.core
        found = [(grp, z, c) for z in self.planes for c in (core, 1 - core)]
        return found + [(grp, plane, 1 - core), (self.side, plane, core), (self.up, plane, core)]

    def other(self, j):
        return self.core if j == 0 else 1 - self.core

    def send(self, src, dst, send, recv, grp, plane, core):
        copy = remote(src, dst, send, recv, grp, plane, core)
        copy.start()
        self.left.append(copy.wait_send)

    def got(self, here, send, recv):
        remote(here, here, send, recv, self.side, self.plane, self.core).wait_recv()

    def first(self, n):
        u = self.units[n]
        loc, near_s, near_r, z_s, z_r = self.sems[:5]
        for i, z in enumerate(self.planes):
            for j in range(2):
                if u.split:
                    dst = u.block(self.plane, 0, self.grp)
                    self.send(u.mine(j, self.grp), dst, z_s.at[n, i, j], z_r.at[n, i, j], self.grp, z, self.other(j))
                else:
                    dst = u.block(self.plane, j, self.grp)
                    self.send(u.mine(j, self.grp), dst, z_s.at[n, i, j], z_r.at[n, i, j], self.grp, z, self.core)
        if u.split:
            for q in range(4):
                dst = u.block(self.plane, 0, q)
                self.send(u.mine(1, q), dst, near_s.at[n, q], near_r.at[n, q], self.grp, self.plane, 1 - self.core)
                copy = pltpu.make_async_copy(u.mine(0, q), dst, loc.at[n, q])
                copy.start()
                self.left.append(copy.wait)
        else:
            copy = pltpu.make_async_copy(u.shard, u.own(self.plane), loc.at[n, 0])
            copy.start()
            self.left.append(copy.wait)

    def first_in(self, n):
        u = self.units[n]
        for i, z in enumerate(self.origins):
            for j in range(2):
                self.got(u.block(z, j, self.grp), self.sems[3].at[n, i, j], self.sems[4].at[n, i, j])

    def near_in(self, n):
        u = self.units[n]
        if u.split:
            for q in range(4):
                self.got(u.block(self.plane, 1, q), self.sems[1].at[n, q], self.sems[2].at[n, q])

    def second(self, n, here=False):
        u = self.units[n]
        z_s, z_r, xy_s, xy_r = self.sems[3:7]
        for i, z in enumerate(self.origins):
            for j in range(2):
                block = u.block(z, j, self.grp)
                if not here:
                    self.got(block, z_s.at[n, i, j], z_r.at[n, i, j])
                for t, to in enumerate((self.side, self.up)):
                    self.send(block, block, xy_s.at[n, i, j, t], xy_r.at[n, i, j, t], to, self.plane, self.core)

    def third(self, n):
        u = self.units[n]
        xy_s, xy_r, fw_s, fw_r = self.sems[5:9]
        for i, z in enumerate(self.origins):
            for t, (origin, to) in enumerate(((self.side, self.up), (self.up, self.side))):
                block = u.block(z, t, origin)
                self.got(block, xy_s.at[n, i, t, t], xy_r.at[n, i, t, t])
                self.send(block, block, fw_s.at[n, i, t], fw_r.at[n, i, t], to, self.plane, self.core)

    def last(self, n):
        u = self.units[n]
        xy_s, xy_r, fw_s, fw_r = self.sems[5:9]
        for i, z in enumerate(self.origins):
            for t, origin in enumerate((self.side, self.up)):
                self.got(u.block(z, 1 - t, origin), xy_s.at[n, i, 1 - t, t], xy_r.at[n, i, 1 - t, t])
            for t in range(2):
                self.got(u.block(z, t, 3 - self.grp), fw_s.at[n, i, t], fw_r.at[n, i, t])

    def sent_all(self, firsts, rest):
        loc, near_s, near_r, z_s, z_r, xy_s, xy_r, fw_s, fw_r = self.sems

        def out(block, send, recv):
            remote(block, block, send, recv, self.side, self.plane, self.core).wait_send()

        for n in firsts:
            u = self.units[n]
            for i in range(3):
                for j in range(2):
                    out(u.block(self.plane, j, self.grp), z_s.at[n, i, j], z_r.at[n, i, j])
            if u.split:
                for q in range(4):
                    out(u.block(self.plane, 0, q), near_s.at[n, q], near_r.at[n, q])
                    pltpu.make_async_copy(u.mine(0, q), u.block(self.plane, 0, q), loc.at[n, q]).wait()
            else:
                pltpu.make_async_copy(u.shard, u.own(self.plane), loc.at[n, 0]).wait()
        for n in rest:
            u = self.units[n]
            for i, z in enumerate(self.origins):
                for j in range(2):
                    for t in range(2):
                        out(u.block(z, j, self.grp), xy_s.at[n, i, j, t], xy_r.at[n, i, j, t])
                for t, origin in enumerate((self.side, self.up)):
                    out(u.block(z, t, origin), fw_s.at[n, i, t], fw_r.at[n, i, t])

    def drain(self):
        for wait in self.left:
            wait()
        self.left = []


def start_kernel(heads, kv_heads, x_ref, dy_ref, wq_ref, wk_ref, wv_ref, wo_ref, gate_ref, ga_ref, gf_ref,
                 pack_out, gate_out, x_out, dy_out, pack, gate, trade_s, trade_r, own_s, *sems):
    _, _, core = where_am_i()
    q_cols, kv_cols, span = heads * HEAD, kv_heads * HEAD, x_ref.shape[1]
    cols = pack.shape[1] // 8
    gain = ga_ref[...].astype(F32)
    for k in range(2):
        parts = [(wq_ref[:, k * q_cols : (k + 1) * q_cols].astype(F32) * gain).astype(BF16)]
        parts += [(w[:, k * kv_cols : (k + 1) * kv_cols].astype(F32) * gain).astype(BF16) for w in (wk_ref, wv_ref)]
        row = jnp.concatenate(parts + [wo_ref[:, k * q_cols : (k + 1) * q_cols]], 1)
        for q in range(4):
            pack[:, (2 * q + k) * cols : (2 * q + k + 1) * cols] = row[:, q * cols : (q + 1) * cols]
    gather = Gather([Columns(core, pack, pack_out), Columns(core, gate, gate_out)], sems)
    greet(gather.partners())
    gather.first(0)
    gate[...] = (gate_ref[...].astype(F32) * gf_ref[...].astype(F32)).astype(BF16)
    waits = []

    def trade(ref, out, which):
        for s in range(ref.shape[0]):
            def rows(owner):
                return out.at[pl.ds(pl.multiple_of((2 * s + owner) * span, 16), span), :]
            copy = remote(ref.at[s], rows(core), trade_s.at[which, s], trade_r.at[which, s], gather.grp, gather.plane, 1 - core)
            copy.start()
            gather.left.append(copy.wait_send)
            copy = pltpu.make_async_copy(ref.at[s], rows(core), own_s.at[which, s])
            copy.start()
            gather.left.append(copy.wait)
            waits.append((rows(1 - core), trade_s.at[which, s], trade_r.at[which, s]))

    trade(x_ref, x_out, 0)
    gather.second(0)
    gather.first(1)
    trade(dy_ref, dy_out, 1)
    gather.third(0)
    gather.last(0)
    gather.near_in(0)
    gather.near_in(1)
    for wait in waits:
        gather.got(*wait)
    gather.first_in(1)
    gather.drain()


def start(x, dy, wq, wk, wv, wo, gate, gain_attn, gain_ffn, heads, kv_heads):
    count, span, width = x.shape
    shard, hidden = gate.shape
    cols = 2 * (heads + kv_heads) * HEAD
    shape = jax.ShapeDtypeStruct
    return pl.pallas_call(
        functools.partial(start_kernel, heads, kv_heads),
        in_specs=[VMEM] * 9,
        out_specs=(ANY,) * 4,
        out_shape=(
            shape((8 * shard, cols), BF16),
            shape((8 * shard, hidden // 2), BF16),
            shape((2 * count * span, width), BF16),
            shape((2 * count * span, width), BF16),
        ),
        scratch_shapes=[pltpu.VMEM((shard, 2 * cols), BF16), pltpu.VMEM((shard, hidden), BF16)]
        + [DMA((2, count))] * 3
        + Gather.semaphores(2),
        compiler_params=pltpu.CompilerParams(collective_id=0, has_side_effects=True, vmem_limit_bytes=48 * 2**20),
        name="start",
    )(x, dy, wq, wk, wv, wo, gate, gain_attn, gain_ffn)


def front_kernel(heads, kv_heads, blocks, prefix_ref, x_ref, own_ref, w_ref, up_ref, gf_ref, cos_ref, sin_ref, gate_in, down_ref,
                 n_ref, qt_ref, kvt_ref, kv_ref, ot_ref, lse_ref, wo_ref, x1_ref, inv_ref, two_out, gate_out, up_out, down_out,
                 up_s, wo_send, wo_recv, part_mine, part_send, part_recv, two_mine,
                 wo_sem, part_sem, two_sem, own_sem, *sems):
    step = pl.program_id(0)
    grp, plane, core = where_am_i()
    count = prefix_ref.shape[0]
    tiles = count * blocks
    groups = heads // kv_heads
    q_cols, kv_cols = heads * HEAD, kv_heads * HEAD
    width = x_ref.shape[1]
    half = blocks // 2
    gather = Gather([Columns(core, up_s, gate_out), Columns(core, up_s, up_out), Rows(core, down_ref, down_out)], sems)

    def at(when):
        return pl.when(step == when)

    def out_weight(owner):
        return w_ref[pl.ds(pl.multiple_of(owner * q_cols, 16), q_cols), q_cols + 2 * kv_cols :]

    def wo_copy():
        return remote(wo_send, wo_recv, wo_sem.at[0], wo_sem.at[1], grp, plane, 1 - core)

    @at(0)
    def _():
        greet(gather.partners())
        gather.second(0, here=True)
        wo_send[...] = out_weight(1 - core)
        wo_copy().start()
        up_s[...] = (up_ref[...].astype(F32) * gf_ref[...].astype(F32)).astype(BF16)
        gather.first(1)

    @at(tiles - 1)
    def _():
        wo_copy().wait()
        mine, other = out_weight(core), wo_recv[...]
        wo_ref[...] = jnp.concatenate([jnp.where(core == 0, mine, other), jnp.where(core == 0, other, mine)], 1)

    @at(tiles)
    def _():
        gather.first(2)
        gather.third(0)

    @at(tiles + 1)
    def _():
        gather.second(1)

    @at(tiles + 3)
    def _():
        gather.third(1)

    @at(tiles + 4)
    def _():
        gather.second(2)

    @at(tiles + 6)
    def _():
        gather.third(2)

    @pl.when(step < tiles)
    def _():
        x = x_ref[...].astype(F32)
        normed = (x * lax.rsqrt(jnp.mean(x * x, -1, keepdims=True) + epsilon)).astype(BF16)
        n_ref[...] = normed
        flat = dot(normed, w_ref[:, : q_cols + 2 * kv_cols])
        across = flat.T
        tokens = pl.ds(pl.multiple_of(step * BLOCK, BLOCK), BLOCK)
        here = pl.ds(pl.multiple_of(lax.rem(step, blocks) * BLOCK, BLOCK), BLOCK)
        cosine, sine = cos_ref[:, here], sin_ref[:, here]
        for h in range(heads):
            rows = turned(across[h * HEAD : (h + 1) * HEAD], cosine, sine, 1.0)
            qt_ref[h * HEAD : (h + 1) * HEAD, tokens] = (rows * TO_LOG2).astype(BF16)
        keys = [across[q_cols + h * HEAD : q_cols + (h + 1) * HEAD] for h in range(kv_heads)]
        keys = jnp.concatenate([turned(rows, cosine, sine, 1.0) for rows in keys], 0)
        kvt_ref[:kv_cols, tokens] = keys.astype(BF16)
        kvt_ref[kv_cols:, tokens] = across[q_cols + kv_cols :].astype(BF16)
        kv_ref[tokens, :kv_cols] = keys.T.astype(BF16)
        kv_ref[tokens, kv_cols:] = flat[:, q_cols + kv_cols :].astype(BF16)

    def rows_of(tile, owner):
        start = (tile // half) * blocks + owner * half + lax.rem(tile, half)
        return two_out.at[pl.ds(pl.multiple_of(start * BLOCK, BLOCK), BLOCK), :]

    def part_copy(slot):
        return remote(part_send.at[slot], part_recv.at[slot], part_sem.at[0, slot], part_sem.at[1, slot], grp, plane, 1 - core)

    def two_copy(slot):
        there = rows_of(slot, core)
        return remote(two_mine.at[slot], there, two_sem.at[0, slot], two_sem.at[1, slot], grp, plane, 1 - core)

    def two_keep(slot):
        return pltpu.make_async_copy(two_mine.at[slot], rows_of(slot, core), own_sem.at[slot])

    def finish(turn):
        block, s = lax.rem(turn, blocks), turn // blocks
        slot = s * half + lax.rem(block, half)

        @pl.when(block // half == core)
        def _():
            part_copy(slot).wait_recv()
            rows = pl.ds(pl.multiple_of(slot * BLOCK, BLOCK), BLOCK)
            middle = own_ref[rows, :].astype(F32) + part_mine[slot].astype(F32) + part_recv[slot].astype(F32)
            x1_ref[rows, :] = middle
            inverse = lax.rsqrt(jnp.mean(middle * middle, -1, keepdims=True) + epsilon)
            inv_ref[rows, :] = inverse
            two_mine[slot] = (middle * inverse).astype(BF16)
            two_copy(slot).start()
            two_keep(slot).start()

    def run(block):
        n = reach(block)
        turn = step - tiles
        s = turn // blocks
        prefix = prefix_ref[s]
        base = pl.multiple_of(s * blocks * BLOCK, BLOCK)
        tokens = pl.ds(pl.multiple_of(turn * BLOCK, BLOCK), BLOCK)

        def score(h):
            kh = h // groups
            keys = kv_ref[pl.ds(base, n), kh * HEAD : (kh + 1) * HEAD]
            return scores_of(keys, qt_ref[h * HEAD : (h + 1) * HEAD, tokens], prefix, block)

        def mix(h, weights, total):
            kh = h // groups
            vt = kvt_ref[kv_cols + kh * HEAD : kv_cols + (kh + 1) * HEAD, pl.ds(base, n)]
            ot_ref[h * HEAD : (h + 1) * HEAD, tokens] = (dot(vt, weights) / total).astype(BF16)

        later, held = score(0), None
        for h in range(heads):
            scores = later
            if h + 1 < heads:
                later = score(h + 1)
            peak = jnp.max(scores, 0, keepdims=True)
            weights = jnp.exp2(scores - peak)
            total = jnp.sum(weights, 0, keepdims=True)
            lse_ref[h : h + 1, tokens] = peak + jnp.log2(total)
            if held:
                mix(*held)
            held = (h, weights.astype(BF16), total)
        mix(*held)
        part = dot(ot_ref[:, tokens], wo_ref[...], TN).astype(BF16)
        slot = s * half + block % half

        @pl.when(core == block // half)
        def _():
            part_mine[slot] = part

        @pl.when(core != block // half)
        def _():
            part_send[slot] = part
            part_copy(slot).start()

    @pl.when(step > tiles)
    def _():
        finish(step - tiles - 1)

    for block in range(blocks):
        pl.when((step >= tiles) & (lax.rem(step, blocks) == block))(functools.partial(run, block))

    @at(2 * tiles - 1)
    def _():
        finish(step - tiles)
        for n in range(3):
            gather.last(n)
        gather.near_in(1)
        for slot in range(count * half):
            part_copy(slot).wait_send()
            two_copy(slot).wait_send()
            two_keep(slot).wait()
            there = rows_of(slot, 1 - core)
            remote(there, there, two_sem.at[0, slot], two_sem.at[1, slot], grp, plane, 1 - core).wait_recv()
        gather.sent_all((1, 2), (0, 1, 2))


def front(prefix, x, own, pack, gate_part, up, down, gain_ffn, cosine, sine, heads, kv_heads, length):
    tokens, width = x.shape
    count, blocks = tokens // length, length // BLOCK
    tiles = tokens // BLOCK
    slots = tiles // 2
    q_cols, kv_cols = heads * HEAD, kv_heads * HEAD
    shape = jax.ShapeDtypeStruct
    once = pl.Buffered(1)

    def fixed(*dims):
        return pl.BlockSpec(dims, lambda i: (0,) * len(dims), pipeline_mode=once)

    tile = pl.BlockSpec((BLOCK, width), lambda i: (jnp.minimum(i, tiles - 1), 0))
    return pl.pallas_call(
        functools.partial(front_kernel, heads, kv_heads, blocks),
        grid=(2 * tiles,),
        in_specs=[
            pl.BlockSpec(memory_space=pltpu.SMEM),
            tile,
            fixed(tokens // 2, width),
            fixed(*pack.shape),
            fixed(*up.shape),
            fixed(*gain_ffn.shape),
            fixed(*cosine.shape),
            fixed(*sine.shape),
            ANY,
            fixed(*down.shape),
        ],
        out_specs=(
            tile,
            fixed(q_cols, tokens),
            fixed(2 * kv_cols, tokens),
            fixed(tokens, 2 * kv_cols),
            fixed(q_cols, tokens),
            fixed(heads, tokens),
            fixed(q_cols, width),
            fixed(tokens // 2, width),
            fixed(tokens // 2, 1),
            ANY, ANY, ANY, ANY,
        ),
        out_shape=(
            shape((tokens, width), BF16),
            shape((q_cols, tokens), BF16),
            shape((2 * kv_cols, tokens), BF16),
            shape((tokens, 2 * kv_cols), BF16),
            shape((q_cols, tokens), BF16),
            shape((heads, tokens), F32),
            shape((q_cols, width), BF16),
            shape((tokens // 2, width), F32),
            shape((tokens // 2, 1), F32),
            shape((tokens, width), BF16),
            shape(gate_part.shape, BF16),
            shape(gate_part.shape, BF16),
            shape((4 * down.shape[0], width), BF16),
        ),
        input_output_aliases={8: 10},
        scratch_shapes=[
            pltpu.VMEM(up.shape, BF16),
            pltpu.VMEM((q_cols, q_cols), BF16),
            pltpu.VMEM((q_cols, q_cols), BF16),
        ]
        + [pltpu.VMEM((slots, BLOCK, width), BF16)] * 4
        + [DMA((2,)), DMA((2, slots)), DMA((2, slots)), DMA((slots,))]
        + Gather.semaphores(3),
        compiler_params=pltpu.CompilerParams(collective_id=1, has_side_effects=True, vmem_limit_bytes=60 * 2**20),
        cost_estimate=pl.CostEstimate(flops=2 * tokens * width * 1536, bytes_accessed=16 * tokens * width, transcendentals=0),
        name="front",
    )(prefix, x, own, pack, up, gain_ffn, cosine, sine, gate_part, down)


def feed_kernel(n_ref, gate_ref, up_ref, down_ref, hidden_ref, by_up_ref, by_gate_ref, part_ref):
    n = n_ref[...]
    gate = dot(n, gate_ref[...])
    upward = dot(n, up_ref[...])
    sigma = 1.0 / (1.0 + jnp.exp(-gate))
    silu = gate * sigma
    hidden = (silu * upward).astype(BF16)
    hidden_ref[...] = hidden
    by_up_ref[...] = silu.astype(BF16)
    by_gate_ref[...] = (upward * sigma * (1.0 + gate - silu)).astype(BF16)
    part_ref[...] = dot(hidden, down_ref[...]).astype(BF16)


def feed(n, gate, up, down):
    tokens, width = n.shape
    units = gate.shape[1]
    shape = jax.ShapeDtypeStruct
    once = pl.Buffered(1)
    tile = lambda cols: pl.BlockSpec((BLOCK, cols), lambda i: (i, 0))
    fixed = lambda a: pl.BlockSpec(a.shape, lambda i: (0, 0), pipeline_mode=once)
    return pl.pallas_call(
        feed_kernel,
        grid=(tokens // BLOCK,),
        in_specs=[tile(width), fixed(gate), fixed(up), fixed(down)],
        out_specs=(tile(units), tile(units), tile(units), tile(width)),
        out_shape=(shape((tokens, units), BF16),) * 3 + (shape((tokens, width), BF16),),
        compiler_params=pltpu.CompilerParams(vmem_limit_bytes=48 * 2**20),
        cost_estimate=pl.CostEstimate(flops=6 * tokens * width * units, bytes_accessed=2 * tokens * (3 * units + 2 * width), transcendentals=tokens * units),
        name="feed",
    )(n, gate, up, down)


def finish_kernel(heads, kv_heads, pack_ref, gate_ref, up_ref, down_ref, wq_ref, wk_ref, wv_ref, wg_ref, wu_ref, ga_ref, gf_ref,
                  q_out, k_out, v_out, o_out, gate_out, up_out, down_out, ga_out, gf_out):
    q_cols, kv_cols = heads * HEAD, kv_heads * HEAD
    cols = pack_ref.shape[1] // 8
    gain = ga_ref[...].astype(F32)
    total = jnp.zeros(gain.shape, F32)
    for k in range(2):
        row = jnp.concatenate([pack_ref[:, (2 * q + k) * cols : (2 * q + k + 1) * cols].astype(F32) for q in range(4)], 1)
        at = 0
        for w, out, size in ((wq_ref, q_out, q_cols), (wk_ref, k_out, kv_cols), (wv_ref, v_out, kv_cols)):
            part, here = row[:, at : at + size], slice(k * size, (k + 1) * size)
            total += jnp.sum(part * w[:, here].astype(F32), -1, keepdims=True)
            out[:, here] = part * gain
            at += size
        o_out[:, k * q_cols : (k + 1) * q_cols] = row[:, at:]
    ga_out[...] = total
    gain = gf_ref[...].astype(F32)
    total = jnp.zeros(gain.shape, F32)
    for ref, w, out in ((gate_ref, wg_ref, gate_out), (up_ref, wu_ref, up_out)):
        part = ref[...].astype(F32)
        total += jnp.sum(part * w[...].astype(F32), -1, keepdims=True)
        out[...] = part * gain
    gf_out[...] = total
    down_out[...] = down_ref[...].astype(F32)


def finish(pack, gate, up, down, wq, wk, wv, wo, wg, wu, ga, gf, heads, kv_heads):
    shape = lambda a: jax.ShapeDtypeStruct(a.shape, F32)
    whole = pl.BlockSpec(memory_space=pltpu.VMEM)
    return pl.pallas_call(
        functools.partial(finish_kernel, heads, kv_heads),
        in_specs=[whole] * 11,
        out_specs=(whole,) * 9,
        out_shape=(shape(wq), shape(wk), shape(wv), shape(wo), shape(wg), shape(wu), shape(down), shape(ga), shape(gf)),
        compiler_params=pltpu.CompilerParams(vmem_limit_bytes=48 * 2**20),
        name="finish",
    )(pack, gate, up, down, wq, wk, wv, wg, wu, ga, gf)


def halves_of(rows, cols, split):
    return (rows // 8, cols // 4) if split else (rows // 32, cols)


class Summand:
    def __init__(self, core, ref, out, split):
        self.core, self.ref, self.out, self.split = core, ref, out, split
        self.rows, self.cols = halves_of(*ref.shape, split)

    def half(self, plane, quarter, path):
        if self.split:
            start = pl.multiple_of((2 * plane + path) * self.rows, 16)
            return self.ref.at[pl.ds(start, self.rows), pl.ds(pl.multiple_of(quarter * self.cols, 128), self.cols)]
        start = pl.multiple_of(((4 * plane + quarter) * 2 + path) * self.rows, 16)
        return self.ref.at[pl.ds(start, self.rows), :]

    def place(self, quarter, j, other):
        if self.split:
            return self.out.at[:, pl.ds(pl.multiple_of((2 * quarter + other) * self.cols, 128), self.cols)]
        return self.out.at[pl.ds(pl.multiple_of((2 * quarter + j) * self.rows, 16), self.rows), :]


class Reduce:
    @staticmethod
    def buffers(halves):
        return [pltpu.VMEM(lead + h, BF16) for h in halves for lead in ((2, 4, 2), (2, 4, 2), (2, 4), (3, 2), (4, 2))]

    @staticmethod
    def semaphores(n):
        return [DMA((n, 2, 4, 2))] * 3 + [DMA((n, 2, 4))] * 2 + [DMA((n, 3))] * 2 + [DMA((n, 4, 2))] * 2

    def __init__(self, units, buffers, sems):
        self.units, self.sems = units, sems
        self.bufs = [buffers[5 * n : 5 * n + 5] for n in range(len(units))]
        self.grp, self.plane, self.core = where_am_i()
        gx, gy = lax.rem(self.grp, 2), self.grp // 2
        self.gx, self.gy = gx, gy
        side, up = self.grp + 1 - 2 * gx, lax.rem(self.grp + 2, 4)
        self.first_to, self.second_to, self.keep = (side, up), (up, side), (gy, gx)
        self.planes = [lax.rem(self.plane + s, 4) for s in (1, 2, 3)]
        self.origins = [lax.rem(self.plane + 4 - s, 4) for s in (1, 2, 3)]
        self.others = [lax.rem(self.grp + s, 4) for s in (1, 2, 3)]
        self.sources = [lax.rem(self.grp + 4 - s, 4) for s in (1, 2, 3)]

    def partners(self):
        grp, plane, core = self.grp, self.plane, self.core
        found = [(grp, z, core) for z in self.planes] + [(grp, plane, 1 - core)]
        return found + [(g, plane, c) for g in self.others for c in (core, 1 - core)]

    def quarter(self, path, i, own):
        if path == 0:
            return 2 * i + (self.gx if own else 1 - self.gx)
        return 2 * (self.gy if own else 1 - self.gy) + i

    def first_copy(self, n, path, z, i):
        _, s1, r1 = self.sems[:3]
        src = self.units[n].half(z, self.quarter(path, i, False), path)
        dst = self.bufs[n][1].at[path, z, i]
        return remote(src, dst, s1.at[n, path, z, i], r1.at[n, path, z, i], self.first_to[path], self.plane, self.core)

    def load_copy(self, n, path, z, i):
        src = self.units[n].half(z, self.quarter(path, i, True), path)
        return pltpu.make_async_copy(src, self.bufs[n][0].at[path, z, i], self.sems[0].at[n, path, z, i])

    def second_copy(self, n, path, z):
        acc, _, second = self.bufs[n][:3]
        s2, r2 = self.sems[3:5]
        src = acc.at[path, z, 1 - self.keep[path]]
        return remote(src, second.at[path, z], s2.at[n, path, z], r2.at[n, path, z], self.second_to[path], self.plane, self.core)

    def third_copy(self, n, i):
        third, fin = self.bufs[n][3:]
        s3, r3 = self.sems[5:7]
        return remote(fin.at[self.planes[i]], third.at[i], s3.at[n, i], r3.at[n, i], self.grp, self.planes[i], self.core)

    def fourth_copy(self, n, i, j, coming=False):
        u, fin = self.units[n], self.bufs[n][4]
        s4, r4 = self.sems[7:9]
        other = (self.core if j == 0 else 1 - self.core) if u.split else self.core
        grp = self.grp if i == 3 else (self.sources if coming else self.others)[i]
        if coming:
            src = dst = u.place(grp, j, other)
        else:
            src = fin.at[self.plane, other if u.split else j]
            dst = u.place(self.grp, j, self.core)
        if i == 3 and not (u.split and j == 1):
            return pltpu.make_async_copy(src, dst, s4.at[n, 3, j])
        return remote(src, dst, s4.at[n, i, j], r4.at[n, i, j], grp, self.plane, other)

    @staticmethod
    def each():
        return [(path, z, i) for z in range(4) for path in range(2) for i in range(2)]

    def a(self, n):
        for path, z, i in self.each():
            self.first_copy(n, path, z, i).start()
            self.load_copy(n, path, z, i).start()

    def b(self, n):
        acc, got = self.bufs[n][:2]
        for z in range(4):
            for path in range(2):
                for i in range(2):
                    self.load_copy(n, path, z, i).wait()
                    self.first_copy(n, path, z, i).wait_recv()
                    acc[path, z, i] = (acc[path, z, i].astype(F32) + got[path, z, i].astype(F32)).astype(BF16)
                self.second_copy(n, path, z).start()

    def c(self, n):
        acc, _, second, _, fin = self.bufs[n]
        for z in range(4):
            for path in range(2):
                self.second_copy(n, path, z).wait_recv()
                fin[z, path] = (acc[path, z, self.keep[path]].astype(F32) + second[path, z].astype(F32)).astype(BF16)
        for i in range(3):
            self.third_copy(n, i).start()

    def d(self, n):
        third, fin = self.bufs[n][3:]
        for i in range(3):
            self.third_copy(n, i).wait_recv()
        for j in range(2):
            total = fin[self.plane, j].astype(F32)
            for i in range(3):
                total += third[i, j].astype(F32)
            fin[self.plane, j] = total.astype(BF16)
        for j in range(2):
            for i in range(4):
                self.fourth_copy(n, i, j).start()

    def e(self, n):
        u = self.units[n]
        for path, z, i in self.each():
            self.first_copy(n, path, z, i).wait_send()
        for z in range(4):
            for path in range(2):
                self.second_copy(n, path, z).wait_send()
        for i in range(3):
            self.third_copy(n, i).wait_send()
        for j in range(2):
            for i in range(4):
                if i == 3 and not (u.split and j == 1):
                    self.fourth_copy(n, i, j).wait()
                else:
                    self.fourth_copy(n, i, j).wait_send()
                    self.fourth_copy(n, i, j, coming=True).wait_recv()


class Trade:
    @staticmethod
    def buffers(slots, width):
        return [pltpu.VMEM((slots, BLOCK, width), BF16)] * 3

    @staticmethod
    def semaphores(slots):
        return [DMA((2, slots))]

    def __init__(self, bufs, sems, blocks):
        self.mine, self.out, self.come = bufs
        self.sem, self.half, self.blocks = sems[0], blocks // 2, blocks
        self.slots = self.mine.shape[0]
        self.grp, self.plane, self.core = where_am_i()

    def copy(self, slot):
        return remote(self.out.at[slot], self.come.at[slot], self.sem.at[0, slot], self.sem.at[1, slot], self.grp, self.plane, 1 - self.core)

    def where(self, turn):
        block = lax.rem(turn, self.blocks)
        return block // self.half, (turn // self.blocks) * self.half + lax.rem(block, self.half)

    def give(self, turn, part):
        owner, slot = self.where(turn)

        @pl.when(self.core == owner)
        def _():
            self.mine[slot] = part

        @pl.when(self.core != owner)
        def _():
            self.out[slot] = part
            self.copy(slot).start()

    def take(self, turn, close):
        owner, slot = self.where(turn)

        @pl.when(self.core == owner)
        def _():
            self.copy(slot).wait_recv()
            close(slot, self.mine[slot].astype(F32) + self.come[slot].astype(F32))

    def drain(self):
        for slot in range(self.slots):
            self.copy(slot).wait_send()

    def rows(self, ref, slot, owner):
        start = (slot // self.half) * self.blocks + owner * self.half + lax.rem(slot, self.half)
        return ref.at[pl.ds(pl.multiple_of(start * BLOCK, BLOCK), BLOCK), :]


def feed_back_kernel(blocks, dy_ref, by_up_ref, by_gate_ref, n_ref, gate_ref, up_ref, down_ref, own_dy_ref, own_n_ref, inv_ref, grad_ref,
                     g_gate_ref, g_up_ref, dx_out, r_down_out,
                     turned_n, d_gate, d_up, dx_mine, dx_sem, keep_sem, *rest):
    step = pl.program_id(0)
    tiles = turned_n.shape[1] // BLOCK
    cuts = d_gate.shape[1] // BLOCK
    last = 2 * tiles + cuts - 1
    trade = Trade(rest[:3], rest[3:4], blocks)
    grp, plane, core = where_am_i()
    reduce = Reduce([Summand(core, grad_ref, r_down_out, False)], rest[4:9], rest[9:])

    def at(when):
        return pl.when(step == when)

    @at(0)
    def _():
        greet(reduce.partners())
        reduce.a(0)

    @at(tiles + 1)
    def _():
        reduce.b(0)

    @at(tiles + 4)
    def _():
        reduce.c(0)

    @at(tiles + cuts + 3)
    def _():
        reduce.d(0)

    @pl.when(step < tiles)
    def _():
        rows = pl.ds(pl.multiple_of(step * BLOCK, BLOCK), BLOCK)
        grad = dot(dy_ref[...], down_ref[...], NT)
        d_up[rows, :] = (grad * by_up_ref[...].astype(F32)).astype(BF16)
        d_gate[rows, :] = (grad * by_gate_ref[...].astype(F32)).astype(BF16)
        turned_n[:, rows] = n_ref[...].T

    @pl.when((step >= tiles) & (step < tiles + cuts))
    def _():
        cols = pl.ds(pl.multiple_of((step - tiles) * BLOCK, BLOCK), BLOCK)
        g_gate_ref[...] = dot(turned_n[...], d_gate[:, cols]).astype(BF16)
        g_up_ref[...] = dot(turned_n[...], d_up[:, cols]).astype(BF16)

    def there(slot, owner):
        return trade.rows(dx_out, slot, owner)

    def dx_copy(slot):
        return remote(dx_mine.at[slot], there(slot, core), dx_sem.at[0, slot], dx_sem.at[1, slot], grp, plane, 1 - core)

    def dx_keep(slot):
        return pltpu.make_async_copy(dx_mine.at[slot], there(slot, core), keep_sem.at[slot])

    def close(slot, grad):
        rows = pl.ds(pl.multiple_of(slot * BLOCK, BLOCK), BLOCK)
        normed = own_n_ref[rows, :].astype(F32)
        back = grad - normed * jnp.mean(grad * normed, -1, keepdims=True)
        dx_mine[slot] = (own_dy_ref[rows, :].astype(F32) + inv_ref[rows, :] * back).astype(BF16)
        dx_copy(slot).start()
        dx_keep(slot).start()

    @pl.when(step > tiles + cuts)
    def _():
        trade.take(step - tiles - cuts - 1, close)

    @pl.when(step >= tiles + cuts)
    def _():
        turn = step - tiles - cuts
        rows = pl.ds(pl.multiple_of(turn * BLOCK, BLOCK), BLOCK)
        part = dot(d_gate[rows, :], gate_ref[...], NT) + dot(d_up[rows, :], up_ref[...], NT)
        trade.give(turn, part.astype(BF16))

    @at(last)
    def _():
        trade.take(tiles - 1, close)
        reduce.e(0)
        trade.drain()
        for slot in range(trade.slots):
            dx_copy(slot).wait_send()
            dx_keep(slot).wait()
            here = there(slot, 1 - core)
            remote(here, here, dx_sem.at[0, slot], dx_sem.at[1, slot], grp, plane, 1 - core).wait_recv()


def feed_back(dy, by_up, by_gate, n, gate, up, down, own_dy, own_n, inverse, grad_down, length):
    tokens, width = dy.shape
    units = gate.shape[1]
    blocks, tiles, cuts = length // BLOCK, tokens // BLOCK, units // BLOCK
    slots = tiles // 2
    shape = jax.ShapeDtypeStruct
    once = pl.Buffered(1)
    early = lambda cols: pl.BlockSpec((BLOCK, cols), lambda i: (jnp.minimum(i, tiles - 1), 0))
    fixed = lambda a: pl.BlockSpec(a.shape, lambda i: (0, 0), pipeline_mode=once)
    cut = pl.BlockSpec((width, BLOCK), lambda i: (0, jnp.clip(i - tiles, 0, cuts - 1)))
    return pl.pallas_call(
        functools.partial(feed_back_kernel, blocks),
        grid=(2 * tiles + cuts,),
        in_specs=[early(width), early(units), early(units), early(width)]
        + [fixed(a) for a in (gate, up, down, own_dy, own_n, inverse)]
        + [ANY],
        out_specs=(cut, cut, ANY, ANY),
        out_shape=(
            shape((width, units), BF16),
            shape((width, units), BF16),
            shape((tokens, width), BF16),
            shape((grad_down.shape[0] // 4, width), BF16),
        ),
        scratch_shapes=[
            pltpu.VMEM((width, tokens), BF16),
            pltpu.VMEM((tokens, units), BF16),
            pltpu.VMEM((tokens, units), BF16),
            pltpu.VMEM((slots, BLOCK, width), BF16),
            DMA((2, slots)),
            DMA((slots,)),
        ]
        + Trade.buffers(slots, width)
        + Trade.semaphores(slots)
        + Reduce.buffers([halves_of(*grad_down.shape, False)])
        + Reduce.semaphores(1),
        compiler_params=pltpu.CompilerParams(collective_id=2, has_side_effects=True, vmem_limit_bytes=62 * 2**20),
        name="feed_back",
    )(dy, by_up, by_gate, n, gate, up, down, own_dy, own_n, inverse, grad_down)


def back_kernel(heads, kv_heads, blocks, prefix_ref, qt_ref, kv_ref, kt_ref, lse_ref, ot_ref, dx_ref, n_ref, own_ref, wo_ref, w_ref,
                cos_ref, sin_ref, g_gate_ref, g_up_ref,
                grad_out, r_pack_out, r_gate_out, r_up_out,
                dot_ref, dk_ref, dv_ref, dt, g_pack, g_wo, wo_send, wo_come, wo_sem, *rest):
    step = pl.program_id(0)
    grp, plane, core = where_am_i()
    tokens, width = dx_ref.shape
    tiles, half, length = tokens // BLOCK, blocks // 2, blocks * BLOCK
    groups = heads // kv_heads
    q_cols, kv_cols = heads * HEAD, kv_heads * HEAD
    qkv = q_cols + 2 * kv_cols
    thirds = 3
    cut = width // thirds
    trade = Trade(rest[:3], rest[3:4], blocks)
    units = [Summand(core, g_gate_ref, r_gate_out, True), Summand(core, g_up_ref, r_up_out, True), Summand(core, g_pack, r_pack_out, True)]
    reduce = Reduce(units, rest[4:19], rest[19:])
    turn = lax.rem(step, blocks)

    def at(when):
        return pl.when(step == when)

    def wo_copy():
        return remote(wo_send, wo_come, wo_sem.at[0], wo_sem.at[1], grp, plane, 1 - core)

    @at(0)
    def _():
        greet(reduce.partners())
        reduce.a(0)

    for j in range(thirds):
        @at(1 + j)
        def _(j=j):
            g_wo[:, j * cut : (j + 1) * cut] = dot(ot_ref[...], dx_ref[:, j * cut : (j + 1) * cut]).astype(BF16)

    @at(1 + thirds)
    def _():
        low, high = g_wo[:, :q_cols], g_wo[:, q_cols:]
        wo_send[...] = jnp.where(core == 0, high, low)
        wo_copy().start()
        g_pack[pl.ds(pl.multiple_of(core * q_cols, 16), q_cols), qkv:] = jnp.where(core == 0, low, high)

    @at(3)
    def _():
        reduce.a(1)

    @at(5)
    def _():
        reduce.b(0)

    @at(tiles)
    def _():
        reduce.b(1)
        reduce.c(0)

    @at(tiles + thirds)
    def _():
        wo_copy().wait()
        g_pack[pl.ds(pl.multiple_of((1 - core) * q_cols, 16), q_cols), qkv:] = wo_come[...]
        reduce.a(2)

    @pl.when((step < tiles) & (turn == 0))
    def _():
        dk_ref[...] = jnp.zeros_like(dk_ref)
        dv_ref[...] = jnp.zeros_like(dv_ref)

    @pl.when(step < tiles)
    def _():
        rows = pl.ds(pl.multiple_of(step * BLOCK, BLOCK), BLOCK)
        dot_ref[...] = dot(wo_ref[...], dx_ref[rows, :], NT).astype(BF16)

    def run(block):
        n = reach(block)
        prefix = prefix_ref[step // blocks]
        tokens_here = pl.ds(pl.multiple_of(step * BLOCK, BLOCK), BLOCK)
        here = pl.ds(block * BLOCK, BLOCK)
        cosine, sine = cos_ref[:, here], sin_ref[:, here]

        def score(h):
            kh = h // groups
            own = slice(h * HEAD, (h + 1) * HEAD)
            keys = kv_ref[:n, kh * HEAD : (kh + 1) * HEAD]
            values = kv_ref[:n, kv_cols + kh * HEAD : kv_cols + (kh + 1) * HEAD]
            return scores_of(keys, qt_ref[own, :], prefix, block), dot(values, dot_ref[own, :])

        later = score(0)
        for h in range(heads):
            kh = h // groups
            own = slice(h * HEAD, (h + 1) * HEAD)
            kt = kt_ref[kh * HEAD : (kh + 1) * HEAD, :n]
            query, grad = qt_ref[own, :], dot_ref[own, :]
            delta = jnp.sum(grad.astype(F32) * ot_ref[own, tokens_here].astype(F32), 0, keepdims=True)
            scores, grad_probs = later
            if h + 1 < heads:
                later = score(h + 1)
            probs = jnp.exp2(scores - lse_ref[h : h + 1, :])
            grad_scores = (probs * (grad_probs - delta)).astype(BF16)
            dv_ref[kh, :, :n] += dot(grad, probs.astype(BF16), NT)
            dk_ref[kh, :, :n] += dot(query, grad_scores, NT)
            grad_query = turned(dot(kt, grad_scores), cosine, sine, -1.0)
            dt[own, tokens_here] = (grad_query * (1.0 / math.sqrt(HEAD))).astype(BF16)

    for block in range(blocks):
        pl.when((step < tiles) & (turn == block))(functools.partial(run, block))

    @pl.when((step < tiles) & (turn == blocks - 1))
    def _():
        sequence = pl.ds(pl.multiple_of((step // blocks) * length, length), length)
        for kh in range(kv_heads):
            rows = turned(dk_ref[kh], cos_ref[...], sin_ref[...], -1.0) * math.log(2.0)
            dt[q_cols + kh * HEAD : q_cols + (kh + 1) * HEAD, sequence] = rows.astype(BF16)
            start = q_cols + kv_cols + kh * HEAD
            dt[start : start + HEAD, sequence] = dv_ref[kh].astype(BF16)

    for j in range(thirds):
        @at(tiles + j)
        def _(j=j):
            across = dot(dt[...], n_ref[...])
            g_pack[j * cut : (j + 1) * cut, :qkv] = across.T.astype(BF16)

    def close(slot, grad):
        rows = pl.ds(pl.multiple_of(slot * BLOCK, BLOCK), BLOCK)
        x = own_ref[rows, :].astype(F32)
        inverse = lax.rsqrt(jnp.mean(x * x, -1, keepdims=True) + epsilon)
        normed = x * inverse
        back = inverse * (grad - normed * jnp.mean(grad * normed, -1, keepdims=True))
        grad_out[rows, :] = (trade.rows(dx_ref, slot, core)[...].astype(F32) + back).astype(BF16)

    first = tiles + thirds

    @pl.when(step > first)
    def _():
        trade.take(step - first - 1, close)

    @pl.when(step >= first)
    def _():
        rows = pl.ds(pl.multiple_of((step - first) * BLOCK, BLOCK), BLOCK)
        part = dot(dt[:, rows].T, w_ref[:, :qkv], NT)
        trade.give(step - first, part.astype(BF16))

    @at(first + 2)
    def _():
        reduce.c(1)

    @at(first + 4)
    def _():
        reduce.d(0)

    @at(first + tiles - 1)
    def _():
        trade.take(tiles - 1, close)
        reduce.b(2)
        reduce.d(1)
        reduce.c(2)
        reduce.d(2)
        for n in range(3):
            reduce.e(n)
        trade.drain()


def back(prefix, qt, kv, kvt, lse, ot, dx, n, own, wo, pack, cosine, sine, g_gate, g_up, heads, kv_heads, length):
    tokens, width = dx.shape
    count, blocks, tiles = tokens // length, length // BLOCK, tokens // BLOCK
    slots = tiles // 2
    q_cols, kv_cols = heads * HEAD, kv_heads * HEAD
    shape = jax.ShapeDtypeStruct
    once = pl.Buffered(1)
    fixed = lambda a: pl.BlockSpec(a.shape, lambda i: (0,) * a.ndim, pipeline_mode=once)
    early = lambda i: jnp.minimum(i, tiles - 1)
    shards = [shape((g.shape[0] // 8, g.shape[1] * 2), BF16) for g in (pack, g_gate, g_up)]
    return pl.pallas_call(
        functools.partial(back_kernel, heads, kv_heads, blocks),
        grid=(2 * tiles + 3,),
        in_specs=[
            pl.BlockSpec(memory_space=pltpu.SMEM),
            pl.BlockSpec((q_cols, BLOCK), lambda i: (0, early(i))),
            pl.BlockSpec((length, 2 * kv_cols), lambda i: (early(i) // blocks, 0)),
            pl.BlockSpec((kv_cols, length), lambda i: (0, early(i) // blocks)),
            pl.BlockSpec((heads, BLOCK), lambda i: (0, early(i))),
        ]
        + [fixed(ot), fixed(dx), pl.BlockSpec((tokens, width // 3), lambda i: (0, jnp.clip(i - tiles, 0, 2)))]
        + [fixed(a) for a in (own, wo, pack, cosine, sine)]
        + [ANY, ANY],
        out_specs=(fixed(own), ANY, ANY, ANY),
        out_shape=[shape(own.shape, BF16)] + shards,
        scratch_shapes=[
            pltpu.VMEM((q_cols, BLOCK), BF16),
            pltpu.VMEM((kv_heads, HEAD, length), F32),
            pltpu.VMEM((kv_heads, HEAD, length), F32),
            pltpu.VMEM((q_cols + 2 * kv_cols, tokens), BF16),
            pltpu.VMEM(pack.shape, BF16),
            pltpu.VMEM(wo.shape, BF16),
            pltpu.VMEM((q_cols, q_cols), BF16),
            pltpu.VMEM((q_cols, q_cols), BF16),
            DMA((2,)),
        ]
        + Trade.buffers(slots, width)
        + Trade.semaphores(slots)
        + Reduce.buffers([halves_of(*g.shape, True) for g in (g_gate, g_up, pack)])
        + Reduce.semaphores(3),
        compiler_params=pltpu.CompilerParams(collective_id=3, has_side_effects=True, vmem_limit_bytes=62 * 2**20),
        name="back",
    )(prefix, qt, kv, kvt, lse, ot, dx, n, own, wo, pack, cosine, sine, g_gate, g_up)


SWAP = [(0, 1), (1, 0)]


def trade(mine):
    return lax.ppermute(mine, "ctx", SWAP)


def part_of(array, which, axis):
    size = array.shape[axis] // 2
    return lax.dynamic_slice_in_dim(array, which * size, size, axis)


def tables(length):
    frequency = np.float32(10000.0) ** (-np.arange(HEAD // 2, dtype=np.float32) * np.float32(2.0) / np.float32(HEAD))
    angles = frequency[:, None] * np.arange(length, dtype=np.float32)[None, :]
    return jnp.asarray(np.cos(angles)), jnp.asarray(np.sin(angles))


def paired(
    activations_in,
    prefix_len,
    attn_gain,
    query_weight,
    key_weight,
    value_weight,
    out_weight,
    ffn_gain,
    gate_weight,
    up_weight,
    down_weight,
    cotangent,
):
    micro, seq_count, span, width = activations_in.shape
    count, length = micro * seq_count, 2 * span
    core = lax.axis_index("ctx")
    heads, kv_heads = HEADS // 2, KV_HEADS // 2

    own_x = activations_in.reshape(count, span, width)
    own_dy = cotangent.reshape(count, span, width)

    def summed(part):
        part = part.reshape(count, length, width)
        theirs = trade(part_of(part, 1 - core, 1))
        return part_of(part, core, 1).astype(F32) + theirs.astype(F32)

    gain_attn, gain_ffn = attn_gain[:, None], ffn_gain[:, None]
    pack, gate_part, full_x, full_dy = start(
        own_x, own_dy, query_weight, key_weight, value_weight, out_weight, gate_weight, gain_attn, gain_ffn, heads, kv_heads
    )
    cosine, sine = tables(length)
    prefix = prefix_len.reshape(count)
    normed_one, qt, kvt, kv, ot, lse, w_out, middle, inverse, full_two, w_gate, w_up, w_down = front(
        prefix, full_x, own_x.reshape(count * span, width), pack, gate_part, up_weight, down_weight, gain_ffn, cosine, sine,
        heads, kv_heads, length,
    )
    hidden, by_up, by_gate, part = feed(full_two, w_gate, w_up, w_down)
    result = middle.reshape(count, span, width) + summed(part)
    grad_down = dot(hidden, full_dy, TN).astype(BF16)
    own_two = part_of(full_two.reshape(count, length, width), core, 1).reshape(count * span, width)
    grad_gate, grad_up, full_dx, r_down = feed_back(
        full_dy, by_up, by_gate, full_two, w_gate, w_up, w_down, own_dy.reshape(count * span, width), own_two, inverse,
        grad_down, length,
    )
    grad_inputs, r_pack, r_gate, r_up = back(
        prefix, qt, kv, kvt, lse, ot, full_dx, normed_one, own_x.reshape(count * span, width), w_out, pack, cosine, sine,
        grad_gate, grad_up, heads, kv_heads, length,
    )
    g_q, g_k, g_v, g_o, g_gate, g_up, g_down, g_ga, g_gf = finish(
        r_pack, r_gate, r_up, r_down, query_weight, key_weight, value_weight, out_weight, gate_weight, up_weight, gain_attn, gain_ffn,
        heads, kv_heads,
    )
    shape = activations_in.shape
    return (
        result.astype(BF16).reshape(shape),
        grad_inputs.reshape(shape),
        g_ga[:, 0],
        g_q,
        g_k,
        g_v,
        g_o,
        g_gf[:, 0],
        g_gate,
        g_up,
        g_down,
    )


def solution(mesh):
    small = dict(mesh.shape) == {"grp": 4, "fsdp": 4, "ctx": 2}

    return jax.shard_map(
        paired if small else local,
        mesh=mesh,
        in_specs=(
            P(None, ("grp", "fsdp"), "ctx", None),
            P(None, ("grp", "fsdp")),
            P(("fsdp", "ctx")),
            P(("fsdp", "ctx"), None),
            P(("fsdp", "ctx"), None),
            P(("fsdp", "ctx"), None),
            P(("fsdp", "ctx"), None),
            P(("fsdp", "ctx")),
            P(("fsdp", "ctx"), None),
            P(("fsdp", "ctx"), None),
            P(("fsdp", "ctx"), None),
            P(None, ("grp", "fsdp"), "ctx", None),
        ),
        out_specs=(
            P(None, ("grp", "fsdp"), "ctx", None),
            P(None, ("grp", "fsdp"), "ctx", None),
            P(("fsdp", "ctx")),
            P(("fsdp", "ctx"), None),
            P(("fsdp", "ctx"), None),
            P(("fsdp", "ctx"), None),
            P(("fsdp", "ctx"), None),
            P(("fsdp", "ctx")),
            P(("fsdp", "ctx"), None),
            P(("fsdp", "ctx"), None),
            P(("fsdp", "ctx"), None),
        ),
        check_vma=False,
    )
```

```python
import functools
import math

import jax
import jax.numpy as jnp
import numpy as np
from jax import lax
from jax.experimental import pallas as pl
from jax.experimental.pallas import tpu as pltpu
from jax.sharding import PartitionSpec as P

HEADS = 18
KV_HEADS = 6
HEAD = 64


epsilon = 1e-05


def shortened(array):

    def short(part):
        return part.astype(jnp.bfloat16) if part.dtype == jnp.float32 else part

    return jax.tree.map(short, array)


def rotary_tables(positions):
    halfway = HEAD // 2
    frequency = 10000.0 ** (-jnp.arange(halfway, dtype=jnp.float32) * 2.0 / HEAD)
    angles = positions.astype(jnp.float32)[:, None] * frequency[None, :]
    return (jnp.cos(angles)[:, None, :], jnp.sin(angles)[:, None, :])


def rotate(values, cosine, sine):
    halfway = values.shape[-1] // 2
    first = values[..., :halfway]
    second = values[..., halfway:]
    return jnp.concatenate([first * cosine - second * sine, second * cosine + first * sine], -1)


def rotate_back(values, cosine, sine):
    halfway = values.shape[-1] // 2
    first = values[..., :halfway]
    second = values[..., halfway:]
    return jnp.concatenate([first * cosine + second * sine, second * cosine - first * sine], -1)


def norm_back(grad_normed, normed, inverse):
    return inverse * (grad_normed - normed * jnp.mean(grad_normed * normed, -1, keepdims=True))


def flatten_all(grads):
    return tuple((g.reshape(-1) for g in grads))


def local(
    activations_in,
    prefix_len,
    attn_gain,
    query_weight,
    key_weight,
    value_weight,
    out_weight,
    ffn_gain,
    gate_weight,
    up_weight,
    down_weight,
    cotangent,
):
    micro, seq_count, span, width = activations_in.shape
    rows = seq_count * span
    length = span * lax.axis_size("ctx")
    groups = HEADS // KV_HEADS
    scale = 1.0 / math.sqrt(HEAD)
    shards = (
        attn_gain,
        query_weight,
        key_weight,
        value_weight,
        out_weight,
        ffn_gain,
        gate_weight,
        up_weight,
        down_weight,
    )
    offset = lax.axis_index("ctx") * span
    query_pos = offset + jnp.arange(span, dtype=jnp.int32)
    key_pos = jnp.arange(length, dtype=jnp.int32)
    cosine, sine = rotary_tables(jnp.tile(query_pos, seq_count))

    def visibility(prefix):
        return (key_pos[None, :] <= query_pos[:, None]) | (key_pos[None, :] < prefix)

    def attend(item):
        query, keys, values, prefix = item
        scores = (
            jnp.einsum("qhgd,khd->hgqk", query, keys, preferred_element_type=jnp.float32) * scale
        )
        scores = jnp.where(visibility(prefix), scores, -1e30)
        peak = jnp.max(scores, -1, keepdims=True)
        weights = jnp.exp(scores - peak)
        totals = jnp.sum(weights, -1, keepdims=True)
        probs = (weights / totals).astype(jnp.bfloat16)
        mixed = jnp.einsum("hgqk,khd->qhgd", probs, values, preferred_element_type=jnp.float32)
        return (mixed.reshape(span, HEADS * HEAD), (peak + jnp.log(totals))[..., 0])

    def attend_back(item):
        query, keys, values, prefix, log_total, grad_mixed = item
        scores = (
            jnp.einsum("qhgd,khd->hgqk", query, keys, preferred_element_type=jnp.float32) * scale
        )
        probs = jnp.where(visibility(prefix), jnp.exp(scores - log_total[..., None]), 0.0)
        grad_probs = jnp.einsum(
            "qhgd,khd->hgqk", grad_mixed, values, preferred_element_type=jnp.float32
        )
        grad_scores = (
            probs * (grad_probs - jnp.sum(probs * grad_probs, -1, keepdims=True))
        ).astype(jnp.bfloat16)
        grad_query = (
            jnp.einsum("hgqk,khd->qhgd", grad_scores, keys, preferred_element_type=jnp.float32)
            * scale
        )
        grad_keys = (
            jnp.einsum("hgqk,qhgd->khd", grad_scores, query, preferred_element_type=jnp.float32)
            * scale
        )
        grad_values = jnp.einsum(
            "hgqk,qhgd->khd",
            probs.astype(jnp.bfloat16),
            grad_mixed,
            preferred_element_type=jnp.float32,
        )
        return (
            grad_query.reshape(span, HEADS * HEAD),
            grad_keys.reshape(length, KV_HEADS * HEAD),
            grad_values.reshape(length, KV_HEADS * HEAD),
        )

    outputs = []
    input_grads = []
    collected = None
    for index in range(micro):
        full = (
            lax.all_gather(shards[0], ("fsdp", "ctx"), axis=0, tiled=True),
            lax.all_gather(shards[1], ("fsdp", "ctx"), axis=0, tiled=True),
            lax.all_gather(shards[2], ("fsdp", "ctx"), axis=0, tiled=True),
            lax.all_gather(shards[3], ("fsdp", "ctx"), axis=0, tiled=True),
            lax.all_gather(shards[4], ("fsdp", "ctx"), axis=0, tiled=True),
            lax.all_gather(shards[5], ("fsdp", "ctx"), axis=0, tiled=True),
            lax.all_gather(shards[6], ("fsdp", "ctx"), axis=0, tiled=True),
            lax.all_gather(shards[7], ("fsdp", "ctx"), axis=0, tiled=True),
            lax.all_gather(shards[8], ("fsdp", "ctx"), axis=0, tiled=True),
        )
        gain_attn, w_query, w_key, w_value, w_out, gain_ffn, w_gate, w_up, w_down = full
        inputs = activations_in[index].reshape(rows, width).astype(jnp.float32)
        inverse_one = lax.rsqrt(jnp.mean(inputs * inputs, -1, keepdims=True) + epsilon)
        normed_one = inputs * inverse_one
        first_in = (normed_one * gain_attn).astype(jnp.bfloat16)
        query_lin = jnp.dot(first_in, w_query, preferred_element_type=jnp.float32)
        key_lin = jnp.dot(first_in, w_key, preferred_element_type=jnp.float32)
        value_lin = jnp.dot(first_in, w_value, preferred_element_type=jnp.float32)
        query_rot = rotate(query_lin.reshape(rows, HEADS, HEAD), cosine, sine).astype(jnp.bfloat16)
        key_rot = rotate(key_lin.reshape(rows, KV_HEADS, HEAD), cosine, sine).astype(jnp.bfloat16)
        key_rot = key_rot.reshape(seq_count, span, KV_HEADS * HEAD)
        value_low = value_lin.astype(jnp.bfloat16).reshape(seq_count, span, KV_HEADS * HEAD)
        key_all, value_all = (
            lax.all_gather(key_rot, "ctx", axis=1, tiled=True),
            lax.all_gather(value_low, "ctx", axis=1, tiled=True),
        )
        query_split = query_rot.reshape(seq_count, span, KV_HEADS, groups, HEAD)
        key_split = key_all.reshape(seq_count, length, KV_HEADS, HEAD)
        value_split = value_all.reshape(seq_count, length, KV_HEADS, HEAD)
        mixed_all, log_totals = lax.map(
            attend, (query_split, key_split, value_split, prefix_len[index])
        )
        attn_low = mixed_all.reshape(rows, HEADS * HEAD).astype(jnp.bfloat16)
        middle = inputs + jnp.dot(attn_low, w_out, preferred_element_type=jnp.float32)
        inverse_two = lax.rsqrt(jnp.mean(middle * middle, -1, keepdims=True) + epsilon)
        normed_two = middle * inverse_two
        second_in = (normed_two * gain_ffn).astype(jnp.bfloat16)
        gate = jnp.dot(second_in, w_gate, preferred_element_type=jnp.float32)
        upward = jnp.dot(second_in, w_up, preferred_element_type=jnp.float32)
        hidden = (jax.nn.silu(gate) * upward).astype(jnp.bfloat16)
        result = middle + jnp.dot(hidden, w_down, preferred_element_type=jnp.float32)
        outputs.append(result.astype(jnp.bfloat16).reshape(seq_count, span, width))
        back = (
            lax.all_gather(shards[0], ("fsdp", "ctx"), axis=0, tiled=True),
            lax.all_gather(shards[1], ("fsdp", "ctx"), axis=0, tiled=True),
            lax.all_gather(shards[2], ("fsdp", "ctx"), axis=0, tiled=True),
            lax.all_gather(shards[3], ("fsdp", "ctx"), axis=0, tiled=True),
            lax.all_gather(shards[4], ("fsdp", "ctx"), axis=0, tiled=True),
            lax.all_gather(shards[5], ("fsdp", "ctx"), axis=0, tiled=True),
            lax.all_gather(shards[6], ("fsdp", "ctx"), axis=0, tiled=True),
            lax.all_gather(shards[7], ("fsdp", "ctx"), axis=0, tiled=True),
            lax.all_gather(shards[8], ("fsdp", "ctx"), axis=0, tiled=True),
        )
        gain_attn, w_query, w_key, w_value, w_out, gain_ffn, w_gate, w_up, w_down = back
        grad_y = cotangent[index].reshape(rows, width).astype(jnp.float32)
        grad_y_low = grad_y.astype(jnp.bfloat16)
        grad_wdown = jnp.einsum("rf,rd->fd", hidden, grad_y_low, preferred_element_type=jnp.float32)
        grad_hidden = jnp.einsum(
            "rd,fd->rf", grad_y_low, w_down, preferred_element_type=jnp.float32
        )
        sigma = jax.nn.sigmoid(gate)
        grad_up_low = (grad_hidden * gate * sigma).astype(jnp.bfloat16)
        grad_gate_low = (grad_hidden * upward * sigma * (1.0 + gate * (1.0 - sigma))).astype(
            jnp.bfloat16
        )
        grad_wgate = jnp.einsum(
            "rd,rf->df", second_in, grad_gate_low, preferred_element_type=jnp.float32
        )
        grad_wup = jnp.einsum(
            "rd,rf->df", second_in, grad_up_low, preferred_element_type=jnp.float32
        )
        grad_second = jnp.einsum(
            "rf,df->rd", grad_gate_low, w_gate, preferred_element_type=jnp.float32
        ) + jnp.einsum("rf,df->rd", grad_up_low, w_up, preferred_element_type=jnp.float32)
        grad_gain_ffn = jnp.sum(grad_second * normed_two, 0)
        grad_middle = grad_y + norm_back(grad_second * gain_ffn, normed_two, inverse_two)
        grad_branch_low = grad_middle.astype(jnp.bfloat16)
        grad_wout = jnp.einsum(
            "ra,rd->ad", attn_low, grad_branch_low, preferred_element_type=jnp.float32
        )
        grad_attn_low = jnp.einsum(
            "rd,ad->ra", grad_branch_low, w_out, preferred_element_type=jnp.float32
        ).astype(jnp.bfloat16)
        grad_mixed = grad_attn_low.reshape(seq_count, span, KV_HEADS, groups, HEAD)
        grad_query_rot, grad_key_part, grad_value_part = lax.map(
            attend_back,
            (query_split, key_split, value_split, prefix_len[index], log_totals, grad_mixed),
        )
        grad_key_own, grad_value_own = (
            lax.psum_scatter(
                grad_key_part.astype(jnp.bfloat16), "ctx", scatter_dimension=1, tiled=True
            ).astype(jnp.float32),
            lax.psum_scatter(
                grad_value_part.astype(jnp.bfloat16), "ctx", scatter_dimension=1, tiled=True
            ).astype(jnp.float32),
        )
        grad_query = rotate_back(grad_query_rot.reshape(rows, HEADS, HEAD), cosine, sine)
        grad_query = grad_query.reshape(rows, HEADS * HEAD).astype(jnp.bfloat16)
        grad_key = rotate_back(grad_key_own.reshape(rows, KV_HEADS, HEAD), cosine, sine)
        grad_key = grad_key.reshape(rows, KV_HEADS * HEAD).astype(jnp.bfloat16)
        grad_value = grad_value_own.reshape(rows, KV_HEADS * HEAD).astype(jnp.bfloat16)
        grad_wquery = jnp.einsum(
            "rd,rq->dq", first_in, grad_query, preferred_element_type=jnp.float32
        )
        grad_wkey = jnp.einsum("rd,rq->dq", first_in, grad_key, preferred_element_type=jnp.float32)
        grad_wvalue = jnp.einsum(
            "rd,rq->dq", first_in, grad_value, preferred_element_type=jnp.float32
        )
        grad_first = (
            jnp.einsum("rq,dq->rd", grad_query, w_query, preferred_element_type=jnp.float32)
            + jnp.einsum("rq,dq->rd", grad_key, w_key, preferred_element_type=jnp.float32)
            + jnp.einsum("rq,dq->rd", grad_value, w_value, preferred_element_type=jnp.float32)
        )
        grad_gain_attn = jnp.sum(grad_first * normed_one, 0)
        grad_inputs = grad_middle + norm_back(grad_first * gain_attn, normed_one, inverse_one)
        input_grads.append(grad_inputs.astype(jnp.bfloat16).reshape(seq_count, span, width))
        grads = flatten_all(
            (
                grad_gain_attn,
                grad_wquery,
                grad_wkey,
                grad_wvalue,
                grad_wout,
                grad_gain_ffn,
                grad_wgate,
                grad_wup,
                grad_wdown,
            )
        )
        pieces = lax.psum_scatter(grads, ("fsdp", "ctx"), scatter_dimension=0, tiled=True)
        if index == 0:
            collected = pieces
        else:
            collected = tuple((a + b for a, b in zip(collected, pieces)))
    summed = jax.tree.map(
        lambda part: part.astype(jnp.float32), lax.psum(shortened(collected), "grp")
    )
    shaped = tuple((s.reshape(w.shape) for s, w in zip(summed, shards)))
    return (
        jnp.stack(outputs, 0),
        jnp.stack(input_grads, 0),
        shaped[0],
        shaped[1],
        shaped[2],
        shaped[3],
        shaped[4],
        shaped[5],
        shaped[6],
        shaped[7],
        shaped[8],
    )


BLOCK = 256
TO_LOG2 = math.log2(math.e) / math.sqrt(HEAD)
F32, BF16 = jnp.float32, jnp.bfloat16
NN = (((1,), (0,)), ((), ()))
NT = (((1,), (1,)), ((), ()))
TN = (((0,), (0,)), ((), ()))


def dot(a, b, dims=NN):
    return lax.dot_general(a, b, dims, preferred_element_type=F32)


def turned(rows, cosine, sine, sign):
    a, b = rows[: HEAD // 2], rows[HEAD // 2 :]
    return jnp.concatenate([a * cosine - sign * b * sine, b * cosine + sign * a * sine], 0)


def masked(scores, prefix, first, block):
    key = first + lax.broadcasted_iota(jnp.int32, scores.shape, 0)
    query = block * BLOCK + lax.broadcasted_iota(jnp.int32, scores.shape, 1)
    return jnp.where((key <= query) | (key < prefix), scores, -1e30)


def reach(block):
    return max(2, block + 1) * BLOCK


def scores_of(keys, query, prefix, block):
    clear = block * BLOCK
    edge = masked(dot(keys[clear:], query), prefix, clear, block)
    if not clear:
        return edge
    return jnp.concatenate([dot(keys[:clear], query), edge], 0)


MESH = pl.DeviceIdType.MESH
DMA = pltpu.SemaphoreType.DMA
ANY = pl.BlockSpec(memory_space=pl.ANY)
VMEM = pl.BlockSpec(memory_space=pltpu.VMEM)


def where_am_i():
    return lax.axis_index("grp"), lax.axis_index("fsdp"), lax.axis_index("ctx")


def remote(src, dst, send, recv, grp, fsdp, ctx):
    return pltpu.make_async_remote_copy(
        src_ref=src,
        dst_ref=dst,
        send_sem=send,
        recv_sem=recv,
        device_id={"grp": grp, "fsdp": fsdp, "ctx": ctx},
        device_id_type=MESH,
    )


def greet(partners):
    barrier = pltpu.get_barrier_semaphore()
    for grp, fsdp, ctx in partners:
        pl.semaphore_signal(
            barrier, inc=1, device_id={"grp": grp, "fsdp": fsdp, "ctx": ctx}, device_id_type=MESH
        )
    pl.semaphore_wait(barrier, len(partners))


class Columns:
    split = True

    def __init__(self, core, shard, out):
        self.core, self.shard, self.out = core, shard, out
        self.rows, self.cols = shard.shape[0], out.shape[1] // 4

    def mine(self, j, quarter):
        to = self.core if j == 0 else 1 - self.core
        return self.shard.at[:, pl.ds(pl.multiple_of((2 * quarter + to) * self.cols, 128), self.cols)]

    def block(self, plane, j, quarter):
        owner = self.core if j == 0 else 1 - self.core
        start = pl.multiple_of((2 * plane + owner) * self.rows, 16)
        return self.out.at[pl.ds(start, self.rows), pl.ds(pl.multiple_of(quarter * self.cols, 128), self.cols)]


class Rows:
    split = False

    def __init__(self, core, shard, out):
        self.core, self.shard, self.out = core, shard, out
        self.rows = out.shape[0] // 32

    def mine(self, j, quarter):
        return self.shard.at[pl.ds(pl.multiple_of((2 * quarter + j) * self.rows, 16), self.rows), :]

    def block(self, plane, j, quarter):
        start = pl.multiple_of((8 * plane + 2 * quarter + j) * self.rows, 16)
        return self.out.at[pl.ds(start, self.rows), :]

    def own(self, plane):
        return self.out.at[pl.ds(pl.multiple_of(plane * 8 * self.rows, 16), 8 * self.rows), :]


class Gather:
    @staticmethod
    def semaphores(count):
        return [DMA((count, 4)), DMA((count, 4)), DMA((count, 4))] + [DMA((count, 3, 2))] * 2 + [DMA((count, 3, 2, 2))] * 2 + [DMA((count, 3, 2))] * 2

    def __init__(self, units, sems):
        self.units, self.sems = units, sems
        self.grp, self.plane, self.core = where_am_i()
        self.side = self.grp + 1 - 2 * lax.rem(self.grp, 2)
        self.up = lax.rem(self.grp + 2, 4)
        self.planes = [lax.rem(self.plane + s, 4) for s in (1, 2, 3)]
        self.origins = [lax.rem(self.plane + 4 - s, 4) for s in (1, 2, 3)]
        self.left = []

    def partners(self):
        grp, plane, core = self.grp, self.plane, self.core
        found = [(grp, z, c) for z in self.planes for c in (core, 1 - core)]
        return found + [(grp, plane, 1 - core), (self.side, plane, core), (self.up, plane, core)]

    def other(self, j):
        return self.core if j == 0 else 1 - self.core

    def send(self, src, dst, send, recv, grp, plane, core):
        copy = remote(src, dst, send, recv, grp, plane, core)
        copy.start()
        self.left.append(copy.wait_send)

    def got(self, here, send, recv):
        remote(here, here, send, recv, self.side, self.plane, self.core).wait_recv()

    def first(self, n):
        u = self.units[n]
        loc, near_s, near_r, z_s, z_r = self.sems[:5]
        for i, z in enumerate(self.planes):
            for j in range(2):
                if u.split:
                    dst = u.block(self.plane, 0, self.grp)
                    self.send(u.mine(j, self.grp), dst, z_s.at[n, i, j], z_r.at[n, i, j], self.grp, z, self.other(j))
                else:
                    dst = u.block(self.plane, j, self.grp)
                    self.send(u.mine(j, self.grp), dst, z_s.at[n, i, j], z_r.at[n, i, j], self.grp, z, self.core)
        if u.split:
            for q in range(4):
                dst = u.block(self.plane, 0, q)
                self.send(u.mine(1, q), dst, near_s.at[n, q], near_r.at[n, q], self.grp, self.plane, 1 - self.core)
                copy = pltpu.make_async_copy(u.mine(0, q), dst, loc.at[n, q])
                copy.start()
                self.left.append(copy.wait)
        else:
            copy = pltpu.make_async_copy(u.shard, u.own(self.plane), loc.at[n, 0])
            copy.start()
            self.left.append(copy.wait)

    def first_in(self, n):
        u = self.units[n]
        for i, z in enumerate(self.origins):
            for j in range(2):
                self.got(u.block(z, j, self.grp), self.sems[3].at[n, i, j], self.sems[4].at[n, i, j])

    def near_in(self, n):
        u = self.units[n]
        if u.split:
            for q in range(4):
                self.got(u.block(self.plane, 1, q), self.sems[1].at[n, q], self.sems[2].at[n, q])

    def second(self, n, here=False):
        u = self.units[n]
        z_s, z_r, xy_s, xy_r = self.sems[3:7]
        for i, z in enumerate(self.origins):
            for j in range(2):
                block = u.block(z, j, self.grp)
                if not here:
                    self.got(block, z_s.at[n, i, j], z_r.at[n, i, j])
                for t, to in enumerate((self.side, self.up)):
                    self.send(block, block, xy_s.at[n, i, j, t], xy_r.at[n, i, j, t], to, self.plane, self.core)

    def third(self, n):
        u = self.units[n]
        xy_s, xy_r, fw_s, fw_r = self.sems[5:9]
        for i, z in enumerate(self.origins):
            for t, (origin, to) in enumerate(((self.side, self.up), (self.up, self.side))):
                block = u.block(z, t, origin)
                self.got(block, xy_s.at[n, i, t, t], xy_r.at[n, i, t, t])
                self.send(block, block, fw_s.at[n, i, t], fw_r.at[n, i, t], to, self.plane, self.core)

    def last(self, n):
        u = self.units[n]
        xy_s, xy_r, fw_s, fw_r = self.sems[5:9]
        for i, z in enumerate(self.origins):
            for t, origin in enumerate((self.side, self.up)):
                self.got(u.block(z, 1 - t, origin), xy_s.at[n, i, 1 - t, t], xy_r.at[n, i, 1 - t, t])
            for t in range(2):
                self.got(u.block(z, t, 3 - self.grp), fw_s.at[n, i, t], fw_r.at[n, i, t])

    def sent_all(self, firsts, rest):
        loc, near_s, near_r, z_s, z_r, xy_s, xy_r, fw_s, fw_r = self.sems

        def out(block, send, recv):
            remote(block, block, send, recv, self.side, self.plane, self.core).wait_send()

        for n in firsts:
            u = self.units[n]
            for i in range(3):
                for j in range(2):
                    out(u.block(self.plane, j, self.grp), z_s.at[n, i, j], z_r.at[n, i, j])
            if u.split:
                for q in range(4):
                    out(u.block(self.plane, 0, q), near_s.at[n, q], near_r.at[n, q])
                    pltpu.make_async_copy(u.mine(0, q), u.block(self.plane, 0, q), loc.at[n, q]).wait()
            else:
                pltpu.make_async_copy(u.shard, u.own(self.plane), loc.at[n, 0]).wait()
        for n in rest:
            u = self.units[n]
            for i, z in enumerate(self.origins):
                for j in range(2):
                    for t in range(2):
                        out(u.block(z, j, self.grp), xy_s.at[n, i, j, t], xy_r.at[n, i, j, t])
                for t, origin in enumerate((self.side, self.up)):
                    out(u.block(z, t, origin), fw_s.at[n, i, t], fw_r.at[n, i, t])

    def drain(self):
        for wait in self.left:
            wait()
        self.left = []


def start_kernel(heads, kv_heads, x_ref, dy_ref, wq_ref, wk_ref, wv_ref, wo_ref, gate_ref, ga_ref, gf_ref,
                 pack_out, gate_out, x_out, dy_out, pack, gate, trade_s, trade_r, own_s, *sems):
    _, _, core = where_am_i()
    q_cols, kv_cols, span = heads * HEAD, kv_heads * HEAD, x_ref.shape[1]
    cols = pack.shape[1] // 8
    gain = ga_ref[...].astype(F32)
    for k in range(2):
        parts = [(wq_ref[:, k * q_cols : (k + 1) * q_cols].astype(F32) * gain).astype(BF16)]
        parts += [(w[:, k * kv_cols : (k + 1) * kv_cols].astype(F32) * gain).astype(BF16) for w in (wk_ref, wv_ref)]
        row = jnp.concatenate(parts + [wo_ref[:, k * q_cols : (k + 1) * q_cols]], 1)
        for q in range(4):
            pack[:, (2 * q + k) * cols : (2 * q + k + 1) * cols] = row[:, q * cols : (q + 1) * cols]
    gather = Gather([Columns(core, pack, pack_out), Columns(core, gate, gate_out)], sems)
    greet(gather.partners())
    gather.first(0)
    gate[...] = (gate_ref[...].astype(F32) * gf_ref[...].astype(F32)).astype(BF16)
    waits = []

    def trade(ref, out, which):
        for s in range(ref.shape[0]):
            def rows(owner):
                return out.at[pl.ds(pl.multiple_of((2 * s + owner) * span, 16), span), :]
            copy = remote(ref.at[s], rows(core), trade_s.at[which, s], trade_r.at[which, s], gather.grp, gather.plane, 1 - core)
            copy.start()
            gather.left.append(copy.wait_send)
            copy = pltpu.make_async_copy(ref.at[s], rows(core), own_s.at[which, s])
            copy.start()
            gather.left.append(copy.wait)
            waits.append((rows(1 - core), trade_s.at[which, s], trade_r.at[which, s]))

    trade(x_ref, x_out, 0)
    gather.second(0)
    gather.first(1)
    trade(dy_ref, dy_out, 1)
    gather.third(0)
    gather.last(0)
    gather.near_in(0)
    gather.near_in(1)
    for wait in waits:
        gather.got(*wait)
    gather.first_in(1)
    gather.drain()


def start(x, dy, wq, wk, wv, wo, gate, gain_attn, gain_ffn, heads, kv_heads):
    count, span, width = x.shape
    shard, hidden = gate.shape
    cols = 2 * (heads + kv_heads) * HEAD
    shape = jax.ShapeDtypeStruct
    return pl.pallas_call(
        functools.partial(start_kernel, heads, kv_heads),
        grid=(1,),
        in_specs=[pl.BlockSpec(a.shape, lambda i, n=a.ndim: (0,) * n) for a in (x, dy, wq, wk, wv, wo, gate, gain_attn, gain_ffn)],
        out_specs=(ANY,) * 4,
        out_shape=(
            shape((8 * shard, cols), BF16),
            shape((8 * shard, hidden // 2), BF16),
            shape((2 * count * span, width), BF16),
            shape((2 * count * span, width), BF16),
        ),
        scratch_shapes=[pltpu.VMEM((shard, 2 * cols), BF16), pltpu.VMEM((shard, hidden), BF16)]
        + [DMA((2, count))] * 3
        + Gather.semaphores(2),
        compiler_params=pltpu.CompilerParams(collective_id=0, has_side_effects=True, vmem_limit_bytes=62 * 2**20),
        name="start",
    )(x, dy, wq, wk, wv, wo, gate, gain_attn, gain_ffn)


def front_kernel(heads, kv_heads, blocks, prefix_ref, x_ref, own_ref, w_ref, up_ref, gf_ref, cos_ref, sin_ref, gate_in, down_ref,
                 n_ref, qt_ref, kvt_ref, kv_ref, ot_ref, lse_ref, wo_ref, x1_ref, inv_ref, two_out, gate_out, up_out, down_out,
                 up_s, wo_send, wo_recv, part_mine, part_send, part_recv, two_mine,
                 wo_sem, part_sem, two_sem, own_sem, *sems):
    step = pl.program_id(0)
    grp, plane, core = where_am_i()
    count = prefix_ref.shape[0]
    tiles = count * blocks
    groups = heads // kv_heads
    q_cols, kv_cols = heads * HEAD, kv_heads * HEAD
    width = x_ref.shape[1]
    half = blocks // 2
    gather = Gather([Columns(core, up_s, gate_out), Columns(core, up_s, up_out), Rows(core, down_ref, down_out)], sems)

    def at(when):
        return pl.when(step == when)

    def out_weight(owner):
        return w_ref[pl.ds(pl.multiple_of(owner * q_cols, 16), q_cols), q_cols + 2 * kv_cols :]

    def wo_copy():
        return remote(wo_send, wo_recv, wo_sem.at[0], wo_sem.at[1], grp, plane, 1 - core)

    @at(0)
    def _():
        greet(gather.partners())
        gather.second(0, here=True)
        wo_send[...] = out_weight(1 - core)
        wo_copy().start()
        up_s[...] = (up_ref[...].astype(F32) * gf_ref[...].astype(F32)).astype(BF16)
        gather.first(1)

    @at(tiles - 1)
    def _():
        wo_copy().wait()
        mine, other = out_weight(core), wo_recv[...]
        wo_ref[...] = jnp.concatenate([jnp.where(core == 0, mine, other), jnp.where(core == 0, other, mine)], 1)

    @at(tiles)
    def _():
        gather.first(2)
        gather.third(0)

    @at(tiles + 1)
    def _():
        gather.second(1)

    @at(tiles + 3)
    def _():
        gather.third(1)

    @at(tiles + 4)
    def _():
        gather.second(2)

    @at(tiles + 6)
    def _():
        gather.third(2)

    @pl.when(step < tiles)
    def _():
        x = x_ref[...].astype(F32)
        normed = (x * lax.rsqrt(jnp.mean(x * x, -1, keepdims=True) + epsilon)).astype(BF16)
        n_ref[...] = normed
        flat = dot(normed, w_ref[:, : q_cols + 2 * kv_cols])
        across = flat.T
        tokens = pl.ds(pl.multiple_of(step * BLOCK, BLOCK), BLOCK)
        here = pl.ds(pl.multiple_of(lax.rem(step, blocks) * BLOCK, BLOCK), BLOCK)
        cosine, sine = cos_ref[:, here], sin_ref[:, here]
        for h in range(heads):
            rows = turned(across[h * HEAD : (h + 1) * HEAD], cosine, sine, 1.0)
            qt_ref[h * HEAD : (h + 1) * HEAD, tokens] = (rows * TO_LOG2).astype(BF16)
        keys = [across[q_cols + h * HEAD : q_cols + (h + 1) * HEAD] for h in range(kv_heads)]
        keys = jnp.concatenate([turned(rows, cosine, sine, 1.0) for rows in keys], 0)
        kvt_ref[:kv_cols, tokens] = keys.astype(BF16)
        kvt_ref[kv_cols:, tokens] = across[q_cols + kv_cols :].astype(BF16)
        kv_ref[tokens, :kv_cols] = keys.T.astype(BF16)
        kv_ref[tokens, kv_cols:] = flat[:, q_cols + kv_cols :].astype(BF16)

    def rows_of(tile, owner):
        start = (tile // half) * blocks + owner * half + lax.rem(tile, half)
        return two_out.at[pl.ds(pl.multiple_of(start * BLOCK, BLOCK), BLOCK), :]

    def part_copy(slot):
        return remote(part_send.at[slot], part_recv.at[slot], part_sem.at[0, slot], part_sem.at[1, slot], grp, plane, 1 - core)

    def two_copy(slot):
        there = rows_of(slot, core)
        return remote(two_mine.at[slot], there, two_sem.at[0, slot], two_sem.at[1, slot], grp, plane, 1 - core)

    def two_keep(slot):
        return pltpu.make_async_copy(two_mine.at[slot], rows_of(slot, core), own_sem.at[slot])

    def finish(turn):
        block, s = lax.rem(turn, blocks), turn // blocks
        slot = s * half + lax.rem(block, half)

        @pl.when(block // half == core)
        def _():
            part_copy(slot).wait_recv()
            rows = pl.ds(pl.multiple_of(slot * BLOCK, BLOCK), BLOCK)
            middle = own_ref[rows, :].astype(F32) + part_mine[slot].astype(F32) + part_recv[slot].astype(F32)
            x1_ref[rows, :] = middle
            inverse = lax.rsqrt(jnp.mean(middle * middle, -1, keepdims=True) + epsilon)
            inv_ref[rows, :] = inverse
            two_mine[slot] = (middle * inverse).astype(BF16)
            two_copy(slot).start()
            two_keep(slot).start()

    def run(block):
        n = reach(block)
        turn = step - tiles
        s = turn // blocks
        prefix = prefix_ref[s]
        base = pl.multiple_of(s * blocks * BLOCK, BLOCK)
        tokens = pl.ds(pl.multiple_of(turn * BLOCK, BLOCK), BLOCK)

        def score(h):
            kh = h // groups
            keys = kv_ref[pl.ds(base, n), kh * HEAD : (kh + 1) * HEAD]
            return scores_of(keys, qt_ref[h * HEAD : (h + 1) * HEAD, tokens], prefix, block)

        def mix(h, weights, total):
            kh = h // groups
            vt = kvt_ref[kv_cols + kh * HEAD : kv_cols + (kh + 1) * HEAD, pl.ds(base, n)]
            ot_ref[h * HEAD : (h + 1) * HEAD, tokens] = (dot(vt, weights) / total).astype(BF16)

        later, held = score(0), None
        for h in range(heads):
            scores = later
            if h + 1 < heads:
                later = score(h + 1)
            peak = jnp.max(scores, 0, keepdims=True)
            weights = jnp.exp2(scores - peak)
            total = jnp.sum(weights, 0, keepdims=True)
            lse_ref[h : h + 1, tokens] = peak + jnp.log2(total)
            if held:
                mix(*held)
            held = (h, weights.astype(BF16), total)
        mix(*held)
        part = dot(ot_ref[:, tokens], wo_ref[...], TN).astype(BF16)
        slot = s * half + block % half

        @pl.when(core == block // half)
        def _():
            part_mine[slot] = part

        @pl.when(core != block // half)
        def _():
            part_send[slot] = part
            part_copy(slot).start()

    @pl.when(step > tiles)
    def _():
        finish(step - tiles - 1)

    for block in range(blocks):
        pl.when((step >= tiles) & (lax.rem(step, blocks) == block))(functools.partial(run, block))

    @at(2 * tiles - 1)
    def _():
        finish(step - tiles)
        for n in range(3):
            gather.last(n)
        gather.near_in(1)
        for slot in range(count * half):
            part_copy(slot).wait_send()
            two_copy(slot).wait_send()
            two_keep(slot).wait()
            there = rows_of(slot, 1 - core)
            remote(there, there, two_sem.at[0, slot], two_sem.at[1, slot], grp, plane, 1 - core).wait_recv()
        gather.sent_all((1, 2), (0, 1, 2))


def front(prefix, x, own, pack, gate_part, up, down, gain_ffn, cosine, sine, heads, kv_heads, length):
    tokens, width = x.shape
    count, blocks = tokens // length, length // BLOCK
    tiles = tokens // BLOCK
    slots = tiles // 2
    q_cols, kv_cols = heads * HEAD, kv_heads * HEAD
    shape = jax.ShapeDtypeStruct
    once = pl.Buffered(1)

    def fixed(*dims):
        return pl.BlockSpec(dims, lambda i: (0,) * len(dims), pipeline_mode=once)

    tile = pl.BlockSpec((BLOCK, width), lambda i: (jnp.minimum(i, tiles - 1), 0))
    return pl.pallas_call(
        functools.partial(front_kernel, heads, kv_heads, blocks),
        grid=(2 * tiles,),
        in_specs=[
            pl.BlockSpec(memory_space=pltpu.SMEM),
            tile,
            fixed(tokens // 2, width),
            fixed(*pack.shape),
            fixed(*up.shape),
            fixed(*gain_ffn.shape),
            fixed(*cosine.shape),
            fixed(*sine.shape),
            ANY,
            fixed(*down.shape),
        ],
        out_specs=(
            tile,
            fixed(q_cols, tokens),
            fixed(2 * kv_cols, tokens),
            fixed(tokens, 2 * kv_cols),
            fixed(q_cols, tokens),
            fixed(heads, tokens),
            fixed(q_cols, width),
            fixed(tokens // 2, width),
            fixed(tokens // 2, 1),
            ANY, ANY, ANY, ANY,
        ),
        out_shape=(
            shape((tokens, width), BF16),
            shape((q_cols, tokens), BF16),
            shape((2 * kv_cols, tokens), BF16),
            shape((tokens, 2 * kv_cols), BF16),
            shape((q_cols, tokens), BF16),
            shape((heads, tokens), F32),
            shape((q_cols, width), BF16),
            shape((tokens // 2, width), F32),
            shape((tokens // 2, 1), F32),
            shape((tokens, width), BF16),
            shape(gate_part.shape, BF16),
            shape(gate_part.shape, BF16),
            shape((4 * down.shape[0], width), BF16),
        ),
        input_output_aliases={8: 10},
        scratch_shapes=[
            pltpu.VMEM(up.shape, BF16),
            pltpu.VMEM((q_cols, q_cols), BF16),
            pltpu.VMEM((q_cols, q_cols), BF16),
        ]
        + [pltpu.VMEM((slots, BLOCK, width), BF16)] * 4
        + [DMA((2,)), DMA((2, slots)), DMA((2, slots)), DMA((slots,))]
        + Gather.semaphores(3),
        compiler_params=pltpu.CompilerParams(collective_id=1, has_side_effects=True, vmem_limit_bytes=60 * 2**20),
        cost_estimate=pl.CostEstimate(flops=2 * tokens * width * 1536, bytes_accessed=16 * tokens * width, transcendentals=0),
        name="front",
    )(prefix, x, own, pack, up, gain_ffn, cosine, sine, gate_part, down)


def feed_kernel(n_ref, gate_ref, up_ref, down_ref, hidden_ref, by_up_ref, by_gate_ref, part_ref):
    n = n_ref[...]
    gate = dot(n, gate_ref[...])
    upward = dot(n, up_ref[...])
    sigma = 1.0 / (1.0 + jnp.exp(-gate))
    silu = gate * sigma
    hidden = (silu * upward).astype(BF16)
    hidden_ref[...] = hidden
    by_up_ref[...] = silu.astype(BF16)
    by_gate_ref[...] = (upward * sigma * (1.0 + gate - silu)).astype(BF16)
    part_ref[...] = dot(hidden, down_ref[...]).astype(BF16)


def feed(n, gate, up, down):
    tokens, width = n.shape
    units = gate.shape[1]
    shape = jax.ShapeDtypeStruct
    once = pl.Buffered(1)
    tile = lambda cols: pl.BlockSpec((BLOCK, cols), lambda i: (i, 0))
    fixed = lambda a: pl.BlockSpec(a.shape, lambda i: (0, 0), pipeline_mode=once)
    return pl.pallas_call(
        feed_kernel,
        grid=(tokens // BLOCK,),
        in_specs=[tile(width), fixed(gate), fixed(up), fixed(down)],
        out_specs=(tile(units), tile(units), tile(units), tile(width)),
        out_shape=(shape((tokens, units), BF16),) * 3 + (shape((tokens, width), BF16),),
        compiler_params=pltpu.CompilerParams(vmem_limit_bytes=62 * 2**20),
        cost_estimate=pl.CostEstimate(flops=6 * tokens * width * units, bytes_accessed=2 * tokens * (3 * units + 2 * width), transcendentals=tokens * units),
        name="feed",
    )(n, gate, up, down)


def finish_kernel(heads, kv_heads, pack_ref, gate_ref, up_ref, down_ref, wq_ref, wk_ref, wv_ref, wg_ref, wu_ref, ga_ref, gf_ref,
                  q_out, k_out, v_out, o_out, gate_out, up_out, down_out, ga_out, gf_out):
    q_cols, kv_cols = heads * HEAD, kv_heads * HEAD
    cols = pack_ref.shape[1] // 8
    gain = ga_ref[...].astype(F32)
    total = jnp.zeros(gain.shape, F32)
    for k in range(2):
        row = jnp.concatenate([pack_ref[:, (2 * q + k) * cols : (2 * q + k + 1) * cols].astype(F32) for q in range(4)], 1)
        at = 0
        for w, out, size in ((wq_ref, q_out, q_cols), (wk_ref, k_out, kv_cols), (wv_ref, v_out, kv_cols)):
            part, here = row[:, at : at + size], slice(k * size, (k + 1) * size)
            total += jnp.sum(part * w[:, here].astype(F32), -1, keepdims=True)
            out[:, here] = part * gain
            at += size
        o_out[:, k * q_cols : (k + 1) * q_cols] = row[:, at:]
    ga_out[...] = total
    gain = gf_ref[...].astype(F32)
    total = jnp.zeros(gain.shape, F32)
    for ref, w, out in ((gate_ref, wg_ref, gate_out), (up_ref, wu_ref, up_out)):
        part = ref[...].astype(F32)
        total += jnp.sum(part * w[...].astype(F32), -1, keepdims=True)
        out[...] = part * gain
    gf_out[...] = total
    down_out[...] = down_ref[...].astype(F32)


def finish(pack, gate, up, down, wq, wk, wv, wo, wg, wu, ga, gf, heads, kv_heads):
    shape = lambda a: jax.ShapeDtypeStruct(a.shape, F32)
    whole = lambda a: pl.BlockSpec(a.shape, lambda i: (0, 0))
    outs = (shape(wq), shape(wk), shape(wv), shape(wo), shape(wg), shape(wu), shape(down), shape(ga), shape(gf))
    return pl.pallas_call(
        functools.partial(finish_kernel, heads, kv_heads),
        grid=(1,),
        in_specs=[whole(a) for a in (pack, gate, up, down, wq, wk, wv, wg, wu, ga, gf)],
        out_specs=tuple(whole(a) for a in outs),
        out_shape=outs,
        compiler_params=pltpu.CompilerParams(vmem_limit_bytes=62 * 2**20),
        name="finish",
    )(pack, gate, up, down, wq, wk, wv, wg, wu, ga, gf)


def halves_of(rows, cols, split):
    return (rows // 8, cols // 4) if split else (rows // 32, cols)


class Summand:
    def __init__(self, core, ref, out, split, near=False):
        self.core, self.ref, self.out, self.split, self.near = core, ref, out, split, near
        self.rows, self.cols = halves_of(*ref.shape, split)

    def half(self, plane, quarter, path):
        if self.split:
            start = pl.multiple_of((2 * plane + path) * self.rows, 16)
            return self.ref.at[pl.ds(start, self.rows), pl.ds(pl.multiple_of(quarter * self.cols, 128), self.cols)]
        start = pl.multiple_of(((4 * plane + quarter) * 2 + path) * self.rows, 16)
        return self.ref.at[pl.ds(start, self.rows), :]

    def place(self, quarter, j, other):
        if self.split:
            return self.out.at[:, pl.ds(pl.multiple_of((2 * quarter + other) * self.cols, 128), self.cols)]
        return self.out.at[pl.ds(pl.multiple_of((2 * quarter + j) * self.rows, 16), self.rows), :]


class Reduce:
    @staticmethod
    def buffers(halves, near=(), begun=(), left=()):
        found = []
        for n, h in enumerate(halves):
            no_first, no_third = n in begun, n in left
            for lead, unused in (
                ((2, 4, 2), no_first or n in near),
                ((2, 4, 2), no_first),
                ((2, 4), no_first),
                ((3, 2), no_third),
                ((4, 2), False),
            ):
                found.append(pltpu.VMEM((1,) * len(lead) + (16, 128) if unused else lead + h, BF16))
        return found

    @staticmethod
    def semaphores(n):
        return [DMA((n, 2, 4, 2))] * 3 + [DMA((n, 2, 4))] * 2 + [DMA((n, 3))] * 2 + [DMA((n, 4, 2))] * 2

    def __init__(self, units, buffers, sems):
        self.units, self.sems = units, sems
        self.bufs = [buffers[5 * n : 5 * n + 5] for n in range(len(units))]
        self.grp, self.plane, self.core = where_am_i()
        gx, gy = lax.rem(self.grp, 2), self.grp // 2
        self.gx, self.gy = gx, gy
        side, up = self.grp + 1 - 2 * gx, lax.rem(self.grp + 2, 4)
        self.first_to, self.second_to, self.keep = (side, up), (up, side), (gy, gx)
        self.planes = [lax.rem(self.plane + s, 4) for s in (1, 2, 3)]
        self.origins = [lax.rem(self.plane + 4 - s, 4) for s in (1, 2, 3)]
        self.others = [lax.rem(self.grp + s, 4) for s in (1, 2, 3)]
        self.sources = [lax.rem(self.grp + 4 - s, 4) for s in (1, 2, 3)]

    def partners(self):
        grp, plane, core = self.grp, self.plane, self.core
        found = [(grp, z, core) for z in self.planes] + [(grp, plane, 1 - core)]
        return found + [(g, plane, c) for g in self.others for c in (core, 1 - core)]

    def quarter(self, path, i, own):
        if path == 0:
            return 2 * i + (self.gx if own else 1 - self.gx)
        return 2 * (self.gy if own else 1 - self.gy) + i

    def first_copy(self, n, path, z, i):
        _, s1, r1 = self.sems[:3]
        src = self.units[n].half(z, self.quarter(path, i, False), path)
        dst = self.bufs[n][1].at[path, z, i]
        return remote(src, dst, s1.at[n, path, z, i], r1.at[n, path, z, i], self.first_to[path], self.plane, self.core)

    def load_copy(self, n, path, z, i):
        src = self.units[n].half(z, self.quarter(path, i, True), path)
        return pltpu.make_async_copy(src, self.bufs[n][0].at[path, z, i], self.sems[0].at[n, path, z, i])

    def second_copy(self, n, path, z):
        _, got, second = self.bufs[n][:3]
        s2, r2 = self.sems[3:5]
        src = got.at[path, z, 1 - self.keep[path]]
        return remote(src, second.at[path, z], s2.at[n, path, z], r2.at[n, path, z], self.second_to[path], self.plane, self.core)

    def third_copy(self, n, i):
        third, fin = self.bufs[n][3:]
        s3, r3 = self.sems[5:7]
        return remote(fin.at[self.planes[i]], third.at[i], s3.at[n, i], r3.at[n, i], self.grp, self.planes[i], self.core)

    def fourth_copy(self, n, i, j, coming=False):
        u, fin = self.units[n], self.bufs[n][4]
        s4, r4 = self.sems[7:9]
        other = (self.core if j == 0 else 1 - self.core) if u.split else self.core
        grp = self.grp if i == 3 else (self.sources if coming else self.others)[i]
        if coming:
            src = dst = u.place(grp, j, other)
        else:
            src = fin.at[self.plane, other if u.split else j]
            dst = u.place(self.grp, j, self.core)
        if i == 3 and not (u.split and j == 1):
            return pltpu.make_async_copy(src, dst, s4.at[n, 3, j])
        return remote(src, dst, s4.at[n, i, j], r4.at[n, i, j], grp, self.plane, other)

    @staticmethod
    def each():
        return [(path, z, i) for z in range(4) for path in range(2) for i in range(2)]

    def a(self, n):
        for path, z, i in self.each():
            self.first_copy(n, path, z, i).start()
            if not self.units[n].near:
                self.load_copy(n, path, z, i).start()

    def b(self, n):
        u, (acc, got) = self.units[n], self.bufs[n][:2]
        for z in range(4):
            for path in range(2):
                for i in range(2):
                    self.first_copy(n, path, z, i).wait_recv()
                    if u.near:
                        own = u.half(z, self.quarter(path, i, True), path)[...]
                    else:
                        self.load_copy(n, path, z, i).wait()
                        own = acc[path, z, i]
                    got[path, z, i] = (own.astype(F32) + got[path, z, i].astype(F32)).astype(BF16)
                self.second_copy(n, path, z).start()

    def c(self, n, send=True):
        _, got, second, _, fin = self.bufs[n]
        for z in range(4):
            for path in range(2):
                self.second_copy(n, path, z).wait_recv()
                fin[z, path] = (got[path, z, self.keep[path]].astype(F32) + second[path, z].astype(F32)).astype(BF16)
            if send:
                self.third_to(n, z)

    def third_to(self, n, z):
        third, fin = self.bufs[n][3:]
        s3, r3 = self.sems[5:7]
        i = lax.rem(z + 7 - self.plane, 4)

        @pl.when(i != 3)
        def _():
            remote(fin.at[z], third.at[i], s3.at[n, i], r3.at[n, i], self.grp, z, self.core).start()

    def c2(self, n):
        for i in range(3):
            self.third_copy(n, i).start()

    def d(self, n):
        third, fin = self.bufs[n][3:]
        for i in range(3):
            self.third_copy(n, i).wait_recv()
        for j in range(2):
            total = fin[self.plane, j].astype(F32)
            for i in range(3):
                total += third[i, j].astype(F32)
            fin[self.plane, j] = total.astype(BF16)
        for j in range(2):
            for i in range(4):
                self.fourth_copy(n, i, j).start()

    def e1(self, n):
        for path, z, i in self.each():
            self.first_copy(n, path, z, i).wait_send()
        for z in range(4):
            for path in range(2):
                self.second_copy(n, path, z).wait_send()

    def e2(self, n):
        u = self.units[n]
        for i in range(3):
            self.third_copy(n, i).wait_send()
        for j in range(2):
            for i in range(4):
                if i == 3 and not (u.split and j == 1):
                    self.fourth_copy(n, i, j).wait()
                else:
                    self.fourth_copy(n, i, j).wait_send()
                    self.fourth_copy(n, i, j, coming=True).wait_recv()


class Trade:
    @staticmethod
    def buffers(slots, width):
        return [pltpu.VMEM((slots, BLOCK, width), BF16)] * 3

    @staticmethod
    def semaphores(slots):
        return [DMA((2, slots))]

    def __init__(self, bufs, sems, blocks):
        self.mine, self.out, self.come = bufs
        self.sem, self.half, self.blocks = sems[0], blocks // 2, blocks
        self.slots = self.mine.shape[0]
        self.grp, self.plane, self.core = where_am_i()

    def copy(self, slot):
        return remote(self.out.at[slot], self.come.at[slot], self.sem.at[0, slot], self.sem.at[1, slot], self.grp, self.plane, 1 - self.core)

    def where(self, turn):
        block = lax.rem(turn, self.blocks)
        return block // self.half, (turn // self.blocks) * self.half + lax.rem(block, self.half)

    def give(self, turn, part):
        owner, slot = self.where(turn)

        @pl.when(self.core == owner)
        def _():
            self.mine[slot] = part

        @pl.when(self.core != owner)
        def _():
            self.out[slot] = part
            self.copy(slot).start()

    def take(self, turn, close):
        owner, slot = self.where(turn)

        @pl.when(self.core == owner)
        def _():
            self.copy(slot).wait_recv()
            close(slot, self.mine[slot].astype(F32) + self.come[slot].astype(F32))

    def drain(self):
        for slot in range(self.slots):
            self.copy(slot).wait_send()

    def place(self, slot, owner):
        start = (slot // self.half) * self.blocks + owner * self.half + lax.rem(slot, self.half)
        return pl.ds(pl.multiple_of(start * BLOCK, BLOCK), BLOCK)

    def rows(self, ref, slot, owner):
        return ref.at[self.place(slot, owner), :]

    def columns(self, ref, slot, owner):
        return ref.at[:, self.place(slot, owner)]


WIDE = 2 * BLOCK


def feed_back_kernel(blocks, dy_ref, n_ref, gate_ref, up_ref, down_ref, inv_ref, by_up_ref, by_gate_ref, grad_ref,
                     g_gate_ref, g_up_ref, dx_out, r_down_out, begun_ref,
                     turned_n, d_gate, d_up, dx_mine, by_sem, dx_sem, keep_sem, *rest):
    step = pl.program_id(0)
    tiles = turned_n.shape[1] // BLOCK
    cuts = d_gate.shape[1] // WIDE
    second = tiles + 2 * cuts
    last = second + tiles - 1
    trade = Trade(rest[:3], rest[3:4], blocks)
    grp, plane, core = where_am_i()
    units = [Summand(core, grad_ref, r_down_out, False), Summand(core, g_gate_ref, None, True, near=True)]
    reduce = Reduce(units, list(rest[4:13]) + [begun_ref], rest[14:])

    def at(when):
        return pl.when(step == when)

    def tile_rows(tile):
        return pl.ds(pl.multiple_of(tile * BLOCK, BLOCK), BLOCK)

    def by_copies(tile):
        rows = tile_rows(tile)
        return [pltpu.make_async_copy(ref.at[rows, :], to.at[rows, :], by_sem.at[k, tile]) for k, (ref, to) in enumerate(((by_up_ref, d_up), (by_gate_ref, d_gate)))]

    @at(0)
    def _():
        for tile in range(tiles):
            for copy in by_copies(tile):
                copy.start()
        greet(reduce.partners())
        reduce.a(0)

    @at(tiles + 1)
    def _():
        reduce.b(0)

    @at(tiles + cuts)
    def _():
        reduce.a(1)

    @at(tiles + cuts + 1)
    def _():
        reduce.c(0)

    @at(second + 2)
    def _():
        reduce.b(1)

    @at(second + 4)
    def _():
        reduce.d(0)

    @pl.when(step < tiles)
    def _():
        rows = tile_rows(step)
        dy = dy_ref[...]
        grad = dot(dy, down_ref[...], NT)
        for copy in by_copies(step):
            copy.wait()
        d_up[rows, :] = (grad * d_up[rows, :].astype(F32)).astype(BF16)
        d_gate[rows, :] = (grad * d_gate[rows, :].astype(F32)).astype(BF16)
        turned_n[:, rows] = n_ref[...].T
        owner, slot = trade.where(step)

        @pl.when(owner == core)
        def _():
            dx_mine[slot] = dy

    @pl.when((step >= tiles) & (step < tiles + cuts))
    def _():
        cols = pl.ds(pl.multiple_of((step - tiles) * WIDE, WIDE), WIDE)
        g_gate_ref[:, cols] = dot(turned_n[...], d_gate[:, cols]).astype(BF16)

    @pl.when((step >= tiles + cuts) & (step < second))
    def _():
        cols = pl.ds(pl.multiple_of((step - tiles - cuts) * WIDE, WIDE), WIDE)
        g_up_ref[...] = dot(turned_n[...], d_up[:, cols]).astype(BF16)

    def there(slot, owner):
        return trade.rows(dx_out, slot, owner)

    def dx_copy(slot):
        return remote(dx_mine.at[slot], there(slot, core), dx_sem.at[0, slot], dx_sem.at[1, slot], grp, plane, 1 - core)

    def dx_keep(slot):
        return pltpu.make_async_copy(dx_mine.at[slot], there(slot, core), keep_sem.at[slot])

    def close(slot, grad):
        rows = pl.ds(pl.multiple_of(slot * BLOCK, BLOCK), BLOCK)
        normed = trade.columns(turned_n, slot, core)[...].T.astype(F32)
        back = grad - normed * jnp.mean(grad * normed, -1, keepdims=True)
        dx_mine[slot] = (dx_mine[slot].astype(F32) + inv_ref[rows, :] * back).astype(BF16)
        dx_copy(slot).start()
        dx_keep(slot).start()

    @pl.when(step > second)
    def _():
        trade.take(step - second - 1, close)

    @pl.when(step >= second)
    def _():
        turn = step - second
        rows = tile_rows(turn)
        part = dot(d_gate[rows, :], gate_ref[...], NT) + dot(d_up[rows, :], up_ref[...], NT)
        trade.give(turn, part.astype(BF16))

    @at(last)
    def _():
        trade.take(tiles - 1, close)
        reduce.c(1, send=False)
        reduce.e1(0)
        reduce.e2(0)
        reduce.e1(1)
        trade.drain()
        for slot in range(trade.slots):
            dx_copy(slot).wait_send()
            dx_keep(slot).wait()
            here = there(slot, 1 - core)
            remote(here, here, dx_sem.at[0, slot], dx_sem.at[1, slot], grp, plane, 1 - core).wait_recv()


def feed_back(dy, by_up, by_gate, n, gate, up, down, inverse, grad_down, length):
    tokens, width = dy.shape
    units = gate.shape[1]
    blocks, tiles, cuts = length // BLOCK, tokens // BLOCK, units // WIDE
    slots = tiles // 2
    shape = jax.ShapeDtypeStruct
    once = pl.Buffered(1)
    early = lambda cols: pl.BlockSpec((BLOCK, cols), lambda i: (jnp.minimum(i, tiles - 1), 0))
    fixed = lambda a: pl.BlockSpec(a.shape, lambda i: (0,) * len(a.shape), pipeline_mode=once)
    cut = pl.BlockSpec((width, WIDE), lambda i: (0, jnp.clip(i - tiles - cuts, 0, cuts - 1)))
    g_gate = shape((width, units), BF16)
    halves = [halves_of(*grad_down.shape, False), halves_of(width, units, True)]
    begun = shape((4, 2) + halves[1], BF16)
    return pl.pallas_call(
        functools.partial(feed_back_kernel, blocks),
        grid=(2 * tiles + 2 * cuts,),
        in_specs=[early(width), early(width)] + [fixed(a) for a in (gate, up, down, inverse)] + [ANY] * 3,
        out_specs=(fixed(g_gate), cut, ANY, ANY, fixed(begun)),
        out_shape=(
            g_gate,
            g_gate,
            shape((tokens, width), BF16),
            shape((grad_down.shape[0] // 4, width), BF16),
            begun,
        ),
        scratch_shapes=[
            pltpu.VMEM((width, tokens), BF16),
            pltpu.VMEM((tokens, units), BF16),
            pltpu.VMEM((tokens, units), BF16),
            pltpu.VMEM((slots, BLOCK, width), BF16),
            DMA((2, tiles)),
            DMA((2, slots)),
            DMA((slots,)),
        ]
        + Trade.buffers(slots, width)
        + Trade.semaphores(slots)
        + Reduce.buffers(halves, near=(1,), left=(1,))
        + Reduce.semaphores(2),
        compiler_params=pltpu.CompilerParams(collective_id=3, has_side_effects=True, vmem_limit_bytes=62 * 2**20),
        name="feed_back",
    )(dy, n, gate, up, down, inverse, by_up, by_gate, grad_down)


def back_kernel(heads, kv_heads, blocks, prefix_ref, qt_ref, kv_ref, kt_ref, lse_ref, ot_ref, dx_ref, n_ref, own_ref, wo_ref, w_ref,
                cos_ref, sin_ref, begun_ref, g_up_ref,
                grad_out, r_pack_out, r_gate_out, r_up_out,
                dot_ref, dk_ref, dv_ref, dt, g_pack, g_wo, wo_send, wo_come, wo_sem, *rest):
    step = pl.program_id(0)
    grp, plane, core = where_am_i()
    tokens, width = dx_ref.shape
    tiles, half, length = tokens // BLOCK, blocks // 2, blocks * BLOCK
    groups = heads // kv_heads
    q_cols, kv_cols = heads * HEAD, kv_heads * HEAD
    qkv = q_cols + 2 * kv_cols
    thirds = 3
    cut = width // thirds
    trade = Trade(rest[:3], rest[3:4], blocks)
    units = [Summand(core, g_up_ref, r_gate_out, True), Summand(core, g_up_ref, r_up_out, True), Summand(core, g_pack, r_pack_out, True, near=True)]
    reduce = Reduce(units, list(rest[4:8]) + [begun_ref] + list(rest[9:19]), rest[19:])
    turn = lax.rem(step, blocks)

    def at(when):
        return pl.when(step == when)

    def wo_copy():
        return remote(wo_send, wo_come, wo_sem.at[0], wo_sem.at[1], grp, plane, 1 - core)

    @at(0)
    def _():
        greet(reduce.partners())
        reduce.a(1)
        reduce.c2(0)

    for j in range(thirds):
        @at(1 + j)
        def _(j=j):
            g_wo[:, j * cut : (j + 1) * cut] = dot(ot_ref[...], dx_ref[:, j * cut : (j + 1) * cut]).astype(BF16)

    @at(1 + thirds)
    def _():
        low, high = g_wo[:, :q_cols], g_wo[:, q_cols:]
        wo_send[...] = jnp.where(core == 0, high, low)
        wo_copy().start()
        g_pack[pl.ds(pl.multiple_of(core * q_cols, 16), q_cols), qkv:] = jnp.where(core == 0, low, high)

    @at(5)
    def _():
        reduce.b(1)
        reduce.d(0)

    @at(tiles)
    def _():
        reduce.c(1)

    @at(tiles + thirds)
    def _():
        wo_copy().wait()
        g_pack[pl.ds(pl.multiple_of((1 - core) * q_cols, 16), q_cols), qkv:] = wo_come[...]
        reduce.a(2)

    @pl.when((step < tiles) & (turn == 0))
    def _():
        dk_ref[...] = jnp.zeros_like(dk_ref)
        dv_ref[...] = jnp.zeros_like(dv_ref)

    @pl.when(step < tiles)
    def _():
        rows = pl.ds(pl.multiple_of(step * BLOCK, BLOCK), BLOCK)
        dot_ref[...] = dot(wo_ref[...], dx_ref[rows, :], NT).astype(BF16)

    def run(block):
        n = reach(block)
        prefix = prefix_ref[step // blocks]
        tokens_here = pl.ds(pl.multiple_of(step * BLOCK, BLOCK), BLOCK)
        here = pl.ds(block * BLOCK, BLOCK)
        cosine, sine = cos_ref[:, here], sin_ref[:, here]

        def score(h):
            kh = h // groups
            own = slice(h * HEAD, (h + 1) * HEAD)
            keys = kv_ref[:n, kh * HEAD : (kh + 1) * HEAD]
            values = kv_ref[:n, kv_cols + kh * HEAD : kv_cols + (kh + 1) * HEAD]
            return scores_of(keys, qt_ref[own, :], prefix, block), dot(values, dot_ref[own, :])

        later = score(0)
        for h in range(heads):
            kh = h // groups
            own = slice(h * HEAD, (h + 1) * HEAD)
            kt = kt_ref[kh * HEAD : (kh + 1) * HEAD, :n]
            query, grad = qt_ref[own, :], dot_ref[own, :]
            delta = jnp.sum(grad.astype(F32) * ot_ref[own, tokens_here].astype(F32), 0, keepdims=True)
            scores, grad_probs = later
            if h + 1 < heads:
                later = score(h + 1)
            probs = jnp.exp2(scores - lse_ref[h : h + 1, :])
            grad_scores = (probs * (grad_probs - delta)).astype(BF16)
            dv_ref[kh, :, :n] += dot(grad, probs.astype(BF16), NT)
            dk_ref[kh, :, :n] += dot(query, grad_scores, NT)
            grad_query = turned(dot(kt, grad_scores), cosine, sine, -1.0)
            dt[own, tokens_here] = (grad_query * (1.0 / math.sqrt(HEAD))).astype(BF16)

    for block in range(blocks):
        pl.when((step < tiles) & (turn == block))(functools.partial(run, block))

    @pl.when((step < tiles) & (turn == blocks - 1))
    def _():
        sequence = pl.ds(pl.multiple_of((step // blocks) * length, length), length)
        for kh in range(kv_heads):
            rows = turned(dk_ref[kh], cos_ref[...], sin_ref[...], -1.0) * math.log(2.0)
            dt[q_cols + kh * HEAD : q_cols + (kh + 1) * HEAD, sequence] = rows.astype(BF16)
            start = q_cols + kv_cols + kh * HEAD
            dt[start : start + HEAD, sequence] = dv_ref[kh].astype(BF16)

    for j in range(thirds):
        @at(tiles + j)
        def _(j=j):
            across = dot(dt[...], n_ref[...])
            g_pack[j * cut : (j + 1) * cut, :qkv] = across.T.astype(BF16)

    def close(slot, grad):
        rows = pl.ds(pl.multiple_of(slot * BLOCK, BLOCK), BLOCK)
        x = own_ref[rows, :].astype(F32)
        inverse = lax.rsqrt(jnp.mean(x * x, -1, keepdims=True) + epsilon)
        normed = x * inverse
        back = inverse * (grad - normed * jnp.mean(grad * normed, -1, keepdims=True))
        grad_out[rows, :] = (trade.rows(dx_ref, slot, core)[...].astype(F32) + back).astype(BF16)

    first = tiles + thirds

    @pl.when(step > first)
    def _():
        trade.take(step - first - 1, close)

    @pl.when(step >= first)
    def _():
        rows = pl.ds(pl.multiple_of((step - first) * BLOCK, BLOCK), BLOCK)
        part = dot(dt[:, rows].T, w_ref[:, :qkv], NT)
        trade.give(step - first, part.astype(BF16))

    @at(first + 1)
    def _():
        reduce.d(1)

    @at(first + tiles - 1)
    def _():
        trade.take(tiles - 1, close)
        reduce.b(2)
        reduce.c(2)
        reduce.d(2)
        for n in range(3):
            reduce.e2(n)
        for n in (1, 2):
            reduce.e1(n)
        trade.drain()


def back(prefix, qt, kv, kvt, lse, ot, dx, n, own, wo, pack, cosine, sine, begun, g_up, heads, kv_heads, length):
    tokens, width = dx.shape
    count, blocks, tiles = tokens // length, length // BLOCK, tokens // BLOCK
    slots = tiles // 2
    q_cols, kv_cols = heads * HEAD, kv_heads * HEAD
    shape = jax.ShapeDtypeStruct
    once = pl.Buffered(1)
    fixed = lambda a: pl.BlockSpec(a.shape, lambda i: (0,) * a.ndim, pipeline_mode=once)
    early = lambda i: jnp.minimum(i, tiles - 1)
    shards = [shape((g.shape[0] // 8, g.shape[1] * 2), BF16) for g in (pack, g_up, g_up)]
    return pl.pallas_call(
        functools.partial(back_kernel, heads, kv_heads, blocks),
        grid=(2 * tiles + 3,),
        in_specs=[
            pl.BlockSpec(memory_space=pltpu.SMEM),
            pl.BlockSpec((q_cols, BLOCK), lambda i: (0, early(i))),
            pl.BlockSpec((length, 2 * kv_cols), lambda i: (early(i) // blocks, 0)),
            pl.BlockSpec((kv_cols, length), lambda i: (0, early(i) // blocks)),
            pl.BlockSpec((heads, BLOCK), lambda i: (0, early(i))),
        ]
        + [fixed(ot), fixed(dx), pl.BlockSpec((tokens, width // 3), lambda i: (0, jnp.clip(i - tiles, 0, 2)))]
        + [fixed(a) for a in (own, wo, pack, cosine, sine, begun)]
        + [ANY],
        out_specs=(fixed(own), ANY, ANY, ANY),
        out_shape=[shape(own.shape, BF16)] + shards,
        scratch_shapes=[
            pltpu.VMEM((q_cols, BLOCK), BF16),
            pltpu.VMEM((kv_heads, HEAD, length), F32),
            pltpu.VMEM((kv_heads, HEAD, length), F32),
            pltpu.VMEM((q_cols + 2 * kv_cols, tokens), BF16),
            pltpu.VMEM(pack.shape, BF16),
            pltpu.VMEM(wo.shape, BF16),
            pltpu.VMEM((q_cols, q_cols), BF16),
            pltpu.VMEM((q_cols, q_cols), BF16),
            DMA((2,)),
        ]
        + Trade.buffers(slots, width)
        + Trade.semaphores(slots)
        + Reduce.buffers([halves_of(*g.shape, True) for g in (g_up, g_up, pack)], near=(2,), begun=(0,))
        + Reduce.semaphores(3),
        compiler_params=pltpu.CompilerParams(collective_id=4, has_side_effects=True, vmem_limit_bytes=62 * 2**20),
        name="back",
    )(prefix, qt, kv, kvt, lse, ot, dx, n, own, wo, pack, cosine, sine, begun, g_up)


SWAP = [(0, 1), (1, 0)]


def trade(mine):
    return lax.ppermute(mine, "ctx", SWAP)


def part_of(array, which, axis):
    size = array.shape[axis] // 2
    return lax.dynamic_slice_in_dim(array, which * size, size, axis)


def tables(length):
    frequency = np.float32(10000.0) ** (-np.arange(HEAD // 2, dtype=np.float32) * np.float32(2.0) / np.float32(HEAD))
    angles = frequency[:, None] * np.arange(length, dtype=np.float32)[None, :]
    return jnp.asarray(np.cos(angles)), jnp.asarray(np.sin(angles))


def paired(
    activations_in,
    prefix_len,
    attn_gain,
    query_weight,
    key_weight,
    value_weight,
    out_weight,
    ffn_gain,
    gate_weight,
    up_weight,
    down_weight,
    cotangent,
):
    micro, seq_count, span, width = activations_in.shape
    count, length = micro * seq_count, 2 * span
    core = lax.axis_index("ctx")
    heads, kv_heads = HEADS // 2, KV_HEADS // 2

    own_x = activations_in.reshape(count, span, width)
    own_dy = cotangent.reshape(count, span, width)

    def summed(part):
        part = part.reshape(count, length, width)
        theirs = trade(part_of(part, 1 - core, 1))
        return part_of(part, core, 1).astype(F32) + theirs.astype(F32)

    gain_attn, gain_ffn = attn_gain[:, None], ffn_gain[:, None]
    pack, gate_part, full_x, full_dy = start(
        own_x, own_dy, query_weight, key_weight, value_weight, out_weight, gate_weight, gain_attn, gain_ffn, heads, kv_heads
    )
    cosine, sine = tables(length)
    prefix = prefix_len.reshape(count)
    normed_one, qt, kvt, kv, ot, lse, w_out, middle, inverse, full_two, w_gate, w_up, w_down = front(
        prefix, full_x, own_x.reshape(count * span, width), pack, gate_part, up_weight, down_weight, gain_ffn, cosine, sine,
        heads, kv_heads, length,
    )
    hidden, by_up, by_gate, part = feed(full_two, w_gate, w_up, w_down)
    result = middle.reshape(count, span, width) + summed(part)
    grad_down = dot(hidden, full_dy, TN).astype(BF16)
    _, grad_up, full_dx, r_down, begun = feed_back(
        full_dy, by_up, by_gate, full_two, w_gate, w_up, w_down, inverse, grad_down, length
    )
    grad_inputs, r_pack, r_gate, r_up = back(
        prefix, qt, kv, kvt, lse, ot, full_dx, normed_one, own_x.reshape(count * span, width), w_out, pack, cosine, sine,
        begun, grad_up, heads, kv_heads, length,
    )
    g_q, g_k, g_v, g_o, g_gate, g_up, g_down, g_ga, g_gf = finish(
        r_pack, r_gate, r_up, r_down, query_weight, key_weight, value_weight, out_weight, gate_weight, up_weight, gain_attn, gain_ffn,
        heads, kv_heads,
    )
    shape = activations_in.shape
    return (
        result.astype(BF16).reshape(shape),
        grad_inputs.reshape(shape),
        g_ga[:, 0],
        g_q,
        g_k,
        g_v,
        g_o,
        g_gf[:, 0],
        g_gate,
        g_up,
        g_down,
    )


def solution(mesh):
    small = dict(mesh.shape) == {"grp": 4, "fsdp": 4, "ctx": 2}

    return jax.shard_map(
        paired if small else local,
        mesh=mesh,
        in_specs=(
            P(None, ("grp", "fsdp"), "ctx", None),
            P(None, ("grp", "fsdp")),
            P(("fsdp", "ctx")),
            P(("fsdp", "ctx"), None),
            P(("fsdp", "ctx"), None),
            P(("fsdp", "ctx"), None),
            P(("fsdp", "ctx"), None),
            P(("fsdp", "ctx")),
            P(("fsdp", "ctx"), None),
            P(("fsdp", "ctx"), None),
            P(("fsdp", "ctx"), None),
            P(None, ("grp", "fsdp"), "ctx", None),
        ),
        out_specs=(
            P(None, ("grp", "fsdp"), "ctx", None),
            P(None, ("grp", "fsdp"), "ctx", None),
            P(("fsdp", "ctx")),
            P(("fsdp", "ctx"), None),
            P(("fsdp", "ctx"), None),
            P(("fsdp", "ctx"), None),
            P(("fsdp", "ctx"), None),
            P(("fsdp", "ctx")),
            P(("fsdp", "ctx"), None),
            P(("fsdp", "ctx"), None),
            P(("fsdp", "ctx"), None),
        ),
        check_vma=False,
    )
```

```python
import functools
import math

import jax
import jax.numpy as jnp
import numpy as np
from jax import lax
from jax.experimental import pallas as pl
from jax.experimental.pallas import tpu as pltpu
from jax.sharding import PartitionSpec as P

HEADS = 18
KV_HEADS = 6
HEAD = 64


epsilon = 1e-05


def shortened(array):

    def short(part):
        return part.astype(jnp.bfloat16) if part.dtype == jnp.float32 else part

    return jax.tree.map(short, array)


def rotary_tables(positions):
    halfway = HEAD // 2
    frequency = 10000.0 ** (-jnp.arange(halfway, dtype=jnp.float32) * 2.0 / HEAD)
    angles = positions.astype(jnp.float32)[:, None] * frequency[None, :]
    return (jnp.cos(angles)[:, None, :], jnp.sin(angles)[:, None, :])


def rotate(values, cosine, sine):
    halfway = values.shape[-1] // 2
    first = values[..., :halfway]
    second = values[..., halfway:]
    return jnp.concatenate([first * cosine - second * sine, second * cosine + first * sine], -1)


def rotate_back(values, cosine, sine):
    halfway = values.shape[-1] // 2
    first = values[..., :halfway]
    second = values[..., halfway:]
    return jnp.concatenate([first * cosine + second * sine, second * cosine - first * sine], -1)


def norm_back(grad_normed, normed, inverse):
    return inverse * (grad_normed - normed * jnp.mean(grad_normed * normed, -1, keepdims=True))


def flatten_all(grads):
    return tuple((g.reshape(-1) for g in grads))


def local(
    activations_in,
    prefix_len,
    attn_gain,
    query_weight,
    key_weight,
    value_weight,
    out_weight,
    ffn_gain,
    gate_weight,
    up_weight,
    down_weight,
    cotangent,
):
    micro, seq_count, span, width = activations_in.shape
    rows = seq_count * span
    length = span * lax.axis_size("ctx")
    groups = HEADS // KV_HEADS
    scale = 1.0 / math.sqrt(HEAD)
    shards = (
        attn_gain,
        query_weight,
        key_weight,
        value_weight,
        out_weight,
        ffn_gain,
        gate_weight,
        up_weight,
        down_weight,
    )
    offset = lax.axis_index("ctx") * span
    query_pos = offset + jnp.arange(span, dtype=jnp.int32)
    key_pos = jnp.arange(length, dtype=jnp.int32)
    cosine, sine = rotary_tables(jnp.tile(query_pos, seq_count))

    def visibility(prefix):
        return (key_pos[None, :] <= query_pos[:, None]) | (key_pos[None, :] < prefix)

    def attend(item):
        query, keys, values, prefix = item
        scores = (
            jnp.einsum("qhgd,khd->hgqk", query, keys, preferred_element_type=jnp.float32) * scale
        )
        scores = jnp.where(visibility(prefix), scores, -1e30)
        peak = jnp.max(scores, -1, keepdims=True)
        weights = jnp.exp(scores - peak)
        totals = jnp.sum(weights, -1, keepdims=True)
        probs = (weights / totals).astype(jnp.bfloat16)
        mixed = jnp.einsum("hgqk,khd->qhgd", probs, values, preferred_element_type=jnp.float32)
        return (mixed.reshape(span, HEADS * HEAD), (peak + jnp.log(totals))[..., 0])

    def attend_back(item):
        query, keys, values, prefix, log_total, grad_mixed = item
        scores = (
            jnp.einsum("qhgd,khd->hgqk", query, keys, preferred_element_type=jnp.float32) * scale
        )
        probs = jnp.where(visibility(prefix), jnp.exp(scores - log_total[..., None]), 0.0)
        grad_probs = jnp.einsum(
            "qhgd,khd->hgqk", grad_mixed, values, preferred_element_type=jnp.float32
        )
        grad_scores = (
            probs * (grad_probs - jnp.sum(probs * grad_probs, -1, keepdims=True))
        ).astype(jnp.bfloat16)
        grad_query = (
            jnp.einsum("hgqk,khd->qhgd", grad_scores, keys, preferred_element_type=jnp.float32)
            * scale
        )
        grad_keys = (
            jnp.einsum("hgqk,qhgd->khd", grad_scores, query, preferred_element_type=jnp.float32)
            * scale
        )
        grad_values = jnp.einsum(
            "hgqk,qhgd->khd",
            probs.astype(jnp.bfloat16),
            grad_mixed,
            preferred_element_type=jnp.float32,
        )
        return (
            grad_query.reshape(span, HEADS * HEAD),
            grad_keys.reshape(length, KV_HEADS * HEAD),
            grad_values.reshape(length, KV_HEADS * HEAD),
        )

    outputs = []
    input_grads = []
    collected = None
    for index in range(micro):
        full = (
            lax.all_gather(shards[0], ("fsdp", "ctx"), axis=0, tiled=True),
            lax.all_gather(shards[1], ("fsdp", "ctx"), axis=0, tiled=True),
            lax.all_gather(shards[2], ("fsdp", "ctx"), axis=0, tiled=True),
            lax.all_gather(shards[3], ("fsdp", "ctx"), axis=0, tiled=True),
            lax.all_gather(shards[4], ("fsdp", "ctx"), axis=0, tiled=True),
            lax.all_gather(shards[5], ("fsdp", "ctx"), axis=0, tiled=True),
            lax.all_gather(shards[6], ("fsdp", "ctx"), axis=0, tiled=True),
            lax.all_gather(shards[7], ("fsdp", "ctx"), axis=0, tiled=True),
            lax.all_gather(shards[8], ("fsdp", "ctx"), axis=0, tiled=True),
        )
        gain_attn, w_query, w_key, w_value, w_out, gain_ffn, w_gate, w_up, w_down = full
        inputs = activations_in[index].reshape(rows, width).astype(jnp.float32)
        inverse_one = lax.rsqrt(jnp.mean(inputs * inputs, -1, keepdims=True) + epsilon)
        normed_one = inputs * inverse_one
        first_in = (normed_one * gain_attn).astype(jnp.bfloat16)
        query_lin = jnp.dot(first_in, w_query, preferred_element_type=jnp.float32)
        key_lin = jnp.dot(first_in, w_key, preferred_element_type=jnp.float32)
        value_lin = jnp.dot(first_in, w_value, preferred_element_type=jnp.float32)
        query_rot = rotate(query_lin.reshape(rows, HEADS, HEAD), cosine, sine).astype(jnp.bfloat16)
        key_rot = rotate(key_lin.reshape(rows, KV_HEADS, HEAD), cosine, sine).astype(jnp.bfloat16)
        key_rot = key_rot.reshape(seq_count, span, KV_HEADS * HEAD)
        value_low = value_lin.astype(jnp.bfloat16).reshape(seq_count, span, KV_HEADS * HEAD)
        key_all, value_all = (
            lax.all_gather(key_rot, "ctx", axis=1, tiled=True),
            lax.all_gather(value_low, "ctx", axis=1, tiled=True),
        )
        query_split = query_rot.reshape(seq_count, span, KV_HEADS, groups, HEAD)
        key_split = key_all.reshape(seq_count, length, KV_HEADS, HEAD)
        value_split = value_all.reshape(seq_count, length, KV_HEADS, HEAD)
        mixed_all, log_totals = lax.map(
            attend, (query_split, key_split, value_split, prefix_len[index])
        )
        attn_low = mixed_all.reshape(rows, HEADS * HEAD).astype(jnp.bfloat16)
        middle = inputs + jnp.dot(attn_low, w_out, preferred_element_type=jnp.float32)
        inverse_two = lax.rsqrt(jnp.mean(middle * middle, -1, keepdims=True) + epsilon)
        normed_two = middle * inverse_two
        second_in = (normed_two * gain_ffn).astype(jnp.bfloat16)
        gate = jnp.dot(second_in, w_gate, preferred_element_type=jnp.float32)
        upward = jnp.dot(second_in, w_up, preferred_element_type=jnp.float32)
        hidden = (jax.nn.silu(gate) * upward).astype(jnp.bfloat16)
        result = middle + jnp.dot(hidden, w_down, preferred_element_type=jnp.float32)
        outputs.append(result.astype(jnp.bfloat16).reshape(seq_count, span, width))
        back = (
            lax.all_gather(shards[0], ("fsdp", "ctx"), axis=0, tiled=True),
            lax.all_gather(shards[1], ("fsdp", "ctx"), axis=0, tiled=True),
            lax.all_gather(shards[2], ("fsdp", "ctx"), axis=0, tiled=True),
            lax.all_gather(shards[3], ("fsdp", "ctx"), axis=0, tiled=True),
            lax.all_gather(shards[4], ("fsdp", "ctx"), axis=0, tiled=True),
            lax.all_gather(shards[5], ("fsdp", "ctx"), axis=0, tiled=True),
            lax.all_gather(shards[6], ("fsdp", "ctx"), axis=0, tiled=True),
            lax.all_gather(shards[7], ("fsdp", "ctx"), axis=0, tiled=True),
            lax.all_gather(shards[8], ("fsdp", "ctx"), axis=0, tiled=True),
        )
        gain_attn, w_query, w_key, w_value, w_out, gain_ffn, w_gate, w_up, w_down = back
        grad_y = cotangent[index].reshape(rows, width).astype(jnp.float32)
        grad_y_low = grad_y.astype(jnp.bfloat16)
        grad_wdown = jnp.einsum("rf,rd->fd", hidden, grad_y_low, preferred_element_type=jnp.float32)
        grad_hidden = jnp.einsum(
            "rd,fd->rf", grad_y_low, w_down, preferred_element_type=jnp.float32
        )
        sigma = jax.nn.sigmoid(gate)
        grad_up_low = (grad_hidden * gate * sigma).astype(jnp.bfloat16)
        grad_gate_low = (grad_hidden * upward * sigma * (1.0 + gate * (1.0 - sigma))).astype(
            jnp.bfloat16
        )
        grad_wgate = jnp.einsum(
            "rd,rf->df", second_in, grad_gate_low, preferred_element_type=jnp.float32
        )
        grad_wup = jnp.einsum(
            "rd,rf->df", second_in, grad_up_low, preferred_element_type=jnp.float32
        )
        grad_second = jnp.einsum(
            "rf,df->rd", grad_gate_low, w_gate, preferred_element_type=jnp.float32
        ) + jnp.einsum("rf,df->rd", grad_up_low, w_up, preferred_element_type=jnp.float32)
        grad_gain_ffn = jnp.sum(grad_second * normed_two, 0)
        grad_middle = grad_y + norm_back(grad_second * gain_ffn, normed_two, inverse_two)
        grad_branch_low = grad_middle.astype(jnp.bfloat16)
        grad_wout = jnp.einsum(
            "ra,rd->ad", attn_low, grad_branch_low, preferred_element_type=jnp.float32
        )
        grad_attn_low = jnp.einsum(
            "rd,ad->ra", grad_branch_low, w_out, preferred_element_type=jnp.float32
        ).astype(jnp.bfloat16)
        grad_mixed = grad_attn_low.reshape(seq_count, span, KV_HEADS, groups, HEAD)
        grad_query_rot, grad_key_part, grad_value_part = lax.map(
            attend_back,
            (query_split, key_split, value_split, prefix_len[index], log_totals, grad_mixed),
        )
        grad_key_own, grad_value_own = (
            lax.psum_scatter(
                grad_key_part.astype(jnp.bfloat16), "ctx", scatter_dimension=1, tiled=True
            ).astype(jnp.float32),
            lax.psum_scatter(
                grad_value_part.astype(jnp.bfloat16), "ctx", scatter_dimension=1, tiled=True
            ).astype(jnp.float32),
        )
        grad_query = rotate_back(grad_query_rot.reshape(rows, HEADS, HEAD), cosine, sine)
        grad_query = grad_query.reshape(rows, HEADS * HEAD).astype(jnp.bfloat16)
        grad_key = rotate_back(grad_key_own.reshape(rows, KV_HEADS, HEAD), cosine, sine)
        grad_key = grad_key.reshape(rows, KV_HEADS * HEAD).astype(jnp.bfloat16)
        grad_value = grad_value_own.reshape(rows, KV_HEADS * HEAD).astype(jnp.bfloat16)
        grad_wquery = jnp.einsum(
            "rd,rq->dq", first_in, grad_query, preferred_element_type=jnp.float32
        )
        grad_wkey = jnp.einsum("rd,rq->dq", first_in, grad_key, preferred_element_type=jnp.float32)
        grad_wvalue = jnp.einsum(
            "rd,rq->dq", first_in, grad_value, preferred_element_type=jnp.float32
        )
        grad_first = (
            jnp.einsum("rq,dq->rd", grad_query, w_query, preferred_element_type=jnp.float32)
            + jnp.einsum("rq,dq->rd", grad_key, w_key, preferred_element_type=jnp.float32)
            + jnp.einsum("rq,dq->rd", grad_value, w_value, preferred_element_type=jnp.float32)
        )
        grad_gain_attn = jnp.sum(grad_first * normed_one, 0)
        grad_inputs = grad_middle + norm_back(grad_first * gain_attn, normed_one, inverse_one)
        input_grads.append(grad_inputs.astype(jnp.bfloat16).reshape(seq_count, span, width))
        grads = flatten_all(
            (
                grad_gain_attn,
                grad_wquery,
                grad_wkey,
                grad_wvalue,
                grad_wout,
                grad_gain_ffn,
                grad_wgate,
                grad_wup,
                grad_wdown,
            )
        )
        pieces = lax.psum_scatter(grads, ("fsdp", "ctx"), scatter_dimension=0, tiled=True)
        if index == 0:
            collected = pieces
        else:
            collected = tuple((a + b for a, b in zip(collected, pieces)))
    summed = jax.tree.map(
        lambda part: part.astype(jnp.float32), lax.psum(shortened(collected), "grp")
    )
    shaped = tuple((s.reshape(w.shape) for s, w in zip(summed, shards)))
    return (
        jnp.stack(outputs, 0),
        jnp.stack(input_grads, 0),
        shaped[0],
        shaped[1],
        shaped[2],
        shaped[3],
        shaped[4],
        shaped[5],
        shaped[6],
        shaped[7],
        shaped[8],
    )


BLOCK = 256
TO_LOG2 = math.log2(math.e) / math.sqrt(HEAD)
F32, BF16 = jnp.float32, jnp.bfloat16
NN = (((1,), (0,)), ((), ()))
NT = (((1,), (1,)), ((), ()))
TN = (((0,), (0,)), ((), ()))


def dot(a, b, dims=NN):
    return lax.dot_general(a, b, dims, preferred_element_type=F32)


def turned(rows, cosine, sine, sign):
    a, b = rows[: HEAD // 2], rows[HEAD // 2 :]
    return jnp.concatenate([a * cosine - sign * b * sine, b * cosine + sign * a * sine], 0)


def masked(scores, prefix, first, block):
    key = first + lax.broadcasted_iota(jnp.int32, scores.shape, 0)
    query = block * BLOCK + lax.broadcasted_iota(jnp.int32, scores.shape, 1)
    return jnp.where((key <= query) | (key < prefix), scores, -1e30)


def reach(block):
    return max(2, block + 1) * BLOCK


def scores_of(keys, query, prefix, block):
    clear = block * BLOCK
    edge = masked(dot(keys[clear:], query), prefix, clear, block)
    if not clear:
        return edge
    return jnp.concatenate([dot(keys[:clear], query), edge], 0)


MESH = pl.DeviceIdType.MESH
DMA = pltpu.SemaphoreType.DMA
ANY = pl.BlockSpec(memory_space=pl.ANY)
VMEM = pl.BlockSpec(memory_space=pltpu.VMEM)


def where_am_i():
    return lax.axis_index("grp"), lax.axis_index("fsdp"), lax.axis_index("ctx")


def remote(src, dst, send, recv, grp, fsdp, ctx):
    return pltpu.make_async_remote_copy(
        src_ref=src,
        dst_ref=dst,
        send_sem=send,
        recv_sem=recv,
        device_id={"grp": grp, "fsdp": fsdp, "ctx": ctx},
        device_id_type=MESH,
    )


def greet(partners):
    barrier = pltpu.get_barrier_semaphore()
    for grp, fsdp, ctx in partners:
        pl.semaphore_signal(
            barrier, inc=1, device_id={"grp": grp, "fsdp": fsdp, "ctx": ctx}, device_id_type=MESH
        )
    pl.semaphore_wait(barrier, len(partners))


class Columns:
    split = True

    def __init__(self, core, shard, out):
        self.core, self.shard, self.out = core, shard, out
        self.rows, self.cols = shard.shape[0], out.shape[1] // 4

    def mine(self, j, quarter):
        to = self.core if j == 0 else 1 - self.core
        return self.shard.at[:, pl.ds(pl.multiple_of((2 * quarter + to) * self.cols, 128), self.cols)]

    def block(self, plane, j, quarter):
        owner = self.core if j == 0 else 1 - self.core
        start = pl.multiple_of((2 * plane + owner) * self.rows, 16)
        return self.out.at[pl.ds(start, self.rows), pl.ds(pl.multiple_of(quarter * self.cols, 128), self.cols)]


class Rows:
    split = False

    def __init__(self, core, shard, out):
        self.core, self.shard, self.out = core, shard, out
        self.rows = out.shape[0] // 32

    def mine(self, j, quarter):
        return self.shard.at[pl.ds(pl.multiple_of((2 * quarter + j) * self.rows, 16), self.rows), :]

    def block(self, plane, j, quarter):
        start = pl.multiple_of((8 * plane + 2 * quarter + j) * self.rows, 16)
        return self.out.at[pl.ds(start, self.rows), :]

    def own(self, plane):
        return self.out.at[pl.ds(pl.multiple_of(plane * 8 * self.rows, 16), 8 * self.rows), :]


class Gather:
    @staticmethod
    def semaphores(count):
        return [DMA((count, 4)), DMA((count, 4)), DMA((count, 4))] + [DMA((count, 3, 2))] * 2 + [DMA((count, 3, 2, 2))] * 2 + [DMA((count, 3, 2))] * 2

    def __init__(self, units, sems):
        self.units, self.sems = units, sems
        self.grp, self.plane, self.core = where_am_i()
        self.side = self.grp + 1 - 2 * lax.rem(self.grp, 2)
        self.up = lax.rem(self.grp + 2, 4)
        self.planes = [lax.rem(self.plane + s, 4) for s in (1, 2, 3)]
        self.origins = [lax.rem(self.plane + 4 - s, 4) for s in (1, 2, 3)]
        self.left = []

    def partners(self):
        grp, plane, core = self.grp, self.plane, self.core
        found = [(grp, z, c) for z in self.planes for c in (core, 1 - core)]
        return found + [(grp, plane, 1 - core), (self.side, plane, core), (self.up, plane, core)]

    def other(self, j):
        return self.core if j == 0 else 1 - self.core

    def send(self, src, dst, send, recv, grp, plane, core):
        copy = remote(src, dst, send, recv, grp, plane, core)
        copy.start()
        self.left.append(copy.wait_send)

    def got(self, here, send, recv):
        remote(here, here, send, recv, self.side, self.plane, self.core).wait_recv()

    def first(self, n):
        u = self.units[n]
        loc, near_s, near_r, z_s, z_r = self.sems[:5]
        for i, z in enumerate(self.planes):
            for j in range(2):
                if u.split:
                    dst = u.block(self.plane, 0, self.grp)
                    self.send(u.mine(j, self.grp), dst, z_s.at[n, i, j], z_r.at[n, i, j], self.grp, z, self.other(j))
                else:
                    dst = u.block(self.plane, j, self.grp)
                    self.send(u.mine(j, self.grp), dst, z_s.at[n, i, j], z_r.at[n, i, j], self.grp, z, self.core)
        if u.split:
            for q in range(4):
                dst = u.block(self.plane, 0, q)
                self.send(u.mine(1, q), dst, near_s.at[n, q], near_r.at[n, q], self.grp, self.plane, 1 - self.core)
                copy = pltpu.make_async_copy(u.mine(0, q), dst, loc.at[n, q])
                copy.start()
                self.left.append(copy.wait)
        else:
            copy = pltpu.make_async_copy(u.shard, u.own(self.plane), loc.at[n, 0])
            copy.start()
            self.left.append(copy.wait)

    def first_in(self, n):
        u = self.units[n]
        for i, z in enumerate(self.origins):
            for j in range(2):
                self.got(u.block(z, j, self.grp), self.sems[3].at[n, i, j], self.sems[4].at[n, i, j])

    def near_in(self, n):
        u = self.units[n]
        if u.split:
            for q in range(4):
                self.got(u.block(self.plane, 1, q), self.sems[1].at[n, q], self.sems[2].at[n, q])

    def second(self, n, here=False):
        u = self.units[n]
        z_s, z_r, xy_s, xy_r = self.sems[3:7]
        for i, z in enumerate(self.origins):
            for j in range(2):
                block = u.block(z, j, self.grp)
                if not here:
                    self.got(block, z_s.at[n, i, j], z_r.at[n, i, j])
                for t, to in enumerate((self.side, self.up)):
                    self.send(block, block, xy_s.at[n, i, j, t], xy_r.at[n, i, j, t], to, self.plane, self.core)

    def third(self, n):
        u = self.units[n]
        xy_s, xy_r, fw_s, fw_r = self.sems[5:9]
        for i, z in enumerate(self.origins):
            for t, (origin, to) in enumerate(((self.side, self.up), (self.up, self.side))):
                block = u.block(z, t, origin)
                self.got(block, xy_s.at[n, i, t, t], xy_r.at[n, i, t, t])
                self.send(block, block, fw_s.at[n, i, t], fw_r.at[n, i, t], to, self.plane, self.core)

    def last(self, n):
        u = self.units[n]
        xy_s, xy_r, fw_s, fw_r = self.sems[5:9]
        for i, z in enumerate(self.origins):
            for t, origin in enumerate((self.side, self.up)):
                self.got(u.block(z, 1 - t, origin), xy_s.at[n, i, 1 - t, t], xy_r.at[n, i, 1 - t, t])
            for t in range(2):
                self.got(u.block(z, t, 3 - self.grp), fw_s.at[n, i, t], fw_r.at[n, i, t])

    def sent_all(self, firsts, rest):
        loc, near_s, near_r, z_s, z_r, xy_s, xy_r, fw_s, fw_r = self.sems

        def out(block, send, recv):
            remote(block, block, send, recv, self.side, self.plane, self.core).wait_send()

        for n in firsts:
            u = self.units[n]
            for i in range(3):
                for j in range(2):
                    out(u.block(self.plane, j, self.grp), z_s.at[n, i, j], z_r.at[n, i, j])
            if u.split:
                for q in range(4):
                    out(u.block(self.plane, 0, q), near_s.at[n, q], near_r.at[n, q])
                    pltpu.make_async_copy(u.mine(0, q), u.block(self.plane, 0, q), loc.at[n, q]).wait()
            else:
                pltpu.make_async_copy(u.shard, u.own(self.plane), loc.at[n, 0]).wait()
        for n in rest:
            u = self.units[n]
            for i, z in enumerate(self.origins):
                for j in range(2):
                    for t in range(2):
                        out(u.block(z, j, self.grp), xy_s.at[n, i, j, t], xy_r.at[n, i, j, t])
                for t, origin in enumerate((self.side, self.up)):
                    out(u.block(z, t, origin), fw_s.at[n, i, t], fw_r.at[n, i, t])

    def drain(self):
        for wait in self.left:
            wait()
        self.left = []


def upright(row_ref):
    return jnp.broadcast_to(row_ref[...].astype(F32), (8, row_ref.shape[1])).T[:, :1]


def start_kernel(heads, kv_heads, x_ref, dy_ref, wq_ref, wk_ref, wv_ref, wo_ref, gate_ref, ga_ref, gf_ref,
                 pack_out, gate_out, x_out, dy_out, pack, gate, trade_s, trade_r, own_s, *sems):
    _, _, core = where_am_i()
    q_cols, kv_cols, span = heads * HEAD, kv_heads * HEAD, x_ref.shape[1]
    cols = pack.shape[1] // 8
    gain = upright(ga_ref)
    for k in range(2):
        parts = [(wq_ref[:, k * q_cols : (k + 1) * q_cols].astype(F32) * gain).astype(BF16)]
        parts += [(w[:, k * kv_cols : (k + 1) * kv_cols].astype(F32) * gain).astype(BF16) for w in (wk_ref, wv_ref)]
        row = jnp.concatenate(parts + [wo_ref[:, k * q_cols : (k + 1) * q_cols]], 1)
        for q in range(4):
            pack[:, (2 * q + k) * cols : (2 * q + k + 1) * cols] = row[:, q * cols : (q + 1) * cols]
    gather = Gather([Columns(core, pack, pack_out), Columns(core, gate, gate_out)], sems)
    greet(gather.partners())
    gather.first(0)
    gate[...] = (gate_ref[...].astype(F32) * upright(gf_ref)).astype(BF16)
    waits = []

    def trade(ref, out, which):
        for s in range(ref.shape[0]):
            def rows(owner):
                return out.at[pl.ds(pl.multiple_of((2 * s + owner) * span, 16), span), :]
            copy = remote(ref.at[s], rows(core), trade_s.at[which, s], trade_r.at[which, s], gather.grp, gather.plane, 1 - core)
            copy.start()
            gather.left.append(copy.wait_send)
            copy = pltpu.make_async_copy(ref.at[s], rows(core), own_s.at[which, s])
            copy.start()
            gather.left.append(copy.wait)
            waits.append((rows(1 - core), trade_s.at[which, s], trade_r.at[which, s]))

    trade(x_ref, x_out, 0)
    gather.second(0)
    gather.first(1)
    trade(dy_ref, dy_out, 1)
    gather.third(0)
    gather.last(0)
    gather.near_in(0)
    gather.near_in(1)
    for wait in waits:
        gather.got(*wait)
    gather.first_in(1)
    gather.drain()


def start(x, dy, wq, wk, wv, wo, gate, gain_attn, gain_ffn, heads, kv_heads):
    count, span, width = x.shape
    shard, hidden = gate.shape
    cols = 2 * (heads + kv_heads) * HEAD
    shape = jax.ShapeDtypeStruct
    return pl.pallas_call(
        functools.partial(start_kernel, heads, kv_heads),
        grid=(1,),
        in_specs=[pl.BlockSpec(a.shape, lambda i, n=a.ndim: (0,) * n) for a in (x, dy, wq, wk, wv, wo, gate, gain_attn, gain_ffn)],
        out_specs=(ANY,) * 4,
        out_shape=(
            shape((8 * shard, cols), BF16),
            shape((8 * shard, hidden // 2), BF16),
            shape((2 * count * span, width), BF16),
            shape((2 * count * span, width), BF16),
        ),
        scratch_shapes=[pltpu.VMEM((shard, 2 * cols), BF16), pltpu.VMEM((shard, hidden), BF16)]
        + [DMA((2, count))] * 3
        + Gather.semaphores(2),
        compiler_params=pltpu.CompilerParams(collective_id=0, has_side_effects=True, vmem_limit_bytes=62 * 2**20),
        name="start",
    )(x, dy, wq, wk, wv, wo, gate, gain_attn, gain_ffn)


def front_kernel(heads, kv_heads, blocks, prefix_ref, x_ref, own_ref, w_ref, up_ref, gf_ref, cos_ref, sin_ref, gate_in, down_ref,
                 n_ref, qt_ref, kvt_ref, kv_ref, ot_ref, lse_ref, wo_ref, x1_ref, inv_ref, two_out, gate_out, up_out, down_out,
                 up_s, wo_send, wo_recv, part_mine, part_send, part_recv, two_mine,
                 wo_sem, part_sem, two_sem, own_sem, *sems):
    step = pl.program_id(0)
    grp, plane, core = where_am_i()
    count = prefix_ref.shape[0]
    tiles = count * blocks
    groups = heads // kv_heads
    q_cols, kv_cols = heads * HEAD, kv_heads * HEAD
    width = x_ref.shape[1]
    half = blocks // 2
    gather = Gather([Columns(core, up_s, gate_out), Columns(core, up_s, up_out), Rows(core, down_ref, down_out)], sems)

    def at(when):
        return pl.when(step == when)

    def out_weight(owner):
        return w_ref[pl.ds(pl.multiple_of(owner * q_cols, 16), q_cols), q_cols + 2 * kv_cols :]

    def wo_copy():
        return remote(wo_send, wo_recv, wo_sem.at[0], wo_sem.at[1], grp, plane, 1 - core)

    @at(0)
    def _():
        greet(gather.partners())
        gather.second(0, here=True)
        wo_send[...] = out_weight(1 - core)
        wo_copy().start()
        up_s[...] = (up_ref[...].astype(F32) * upright(gf_ref)).astype(BF16)
        gather.first(1)

    @at(tiles - 1)
    def _():
        wo_copy().wait()
        mine, other = out_weight(core), wo_recv[...]
        wo_ref[...] = jnp.concatenate([jnp.where(core == 0, mine, other), jnp.where(core == 0, other, mine)], 1)

    @at(tiles)
    def _():
        gather.first(2)
        gather.third(0)

    @at(tiles + 1)
    def _():
        gather.second(1)

    @at(tiles + 4)
    def _():
        gather.third(1)

    @at(tiles + 5)
    def _():
        gather.second(2)

    @pl.when(step < tiles)
    def _():
        x = x_ref[...].astype(F32)
        normed = (x * lax.rsqrt(jnp.mean(x * x, -1, keepdims=True) + epsilon)).astype(BF16)
        n_ref[...] = normed
        flat = dot(normed, w_ref[:, : q_cols + 2 * kv_cols])
        across = flat.T
        tokens = pl.ds(pl.multiple_of(step * BLOCK, BLOCK), BLOCK)
        here = pl.ds(pl.multiple_of(lax.rem(step, blocks) * BLOCK, BLOCK), BLOCK)
        cosine, sine = cos_ref[:, here], sin_ref[:, here]
        for h in range(heads):
            rows = turned(across[h * HEAD : (h + 1) * HEAD], cosine, sine, 1.0)
            qt_ref[h * HEAD : (h + 1) * HEAD, tokens] = (rows * TO_LOG2).astype(BF16)
        keys = [across[q_cols + h * HEAD : q_cols + (h + 1) * HEAD] for h in range(kv_heads)]
        keys = jnp.concatenate([turned(rows, cosine, sine, 1.0) for rows in keys], 0)
        kvt_ref[:kv_cols, tokens] = keys.astype(BF16)
        kvt_ref[kv_cols:, tokens] = across[q_cols + kv_cols :].astype(BF16)
        kv_ref[tokens, :kv_cols] = keys.T.astype(BF16)
        kv_ref[tokens, kv_cols:] = flat[:, q_cols + kv_cols :].astype(BF16)

    def rows_of(tile, owner):
        start = (tile // half) * blocks + owner * half + lax.rem(tile, half)
        return two_out.at[pl.ds(pl.multiple_of(start * BLOCK, BLOCK), BLOCK), :]

    def part_copy(slot):
        return remote(part_send.at[slot], part_recv.at[slot], part_sem.at[0, slot], part_sem.at[1, slot], grp, plane, 1 - core)

    def two_copy(slot):
        there = rows_of(slot, core)
        return remote(two_mine.at[slot], there, two_sem.at[0, slot], two_sem.at[1, slot], grp, plane, 1 - core)

    def two_keep(slot):
        return pltpu.make_async_copy(two_mine.at[slot], rows_of(slot, core), own_sem.at[slot])

    def finish(turn):
        block, s = lax.rem(turn, blocks), turn // blocks
        slot = s * half + lax.rem(block, half)

        @pl.when(block // half == core)
        def _():
            part_copy(slot).wait_recv()
            rows = pl.ds(pl.multiple_of(slot * BLOCK, BLOCK), BLOCK)
            middle = own_ref[rows, :].astype(F32) + part_mine[slot].astype(F32) + part_recv[slot].astype(F32)
            x1_ref[rows, :] = middle
            inverse = lax.rsqrt(jnp.mean(middle * middle, -1, keepdims=True) + epsilon)
            inv_ref[rows, :] = inverse
            two_mine[slot] = (middle * inverse).astype(BF16)
            two_copy(slot).start()
            two_keep(slot).start()

    def run(block):
        n = reach(block)
        turn = step - tiles
        s = turn // blocks
        prefix = prefix_ref[s]
        base = pl.multiple_of(s * blocks * BLOCK, BLOCK)
        tokens = pl.ds(pl.multiple_of(turn * BLOCK, BLOCK), BLOCK)

        def score(h):
            kh = h // groups
            keys = kv_ref[pl.ds(base, n), kh * HEAD : (kh + 1) * HEAD]
            return scores_of(keys, qt_ref[h * HEAD : (h + 1) * HEAD, tokens], prefix, block)

        def mix(h, weights, total):
            kh = h // groups
            vt = kvt_ref[kv_cols + kh * HEAD : kv_cols + (kh + 1) * HEAD, pl.ds(base, n)]
            ot_ref[h * HEAD : (h + 1) * HEAD, tokens] = (dot(vt, weights) / total).astype(BF16)

        later, held = score(0), None
        for h in range(heads):
            scores = later
            if h + 1 < heads:
                later = score(h + 1)
            peak = jnp.max(scores, 0, keepdims=True)
            weights = jnp.exp2(scores - peak)
            total = jnp.sum(weights, 0, keepdims=True)
            lse_ref[h : h + 1, tokens] = peak + jnp.log2(total)
            if held:
                mix(*held)
            held = (h, weights.astype(BF16), total)
        mix(*held)
        part = dot(ot_ref[:, tokens], wo_ref[...], TN).astype(BF16)
        slot = s * half + block % half

        @pl.when(core == block // half)
        def _():
            part_mine[slot] = part

        @pl.when(core != block // half)
        def _():
            part_send[slot] = part
            part_copy(slot).start()

    @pl.when(step > tiles)
    def _():
        finish(step - tiles - 1)

    for block in range(blocks):
        pl.when((step >= tiles) & (lax.rem(step, blocks) == block))(functools.partial(run, block))

    @at(2 * tiles - 1)
    def _():
        gather.third(2)
        finish(step - tiles)
        for n in range(3):
            gather.last(n)
        gather.near_in(1)
        for slot in range(count * half):
            part_copy(slot).wait_send()
            two_copy(slot).wait_send()
            two_keep(slot).wait()
            there = rows_of(slot, 1 - core)
            remote(there, there, two_sem.at[0, slot], two_sem.at[1, slot], grp, plane, 1 - core).wait_recv()
        gather.sent_all((1, 2), (0, 1, 2))


def front(prefix, x, own, pack, gate_part, up, down, gain_ffn, cosine, sine, heads, kv_heads, length):
    tokens, width = x.shape
    count, blocks = tokens // length, length // BLOCK
    tiles = tokens // BLOCK
    slots = tiles // 2
    q_cols, kv_cols = heads * HEAD, kv_heads * HEAD
    shape = jax.ShapeDtypeStruct
    once = pl.Buffered(1)

    def fixed(*dims):
        return pl.BlockSpec(dims, lambda i: (0,) * len(dims), pipeline_mode=once)

    tile = pl.BlockSpec((BLOCK, width), lambda i: (jnp.minimum(i, tiles - 1), 0))
    return pl.pallas_call(
        functools.partial(front_kernel, heads, kv_heads, blocks),
        grid=(2 * tiles,),
        in_specs=[
            pl.BlockSpec(memory_space=pltpu.SMEM),
            tile,
            fixed(tokens // 2, width),
            fixed(*pack.shape),
            fixed(*up.shape),
            fixed(*gain_ffn.shape),
            fixed(*cosine.shape),
            fixed(*sine.shape),
            ANY,
            fixed(*down.shape),
        ],
        out_specs=(
            tile,
            fixed(q_cols, tokens),
            fixed(2 * kv_cols, tokens),
            fixed(tokens, 2 * kv_cols),
            fixed(q_cols, tokens),
            fixed(heads, tokens),
            fixed(q_cols, width),
            fixed(tokens // 2, width),
            fixed(tokens // 2, 1),
            ANY, ANY, ANY, ANY,
        ),
        out_shape=(
            shape((tokens, width), BF16),
            shape((q_cols, tokens), BF16),
            shape((2 * kv_cols, tokens), BF16),
            shape((tokens, 2 * kv_cols), BF16),
            shape((q_cols, tokens), BF16),
            shape((heads, tokens), F32),
            shape((q_cols, width), BF16),
            shape((tokens // 2, width), F32),
            shape((tokens // 2, 1), F32),
            shape((tokens, width), BF16),
            shape(gate_part.shape, BF16),
            shape(gate_part.shape, BF16),
            shape((4 * down.shape[0], width), BF16),
        ),
        input_output_aliases={8: 10},
        scratch_shapes=[
            pltpu.VMEM(up.shape, BF16),
            pltpu.VMEM((q_cols, q_cols), BF16),
            pltpu.VMEM((q_cols, q_cols), BF16),
        ]
        + [pltpu.VMEM((slots, BLOCK, width), BF16)] * 4
        + [DMA((2,)), DMA((2, slots)), DMA((2, slots)), DMA((slots,))]
        + Gather.semaphores(3),
        compiler_params=pltpu.CompilerParams(collective_id=1, has_side_effects=True, vmem_limit_bytes=60 * 2**20),
        cost_estimate=pl.CostEstimate(flops=2 * tokens * width * 1536, bytes_accessed=16 * tokens * width, transcendentals=0),
        name="front",
    )(prefix, x, own, pack, up, gain_ffn, cosine, sine, gate_part, down)


def feed_kernel(half, core_ref, n_ref, gate_ref, up_ref, down_ref, hidden_ref, by_up_ref, by_gate_ref, mine_ref, theirs_ref):
    n = n_ref[...]
    gate = dot(n, gate_ref[...])
    upward = dot(n, up_ref[...])
    sigma = 1.0 / (1.0 + jnp.exp(-gate))
    silu = gate * sigma
    hidden = (silu * upward).astype(BF16)
    hidden_ref[...] = hidden
    by_up_ref[...] = silu.astype(BF16)
    by_gate_ref[...] = (upward * sigma * (1.0 + gate - silu)).astype(BF16)
    part = dot(hidden, down_ref[...]).astype(BF16)
    own = lax.rem(pl.program_id(0) // half, 2) == core_ref[0]

    @pl.when(own)
    def _():
        mine_ref[...] = part

    @pl.when(jnp.logical_not(own))
    def _():
        theirs_ref[...] = part


def feed(core, n, gate, up, down, length):
    tokens, width = n.shape
    units = gate.shape[1]
    shape = jax.ShapeDtypeStruct
    once = pl.Buffered(1)
    half = length // BLOCK // 2
    tile = lambda cols: pl.BlockSpec((BLOCK, cols), lambda i, core: (i, 0))
    fixed = lambda a: pl.BlockSpec(a.shape, lambda i, core: (0, 0), pipeline_mode=once)

    def slot(i, owner):
        whole, rest = i // (2 * half), lax.rem(i, 2 * half)
        return whole * half + jnp.clip(rest - owner * half, 0, half - 1)

    mine = pl.BlockSpec((BLOCK, width), lambda i, core: (slot(i, core[0]), 0))
    theirs = pl.BlockSpec((BLOCK, width), lambda i, core: (slot(i, 1 - core[0]), 0))
    return pl.pallas_call(
        functools.partial(feed_kernel, half),
        grid_spec=pltpu.PrefetchScalarGridSpec(
            num_scalar_prefetch=1,
            grid=(tokens // BLOCK,),
            in_specs=[tile(width), fixed(gate), fixed(up), fixed(down)],
            out_specs=(tile(units), tile(units), tile(units), mine, theirs),
        ),
        out_shape=(shape((tokens, units), BF16),) * 3 + (shape((tokens // 2, width), BF16),) * 2,
        compiler_params=pltpu.CompilerParams(vmem_limit_bytes=62 * 2**20),
        cost_estimate=pl.CostEstimate(flops=6 * tokens * width * units, bytes_accessed=2 * tokens * (3 * units + 2 * width), transcendentals=tokens * units),
        name="feed",
    )(core, n, gate, up, down)


def finish_kernel(heads, kv_heads, pack_ref, gate_ref, up_ref, down_ref, wq_ref, wk_ref, wv_ref, wg_ref, wu_ref, ga_ref, gf_ref,
                  q_out, k_out, v_out, o_out, gate_out, up_out, down_out, ga_out, gf_out):
    q_cols, kv_cols = heads * HEAD, kv_heads * HEAD
    cols = pack_ref.shape[1] // 8
    gain = upright(ga_ref)
    total = jnp.zeros(gain.shape, F32)
    for k in range(2):
        row = jnp.concatenate([pack_ref[:, (2 * q + k) * cols : (2 * q + k + 1) * cols].astype(F32) for q in range(4)], 1)
        at = 0
        for w, out, size in ((wq_ref, q_out, q_cols), (wk_ref, k_out, kv_cols), (wv_ref, v_out, kv_cols)):
            part, here = row[:, at : at + size], slice(k * size, (k + 1) * size)
            total += jnp.sum(part * w[:, here].astype(F32), -1, keepdims=True)
            out[:, here] = part * gain
            at += size
        o_out[:, k * q_cols : (k + 1) * q_cols] = row[:, at:]
    ga_out[...] = jnp.broadcast_to(total, (total.shape[0], 8)).T[:1]
    gain = upright(gf_ref)
    total = jnp.zeros(gain.shape, F32)
    for ref, w, out in ((gate_ref, wg_ref, gate_out), (up_ref, wu_ref, up_out)):
        part = ref[...].astype(F32)
        total += jnp.sum(part * w[...].astype(F32), -1, keepdims=True)
        out[...] = part * gain
    gf_out[...] = jnp.broadcast_to(total, (total.shape[0], 8)).T[:1]
    down_out[...] = down_ref[...].astype(F32)


def finish(pack, gate, up, down, wq, wk, wv, wo, wg, wu, ga, gf, heads, kv_heads):
    shape = lambda a: jax.ShapeDtypeStruct(a.shape, F32)
    whole = lambda a: pl.BlockSpec(a.shape, lambda i: (0, 0))
    outs = (shape(wq), shape(wk), shape(wv), shape(wo), shape(wg), shape(wu), shape(down), shape(ga), shape(gf))
    return pl.pallas_call(
        functools.partial(finish_kernel, heads, kv_heads),
        grid=(1,),
        in_specs=[whole(a) for a in (pack, gate, up, down, wq, wk, wv, wg, wu, ga, gf)],
        out_specs=tuple(whole(a) for a in outs),
        out_shape=outs,
        compiler_params=pltpu.CompilerParams(vmem_limit_bytes=62 * 2**20),
        name="finish",
    )(pack, gate, up, down, wq, wk, wv, wg, wu, ga, gf)


def halves_of(rows, cols, split):
    return (rows // 8, cols // 4) if split else (rows // 32, cols)


class Summand:
    def __init__(self, core, ref, out, split, near=False):
        self.core, self.ref, self.out, self.split, self.near = core, ref, out, split, near
        self.rows, self.cols = halves_of(*ref.shape, split)

    def half(self, plane, quarter, path):
        if self.split:
            start = pl.multiple_of((2 * plane + path) * self.rows, 16)
            return self.ref.at[pl.ds(start, self.rows), pl.ds(pl.multiple_of(quarter * self.cols, 128), self.cols)]
        start = pl.multiple_of(((4 * plane + quarter) * 2 + path) * self.rows, 16)
        return self.ref.at[pl.ds(start, self.rows), :]

    def place(self, quarter, j, other):
        if self.split:
            return self.out.at[:, pl.ds(pl.multiple_of((2 * quarter + other) * self.cols, 128), self.cols)]
        return self.out.at[pl.ds(pl.multiple_of((2 * quarter + j) * self.rows, 16), self.rows), :]


class Reduce:
    @staticmethod
    def buffers(halves, near=(), begun=(), left=()):
        found = []
        for n, h in enumerate(halves):
            no_first, no_third = n in begun, n in left
            for lead, unused in (
                ((2, 4, 2), no_first or n in near),
                ((2, 4, 2), no_first),
                ((2, 4), no_first),
                ((3, 2), no_third),
                ((4, 2), False),
            ):
                found.append(pltpu.VMEM((1,) * len(lead) + (16, 128) if unused else lead + h, BF16))
        return found

    @staticmethod
    def semaphores(n):
        return [DMA((n, 2, 4, 2))] * 3 + [DMA((n, 2, 4))] * 2 + [DMA((n, 3))] * 2 + [DMA((n, 4, 2))] * 2

    def __init__(self, units, buffers, sems):
        self.units, self.sems = units, sems
        self.bufs = [buffers[5 * n : 5 * n + 5] for n in range(len(units))]
        self.grp, self.plane, self.core = where_am_i()
        gx, gy = lax.rem(self.grp, 2), self.grp // 2
        self.gx, self.gy = gx, gy
        side, up = self.grp + 1 - 2 * gx, lax.rem(self.grp + 2, 4)
        self.first_to, self.second_to, self.keep = (side, up), (up, side), (gy, gx)
        self.planes = [lax.rem(self.plane + s, 4) for s in (1, 2, 3)]
        self.origins = [lax.rem(self.plane + 4 - s, 4) for s in (1, 2, 3)]
        self.others = [lax.rem(self.grp + s, 4) for s in (1, 2, 3)]
        self.sources = [lax.rem(self.grp + 4 - s, 4) for s in (1, 2, 3)]

    def partners(self):
        grp, plane, core = self.grp, self.plane, self.core
        found = [(grp, z, core) for z in self.planes] + [(grp, plane, 1 - core)]
        return found + [(g, plane, c) for g in self.others for c in (core, 1 - core)]

    def quarter(self, path, i, own):
        if path == 0:
            return 2 * i + (self.gx if own else 1 - self.gx)
        return 2 * (self.gy if own else 1 - self.gy) + i

    def first_copy(self, n, path, z, i):
        _, s1, r1 = self.sems[:3]
        src = self.units[n].half(z, self.quarter(path, i, False), path)
        dst = self.bufs[n][1].at[path, z, i]
        return remote(src, dst, s1.at[n, path, z, i], r1.at[n, path, z, i], self.first_to[path], self.plane, self.core)

    def load_copy(self, n, path, z, i):
        src = self.units[n].half(z, self.quarter(path, i, True), path)
        return pltpu.make_async_copy(src, self.bufs[n][0].at[path, z, i], self.sems[0].at[n, path, z, i])

    def second_copy(self, n, path, z):
        _, got, second = self.bufs[n][:3]
        s2, r2 = self.sems[3:5]
        src = got.at[path, z, 1 - self.keep[path]]
        return remote(src, second.at[path, z], s2.at[n, path, z], r2.at[n, path, z], self.second_to[path], self.plane, self.core)

    def third_copy(self, n, i):
        third, fin = self.bufs[n][3:]
        s3, r3 = self.sems[5:7]
        return remote(fin.at[self.planes[i]], third.at[i], s3.at[n, i], r3.at[n, i], self.grp, self.planes[i], self.core)

    def fourth_copy(self, n, i, j, coming=False):
        u, fin = self.units[n], self.bufs[n][4]
        s4, r4 = self.sems[7:9]
        other = (self.core if j == 0 else 1 - self.core) if u.split else self.core
        grp = self.grp if i == 3 else (self.sources if coming else self.others)[i]
        if coming:
            src = dst = u.place(grp, j, other)
        else:
            src = fin.at[self.plane, other if u.split else j]
            dst = u.place(self.grp, j, self.core)
        if i == 3 and not (u.split and j == 1):
            return pltpu.make_async_copy(src, dst, s4.at[n, 3, j])
        return remote(src, dst, s4.at[n, i, j], r4.at[n, i, j], grp, self.plane, other)

    @staticmethod
    def each():
        return [(path, z, i) for z in range(4) for path in range(2) for i in range(2)]

    def a(self, n):
        for path, z, i in self.each():
            self.first_copy(n, path, z, i).start()
            if not self.units[n].near:
                self.load_copy(n, path, z, i).start()

    def b(self, n):
        u, (acc, got) = self.units[n], self.bufs[n][:2]
        for z in range(4):
            for path in range(2):
                for i in range(2):
                    self.first_copy(n, path, z, i).wait_recv()
                    if u.near:
                        own = u.half(z, self.quarter(path, i, True), path)[...]
                    else:
                        self.load_copy(n, path, z, i).wait()
                        own = acc[path, z, i]
                    got[path, z, i] = (own.astype(F32) + got[path, z, i].astype(F32)).astype(BF16)
                self.second_copy(n, path, z).start()

    def c(self, n, send=True):
        _, got, second, _, fin = self.bufs[n]
        for z in range(4):
            for path in range(2):
                self.second_copy(n, path, z).wait_recv()
                fin[z, path] = (got[path, z, self.keep[path]].astype(F32) + second[path, z].astype(F32)).astype(BF16)
            if send:
                self.third_to(n, z)

    def third_to(self, n, z):
        third, fin = self.bufs[n][3:]
        s3, r3 = self.sems[5:7]
        i = lax.rem(z + 7 - self.plane, 4)

        @pl.when(i != 3)
        def _():
            remote(fin.at[z], third.at[i], s3.at[n, i], r3.at[n, i], self.grp, z, self.core).start()

    def c2(self, n):
        for i in range(3):
            self.third_copy(n, i).start()

    def d(self, n):
        third, fin = self.bufs[n][3:]
        for i in range(3):
            self.third_copy(n, i).wait_recv()
        for j in range(2):
            total = fin[self.plane, j].astype(F32)
            for i in range(3):
                total += third[i, j].astype(F32)
            fin[self.plane, j] = total.astype(BF16)
        for j in range(2):
            for i in range(4):
                self.fourth_copy(n, i, j).start()

    def e1(self, n):
        for path, z, i in self.each():
            self.first_copy(n, path, z, i).wait_send()
        for z in range(4):
            for path in range(2):
                self.second_copy(n, path, z).wait_send()

    def e2(self, n):
        u = self.units[n]
        for i in range(3):
            self.third_copy(n, i).wait_send()
        for j in range(2):
            for i in range(4):
                if i == 3 and not (u.split and j == 1):
                    self.fourth_copy(n, i, j).wait()
                else:
                    self.fourth_copy(n, i, j).wait_send()
                    self.fourth_copy(n, i, j, coming=True).wait_recv()


class Trade:
    @staticmethod
    def buffers(slots, width):
        return [pltpu.VMEM((slots, BLOCK, width), BF16)] * 3

    @staticmethod
    def semaphores(slots):
        return [DMA((2, slots))]

    def __init__(self, bufs, sems, blocks):
        self.mine, self.out, self.come = bufs
        self.sem, self.half, self.blocks = sems[0], blocks // 2, blocks
        self.slots = self.mine.shape[0]
        self.grp, self.plane, self.core = where_am_i()

    def copy(self, slot):
        return remote(self.out.at[slot], self.come.at[slot], self.sem.at[0, slot], self.sem.at[1, slot], self.grp, self.plane, 1 - self.core)

    def where(self, turn):
        block = lax.rem(turn, self.blocks)
        return block // self.half, (turn // self.blocks) * self.half + lax.rem(block, self.half)

    def give(self, turn, part):
        owner, slot = self.where(turn)

        @pl.when(self.core == owner)
        def _():
            self.mine[slot] = part

        @pl.when(self.core != owner)
        def _():
            self.out[slot] = part
            self.copy(slot).start()

    def take(self, turn, close):
        owner, slot = self.where(turn)

        @pl.when(self.core == owner)
        def _():
            self.copy(slot).wait_recv()
            close(slot, self.mine[slot].astype(F32) + self.come[slot].astype(F32))

    def drain(self):
        for slot in range(self.slots):
            self.copy(slot).wait_send()

    def place(self, slot, owner):
        start = (slot // self.half) * self.blocks + owner * self.half + lax.rem(slot, self.half)
        return pl.ds(pl.multiple_of(start * BLOCK, BLOCK), BLOCK)

    def rows(self, ref, slot, owner):
        return ref.at[self.place(slot, owner), :]

    def columns(self, ref, slot, owner):
        return ref.at[:, self.place(slot, owner)]


WIDE = 2 * BLOCK


def feed_back_kernel(blocks, dy_ref, n_ref, gate_ref, up_ref, down_ref, inv_ref, by_up_ref, by_gate_ref, grad_ref,
                     g_gate_ref, g_up_ref, dx_out, r_down_out, begun_ref,
                     turned_n, d_gate, d_up, dx_mine, by_sem, dx_sem, keep_sem, *rest):
    step = pl.program_id(0)
    tiles = turned_n.shape[1] // BLOCK
    cuts = d_gate.shape[1] // WIDE
    second = tiles + 2 * cuts
    last = second + tiles - 1
    trade = Trade(rest[:3], rest[3:4], blocks)
    grp, plane, core = where_am_i()
    units = [Summand(core, grad_ref, r_down_out, False), Summand(core, g_gate_ref, None, True, near=True)]
    reduce = Reduce(units, list(rest[4:13]) + [begun_ref], rest[14:])

    def at(when):
        return pl.when(step == when)

    def tile_rows(tile):
        return pl.ds(pl.multiple_of(tile * BLOCK, BLOCK), BLOCK)

    def by_copies(tile):
        rows = tile_rows(tile)
        return [pltpu.make_async_copy(ref.at[rows, :], to.at[rows, :], by_sem.at[k, tile]) for k, (ref, to) in enumerate(((by_up_ref, d_up), (by_gate_ref, d_gate)))]

    @at(0)
    def _():
        for tile in range(tiles):
            for copy in by_copies(tile):
                copy.start()
        greet(reduce.partners())
        reduce.a(0)

    @at(tiles + 1)
    def _():
        reduce.b(0)

    @at(tiles + cuts)
    def _():
        reduce.a(1)

    @at(tiles + cuts + 1)
    def _():
        reduce.c(0)

    @at(second + 4)
    def _():
        reduce.b(1)
        reduce.d(0)

    @pl.when(step < tiles)
    def _():
        rows = tile_rows(step)
        dy = dy_ref[...]
        grad = dot(dy, down_ref[...], NT)
        for copy in by_copies(step):
            copy.wait()
        d_up[rows, :] = (grad * d_up[rows, :].astype(F32)).astype(BF16)
        d_gate[rows, :] = (grad * d_gate[rows, :].astype(F32)).astype(BF16)
        turned_n[:, rows] = n_ref[...].T
        owner, slot = trade.where(step)

        @pl.when(owner == core)
        def _():
            dx_mine[slot] = dy

    @pl.when((step >= tiles) & (step < tiles + cuts))
    def _():
        cols = pl.ds(pl.multiple_of((step - tiles) * WIDE, WIDE), WIDE)
        g_gate_ref[:, cols] = dot(turned_n[...], d_gate[:, cols]).astype(BF16)

    @pl.when((step >= tiles + cuts) & (step < second))
    def _():
        cols = pl.ds(pl.multiple_of((step - tiles - cuts) * WIDE, WIDE), WIDE)
        g_up_ref[...] = dot(turned_n[...], d_up[:, cols]).astype(BF16)

    def there(slot, owner):
        return trade.rows(dx_out, slot, owner)

    def dx_copy(slot):
        return remote(dx_mine.at[slot], there(slot, core), dx_sem.at[0, slot], dx_sem.at[1, slot], grp, plane, 1 - core)

    def dx_keep(slot):
        return pltpu.make_async_copy(dx_mine.at[slot], there(slot, core), keep_sem.at[slot])

    def close(slot, grad):
        rows = pl.ds(pl.multiple_of(slot * BLOCK, BLOCK), BLOCK)
        normed = trade.columns(turned_n, slot, core)[...].T.astype(F32)
        back = grad - normed * jnp.mean(grad * normed, -1, keepdims=True)
        dx_mine[slot] = (dx_mine[slot].astype(F32) + inv_ref[rows, :] * back).astype(BF16)
        dx_copy(slot).start()
        dx_keep(slot).start()

    @pl.when(step > second)
    def _():
        trade.take(step - second - 1, close)

    @pl.when(step >= second)
    def _():
        turn = step - second
        rows = tile_rows(turn)
        part = dot(d_gate[rows, :], gate_ref[...], NT) + dot(d_up[rows, :], up_ref[...], NT)
        trade.give(turn, part.astype(BF16))

    @at(last)
    def _():
        trade.take(tiles - 1, close)
        reduce.c(1, send=False)
        reduce.e1(0)
        reduce.e2(0)
        reduce.e1(1)
        trade.drain()
        for slot in range(trade.slots):
            dx_copy(slot).wait_send()
            dx_keep(slot).wait()
            here = there(slot, 1 - core)
            remote(here, here, dx_sem.at[0, slot], dx_sem.at[1, slot], grp, plane, 1 - core).wait_recv()


def feed_back(dy, by_up, by_gate, n, gate, up, down, inverse, grad_down, length):
    tokens, width = dy.shape
    units = gate.shape[1]
    blocks, tiles, cuts = length // BLOCK, tokens // BLOCK, units // WIDE
    slots = tiles // 2
    shape = jax.ShapeDtypeStruct
    once = pl.Buffered(1)
    early = lambda cols: pl.BlockSpec((BLOCK, cols), lambda i: (jnp.minimum(i, tiles - 1), 0))
    fixed = lambda a: pl.BlockSpec(a.shape, lambda i: (0,) * len(a.shape), pipeline_mode=once)
    cut = pl.BlockSpec((width, WIDE), lambda i: (0, jnp.clip(i - tiles - cuts, 0, cuts - 1)))
    g_gate = shape((width, units), BF16)
    halves = [halves_of(*grad_down.shape, False), halves_of(width, units, True)]
    begun = shape((4, 2) + halves[1], BF16)
    return pl.pallas_call(
        functools.partial(feed_back_kernel, blocks),
        grid=(2 * tiles + 2 * cuts,),
        in_specs=[early(width), early(width)] + [fixed(a) for a in (gate, up, down, inverse)] + [ANY] * 3,
        out_specs=(fixed(g_gate), cut, ANY, ANY, fixed(begun)),
        out_shape=(
            g_gate,
            g_gate,
            shape((tokens, width), BF16),
            shape((grad_down.shape[0] // 4, width), BF16),
            begun,
        ),
        scratch_shapes=[
            pltpu.VMEM((width, tokens), BF16),
            pltpu.VMEM((tokens, units), BF16),
            pltpu.VMEM((tokens, units), BF16),
            pltpu.VMEM((slots, BLOCK, width), BF16),
            DMA((2, tiles)),
            DMA((2, slots)),
            DMA((slots,)),
        ]
        + Trade.buffers(slots, width)
        + Trade.semaphores(slots)
        + Reduce.buffers(halves, near=(1,), left=(1,))
        + Reduce.semaphores(2),
        compiler_params=pltpu.CompilerParams(collective_id=3, has_side_effects=True, vmem_limit_bytes=62 * 2**20),
        name="feed_back",
    )(dy, n, gate, up, down, inverse, by_up, by_gate, grad_down)


def back_kernel(heads, kv_heads, blocks, prefix_ref, qt_ref, kv_ref, kt_ref, lse_ref, ot_ref, dx_ref, n_ref, own_ref, wo_ref, w_ref,
                cos_ref, sin_ref, begun_ref, g_up_ref,
                grad_out, r_pack_out, r_gate_out, r_up_out,
                dot_ref, dk_ref, dv_ref, dt, g_pack, g_wo, wo_send, wo_come, wo_sem, *rest):
    step = pl.program_id(0)
    grp, plane, core = where_am_i()
    tokens, width = dx_ref.shape
    tiles, half, length = tokens // BLOCK, blocks // 2, blocks * BLOCK
    groups = heads // kv_heads
    q_cols, kv_cols = heads * HEAD, kv_heads * HEAD
    qkv = q_cols + 2 * kv_cols
    thirds = 3
    cut = width // thirds
    trade = Trade(rest[:3], rest[3:4], blocks)
    units = [Summand(core, g_up_ref, r_gate_out, True), Summand(core, g_up_ref, r_up_out, True), Summand(core, g_pack, r_pack_out, True, near=True)]
    reduce = Reduce(units, list(rest[4:8]) + [begun_ref] + list(rest[9:19]), rest[19:])
    turn = lax.rem(step, blocks)

    def at(when):
        return pl.when(step == when)

    def wo_copy():
        return remote(wo_send, wo_come, wo_sem.at[0], wo_sem.at[1], grp, plane, 1 - core)

    @at(0)
    def _():
        greet(reduce.partners())
        reduce.a(1)
        reduce.c2(0)

    for j in range(thirds):
        @at(1 + j)
        def _(j=j):
            g_wo[:, j * cut : (j + 1) * cut] = dot(ot_ref[...], dx_ref[:, j * cut : (j + 1) * cut]).astype(BF16)

    @at(1 + thirds)
    def _():
        low, high = g_wo[:, :q_cols], g_wo[:, q_cols:]
        wo_send[...] = jnp.where(core == 0, high, low)
        wo_copy().start()
        g_pack[pl.ds(pl.multiple_of(core * q_cols, 16), q_cols), qkv:] = jnp.where(core == 0, low, high)

    @at(5)
    def _():
        reduce.b(1)
        reduce.d(0)

    @at(tiles - 1)
    def _():
        reduce.c(1)

    @at(tiles + thirds)
    def _():
        wo_copy().wait()
        g_pack[pl.ds(pl.multiple_of((1 - core) * q_cols, 16), q_cols), qkv:] = wo_come[...]
        reduce.a(2)

    @pl.when((step < tiles) & (turn == 0))
    def _():
        dk_ref[...] = jnp.zeros_like(dk_ref)
        dv_ref[...] = jnp.zeros_like(dv_ref)

    @pl.when(step < tiles)
    def _():
        rows = pl.ds(pl.multiple_of(step * BLOCK, BLOCK), BLOCK)
        dot_ref[...] = dot(wo_ref[...], dx_ref[rows, :], NT).astype(BF16)

    def run(block):
        n = reach(block)
        prefix = prefix_ref[step // blocks]
        tokens_here = pl.ds(pl.multiple_of(step * BLOCK, BLOCK), BLOCK)
        here = pl.ds(block * BLOCK, BLOCK)
        cosine, sine = cos_ref[:, here], sin_ref[:, here]

        def score(h):
            kh = h // groups
            own = slice(h * HEAD, (h + 1) * HEAD)
            keys = kv_ref[:n, kh * HEAD : (kh + 1) * HEAD]
            values = kv_ref[:n, kv_cols + kh * HEAD : kv_cols + (kh + 1) * HEAD]
            return scores_of(keys, qt_ref[own, :], prefix, block), dot(values, dot_ref[own, :])

        later = score(0)
        for h in range(heads):
            kh = h // groups
            own = slice(h * HEAD, (h + 1) * HEAD)
            kt = kt_ref[kh * HEAD : (kh + 1) * HEAD, :n]
            query, grad = qt_ref[own, :], dot_ref[own, :]
            delta = jnp.sum(grad.astype(F32) * ot_ref[own, tokens_here].astype(F32), 0, keepdims=True)
            scores, grad_probs = later
            if h + 1 < heads:
                later = score(h + 1)
            probs = jnp.exp2(scores - lse_ref[h : h + 1, :])
            grad_scores = (probs * (grad_probs - delta)).astype(BF16)
            dv_ref[kh, :, :n] += dot(grad, probs.astype(BF16), NT)
            dk_ref[kh, :, :n] += dot(query, grad_scores, NT)
            grad_query = turned(dot(kt, grad_scores), cosine, sine, -1.0)
            dt[own, tokens_here] = (grad_query * (1.0 / math.sqrt(HEAD))).astype(BF16)

    for block in range(blocks):
        pl.when((step < tiles) & (turn == block))(functools.partial(run, block))

    @pl.when((step < tiles) & (turn == blocks - 1))
    def _():
        sequence = pl.ds(pl.multiple_of((step // blocks) * length, length), length)
        for kh in range(kv_heads):
            rows = turned(dk_ref[kh], cos_ref[...], sin_ref[...], -1.0) * math.log(2.0)
            dt[q_cols + kh * HEAD : q_cols + (kh + 1) * HEAD, sequence] = rows.astype(BF16)
            start = q_cols + kv_cols + kh * HEAD
            dt[start : start + HEAD, sequence] = dv_ref[kh].astype(BF16)

    for j in range(thirds):
        @at(tiles + j)
        def _(j=j):
            across = dot(dt[...], n_ref[...])
            g_pack[j * cut : (j + 1) * cut, :qkv] = across.T.astype(BF16)

    def close(slot, grad):
        rows = pl.ds(pl.multiple_of(slot * BLOCK, BLOCK), BLOCK)
        x = own_ref[rows, :].astype(F32)
        inverse = lax.rsqrt(jnp.mean(x * x, -1, keepdims=True) + epsilon)
        normed = x * inverse
        back = inverse * (grad - normed * jnp.mean(grad * normed, -1, keepdims=True))
        grad_out[rows, :] = (trade.rows(dx_ref, slot, core)[...].astype(F32) + back).astype(BF16)

    first = tiles + thirds

    @pl.when(step > first)
    def _():
        trade.take(step - first - 1, close)

    @pl.when(step >= first)
    def _():
        rows = pl.ds(pl.multiple_of((step - first) * BLOCK, BLOCK), BLOCK)
        part = dot(dt[:, rows].T, w_ref[:, :qkv], NT)
        trade.give(step - first, part.astype(BF16))

    @at(first)
    def _():
        reduce.d(1)

    @at(first + tiles - 1)
    def _():
        trade.take(tiles - 1, close)
        reduce.b(2)
        reduce.c(2)
        reduce.d(2)
        for n in range(3):
            reduce.e2(n)
        for n in (1, 2):
            reduce.e1(n)
        trade.drain()


def back(prefix, qt, kv, kvt, lse, ot, dx, n, own, wo, pack, cosine, sine, begun, g_up, heads, kv_heads, length):
    tokens, width = dx.shape
    count, blocks, tiles = tokens // length, length // BLOCK, tokens // BLOCK
    slots = tiles // 2
    q_cols, kv_cols = heads * HEAD, kv_heads * HEAD
    shape = jax.ShapeDtypeStruct
    once = pl.Buffered(1)
    fixed = lambda a: pl.BlockSpec(a.shape, lambda i: (0,) * a.ndim, pipeline_mode=once)
    early = lambda i: jnp.minimum(i, tiles - 1)
    shards = [shape((g.shape[0] // 8, g.shape[1] * 2), BF16) for g in (pack, g_up, g_up)]
    return pl.pallas_call(
        functools.partial(back_kernel, heads, kv_heads, blocks),
        grid=(2 * tiles + 3,),
        in_specs=[
            pl.BlockSpec(memory_space=pltpu.SMEM),
            pl.BlockSpec((q_cols, BLOCK), lambda i: (0, early(i))),
            pl.BlockSpec((length, 2 * kv_cols), lambda i: (early(i) // blocks, 0)),
            pl.BlockSpec((kv_cols, length), lambda i: (0, early(i) // blocks)),
            pl.BlockSpec((heads, BLOCK), lambda i: (0, early(i))),
        ]
        + [fixed(ot), fixed(dx), pl.BlockSpec((tokens, width // 3), lambda i: (0, jnp.clip(i - tiles, 0, 2)))]
        + [fixed(a) for a in (own, wo, pack, cosine, sine, begun)]
        + [ANY],
        out_specs=(fixed(own), ANY, ANY, ANY),
        out_shape=[shape(own.shape, BF16)] + shards,
        scratch_shapes=[
            pltpu.VMEM((q_cols, BLOCK), BF16),
            pltpu.VMEM((kv_heads, HEAD, length), F32),
            pltpu.VMEM((kv_heads, HEAD, length), F32),
            pltpu.VMEM((q_cols + 2 * kv_cols, tokens), BF16),
            pltpu.VMEM(pack.shape, BF16),
            pltpu.VMEM(wo.shape, BF16),
            pltpu.VMEM((q_cols, q_cols), BF16),
            pltpu.VMEM((q_cols, q_cols), BF16),
            DMA((2,)),
        ]
        + Trade.buffers(slots, width)
        + Trade.semaphores(slots)
        + Reduce.buffers([halves_of(*g.shape, True) for g in (g_up, g_up, pack)], near=(2,), begun=(0,))
        + Reduce.semaphores(3),
        compiler_params=pltpu.CompilerParams(collective_id=4, has_side_effects=True, vmem_limit_bytes=62 * 2**20),
        name="back",
    )(prefix, qt, kv, kvt, lse, ot, dx, n, own, wo, pack, cosine, sine, begun, g_up)


def tables(length):
    frequency = np.float32(10000.0) ** (-np.arange(HEAD // 2, dtype=np.float32) * np.float32(2.0) / np.float32(HEAD))
    angles = frequency[:, None] * np.arange(length, dtype=np.float32)[None, :]
    return jnp.asarray(np.cos(angles)), jnp.asarray(np.sin(angles))


def paired(
    activations_in,
    prefix_len,
    attn_gain,
    query_weight,
    key_weight,
    value_weight,
    out_weight,
    ffn_gain,
    gate_weight,
    up_weight,
    down_weight,
    cotangent,
):
    micro, seq_count, span, width = activations_in.shape
    count, length = micro * seq_count, 2 * span
    heads, kv_heads = HEADS // 2, KV_HEADS // 2

    own_x = activations_in.reshape(count, span, width)
    own_dy = cotangent.reshape(count, span, width)

    gain_attn, gain_ffn = attn_gain[None, :], ffn_gain[None, :]
    pack, gate_part, full_x, full_dy = start(
        own_x, own_dy, query_weight, key_weight, value_weight, out_weight, gate_weight, gain_attn, gain_ffn, heads, kv_heads
    )
    cosine, sine = tables(length)
    prefix = prefix_len.reshape(count)
    normed_one, qt, kvt, kv, ot, lse, w_out, middle, inverse, full_two, w_gate, w_up, w_down = front(
        prefix, full_x, own_x.reshape(count * span, width), pack, gate_part, up_weight, down_weight, gain_ffn, cosine, sine,
        heads, kv_heads, length,
    )
    core = lax.axis_index("ctx").astype(jnp.int32).reshape(1)
    hidden, by_up, by_gate, mine, theirs = feed(core, full_two, w_gate, w_up, w_down, length)
    result = middle + mine.astype(F32) + lax.ppermute(theirs, "ctx", [(0, 1), (1, 0)]).astype(F32)
    grad_down = dot(hidden, full_dy, TN).astype(BF16)
    _, grad_up, full_dx, r_down, begun = feed_back(
        full_dy, by_up, by_gate, full_two, w_gate, w_up, w_down, inverse, grad_down, length
    )
    grad_inputs, r_pack, r_gate, r_up = back(
        prefix, qt, kv, kvt, lse, ot, full_dx, normed_one, own_x.reshape(count * span, width), w_out, pack, cosine, sine,
        begun, grad_up, heads, kv_heads, length,
    )
    g_q, g_k, g_v, g_o, g_gate, g_up, g_down, g_ga, g_gf = finish(
        r_pack, r_gate, r_up, r_down, query_weight, key_weight, value_weight, out_weight, gate_weight, up_weight, gain_attn, gain_ffn,
        heads, kv_heads,
    )
    shape = activations_in.shape
    return (
        result.astype(BF16).reshape(shape),
        grad_inputs.reshape(shape),
        g_ga.reshape(-1),
        g_q,
        g_k,
        g_v,
        g_o,
        g_gf.reshape(-1),
        g_gate,
        g_up,
        g_down,
    )


def solution(mesh):
    small = dict(mesh.shape) == {"grp": 4, "fsdp": 4, "ctx": 2}

    return jax.shard_map(
        paired if small else local,
        mesh=mesh,
        in_specs=(
            P(None, ("grp", "fsdp"), "ctx", None),
            P(None, ("grp", "fsdp")),
            P(("fsdp", "ctx")),
            P(("fsdp", "ctx"), None),
            P(("fsdp", "ctx"), None),
            P(("fsdp", "ctx"), None),
            P(("fsdp", "ctx"), None),
            P(("fsdp", "ctx")),
            P(("fsdp", "ctx"), None),
            P(("fsdp", "ctx"), None),
            P(("fsdp", "ctx"), None),
            P(None, ("grp", "fsdp"), "ctx", None),
        ),
        out_specs=(
            P(None, ("grp", "fsdp"), "ctx", None),
            P(None, ("grp", "fsdp"), "ctx", None),
            P(("fsdp", "ctx")),
            P(("fsdp", "ctx"), None),
            P(("fsdp", "ctx"), None),
            P(("fsdp", "ctx"), None),
            P(("fsdp", "ctx"), None),
            P(("fsdp", "ctx")),
            P(("fsdp", "ctx"), None),
            P(("fsdp", "ctx"), None),
            P(("fsdp", "ctx"), None),
        ),
        check_vma=False,
    )
```

```python
import functools
import math

import jax
import jax.numpy as jnp
import numpy as np
from jax import lax
from jax.experimental import pallas as pl
from jax.experimental.pallas import tpu as pltpu
from jax.sharding import PartitionSpec as P

HEADS = 18
KV_HEADS = 6
HEAD = 64


epsilon = 1e-05


def shortened(array):

    def short(part):
        return part.astype(jnp.bfloat16) if part.dtype == jnp.float32 else part

    return jax.tree.map(short, array)


def rotary_tables(positions):
    halfway = HEAD // 2
    frequency = 10000.0 ** (-jnp.arange(halfway, dtype=jnp.float32) * 2.0 / HEAD)
    angles = positions.astype(jnp.float32)[:, None] * frequency[None, :]
    return (jnp.cos(angles)[:, None, :], jnp.sin(angles)[:, None, :])


def rotate(values, cosine, sine):
    halfway = values.shape[-1] // 2
    first = values[..., :halfway]
    second = values[..., halfway:]
    return jnp.concatenate([first * cosine - second * sine, second * cosine + first * sine], -1)


def rotate_back(values, cosine, sine):
    halfway = values.shape[-1] // 2
    first = values[..., :halfway]
    second = values[..., halfway:]
    return jnp.concatenate([first * cosine + second * sine, second * cosine - first * sine], -1)


def norm_back(grad_normed, normed, inverse):
    return inverse * (grad_normed - normed * jnp.mean(grad_normed * normed, -1, keepdims=True))


def flatten_all(grads):
    return tuple((g.reshape(-1) for g in grads))


def local(
    activations_in,
    prefix_len,
    attn_gain,
    query_weight,
    key_weight,
    value_weight,
    out_weight,
    ffn_gain,
    gate_weight,
    up_weight,
    down_weight,
    cotangent,
):
    micro, seq_count, span, width = activations_in.shape
    rows = seq_count * span
    length = span * lax.axis_size("ctx")
    groups = HEADS // KV_HEADS
    scale = 1.0 / math.sqrt(HEAD)
    shards = (
        attn_gain,
        query_weight,
        key_weight,
        value_weight,
        out_weight,
        ffn_gain,
        gate_weight,
        up_weight,
        down_weight,
    )
    offset = lax.axis_index("ctx") * span
    query_pos = offset + jnp.arange(span, dtype=jnp.int32)
    key_pos = jnp.arange(length, dtype=jnp.int32)
    cosine, sine = rotary_tables(jnp.tile(query_pos, seq_count))

    def visibility(prefix):
        return (key_pos[None, :] <= query_pos[:, None]) | (key_pos[None, :] < prefix)

    def attend(item):
        query, keys, values, prefix = item
        scores = (
            jnp.einsum("qhgd,khd->hgqk", query, keys, preferred_element_type=jnp.float32) * scale
        )
        scores = jnp.where(visibility(prefix), scores, -1e30)
        peak = jnp.max(scores, -1, keepdims=True)
        weights = jnp.exp(scores - peak)
        totals = jnp.sum(weights, -1, keepdims=True)
        probs = (weights / totals).astype(jnp.bfloat16)
        mixed = jnp.einsum("hgqk,khd->qhgd", probs, values, preferred_element_type=jnp.float32)
        return (mixed.reshape(span, HEADS * HEAD), (peak + jnp.log(totals))[..., 0])

    def attend_back(item):
        query, keys, values, prefix, log_total, grad_mixed = item
        scores = (
            jnp.einsum("qhgd,khd->hgqk", query, keys, preferred_element_type=jnp.float32) * scale
        )
        probs = jnp.where(visibility(prefix), jnp.exp(scores - log_total[..., None]), 0.0)
        grad_probs = jnp.einsum(
            "qhgd,khd->hgqk", grad_mixed, values, preferred_element_type=jnp.float32
        )
        grad_scores = (
            probs * (grad_probs - jnp.sum(probs * grad_probs, -1, keepdims=True))
        ).astype(jnp.bfloat16)
        grad_query = (
            jnp.einsum("hgqk,khd->qhgd", grad_scores, keys, preferred_element_type=jnp.float32)
            * scale
        )
        grad_keys = (
            jnp.einsum("hgqk,qhgd->khd", grad_scores, query, preferred_element_type=jnp.float32)
            * scale
        )
        grad_values = jnp.einsum(
            "hgqk,qhgd->khd",
            probs.astype(jnp.bfloat16),
            grad_mixed,
            preferred_element_type=jnp.float32,
        )
        return (
            grad_query.reshape(span, HEADS * HEAD),
            grad_keys.reshape(length, KV_HEADS * HEAD),
            grad_values.reshape(length, KV_HEADS * HEAD),
        )

    outputs = []
    input_grads = []
    collected = None
    for index in range(micro):
        full = (
            lax.all_gather(shards[0], ("fsdp", "ctx"), axis=0, tiled=True),
            lax.all_gather(shards[1], ("fsdp", "ctx"), axis=0, tiled=True),
            lax.all_gather(shards[2], ("fsdp", "ctx"), axis=0, tiled=True),
            lax.all_gather(shards[3], ("fsdp", "ctx"), axis=0, tiled=True),
            lax.all_gather(shards[4], ("fsdp", "ctx"), axis=0, tiled=True),
            lax.all_gather(shards[5], ("fsdp", "ctx"), axis=0, tiled=True),
            lax.all_gather(shards[6], ("fsdp", "ctx"), axis=0, tiled=True),
            lax.all_gather(shards[7], ("fsdp", "ctx"), axis=0, tiled=True),
            lax.all_gather(shards[8], ("fsdp", "ctx"), axis=0, tiled=True),
        )
        gain_attn, w_query, w_key, w_value, w_out, gain_ffn, w_gate, w_up, w_down = full
        inputs = activations_in[index].reshape(rows, width).astype(jnp.float32)
        inverse_one = lax.rsqrt(jnp.mean(inputs * inputs, -1, keepdims=True) + epsilon)
        normed_one = inputs * inverse_one
        first_in = (normed_one * gain_attn).astype(jnp.bfloat16)
        query_lin = jnp.dot(first_in, w_query, preferred_element_type=jnp.float32)
        key_lin = jnp.dot(first_in, w_key, preferred_element_type=jnp.float32)
        value_lin = jnp.dot(first_in, w_value, preferred_element_type=jnp.float32)
        query_rot = rotate(query_lin.reshape(rows, HEADS, HEAD), cosine, sine).astype(jnp.bfloat16)
        key_rot = rotate(key_lin.reshape(rows, KV_HEADS, HEAD), cosine, sine).astype(jnp.bfloat16)
        key_rot = key_rot.reshape(seq_count, span, KV_HEADS * HEAD)
        value_low = value_lin.astype(jnp.bfloat16).reshape(seq_count, span, KV_HEADS * HEAD)
        key_all, value_all = (
            lax.all_gather(key_rot, "ctx", axis=1, tiled=True),
            lax.all_gather(value_low, "ctx", axis=1, tiled=True),
        )
        query_split = query_rot.reshape(seq_count, span, KV_HEADS, groups, HEAD)
        key_split = key_all.reshape(seq_count, length, KV_HEADS, HEAD)
        value_split = value_all.reshape(seq_count, length, KV_HEADS, HEAD)
        mixed_all, log_totals = lax.map(
            attend, (query_split, key_split, value_split, prefix_len[index])
        )
        attn_low = mixed_all.reshape(rows, HEADS * HEAD).astype(jnp.bfloat16)
        middle = inputs + jnp.dot(attn_low, w_out, preferred_element_type=jnp.float32)
        inverse_two = lax.rsqrt(jnp.mean(middle * middle, -1, keepdims=True) + epsilon)
        normed_two = middle * inverse_two
        second_in = (normed_two * gain_ffn).astype(jnp.bfloat16)
        gate = jnp.dot(second_in, w_gate, preferred_element_type=jnp.float32)
        upward = jnp.dot(second_in, w_up, preferred_element_type=jnp.float32)
        hidden = (jax.nn.silu(gate) * upward).astype(jnp.bfloat16)
        result = middle + jnp.dot(hidden, w_down, preferred_element_type=jnp.float32)
        outputs.append(result.astype(jnp.bfloat16).reshape(seq_count, span, width))
        back = (
            lax.all_gather(shards[0], ("fsdp", "ctx"), axis=0, tiled=True),
            lax.all_gather(shards[1], ("fsdp", "ctx"), axis=0, tiled=True),
            lax.all_gather(shards[2], ("fsdp", "ctx"), axis=0, tiled=True),
            lax.all_gather(shards[3], ("fsdp", "ctx"), axis=0, tiled=True),
            lax.all_gather(shards[4], ("fsdp", "ctx"), axis=0, tiled=True),
            lax.all_gather(shards[5], ("fsdp", "ctx"), axis=0, tiled=True),
            lax.all_gather(shards[6], ("fsdp", "ctx"), axis=0, tiled=True),
            lax.all_gather(shards[7], ("fsdp", "ctx"), axis=0, tiled=True),
            lax.all_gather(shards[8], ("fsdp", "ctx"), axis=0, tiled=True),
        )
        gain_attn, w_query, w_key, w_value, w_out, gain_ffn, w_gate, w_up, w_down = back
        grad_y = cotangent[index].reshape(rows, width).astype(jnp.float32)
        grad_y_low = grad_y.astype(jnp.bfloat16)
        grad_wdown = jnp.einsum("rf,rd->fd", hidden, grad_y_low, preferred_element_type=jnp.float32)
        grad_hidden = jnp.einsum(
            "rd,fd->rf", grad_y_low, w_down, preferred_element_type=jnp.float32
        )
        sigma = jax.nn.sigmoid(gate)
        grad_up_low = (grad_hidden * gate * sigma).astype(jnp.bfloat16)
        grad_gate_low = (grad_hidden * upward * sigma * (1.0 + gate * (1.0 - sigma))).astype(
            jnp.bfloat16
        )
        grad_wgate = jnp.einsum(
            "rd,rf->df", second_in, grad_gate_low, preferred_element_type=jnp.float32
        )
        grad_wup = jnp.einsum(
            "rd,rf->df", second_in, grad_up_low, preferred_element_type=jnp.float32
        )
        grad_second = jnp.einsum(
            "rf,df->rd", grad_gate_low, w_gate, preferred_element_type=jnp.float32
        ) + jnp.einsum("rf,df->rd", grad_up_low, w_up, preferred_element_type=jnp.float32)
        grad_gain_ffn = jnp.sum(grad_second * normed_two, 0)
        grad_middle = grad_y + norm_back(grad_second * gain_ffn, normed_two, inverse_two)
        grad_branch_low = grad_middle.astype(jnp.bfloat16)
        grad_wout = jnp.einsum(
            "ra,rd->ad", attn_low, grad_branch_low, preferred_element_type=jnp.float32
        )
        grad_attn_low = jnp.einsum(
            "rd,ad->ra", grad_branch_low, w_out, preferred_element_type=jnp.float32
        ).astype(jnp.bfloat16)
        grad_mixed = grad_attn_low.reshape(seq_count, span, KV_HEADS, groups, HEAD)
        grad_query_rot, grad_key_part, grad_value_part = lax.map(
            attend_back,
            (query_split, key_split, value_split, prefix_len[index], log_totals, grad_mixed),
        )
        grad_key_own, grad_value_own = (
            lax.psum_scatter(
                grad_key_part.astype(jnp.bfloat16), "ctx", scatter_dimension=1, tiled=True
            ).astype(jnp.float32),
            lax.psum_scatter(
                grad_value_part.astype(jnp.bfloat16), "ctx", scatter_dimension=1, tiled=True
            ).astype(jnp.float32),
        )
        grad_query = rotate_back(grad_query_rot.reshape(rows, HEADS, HEAD), cosine, sine)
        grad_query = grad_query.reshape(rows, HEADS * HEAD).astype(jnp.bfloat16)
        grad_key = rotate_back(grad_key_own.reshape(rows, KV_HEADS, HEAD), cosine, sine)
        grad_key = grad_key.reshape(rows, KV_HEADS * HEAD).astype(jnp.bfloat16)
        grad_value = grad_value_own.reshape(rows, KV_HEADS * HEAD).astype(jnp.bfloat16)
        grad_wquery = jnp.einsum(
            "rd,rq->dq", first_in, grad_query, preferred_element_type=jnp.float32
        )
        grad_wkey = jnp.einsum("rd,rq->dq", first_in, grad_key, preferred_element_type=jnp.float32)
        grad_wvalue = jnp.einsum(
            "rd,rq->dq", first_in, grad_value, preferred_element_type=jnp.float32
        )
        grad_first = (
            jnp.einsum("rq,dq->rd", grad_query, w_query, preferred_element_type=jnp.float32)
            + jnp.einsum("rq,dq->rd", grad_key, w_key, preferred_element_type=jnp.float32)
            + jnp.einsum("rq,dq->rd", grad_value, w_value, preferred_element_type=jnp.float32)
        )
        grad_gain_attn = jnp.sum(grad_first * normed_one, 0)
        grad_inputs = grad_middle + norm_back(grad_first * gain_attn, normed_one, inverse_one)
        input_grads.append(grad_inputs.astype(jnp.bfloat16).reshape(seq_count, span, width))
        grads = flatten_all(
            (
                grad_gain_attn,
                grad_wquery,
                grad_wkey,
                grad_wvalue,
                grad_wout,
                grad_gain_ffn,
                grad_wgate,
                grad_wup,
                grad_wdown,
            )
        )
        pieces = lax.psum_scatter(grads, ("fsdp", "ctx"), scatter_dimension=0, tiled=True)
        if index == 0:
            collected = pieces
        else:
            collected = tuple((a + b for a, b in zip(collected, pieces)))
    summed = jax.tree.map(
        lambda part: part.astype(jnp.float32), lax.psum(shortened(collected), "grp")
    )
    shaped = tuple((s.reshape(w.shape) for s, w in zip(summed, shards)))
    return (
        jnp.stack(outputs, 0),
        jnp.stack(input_grads, 0),
        shaped[0],
        shaped[1],
        shaped[2],
        shaped[3],
        shaped[4],
        shaped[5],
        shaped[6],
        shaped[7],
        shaped[8],
    )


BLOCK = 256
TO_LOG2 = math.log2(math.e) / math.sqrt(HEAD)
F32, BF16 = jnp.float32, jnp.bfloat16
NN = (((1,), (0,)), ((), ()))
NT = (((1,), (1,)), ((), ()))
TN = (((0,), (0,)), ((), ()))


def dot(a, b, dims=NN):
    return lax.dot_general(a, b, dims, preferred_element_type=F32)


def turned(rows, cosine, sine, sign):
    a, b = rows[: HEAD // 2], rows[HEAD // 2 :]
    return jnp.concatenate([a * cosine - sign * b * sine, b * cosine + sign * a * sine], 0)


def masked(scores, prefix, first, block):
    key = first + lax.broadcasted_iota(jnp.int32, scores.shape, 0)
    query = block * BLOCK + lax.broadcasted_iota(jnp.int32, scores.shape, 1)
    return jnp.where((key <= query) | (key < prefix), scores, -1e30)


def reach(block):
    return max(2, block + 1) * BLOCK


def scores_of(keys, query, prefix, block):
    clear = block * BLOCK
    edge = masked(dot(keys[clear:], query), prefix, clear, block)
    if not clear:
        return edge
    return jnp.concatenate([dot(keys[:clear], query), edge], 0)


MESH = pl.DeviceIdType.MESH
DMA = pltpu.SemaphoreType.DMA
ANY = pl.BlockSpec(memory_space=pl.ANY)
VMEM = pl.BlockSpec(memory_space=pltpu.VMEM)


def where_am_i():
    return lax.axis_index("grp"), lax.axis_index("fsdp"), lax.axis_index("ctx")


def remote(src, dst, send, recv, grp, fsdp, ctx):
    return pltpu.make_async_remote_copy(
        src_ref=src,
        dst_ref=dst,
        send_sem=send,
        recv_sem=recv,
        device_id={"grp": grp, "fsdp": fsdp, "ctx": ctx},
        device_id_type=MESH,
    )


def greet(partners):
    barrier = pltpu.get_barrier_semaphore()
    for grp, fsdp, ctx in partners:
        pl.semaphore_signal(
            barrier, inc=1, device_id={"grp": grp, "fsdp": fsdp, "ctx": ctx}, device_id_type=MESH
        )
    pl.semaphore_wait(barrier, len(partners))


class Columns:
    split = True

    def __init__(self, core, shard, out):
        self.core, self.shard, self.out = core, shard, out
        self.rows, self.cols = shard.shape[0], out.shape[1] // 4

    def mine(self, j, quarter):
        to = self.core if j == 0 else 1 - self.core
        return self.shard.at[:, pl.ds(pl.multiple_of((2 * quarter + to) * self.cols, 128), self.cols)]

    def block(self, plane, j, quarter):
        owner = self.core if j == 0 else 1 - self.core
        start = pl.multiple_of((2 * plane + owner) * self.rows, 16)
        return self.out.at[pl.ds(start, self.rows), pl.ds(pl.multiple_of(quarter * self.cols, 128), self.cols)]


class Rows:
    split = False

    def __init__(self, core, shard, out):
        self.core, self.shard, self.out = core, shard, out
        self.rows = out.shape[0] // 32

    def mine(self, j, quarter):
        return self.shard.at[pl.ds(pl.multiple_of((2 * quarter + j) * self.rows, 16), self.rows), :]

    def block(self, plane, j, quarter):
        start = pl.multiple_of((8 * plane + 2 * quarter + j) * self.rows, 16)
        return self.out.at[pl.ds(start, self.rows), :]

    def own(self, plane):
        return self.out.at[pl.ds(pl.multiple_of(plane * 8 * self.rows, 16), 8 * self.rows), :]


class Gather:
    @staticmethod
    def semaphores(count):
        return [DMA((count, 4)), DMA((count, 4)), DMA((count, 4))] + [DMA((count, 3, 2))] * 2 + [DMA((count, 3, 2, 2))] * 2 + [DMA((count, 3, 2))] * 2

    def __init__(self, units, sems):
        self.units, self.sems = units, sems
        self.grp, self.plane, self.core = where_am_i()
        self.side = self.grp + 1 - 2 * lax.rem(self.grp, 2)
        self.up = lax.rem(self.grp + 2, 4)
        self.planes = [lax.rem(self.plane + s, 4) for s in (1, 2, 3)]
        self.origins = [lax.rem(self.plane + 4 - s, 4) for s in (1, 2, 3)]
        self.left = []

    def partners(self):
        grp, plane, core = self.grp, self.plane, self.core
        found = [(grp, z, c) for z in self.planes for c in (core, 1 - core)]
        return found + [(grp, plane, 1 - core), (self.side, plane, core), (self.up, plane, core)]

    def other(self, j):
        return self.core if j == 0 else 1 - self.core

    def send(self, src, dst, send, recv, grp, plane, core):
        copy = remote(src, dst, send, recv, grp, plane, core)
        copy.start()
        self.left.append(copy.wait_send)

    def got(self, here, send, recv):
        remote(here, here, send, recv, self.side, self.plane, self.core).wait_recv()

    def first(self, n):
        u = self.units[n]
        loc, near_s, near_r, z_s, z_r = self.sems[:5]
        for i, z in enumerate(self.planes):
            for j in range(2):
                if u.split:
                    dst = u.block(self.plane, 0, self.grp)
                    self.send(u.mine(j, self.grp), dst, z_s.at[n, i, j], z_r.at[n, i, j], self.grp, z, self.other(j))
                else:
                    dst = u.block(self.plane, j, self.grp)
                    self.send(u.mine(j, self.grp), dst, z_s.at[n, i, j], z_r.at[n, i, j], self.grp, z, self.core)
        if u.split:
            for q in range(4):
                dst = u.block(self.plane, 0, q)
                self.send(u.mine(1, q), dst, near_s.at[n, q], near_r.at[n, q], self.grp, self.plane, 1 - self.core)
                copy = pltpu.make_async_copy(u.mine(0, q), dst, loc.at[n, q])
                copy.start()
                self.left.append(copy.wait)
        else:
            copy = pltpu.make_async_copy(u.shard, u.own(self.plane), loc.at[n, 0])
            copy.start()
            self.left.append(copy.wait)

    def first_in(self, n):
        u = self.units[n]
        for i, z in enumerate(self.origins):
            for j in range(2):
                self.got(u.block(z, j, self.grp), self.sems[3].at[n, i, j], self.sems[4].at[n, i, j])

    def near_in(self, n):
        u = self.units[n]
        if u.split:
            for q in range(4):
                self.got(u.block(self.plane, 1, q), self.sems[1].at[n, q], self.sems[2].at[n, q])

    def second(self, n, here=False):
        u = self.units[n]
        z_s, z_r, xy_s, xy_r = self.sems[3:7]
        for i, z in enumerate(self.origins):
            for j in range(2):
                block = u.block(z, j, self.grp)
                if not here:
                    self.got(block, z_s.at[n, i, j], z_r.at[n, i, j])
                for t, to in enumerate((self.side, self.up)):
                    self.send(block, block, xy_s.at[n, i, j, t], xy_r.at[n, i, j, t], to, self.plane, self.core)

    def third(self, n):
        u = self.units[n]
        xy_s, xy_r, fw_s, fw_r = self.sems[5:9]
        for i, z in enumerate(self.origins):
            for t, (origin, to) in enumerate(((self.side, self.up), (self.up, self.side))):
                block = u.block(z, t, origin)
                self.got(block, xy_s.at[n, i, t, t], xy_r.at[n, i, t, t])
                self.send(block, block, fw_s.at[n, i, t], fw_r.at[n, i, t], to, self.plane, self.core)

    def last(self, n):
        u = self.units[n]
        xy_s, xy_r, fw_s, fw_r = self.sems[5:9]
        for i, z in enumerate(self.origins):
            for t, origin in enumerate((self.side, self.up)):
                self.got(u.block(z, 1 - t, origin), xy_s.at[n, i, 1 - t, t], xy_r.at[n, i, 1 - t, t])
            for t in range(2):
                self.got(u.block(z, t, 3 - self.grp), fw_s.at[n, i, t], fw_r.at[n, i, t])

    def sent_all(self, firsts, rest):
        loc, near_s, near_r, z_s, z_r, xy_s, xy_r, fw_s, fw_r = self.sems

        def out(block, send, recv):
            remote(block, block, send, recv, self.side, self.plane, self.core).wait_send()

        for n in firsts:
            u = self.units[n]
            for i in range(3):
                for j in range(2):
                    out(u.block(self.plane, j, self.grp), z_s.at[n, i, j], z_r.at[n, i, j])
            if u.split:
                for q in range(4):
                    out(u.block(self.plane, 0, q), near_s.at[n, q], near_r.at[n, q])
                    pltpu.make_async_copy(u.mine(0, q), u.block(self.plane, 0, q), loc.at[n, q]).wait()
            else:
                pltpu.make_async_copy(u.shard, u.own(self.plane), loc.at[n, 0]).wait()
        for n in rest:
            u = self.units[n]
            for i, z in enumerate(self.origins):
                for j in range(2):
                    for t in range(2):
                        out(u.block(z, j, self.grp), xy_s.at[n, i, j, t], xy_r.at[n, i, j, t])
                for t, origin in enumerate((self.side, self.up)):
                    out(u.block(z, t, origin), fw_s.at[n, i, t], fw_r.at[n, i, t])

    def drain(self):
        for wait in self.left:
            wait()
        self.left = []


def upright(row_ref):
    return jnp.broadcast_to(row_ref[...].astype(F32), (8, row_ref.shape[1])).T[:, :1]


def start_kernel(heads, kv_heads, x_ref, dy_ref, wq_ref, wk_ref, wv_ref, wo_ref, gate_ref, ga_ref, gf_ref,
                 pack_out, gate_out, x_out, dy_out, pack, gate, trade_s, trade_r, own_s, *sems):
    _, _, core = where_am_i()
    q_cols, kv_cols, span = heads * HEAD, kv_heads * HEAD, x_ref.shape[1]
    cols = pack.shape[1] // 8
    gain = upright(ga_ref)
    for k in range(2):
        parts = [(wq_ref[:, k * q_cols : (k + 1) * q_cols].astype(F32) * gain).astype(BF16)]
        parts += [(w[:, k * kv_cols : (k + 1) * kv_cols].astype(F32) * gain).astype(BF16) for w in (wk_ref, wv_ref)]
        row = jnp.concatenate(parts + [wo_ref[:, k * q_cols : (k + 1) * q_cols]], 1)
        for q in range(4):
            pack[:, (2 * q + k) * cols : (2 * q + k + 1) * cols] = row[:, q * cols : (q + 1) * cols]
    gather = Gather([Columns(core, pack, pack_out), Columns(core, gate, gate_out)], sems)
    greet(gather.partners())
    gather.first(0)
    gate[...] = (gate_ref[...].astype(F32) * upright(gf_ref)).astype(BF16)
    waits = []

    def trade(ref, out, which):
        for s in range(ref.shape[0]):
            def rows(owner):
                return out.at[pl.ds(pl.multiple_of((2 * s + owner) * span, 16), span), :]
            copy = remote(ref.at[s], rows(core), trade_s.at[which, s], trade_r.at[which, s], gather.grp, gather.plane, 1 - core)
            copy.start()
            gather.left.append(copy.wait_send)
            copy = pltpu.make_async_copy(ref.at[s], rows(core), own_s.at[which, s])
            copy.start()
            gather.left.append(copy.wait)
            waits.append((rows(1 - core), trade_s.at[which, s], trade_r.at[which, s]))

    trade(x_ref, x_out, 0)
    gather.second(0)
    gather.first(1)
    trade(dy_ref, dy_out, 1)
    gather.third(0)
    gather.last(0)
    gather.near_in(0)
    gather.near_in(1)
    for wait in waits:
        gather.got(*wait)
    gather.first_in(1)
    gather.drain()


def start(x, dy, wq, wk, wv, wo, gate, gain_attn, gain_ffn, heads, kv_heads):
    count, span, width = x.shape
    shard, hidden = gate.shape
    cols = 2 * (heads + kv_heads) * HEAD
    shape = jax.ShapeDtypeStruct
    return pl.pallas_call(
        functools.partial(start_kernel, heads, kv_heads),
        grid=(1,),
        in_specs=[pl.BlockSpec(a.shape, lambda i, n=a.ndim: (0,) * n) for a in (x, dy, wq, wk, wv, wo, gate, gain_attn, gain_ffn)],
        out_specs=(ANY,) * 4,
        out_shape=(
            shape((8 * shard, cols), BF16),
            shape((8 * shard, hidden // 2), BF16),
            shape((2 * count * span, width), BF16),
            shape((2 * count * span, width), BF16),
        ),
        scratch_shapes=[pltpu.VMEM((shard, 2 * cols), BF16), pltpu.VMEM((shard, hidden), BF16)]
        + [DMA((2, count))] * 3
        + Gather.semaphores(2),
        compiler_params=pltpu.CompilerParams(collective_id=0, has_side_effects=True, vmem_limit_bytes=62 * 2**20),
        name="start",
    )(x, dy, wq, wk, wv, wo, gate, gain_attn, gain_ffn)


def front_kernel(heads, kv_heads, blocks, prefix_ref, x_ref, own_ref, w_ref, up_ref, gf_ref, cos_ref, sin_ref, gate_in, down_ref,
                 n_ref, qt_ref, kvt_ref, kv_ref, ot_ref, lse_ref, wo_ref, x1_ref, inv_ref, two_out, gate_out, up_out, down_out,
                 up_s, wo_send, wo_recv, part_mine, part_send, part_recv, two_mine,
                 wo_sem, part_sem, two_sem, own_sem, *sems):
    step = pl.program_id(0)
    grp, plane, core = where_am_i()
    count = prefix_ref.shape[0]
    tiles = count * blocks
    groups = heads // kv_heads
    q_cols, kv_cols = heads * HEAD, kv_heads * HEAD
    width = x_ref.shape[1]
    half = blocks // 2
    gather = Gather([Columns(core, up_s, gate_out), Columns(core, up_s, up_out), Rows(core, down_ref, down_out)], sems)

    def at(when):
        return pl.when(step == when)

    def out_weight(owner):
        return w_ref[pl.ds(pl.multiple_of(owner * q_cols, 16), q_cols), q_cols + 2 * kv_cols :]

    def wo_copy():
        return remote(wo_send, wo_recv, wo_sem.at[0], wo_sem.at[1], grp, plane, 1 - core)

    @at(0)
    def _():
        greet(gather.partners())
        gather.second(0, here=True)
        wo_send[...] = out_weight(1 - core)
        wo_copy().start()
        up_s[...] = (up_ref[...].astype(F32) * upright(gf_ref)).astype(BF16)
        gather.first(1)

    @at(tiles - 1)
    def _():
        wo_copy().wait()
        mine, other = out_weight(core), wo_recv[...]
        wo_ref[...] = jnp.concatenate([jnp.where(core == 0, mine, other), jnp.where(core == 0, other, mine)], 1)

    @at(tiles)
    def _():
        gather.first(2)
        gather.third(0)

    @at(tiles + 1)
    def _():
        gather.second(1)

    @at(tiles + 4)
    def _():
        gather.third(1)

    @at(tiles + 5)
    def _():
        gather.second(2)

    @pl.when(step < tiles)
    def _():
        x = x_ref[...].astype(F32)
        normed = (x * lax.rsqrt(jnp.mean(x * x, -1, keepdims=True) + epsilon)).astype(BF16)
        n_ref[...] = normed
        flat = dot(normed, w_ref[:, : q_cols + 2 * kv_cols])
        across = flat.T
        tokens = pl.ds(pl.multiple_of(step * BLOCK, BLOCK), BLOCK)
        here = pl.ds(pl.multiple_of(lax.rem(step, blocks) * BLOCK, BLOCK), BLOCK)
        cosine, sine = cos_ref[:, here], sin_ref[:, here]
        for h in range(heads):
            rows = turned(across[h * HEAD : (h + 1) * HEAD], cosine, sine, 1.0)
            qt_ref[h * HEAD : (h + 1) * HEAD, tokens] = (rows * TO_LOG2).astype(BF16)
        keys = [across[q_cols + h * HEAD : q_cols + (h + 1) * HEAD] for h in range(kv_heads)]
        keys = jnp.concatenate([turned(rows, cosine, sine, 1.0) for rows in keys], 0)
        kvt_ref[:kv_cols, tokens] = keys.astype(BF16)
        kvt_ref[kv_cols:, tokens] = across[q_cols + kv_cols :].astype(BF16)
        kv_ref[tokens, :kv_cols] = keys.T.astype(BF16)
        kv_ref[tokens, kv_cols:] = flat[:, q_cols + kv_cols :].astype(BF16)

    def rows_of(tile, owner):
        start = (tile // half) * blocks + owner * half + lax.rem(tile, half)
        return two_out.at[pl.ds(pl.multiple_of(start * BLOCK, BLOCK), BLOCK), :]

    def part_copy(slot):
        return remote(part_send.at[slot], part_recv.at[slot], part_sem.at[0, slot], part_sem.at[1, slot], grp, plane, 1 - core)

    def two_copy(slot):
        there = rows_of(slot, core)
        return remote(two_mine.at[slot], there, two_sem.at[0, slot], two_sem.at[1, slot], grp, plane, 1 - core)

    def two_keep(slot):
        return pltpu.make_async_copy(two_mine.at[slot], rows_of(slot, core), own_sem.at[slot])

    def finish(turn):
        block, s = lax.rem(turn, blocks), turn // blocks
        slot = s * half + lax.rem(block, half)

        @pl.when(block // half == core)
        def _():
            part_copy(slot).wait_recv()
            rows = pl.ds(pl.multiple_of(slot * BLOCK, BLOCK), BLOCK)
            middle = own_ref[rows, :].astype(F32) + part_mine[slot].astype(F32) + part_recv[slot].astype(F32)
            x1_ref[rows, :] = middle
            inverse = lax.rsqrt(jnp.mean(middle * middle, -1, keepdims=True) + epsilon)
            inv_ref[rows, :] = inverse
            two_mine[slot] = (middle * inverse).astype(BF16)
            two_copy(slot).start()
            two_keep(slot).start()

    def run(block):
        n = reach(block)
        turn = step - tiles
        s = turn // blocks
        prefix = prefix_ref[s]
        base = pl.multiple_of(s * blocks * BLOCK, BLOCK)
        tokens = pl.ds(pl.multiple_of(turn * BLOCK, BLOCK), BLOCK)

        def score(h):
            kh = h // groups
            keys = kv_ref[pl.ds(base, n), kh * HEAD : (kh + 1) * HEAD]
            return scores_of(keys, qt_ref[h * HEAD : (h + 1) * HEAD, tokens], prefix, block)

        def mix(h, weights, total):
            kh = h // groups
            vt = kvt_ref[kv_cols + kh * HEAD : kv_cols + (kh + 1) * HEAD, pl.ds(base, n)]
            ot_ref[h * HEAD : (h + 1) * HEAD, tokens] = (dot(vt, weights) / total).astype(BF16)

        later, held = score(0), None
        for h in range(heads):
            scores = later
            if h + 1 < heads:
                later = score(h + 1)
            peak = jnp.max(scores, 0, keepdims=True)
            weights = jnp.exp2(scores - peak)
            total = jnp.sum(weights, 0, keepdims=True)
            lse_ref[h : h + 1, tokens] = peak + jnp.log2(total)
            if held:
                mix(*held)
            held = (h, weights.astype(BF16), total)
        mix(*held)
        part = dot(ot_ref[:, tokens], wo_ref[...], TN).astype(BF16)
        slot = s * half + block % half

        @pl.when(core == block // half)
        def _():
            part_mine[slot] = part

        @pl.when(core != block // half)
        def _():
            part_send[slot] = part
            part_copy(slot).start()

    @pl.when(step > tiles)
    def _():
        finish(step - tiles - 1)

    for block in range(blocks):
        pl.when((step >= tiles) & (lax.rem(step, blocks) == block))(functools.partial(run, block))

    @at(2 * tiles - 1)
    def _():
        gather.third(2)
        finish(step - tiles)
        for n in range(3):
            gather.last(n)
        gather.near_in(1)
        for slot in range(count * half):
            part_copy(slot).wait_send()
            two_copy(slot).wait_send()
            two_keep(slot).wait()
            there = rows_of(slot, 1 - core)
            remote(there, there, two_sem.at[0, slot], two_sem.at[1, slot], grp, plane, 1 - core).wait_recv()
        gather.sent_all((1, 2), (0, 1, 2))


def front(prefix, x, own, pack, gate_part, up, down, gain_ffn, cosine, sine, heads, kv_heads, length):
    tokens, width = x.shape
    count, blocks = tokens // length, length // BLOCK
    tiles = tokens // BLOCK
    slots = tiles // 2
    q_cols, kv_cols = heads * HEAD, kv_heads * HEAD
    shape = jax.ShapeDtypeStruct
    once = pl.Buffered(1)

    def fixed(*dims):
        return pl.BlockSpec(dims, lambda i: (0,) * len(dims), pipeline_mode=once)

    tile = pl.BlockSpec((BLOCK, width), lambda i: (jnp.minimum(i, tiles - 1), 0))
    return pl.pallas_call(
        functools.partial(front_kernel, heads, kv_heads, blocks),
        grid=(2 * tiles,),
        in_specs=[
            pl.BlockSpec(memory_space=pltpu.SMEM),
            tile,
            fixed(tokens // 2, width),
            fixed(*pack.shape),
            fixed(*up.shape),
            fixed(*gain_ffn.shape),
            fixed(*cosine.shape),
            fixed(*sine.shape),
            ANY,
            fixed(*down.shape),
        ],
        out_specs=(
            tile,
            fixed(q_cols, tokens),
            fixed(2 * kv_cols, tokens),
            fixed(tokens, 2 * kv_cols),
            fixed(q_cols, tokens),
            fixed(heads, tokens),
            fixed(q_cols, width),
            fixed(tokens // 2, width),
            fixed(tokens // 2, 1),
            ANY, ANY, ANY, ANY,
        ),
        out_shape=(
            shape((tokens, width), BF16),
            shape((q_cols, tokens), BF16),
            shape((2 * kv_cols, tokens), BF16),
            shape((tokens, 2 * kv_cols), BF16),
            shape((q_cols, tokens), BF16),
            shape((heads, tokens), F32),
            shape((q_cols, width), BF16),
            shape((tokens // 2, width), F32),
            shape((tokens // 2, 1), F32),
            shape((tokens, width), BF16),
            shape(gate_part.shape, BF16),
            shape(gate_part.shape, BF16),
            shape((4 * down.shape[0], width), BF16),
        ),
        input_output_aliases={8: 10},
        scratch_shapes=[
            pltpu.VMEM(up.shape, BF16),
            pltpu.VMEM((q_cols, q_cols), BF16),
            pltpu.VMEM((q_cols, q_cols), BF16),
        ]
        + [pltpu.VMEM((slots, BLOCK, width), BF16)] * 4
        + [DMA((2,)), DMA((2, slots)), DMA((2, slots)), DMA((slots,))]
        + Gather.semaphores(3),
        compiler_params=pltpu.CompilerParams(collective_id=1, has_side_effects=True, vmem_limit_bytes=60 * 2**20),
        cost_estimate=pl.CostEstimate(flops=2 * tokens * width * 1536, bytes_accessed=16 * tokens * width, transcendentals=0),
        name="front",
    )(prefix, x, own, pack, up, gain_ffn, cosine, sine, gate_part, down)


def feed_kernel(half, core_ref, n_ref, gate_ref, up_ref, down_ref, hidden_ref, by_up_ref, by_gate_ref, mine_ref, theirs_ref):
    n = n_ref[...]
    gate = dot(n, gate_ref[...])
    upward = dot(n, up_ref[...])
    sigma = 1.0 / (1.0 + jnp.exp(-gate))
    silu = gate * sigma
    hidden = (silu * upward).astype(BF16)
    hidden_ref[...] = hidden
    by_up_ref[...] = silu.astype(BF16)
    by_gate_ref[...] = (upward * sigma * (1.0 + gate - silu)).astype(BF16)
    part = dot(hidden, down_ref[...]).astype(BF16)
    own = lax.rem(pl.program_id(0) // half, 2) == core_ref[0]

    @pl.when(own)
    def _():
        mine_ref[...] = part

    @pl.when(jnp.logical_not(own))
    def _():
        theirs_ref[...] = part


def feed(core, n, gate, up, down, length):
    tokens, width = n.shape
    units = gate.shape[1]
    shape = jax.ShapeDtypeStruct
    once = pl.Buffered(1)
    half = length // BLOCK // 2
    tile = lambda cols: pl.BlockSpec((BLOCK, cols), lambda i, core: (i, 0))
    fixed = lambda a: pl.BlockSpec(a.shape, lambda i, core: (0, 0), pipeline_mode=once)

    def slot(i, owner):
        whole, rest = i // (2 * half), lax.rem(i, 2 * half)
        return whole * half + jnp.clip(rest - owner * half, 0, half - 1)

    mine = pl.BlockSpec((BLOCK, width), lambda i, core: (slot(i, core[0]), 0))
    theirs = pl.BlockSpec((BLOCK, width), lambda i, core: (slot(i, 1 - core[0]), 0))
    return pl.pallas_call(
        functools.partial(feed_kernel, half),
        grid_spec=pltpu.PrefetchScalarGridSpec(
            num_scalar_prefetch=1,
            grid=(tokens // BLOCK,),
            in_specs=[tile(width), fixed(gate), fixed(up), fixed(down)],
            out_specs=(tile(units), tile(units), tile(units), mine, theirs),
        ),
        out_shape=(shape((tokens, units), BF16),) * 3 + (shape((tokens // 2, width), BF16),) * 2,
        compiler_params=pltpu.CompilerParams(vmem_limit_bytes=62 * 2**20),
        cost_estimate=pl.CostEstimate(flops=6 * tokens * width * units, bytes_accessed=2 * tokens * (3 * units + 2 * width), transcendentals=tokens * units),
        name="feed",
    )(core, n, gate, up, down)


def finish_kernel(heads, kv_heads, pack_ref, gate_ref, up_ref, down_ref, wq_ref, wk_ref, wv_ref, wg_ref, wu_ref, ga_ref, gf_ref,
                  q_out, k_out, v_out, o_out, gate_out, up_out, down_out, ga_out, gf_out):
    q_cols, kv_cols = heads * HEAD, kv_heads * HEAD
    cols = pack_ref.shape[1] // 8
    gain = upright(ga_ref)
    total = jnp.zeros(gain.shape, F32)
    for k in range(2):
        row = jnp.concatenate([pack_ref[:, (2 * q + k) * cols : (2 * q + k + 1) * cols].astype(F32) for q in range(4)], 1)
        at = 0
        for w, out, size in ((wq_ref, q_out, q_cols), (wk_ref, k_out, kv_cols), (wv_ref, v_out, kv_cols)):
            part, here = row[:, at : at + size], slice(k * size, (k + 1) * size)
            total += jnp.sum(part * w[:, here].astype(F32), -1, keepdims=True)
            out[:, here] = part * gain
            at += size
        o_out[:, k * q_cols : (k + 1) * q_cols] = row[:, at:]
    ga_out[...] = jnp.broadcast_to(total, (total.shape[0], 8)).T[:1]
    gain = upright(gf_ref)
    total = jnp.zeros(gain.shape, F32)
    for ref, w, out in ((gate_ref, wg_ref, gate_out), (up_ref, wu_ref, up_out)):
        part = ref[...].astype(F32)
        total += jnp.sum(part * w[...].astype(F32), -1, keepdims=True)
        out[...] = part * gain
    gf_out[...] = jnp.broadcast_to(total, (total.shape[0], 8)).T[:1]
    down_out[...] = down_ref[...].astype(F32)


def finish(pack, gate, up, down, wq, wk, wv, wo, wg, wu, ga, gf, heads, kv_heads):
    shape = lambda a: jax.ShapeDtypeStruct(a.shape, F32)
    whole = lambda a: pl.BlockSpec(a.shape, lambda i: (0, 0))
    outs = (shape(wq), shape(wk), shape(wv), shape(wo), shape(wg), shape(wu), shape(down), shape(ga), shape(gf))
    return pl.pallas_call(
        functools.partial(finish_kernel, heads, kv_heads),
        grid=(1,),
        in_specs=[whole(a) for a in (pack, gate, up, down, wq, wk, wv, wg, wu, ga, gf)],
        out_specs=tuple(whole(a) for a in outs),
        out_shape=outs,
        compiler_params=pltpu.CompilerParams(vmem_limit_bytes=62 * 2**20),
        name="finish",
    )(pack, gate, up, down, wq, wk, wv, wg, wu, ga, gf)


def halves_of(rows, cols, split):
    return (rows // 8, cols // 4) if split else (rows // 32, cols)


class Summand:
    def __init__(self, core, ref, out, split, near=False):
        self.core, self.ref, self.out, self.split, self.near = core, ref, out, split, near
        self.rows, self.cols = halves_of(*ref.shape, split)

    def half(self, plane, quarter, path):
        if self.split:
            start = pl.multiple_of((2 * plane + path) * self.rows, 16)
            return self.ref.at[pl.ds(start, self.rows), pl.ds(pl.multiple_of(quarter * self.cols, 128), self.cols)]
        start = pl.multiple_of(((4 * plane + quarter) * 2 + path) * self.rows, 16)
        return self.ref.at[pl.ds(start, self.rows), :]

    def place(self, quarter, j, other):
        if self.split:
            return self.out.at[:, pl.ds(pl.multiple_of((2 * quarter + other) * self.cols, 128), self.cols)]
        return self.out.at[pl.ds(pl.multiple_of((2 * quarter + j) * self.rows, 16), self.rows), :]


class Reduce:
    @staticmethod
    def buffers(halves, near=(), begun=(), left=()):
        found = []
        for n, h in enumerate(halves):
            no_first, no_third = n in begun, n in left
            for lead, unused in (
                ((2, 4, 2), no_first or n in near),
                ((2, 4, 2), no_first),
                ((2, 4), no_first),
                ((3, 2), no_third),
                ((4, 2), False),
            ):
                found.append(pltpu.VMEM((1,) * len(lead) + (16, 128) if unused else lead + h, BF16))
        return found

    @staticmethod
    def semaphores(n):
        return [DMA((n, 2, 4, 2))] * 3 + [DMA((n, 2, 4))] * 2 + [DMA((n, 3))] * 2 + [DMA((n, 4, 2))] * 2

    def __init__(self, units, buffers, sems):
        self.units, self.sems = units, sems
        self.bufs = [buffers[5 * n : 5 * n + 5] for n in range(len(units))]
        self.grp, self.plane, self.core = where_am_i()
        gx, gy = lax.rem(self.grp, 2), self.grp // 2
        self.gx, self.gy = gx, gy
        side, up = self.grp + 1 - 2 * gx, lax.rem(self.grp + 2, 4)
        self.first_to, self.second_to, self.keep = (side, up), (up, side), (gy, gx)
        self.planes = [lax.rem(self.plane + s, 4) for s in (1, 2, 3)]
        self.origins = [lax.rem(self.plane + 4 - s, 4) for s in (1, 2, 3)]
        self.others = [lax.rem(self.grp + s, 4) for s in (1, 2, 3)]
        self.sources = [lax.rem(self.grp + 4 - s, 4) for s in (1, 2, 3)]

    def partners(self):
        grp, plane, core = self.grp, self.plane, self.core
        found = [(grp, z, core) for z in self.planes] + [(grp, plane, 1 - core)]
        return found + [(g, plane, c) for g in self.others for c in (core, 1 - core)]

    def quarter(self, path, i, own):
        if path == 0:
            return 2 * i + (self.gx if own else 1 - self.gx)
        return 2 * (self.gy if own else 1 - self.gy) + i

    def first_copy(self, n, path, z, i):
        _, s1, r1 = self.sems[:3]
        src = self.units[n].half(z, self.quarter(path, i, False), path)
        dst = self.bufs[n][1].at[path, z, i]
        return remote(src, dst, s1.at[n, path, z, i], r1.at[n, path, z, i], self.first_to[path], self.plane, self.core)

    def load_copy(self, n, path, z, i):
        src = self.units[n].half(z, self.quarter(path, i, True), path)
        return pltpu.make_async_copy(src, self.bufs[n][0].at[path, z, i], self.sems[0].at[n, path, z, i])

    def second_copy(self, n, path, z):
        _, got, second = self.bufs[n][:3]
        s2, r2 = self.sems[3:5]
        src = got.at[path, z, 1 - self.keep[path]]
        return remote(src, second.at[path, z], s2.at[n, path, z], r2.at[n, path, z], self.second_to[path], self.plane, self.core)

    def third_copy(self, n, i):
        third, fin = self.bufs[n][3:]
        s3, r3 = self.sems[5:7]
        return remote(fin.at[self.planes[i]], third.at[i], s3.at[n, i], r3.at[n, i], self.grp, self.planes[i], self.core)

    def fourth_copy(self, n, i, j, coming=False):
        u, fin = self.units[n], self.bufs[n][4]
        s4, r4 = self.sems[7:9]
        other = (self.core if j == 0 else 1 - self.core) if u.split else self.core
        grp = self.grp if i == 3 else (self.sources if coming else self.others)[i]
        if coming:
            src = dst = u.place(grp, j, other)
        else:
            src = fin.at[self.plane, other if u.split else j]
            dst = u.place(self.grp, j, self.core)
        if i == 3 and not (u.split and j == 1):
            return pltpu.make_async_copy(src, dst, s4.at[n, 3, j])
        return remote(src, dst, s4.at[n, i, j], r4.at[n, i, j], grp, self.plane, other)

    @staticmethod
    def each(planes=range(4)):
        return [(path, z, i) for z in planes for path in range(2) for i in range(2)]

    def a(self, n, planes=range(4)):
        for path, z, i in self.each(planes):
            self.first_copy(n, path, z, i).start()
            if not self.units[n].near:
                self.load_copy(n, path, z, i).start()

    def b(self, n, planes=range(4)):
        u, (acc, got) = self.units[n], self.bufs[n][:2]
        for z in planes:
            for path in range(2):
                for i in range(2):
                    self.first_copy(n, path, z, i).wait_recv()
                    if u.near:
                        own = u.half(z, self.quarter(path, i, True), path)[...]
                    else:
                        self.load_copy(n, path, z, i).wait()
                        own = acc[path, z, i]
                    got[path, z, i] = (own.astype(F32) + got[path, z, i].astype(F32)).astype(BF16)
                self.second_copy(n, path, z).start()

    def c(self, n, send=True):
        _, got, second, _, fin = self.bufs[n]
        for z in range(4):
            for path in range(2):
                self.second_copy(n, path, z).wait_recv()
                fin[z, path] = (got[path, z, self.keep[path]].astype(F32) + second[path, z].astype(F32)).astype(BF16)
            if send:
                self.third_to(n, z)

    def third_to(self, n, z):
        third, fin = self.bufs[n][3:]
        s3, r3 = self.sems[5:7]
        i = lax.rem(z + 7 - self.plane, 4)

        @pl.when(i != 3)
        def _():
            remote(fin.at[z], third.at[i], s3.at[n, i], r3.at[n, i], self.grp, z, self.core).start()

    def c2(self, n):
        for i in range(3):
            self.third_copy(n, i).start()

    def d(self, n):
        third, fin = self.bufs[n][3:]
        for i in range(3):
            self.third_copy(n, i).wait_recv()
        for j in range(2):
            total = fin[self.plane, j].astype(F32)
            for i in range(3):
                total += third[i, j].astype(F32)
            fin[self.plane, j] = total.astype(BF16)
        for j in range(2):
            for i in range(4):
                self.fourth_copy(n, i, j).start()

    def e1(self, n):
        for path, z, i in self.each():
            self.first_copy(n, path, z, i).wait_send()
        for z in range(4):
            for path in range(2):
                self.second_copy(n, path, z).wait_send()

    def e2(self, n):
        u = self.units[n]
        for i in range(3):
            self.third_copy(n, i).wait_send()
        for j in range(2):
            for i in range(4):
                if i == 3 and not (u.split and j == 1):
                    self.fourth_copy(n, i, j).wait()
                else:
                    self.fourth_copy(n, i, j).wait_send()
                    self.fourth_copy(n, i, j, coming=True).wait_recv()


class Trade:
    @staticmethod
    def buffers(slots, width):
        return [pltpu.VMEM((slots, BLOCK, width), BF16)] * 3

    @staticmethod
    def semaphores(slots):
        return [DMA((2, slots))]

    def __init__(self, bufs, sems, blocks):
        self.mine, self.out, self.come = bufs
        self.sem, self.half, self.blocks = sems[0], blocks // 2, blocks
        self.slots = self.mine.shape[0]
        self.grp, self.plane, self.core = where_am_i()

    def copy(self, slot):
        return remote(self.out.at[slot], self.come.at[slot], self.sem.at[0, slot], self.sem.at[1, slot], self.grp, self.plane, 1 - self.core)

    def where(self, turn):
        block = lax.rem(turn, self.blocks)
        return block // self.half, (turn // self.blocks) * self.half + lax.rem(block, self.half)

    def give(self, turn, part):
        owner, slot = self.where(turn)

        @pl.when(self.core == owner)
        def _():
            self.mine[slot] = part

        @pl.when(self.core != owner)
        def _():
            self.out[slot] = part
            self.copy(slot).start()

    def take(self, turn, close):
        owner, slot = self.where(turn)

        @pl.when(self.core == owner)
        def _():
            self.copy(slot).wait_recv()
            close(slot, self.mine[slot].astype(F32) + self.come[slot].astype(F32))

    def drain(self):
        for slot in range(self.slots):
            self.copy(slot).wait_send()

    def place(self, slot, owner):
        start = (slot // self.half) * self.blocks + owner * self.half + lax.rem(slot, self.half)
        return pl.ds(pl.multiple_of(start * BLOCK, BLOCK), BLOCK)

    def rows(self, ref, slot, owner):
        return ref.at[self.place(slot, owner), :]

    def columns(self, ref, slot, owner):
        return ref.at[:, self.place(slot, owner)]


WIDE = 2 * BLOCK


def feed_back_kernel(blocks, dy_ref, n_ref, gate_ref, up_ref, down_ref, inv_ref, by_up_ref, by_gate_ref, grad_ref,
                     g_gate_ref, g_up_ref, dx_out, r_down_out, begun_ref,
                     turned_n, d_gate, d_up, dx_mine, by_sem, dx_sem, keep_sem, *rest):
    step = pl.program_id(0)
    tiles = turned_n.shape[1] // BLOCK
    cuts = d_gate.shape[1] // WIDE
    second = tiles + 2 * cuts
    last = second + tiles - 1
    trade = Trade(rest[:3], rest[3:4], blocks)
    grp, plane, core = where_am_i()
    units = [Summand(core, grad_ref, r_down_out, False), Summand(core, g_gate_ref, None, True, near=True)]
    reduce = Reduce(units, list(rest[4:13]) + [begun_ref], rest[14:])

    def at(when):
        return pl.when(step == when)

    def tile_rows(tile):
        return pl.ds(pl.multiple_of(tile * BLOCK, BLOCK), BLOCK)

    def by_copies(tile):
        rows = tile_rows(tile)
        return [pltpu.make_async_copy(ref.at[rows, :], to.at[rows, :], by_sem.at[k, tile]) for k, (ref, to) in enumerate(((by_up_ref, d_up), (by_gate_ref, d_gate)))]

    @at(0)
    def _():
        for tile in range(tiles):
            for copy in by_copies(tile):
                copy.start()
        greet(reduce.partners())
        reduce.a(0)

    @at(tiles + 1)
    def _():
        reduce.b(0)

    @at(tiles + cuts)
    def _():
        reduce.a(1)

    @at(tiles + cuts + 1)
    def _():
        reduce.c(0)

    @at(second + 4)
    def _():
        reduce.b(1)
        reduce.d(0)

    @pl.when(step < tiles)
    def _():
        rows = tile_rows(step)
        dy = dy_ref[...]
        grad = dot(dy, down_ref[...], NT)
        for copy in by_copies(step):
            copy.wait()
        d_up[rows, :] = (grad * d_up[rows, :].astype(F32)).astype(BF16)
        d_gate[rows, :] = (grad * d_gate[rows, :].astype(F32)).astype(BF16)
        turned_n[:, rows] = n_ref[...].T
        owner, slot = trade.where(step)

        @pl.when(owner == core)
        def _():
            dx_mine[slot] = dy

    @pl.when((step >= tiles) & (step < tiles + cuts))
    def _():
        cols = pl.ds(pl.multiple_of((step - tiles) * WIDE, WIDE), WIDE)
        g_gate_ref[:, cols] = dot(turned_n[...], d_gate[:, cols]).astype(BF16)

    @pl.when((step >= tiles + cuts) & (step < second))
    def _():
        cols = pl.ds(pl.multiple_of((step - tiles - cuts) * WIDE, WIDE), WIDE)
        g_up_ref[...] = dot(turned_n[...], d_up[:, cols]).astype(BF16)

    def there(slot, owner):
        return trade.rows(dx_out, slot, owner)

    def dx_copy(slot):
        return remote(dx_mine.at[slot], there(slot, core), dx_sem.at[0, slot], dx_sem.at[1, slot], grp, plane, 1 - core)

    def dx_keep(slot):
        return pltpu.make_async_copy(dx_mine.at[slot], there(slot, core), keep_sem.at[slot])

    def close(slot, grad):
        rows = pl.ds(pl.multiple_of(slot * BLOCK, BLOCK), BLOCK)
        normed = trade.columns(turned_n, slot, core)[...].T.astype(F32)
        back = grad - normed * jnp.mean(grad * normed, -1, keepdims=True)
        dx_mine[slot] = (dx_mine[slot].astype(F32) + inv_ref[rows, :] * back).astype(BF16)
        dx_copy(slot).start()
        dx_keep(slot).start()

    @pl.when(step > second)
    def _():
        trade.take(step - second - 1, close)

    @pl.when(step >= second)
    def _():
        turn = step - second
        rows = tile_rows(turn)
        part = dot(d_gate[rows, :], gate_ref[...], NT) + dot(d_up[rows, :], up_ref[...], NT)
        trade.give(turn, part.astype(BF16))

    @at(last)
    def _():
        trade.take(tiles - 1, close)
        reduce.c(1, send=False)
        reduce.e1(0)
        reduce.e2(0)
        reduce.e1(1)
        trade.drain()
        for slot in range(trade.slots):
            dx_copy(slot).wait_send()
            dx_keep(slot).wait()
            here = there(slot, 1 - core)
            remote(here, here, dx_sem.at[0, slot], dx_sem.at[1, slot], grp, plane, 1 - core).wait_recv()


def feed_back(dy, by_up, by_gate, n, gate, up, down, inverse, grad_down, length):
    tokens, width = dy.shape
    units = gate.shape[1]
    blocks, tiles, cuts = length // BLOCK, tokens // BLOCK, units // WIDE
    slots = tiles // 2
    shape = jax.ShapeDtypeStruct
    once = pl.Buffered(1)
    early = lambda cols: pl.BlockSpec((BLOCK, cols), lambda i: (jnp.minimum(i, tiles - 1), 0))
    fixed = lambda a: pl.BlockSpec(a.shape, lambda i: (0,) * len(a.shape), pipeline_mode=once)
    cut = pl.BlockSpec((width, WIDE), lambda i: (0, jnp.clip(i - tiles - cuts, 0, cuts - 1)))
    g_gate = shape((width, units), BF16)
    halves = [halves_of(*grad_down.shape, False), halves_of(width, units, True)]
    begun = shape((4, 2) + halves[1], BF16)
    return pl.pallas_call(
        functools.partial(feed_back_kernel, blocks),
        grid=(2 * tiles + 2 * cuts,),
        in_specs=[early(width), early(width)] + [fixed(a) for a in (gate, up, down, inverse)] + [ANY] * 3,
        out_specs=(fixed(g_gate), cut, ANY, ANY, fixed(begun)),
        out_shape=(
            g_gate,
            g_gate,
            shape((tokens, width), BF16),
            shape((grad_down.shape[0] // 4, width), BF16),
            begun,
        ),
        scratch_shapes=[
            pltpu.VMEM((width, tokens), BF16),
            pltpu.VMEM((tokens, units), BF16),
            pltpu.VMEM((tokens, units), BF16),
            pltpu.VMEM((slots, BLOCK, width), BF16),
            DMA((2, tiles)),
            DMA((2, slots)),
            DMA((slots,)),
        ]
        + Trade.buffers(slots, width)
        + Trade.semaphores(slots)
        + Reduce.buffers(halves, near=(1,), left=(1,))
        + Reduce.semaphores(2),
        compiler_params=pltpu.CompilerParams(collective_id=3, has_side_effects=True, vmem_limit_bytes=62 * 2**20),
        name="feed_back",
    )(dy, n, gate, up, down, inverse, by_up, by_gate, grad_down)


def back_kernel(heads, kv_heads, blocks, prefix_ref, qt_ref, kv_ref, kt_ref, lse_ref, ot_ref, dx_ref, n_ref, own_in, wo_ref, w_in,
                cos_ref, sin_ref, begun_ref, g_up_ref,
                grad_out, r_pack_out, r_gate_out, r_up_out,
                dot_ref, dk_ref, dv_ref, dt, g_pack, g_wo, wo_send, wo_come, own_ref, w_ref, late_sem, wo_sem, *rest):
    step = pl.program_id(0)
    grp, plane, core = where_am_i()
    tokens, width = dx_ref.shape
    tiles, half, length = tokens // BLOCK, blocks // 2, blocks * BLOCK
    groups = heads // kv_heads
    q_cols, kv_cols = heads * HEAD, kv_heads * HEAD
    qkv = q_cols + 2 * kv_cols
    thirds = 3
    cut = width // thirds
    trade = Trade(rest[:3], rest[3:4], blocks)
    units = [Summand(core, g_up_ref, r_gate_out, True), Summand(core, g_up_ref, r_up_out, True), Summand(core, g_pack, r_pack_out, True, near=True)]
    reduce = Reduce(units, list(rest[4:8]) + [begun_ref] + list(rest[9:19]), rest[19:])
    turn = lax.rem(step, blocks)

    def at(when):
        return pl.when(step == when)

    def late():
        return [pltpu.make_async_copy(a, b, late_sem.at[k]) for k, (a, b) in enumerate(((own_in, own_ref), (w_in, w_ref)))]

    def wo_copy():
        return remote(wo_send, wo_come, wo_sem.at[0], wo_sem.at[1], grp, plane, 1 - core)

    @at(0)
    def _():
        for copy in late():
            copy.start()
        greet(reduce.partners())
        reduce.a(1)
        reduce.c2(0)

    for j in range(thirds):
        @at(1 + j)
        def _(j=j):
            g_wo[:, j * cut : (j + 1) * cut] = dot(ot_ref[...], dx_ref[:, j * cut : (j + 1) * cut]).astype(BF16)

    @at(1 + thirds)
    def _():
        low, high = g_wo[:, :q_cols], g_wo[:, q_cols:]
        wo_send[...] = jnp.where(core == 0, high, low)
        wo_copy().start()
        g_pack[pl.ds(pl.multiple_of(core * q_cols, 16), q_cols), qkv:] = jnp.where(core == 0, low, high)

    @at(5)
    def _():
        reduce.b(1)
        reduce.d(0)

    @at(tiles - 1)
    def _():
        reduce.c(1)

    @at(tiles)
    def _():
        for copy in late():
            copy.wait()
        wo_copy().wait()
        g_pack[pl.ds(pl.multiple_of((1 - core) * q_cols, 16), q_cols), qkv:] = wo_come[...]

    @at(tiles + 1)
    def _():
        reduce.a(2, (0,))

    @at(tiles + 2)
    def _():
        reduce.a(2, (1,))

    @at(tiles + thirds)
    def _():
        reduce.a(2, (2, 3))

    @pl.when((step < tiles) & (turn == 0))
    def _():
        dk_ref[...] = jnp.zeros_like(dk_ref)
        dv_ref[...] = jnp.zeros_like(dv_ref)

    @pl.when(step < tiles)
    def _():
        rows = pl.ds(pl.multiple_of(step * BLOCK, BLOCK), BLOCK)
        dot_ref[...] = dot(wo_ref[...], dx_ref[rows, :], NT).astype(BF16)

    def run(block):
        n = reach(block)
        prefix = prefix_ref[step // blocks]
        tokens_here = pl.ds(pl.multiple_of(step * BLOCK, BLOCK), BLOCK)
        here = pl.ds(block * BLOCK, BLOCK)
        cosine, sine = cos_ref[:, here], sin_ref[:, here]

        def score(h):
            kh = h // groups
            own = slice(h * HEAD, (h + 1) * HEAD)
            keys = kv_ref[:n, kh * HEAD : (kh + 1) * HEAD]
            values = kv_ref[:n, kv_cols + kh * HEAD : kv_cols + (kh + 1) * HEAD]
            return scores_of(keys, qt_ref[own, :], prefix, block), dot(values, dot_ref[own, :])

        later = score(0)
        for h in range(heads):
            kh = h // groups
            own = slice(h * HEAD, (h + 1) * HEAD)
            kt = kt_ref[kh * HEAD : (kh + 1) * HEAD, :n]
            query, grad = qt_ref[own, :], dot_ref[own, :]
            delta = jnp.sum(grad.astype(F32) * ot_ref[own, tokens_here].astype(F32), 0, keepdims=True)
            scores, grad_probs = later
            if h + 1 < heads:
                later = score(h + 1)
            probs = jnp.exp2(scores - lse_ref[h : h + 1, :])
            grad_scores = (probs * (grad_probs - delta)).astype(BF16)
            dv_ref[kh, :, :n] += dot(grad, probs.astype(BF16), NT)
            dk_ref[kh, :, :n] += dot(query, grad_scores, NT)
            grad_query = turned(dot(kt, grad_scores), cosine, sine, -1.0)
            dt[own, tokens_here] = (grad_query * (1.0 / math.sqrt(HEAD))).astype(BF16)

    for block in range(blocks):
        pl.when((step < tiles) & (turn == block))(functools.partial(run, block))

    @pl.when((step < tiles) & (turn == blocks - 1))
    def _():
        sequence = pl.ds(pl.multiple_of((step // blocks) * length, length), length)
        for kh in range(kv_heads):
            rows = turned(dk_ref[kh], cos_ref[...], sin_ref[...], -1.0) * math.log(2.0)
            dt[q_cols + kh * HEAD : q_cols + (kh + 1) * HEAD, sequence] = rows.astype(BF16)
            start = q_cols + kv_cols + kh * HEAD
            dt[start : start + HEAD, sequence] = dv_ref[kh].astype(BF16)

    for j in range(thirds):
        @at(tiles + j)
        def _(j=j):
            across = dot(dt[...], n_ref[...])
            g_pack[j * cut : (j + 1) * cut, :qkv] = across.T.astype(BF16)

    def close(slot, grad):
        rows = pl.ds(pl.multiple_of(slot * BLOCK, BLOCK), BLOCK)
        x = own_ref[rows, :].astype(F32)
        inverse = lax.rsqrt(jnp.mean(x * x, -1, keepdims=True) + epsilon)
        normed = x * inverse
        back = inverse * (grad - normed * jnp.mean(grad * normed, -1, keepdims=True))
        grad_out[rows, :] = (trade.rows(dx_ref, slot, core)[...].astype(F32) + back).astype(BF16)

    first = tiles + thirds

    @pl.when(step > first)
    def _():
        trade.take(step - first - 1, close)

    @pl.when(step >= first)
    def _():
        rows = pl.ds(pl.multiple_of((step - first) * BLOCK, BLOCK), BLOCK)
        part = dot(dt[:, rows].T, w_ref[:, :qkv], NT)
        trade.give(step - first, part.astype(BF16))

    @at(first)
    def _():
        reduce.d(1)

    @at(first + 3)
    def _():
        reduce.b(2, (0,))

    @at(first + 6)
    def _():
        reduce.b(2, (1,))

    @at(first + tiles - 1)
    def _():
        trade.take(tiles - 1, close)
        reduce.b(2, (2, 3))
        reduce.c(2)
        reduce.d(2)
        for n in range(3):
            reduce.e2(n)
        for n in (1, 2):
            reduce.e1(n)
        trade.drain()


def back(prefix, qt, kv, kvt, lse, ot, dx, n, own, wo, pack, cosine, sine, begun, g_up, heads, kv_heads, length):
    tokens, width = dx.shape
    count, blocks, tiles = tokens // length, length // BLOCK, tokens // BLOCK
    slots = tiles // 2
    q_cols, kv_cols = heads * HEAD, kv_heads * HEAD
    shape = jax.ShapeDtypeStruct
    once = pl.Buffered(1)
    fixed = lambda a: pl.BlockSpec(a.shape, lambda i: (0,) * a.ndim, pipeline_mode=once)
    early = lambda i: jnp.minimum(i, tiles - 1)
    shards = [shape((g.shape[0] // 8, g.shape[1] * 2), BF16) for g in (pack, g_up, g_up)]
    return pl.pallas_call(
        functools.partial(back_kernel, heads, kv_heads, blocks),
        grid=(2 * tiles + 3,),
        in_specs=[
            pl.BlockSpec(memory_space=pltpu.SMEM),
            pl.BlockSpec((q_cols, BLOCK), lambda i: (0, early(i))),
            pl.BlockSpec((length, 2 * kv_cols), lambda i: (early(i) // blocks, 0)),
            pl.BlockSpec((kv_cols, length), lambda i: (0, early(i) // blocks)),
            pl.BlockSpec((heads, BLOCK), lambda i: (0, early(i))),
        ]
        + [fixed(ot), fixed(dx), pl.BlockSpec((tokens, width // 3), lambda i: (0, jnp.clip(i - tiles, 0, 2)))]
        + [ANY, fixed(wo), ANY]
        + [fixed(a) for a in (cosine, sine, begun)]
        + [ANY],
        out_specs=(fixed(own), ANY, ANY, ANY),
        out_shape=[shape(own.shape, BF16)] + shards,
        scratch_shapes=[
            pltpu.VMEM((q_cols, BLOCK), BF16),
            pltpu.VMEM((kv_heads, HEAD, length), F32),
            pltpu.VMEM((kv_heads, HEAD, length), F32),
            pltpu.VMEM((q_cols + 2 * kv_cols, tokens), BF16),
            pltpu.VMEM(pack.shape, BF16),
            pltpu.VMEM(wo.shape, BF16),
            pltpu.VMEM((q_cols, q_cols), BF16),
            pltpu.VMEM((q_cols, q_cols), BF16),
            pltpu.VMEM(own.shape, BF16),
            pltpu.VMEM(pack.shape, BF16),
            DMA((2,)),
            DMA((2,)),
        ]
        + Trade.buffers(slots, width)
        + Trade.semaphores(slots)
        + Reduce.buffers([halves_of(*g.shape, True) for g in (g_up, g_up, pack)], near=(2,), begun=(0,))
        + Reduce.semaphores(3),
        compiler_params=pltpu.CompilerParams(collective_id=4, has_side_effects=True, vmem_limit_bytes=62 * 2**20),
        name="back",
    )(prefix, qt, kv, kvt, lse, ot, dx, n, own, wo, pack, cosine, sine, begun, g_up)


def tables(length):
    frequency = np.float32(10000.0) ** (-np.arange(HEAD // 2, dtype=np.float32) * np.float32(2.0) / np.float32(HEAD))
    angles = frequency[:, None] * np.arange(length, dtype=np.float32)[None, :]
    return jnp.asarray(np.cos(angles)), jnp.asarray(np.sin(angles))


def paired(
    activations_in,
    prefix_len,
    attn_gain,
    query_weight,
    key_weight,
    value_weight,
    out_weight,
    ffn_gain,
    gate_weight,
    up_weight,
    down_weight,
    cotangent,
):
    micro, seq_count, span, width = activations_in.shape
    count, length = micro * seq_count, 2 * span
    heads, kv_heads = HEADS // 2, KV_HEADS // 2

    own_x = activations_in.reshape(count, span, width)
    own_dy = cotangent.reshape(count, span, width)

    gain_attn, gain_ffn = attn_gain[None, :], ffn_gain[None, :]
    pack, gate_part, full_x, full_dy = start(
        own_x, own_dy, query_weight, key_weight, value_weight, out_weight, gate_weight, gain_attn, gain_ffn, heads, kv_heads
    )
    cosine, sine = tables(length)
    prefix = prefix_len.reshape(count)
    normed_one, qt, kvt, kv, ot, lse, w_out, middle, inverse, full_two, w_gate, w_up, w_down = front(
        prefix, full_x, own_x.reshape(count * span, width), pack, gate_part, up_weight, down_weight, gain_ffn, cosine, sine,
        heads, kv_heads, length,
    )
    core = lax.axis_index("ctx").astype(jnp.int32).reshape(1)
    hidden, by_up, by_gate, mine, theirs = feed(core, full_two, w_gate, w_up, w_down, length)
    result = middle + mine.astype(F32) + lax.ppermute(theirs, "ctx", [(0, 1), (1, 0)]).astype(F32)
    grad_down = dot(hidden, full_dy, TN).astype(BF16)
    _, grad_up, full_dx, r_down, begun = feed_back(
        full_dy, by_up, by_gate, full_two, w_gate, w_up, w_down, inverse, grad_down, length
    )
    grad_inputs, r_pack, r_gate, r_up = back(
        prefix, qt, kv, kvt, lse, ot, full_dx, normed_one, own_x.reshape(count * span, width), w_out, pack, cosine, sine,
        begun, grad_up, heads, kv_heads, length,
    )
    g_q, g_k, g_v, g_o, g_gate, g_up, g_down, g_ga, g_gf = finish(
        r_pack, r_gate, r_up, r_down, query_weight, key_weight, value_weight, out_weight, gate_weight, up_weight, gain_attn, gain_ffn,
        heads, kv_heads,
    )
    shape = activations_in.shape
    return (
        result.astype(BF16).reshape(shape),
        grad_inputs.reshape(shape),
        g_ga.reshape(-1),
        g_q,
        g_k,
        g_v,
        g_o,
        g_gf.reshape(-1),
        g_gate,
        g_up,
        g_down,
    )


def solution(mesh):
    small = dict(mesh.shape) == {"grp": 4, "fsdp": 4, "ctx": 2}

    return jax.shard_map(
        paired if small else local,
        mesh=mesh,
        in_specs=(
            P(None, ("grp", "fsdp"), "ctx", None),
            P(None, ("grp", "fsdp")),
            P(("fsdp", "ctx")),
            P(("fsdp", "ctx"), None),
            P(("fsdp", "ctx"), None),
            P(("fsdp", "ctx"), None),
            P(("fsdp", "ctx"), None),
            P(("fsdp", "ctx")),
            P(("fsdp", "ctx"), None),
            P(("fsdp", "ctx"), None),
            P(("fsdp", "ctx"), None),
            P(None, ("grp", "fsdp"), "ctx", None),
        ),
        out_specs=(
            P(None, ("grp", "fsdp"), "ctx", None),
            P(None, ("grp", "fsdp"), "ctx", None),
            P(("fsdp", "ctx")),
            P(("fsdp", "ctx"), None),
            P(("fsdp", "ctx"), None),
            P(("fsdp", "ctx"), None),
            P(("fsdp", "ctx"), None),
            P(("fsdp", "ctx")),
            P(("fsdp", "ctx"), None),
            P(("fsdp", "ctx"), None),
            P(("fsdp", "ctx"), None),
        ),
        check_vma=False,
    )
```

```python
import functools
import math

import jax
import jax.numpy as jnp
import numpy as np
from jax import lax
from jax.experimental import pallas as pl
from jax.experimental.pallas import tpu as pltpu
from jax.sharding import PartitionSpec as P

HEADS = 18
KV_HEADS = 6
HEAD = 64


epsilon = 1e-05


def shortened(array):

    def short(part):
        return part.astype(jnp.bfloat16) if part.dtype == jnp.float32 else part

    return jax.tree.map(short, array)


def rotary_tables(positions):
    halfway = HEAD // 2
    frequency = 10000.0 ** (-jnp.arange(halfway, dtype=jnp.float32) * 2.0 / HEAD)
    angles = positions.astype(jnp.float32)[:, None] * frequency[None, :]
    return (jnp.cos(angles)[:, None, :], jnp.sin(angles)[:, None, :])


def rotate(values, cosine, sine):
    halfway = values.shape[-1] // 2
    first = values[..., :halfway]
    second = values[..., halfway:]
    return jnp.concatenate([first * cosine - second * sine, second * cosine + first * sine], -1)


def rotate_back(values, cosine, sine):
    halfway = values.shape[-1] // 2
    first = values[..., :halfway]
    second = values[..., halfway:]
    return jnp.concatenate([first * cosine + second * sine, second * cosine - first * sine], -1)


def norm_back(grad_normed, normed, inverse):
    return inverse * (grad_normed - normed * jnp.mean(grad_normed * normed, -1, keepdims=True))


def flatten_all(grads):
    return tuple((g.reshape(-1) for g in grads))


def local(
    activations_in,
    prefix_len,
    attn_gain,
    query_weight,
    key_weight,
    value_weight,
    out_weight,
    ffn_gain,
    gate_weight,
    up_weight,
    down_weight,
    cotangent,
):
    micro, seq_count, span, width = activations_in.shape
    rows = seq_count * span
    length = span * lax.axis_size("ctx")
    groups = HEADS // KV_HEADS
    scale = 1.0 / math.sqrt(HEAD)
    shards = (
        attn_gain,
        query_weight,
        key_weight,
        value_weight,
        out_weight,
        ffn_gain,
        gate_weight,
        up_weight,
        down_weight,
    )
    offset = lax.axis_index("ctx") * span
    query_pos = offset + jnp.arange(span, dtype=jnp.int32)
    key_pos = jnp.arange(length, dtype=jnp.int32)
    cosine, sine = rotary_tables(jnp.tile(query_pos, seq_count))

    def visibility(prefix):
        return (key_pos[None, :] <= query_pos[:, None]) | (key_pos[None, :] < prefix)

    def attend(item):
        query, keys, values, prefix = item
        scores = (
            jnp.einsum("qhgd,khd->hgqk", query, keys, preferred_element_type=jnp.float32) * scale
        )
        scores = jnp.where(visibility(prefix), scores, -1e30)
        peak = jnp.max(scores, -1, keepdims=True)
        weights = jnp.exp(scores - peak)
        totals = jnp.sum(weights, -1, keepdims=True)
        probs = (weights / totals).astype(jnp.bfloat16)
        mixed = jnp.einsum("hgqk,khd->qhgd", probs, values, preferred_element_type=jnp.float32)
        return (mixed.reshape(span, HEADS * HEAD), (peak + jnp.log(totals))[..., 0])

    def attend_back(item):
        query, keys, values, prefix, log_total, grad_mixed = item
        scores = (
            jnp.einsum("qhgd,khd->hgqk", query, keys, preferred_element_type=jnp.float32) * scale
        )
        probs = jnp.where(visibility(prefix), jnp.exp(scores - log_total[..., None]), 0.0)
        grad_probs = jnp.einsum(
            "qhgd,khd->hgqk", grad_mixed, values, preferred_element_type=jnp.float32
        )
        grad_scores = (
            probs * (grad_probs - jnp.sum(probs * grad_probs, -1, keepdims=True))
        ).astype(jnp.bfloat16)
        grad_query = (
            jnp.einsum("hgqk,khd->qhgd", grad_scores, keys, preferred_element_type=jnp.float32)
            * scale
        )
        grad_keys = (
            jnp.einsum("hgqk,qhgd->khd", grad_scores, query, preferred_element_type=jnp.float32)
            * scale
        )
        grad_values = jnp.einsum(
            "hgqk,qhgd->khd",
            probs.astype(jnp.bfloat16),
            grad_mixed,
            preferred_element_type=jnp.float32,
        )
        return (
            grad_query.reshape(span, HEADS * HEAD),
            grad_keys.reshape(length, KV_HEADS * HEAD),
            grad_values.reshape(length, KV_HEADS * HEAD),
        )

    outputs = []
    input_grads = []
    collected = None
    for index in range(micro):
        full = (
            lax.all_gather(shards[0], ("fsdp", "ctx"), axis=0, tiled=True),
            lax.all_gather(shards[1], ("fsdp", "ctx"), axis=0, tiled=True),
            lax.all_gather(shards[2], ("fsdp", "ctx"), axis=0, tiled=True),
            lax.all_gather(shards[3], ("fsdp", "ctx"), axis=0, tiled=True),
            lax.all_gather(shards[4], ("fsdp", "ctx"), axis=0, tiled=True),
            lax.all_gather(shards[5], ("fsdp", "ctx"), axis=0, tiled=True),
            lax.all_gather(shards[6], ("fsdp", "ctx"), axis=0, tiled=True),
            lax.all_gather(shards[7], ("fsdp", "ctx"), axis=0, tiled=True),
            lax.all_gather(shards[8], ("fsdp", "ctx"), axis=0, tiled=True),
        )
        gain_attn, w_query, w_key, w_value, w_out, gain_ffn, w_gate, w_up, w_down = full
        inputs = activations_in[index].reshape(rows, width).astype(jnp.float32)
        inverse_one = lax.rsqrt(jnp.mean(inputs * inputs, -1, keepdims=True) + epsilon)
        normed_one = inputs * inverse_one
        first_in = (normed_one * gain_attn).astype(jnp.bfloat16)
        query_lin = jnp.dot(first_in, w_query, preferred_element_type=jnp.float32)
        key_lin = jnp.dot(first_in, w_key, preferred_element_type=jnp.float32)
        value_lin = jnp.dot(first_in, w_value, preferred_element_type=jnp.float32)
        query_rot = rotate(query_lin.reshape(rows, HEADS, HEAD), cosine, sine).astype(jnp.bfloat16)
        key_rot = rotate(key_lin.reshape(rows, KV_HEADS, HEAD), cosine, sine).astype(jnp.bfloat16)
        key_rot = key_rot.reshape(seq_count, span, KV_HEADS * HEAD)
        value_low = value_lin.astype(jnp.bfloat16).reshape(seq_count, span, KV_HEADS * HEAD)
        key_all, value_all = (
            lax.all_gather(key_rot, "ctx", axis=1, tiled=True),
            lax.all_gather(value_low, "ctx", axis=1, tiled=True),
        )
        query_split = query_rot.reshape(seq_count, span, KV_HEADS, groups, HEAD)
        key_split = key_all.reshape(seq_count, length, KV_HEADS, HEAD)
        value_split = value_all.reshape(seq_count, length, KV_HEADS, HEAD)
        mixed_all, log_totals = lax.map(
            attend, (query_split, key_split, value_split, prefix_len[index])
        )
        attn_low = mixed_all.reshape(rows, HEADS * HEAD).astype(jnp.bfloat16)
        middle = inputs + jnp.dot(attn_low, w_out, preferred_element_type=jnp.float32)
        inverse_two = lax.rsqrt(jnp.mean(middle * middle, -1, keepdims=True) + epsilon)
        normed_two = middle * inverse_two
        second_in = (normed_two * gain_ffn).astype(jnp.bfloat16)
        gate = jnp.dot(second_in, w_gate, preferred_element_type=jnp.float32)
        upward = jnp.dot(second_in, w_up, preferred_element_type=jnp.float32)
        hidden = (jax.nn.silu(gate) * upward).astype(jnp.bfloat16)
        result = middle + jnp.dot(hidden, w_down, preferred_element_type=jnp.float32)
        outputs.append(result.astype(jnp.bfloat16).reshape(seq_count, span, width))
        back = (
            lax.all_gather(shards[0], ("fsdp", "ctx"), axis=0, tiled=True),
            lax.all_gather(shards[1], ("fsdp", "ctx"), axis=0, tiled=True),
            lax.all_gather(shards[2], ("fsdp", "ctx"), axis=0, tiled=True),
            lax.all_gather(shards[3], ("fsdp", "ctx"), axis=0, tiled=True),
            lax.all_gather(shards[4], ("fsdp", "ctx"), axis=0, tiled=True),
            lax.all_gather(shards[5], ("fsdp", "ctx"), axis=0, tiled=True),
            lax.all_gather(shards[6], ("fsdp", "ctx"), axis=0, tiled=True),
            lax.all_gather(shards[7], ("fsdp", "ctx"), axis=0, tiled=True),
            lax.all_gather(shards[8], ("fsdp", "ctx"), axis=0, tiled=True),
        )
        gain_attn, w_query, w_key, w_value, w_out, gain_ffn, w_gate, w_up, w_down = back
        grad_y = cotangent[index].reshape(rows, width).astype(jnp.float32)
        grad_y_low = grad_y.astype(jnp.bfloat16)
        grad_wdown = jnp.einsum("rf,rd->fd", hidden, grad_y_low, preferred_element_type=jnp.float32)
        grad_hidden = jnp.einsum(
            "rd,fd->rf", grad_y_low, w_down, preferred_element_type=jnp.float32
        )
        sigma = jax.nn.sigmoid(gate)
        grad_up_low = (grad_hidden * gate * sigma).astype(jnp.bfloat16)
        grad_gate_low = (grad_hidden * upward * sigma * (1.0 + gate * (1.0 - sigma))).astype(
            jnp.bfloat16
        )
        grad_wgate = jnp.einsum(
            "rd,rf->df", second_in, grad_gate_low, preferred_element_type=jnp.float32
        )
        grad_wup = jnp.einsum(
            "rd,rf->df", second_in, grad_up_low, preferred_element_type=jnp.float32
        )
        grad_second = jnp.einsum(
            "rf,df->rd", grad_gate_low, w_gate, preferred_element_type=jnp.float32
        ) + jnp.einsum("rf,df->rd", grad_up_low, w_up, preferred_element_type=jnp.float32)
        grad_gain_ffn = jnp.sum(grad_second * normed_two, 0)
        grad_middle = grad_y + norm_back(grad_second * gain_ffn, normed_two, inverse_two)
        grad_branch_low = grad_middle.astype(jnp.bfloat16)
        grad_wout = jnp.einsum(
            "ra,rd->ad", attn_low, grad_branch_low, preferred_element_type=jnp.float32
        )
        grad_attn_low = jnp.einsum(
            "rd,ad->ra", grad_branch_low, w_out, preferred_element_type=jnp.float32
        ).astype(jnp.bfloat16)
        grad_mixed = grad_attn_low.reshape(seq_count, span, KV_HEADS, groups, HEAD)
        grad_query_rot, grad_key_part, grad_value_part = lax.map(
            attend_back,
            (query_split, key_split, value_split, prefix_len[index], log_totals, grad_mixed),
        )
        grad_key_own, grad_value_own = (
            lax.psum_scatter(
                grad_key_part.astype(jnp.bfloat16), "ctx", scatter_dimension=1, tiled=True
            ).astype(jnp.float32),
            lax.psum_scatter(
                grad_value_part.astype(jnp.bfloat16), "ctx", scatter_dimension=1, tiled=True
            ).astype(jnp.float32),
        )
        grad_query = rotate_back(grad_query_rot.reshape(rows, HEADS, HEAD), cosine, sine)
        grad_query = grad_query.reshape(rows, HEADS * HEAD).astype(jnp.bfloat16)
        grad_key = rotate_back(grad_key_own.reshape(rows, KV_HEADS, HEAD), cosine, sine)
        grad_key = grad_key.reshape(rows, KV_HEADS * HEAD).astype(jnp.bfloat16)
        grad_value = grad_value_own.reshape(rows, KV_HEADS * HEAD).astype(jnp.bfloat16)
        grad_wquery = jnp.einsum(
            "rd,rq->dq", first_in, grad_query, preferred_element_type=jnp.float32
        )
        grad_wkey = jnp.einsum("rd,rq->dq", first_in, grad_key, preferred_element_type=jnp.float32)
        grad_wvalue = jnp.einsum(
            "rd,rq->dq", first_in, grad_value, preferred_element_type=jnp.float32
        )
        grad_first = (
            jnp.einsum("rq,dq->rd", grad_query, w_query, preferred_element_type=jnp.float32)
            + jnp.einsum("rq,dq->rd", grad_key, w_key, preferred_element_type=jnp.float32)
            + jnp.einsum("rq,dq->rd", grad_value, w_value, preferred_element_type=jnp.float32)
        )
        grad_gain_attn = jnp.sum(grad_first * normed_one, 0)
        grad_inputs = grad_middle + norm_back(grad_first * gain_attn, normed_one, inverse_one)
        input_grads.append(grad_inputs.astype(jnp.bfloat16).reshape(seq_count, span, width))
        grads = flatten_all(
            (
                grad_gain_attn,
                grad_wquery,
                grad_wkey,
                grad_wvalue,
                grad_wout,
                grad_gain_ffn,
                grad_wgate,
                grad_wup,
                grad_wdown,
            )
        )
        pieces = lax.psum_scatter(grads, ("fsdp", "ctx"), scatter_dimension=0, tiled=True)
        if index == 0:
            collected = pieces
        else:
            collected = tuple((a + b for a, b in zip(collected, pieces)))
    summed = jax.tree.map(
        lambda part: part.astype(jnp.float32), lax.psum(shortened(collected), "grp")
    )
    shaped = tuple((s.reshape(w.shape) for s, w in zip(summed, shards)))
    return (
        jnp.stack(outputs, 0),
        jnp.stack(input_grads, 0),
        shaped[0],
        shaped[1],
        shaped[2],
        shaped[3],
        shaped[4],
        shaped[5],
        shaped[6],
        shaped[7],
        shaped[8],
    )


BLOCK = 256
TO_LOG2 = math.log2(math.e) / math.sqrt(HEAD)
F32, BF16 = jnp.float32, jnp.bfloat16
NN = (((1,), (0,)), ((), ()))
NT = (((1,), (1,)), ((), ()))
TN = (((0,), (0,)), ((), ()))


def dot(a, b, dims=NN):
    return lax.dot_general(a, b, dims, preferred_element_type=F32)


def turned(rows, cosine, sine, sign):
    a, b = rows[: HEAD // 2], rows[HEAD // 2 :]
    return jnp.concatenate([a * cosine - sign * b * sine, b * cosine + sign * a * sine], 0)


def masked(scores, prefix, first, block):
    key = first + lax.broadcasted_iota(jnp.int32, scores.shape, 0)
    query = block * BLOCK + lax.broadcasted_iota(jnp.int32, scores.shape, 1)
    return jnp.where((key <= query) | (key < prefix), scores, -1e30)


def reach(block):
    return max(2, block + 1) * BLOCK


def scores_of(keys, query, prefix, block):
    clear = block * BLOCK
    edge = masked(dot(keys[clear:], query), prefix, clear, block)
    if not clear:
        return edge
    return jnp.concatenate([dot(keys[:clear], query), edge], 0)


MESH = pl.DeviceIdType.MESH
DMA = pltpu.SemaphoreType.DMA
ANY = pl.BlockSpec(memory_space=pl.ANY)
VMEM = pl.BlockSpec(memory_space=pltpu.VMEM)


def where_am_i():
    return lax.axis_index("grp"), lax.axis_index("fsdp"), lax.axis_index("ctx")


def remote(src, dst, send, recv, grp, fsdp, ctx):
    return pltpu.make_async_remote_copy(
        src_ref=src,
        dst_ref=dst,
        send_sem=send,
        recv_sem=recv,
        device_id={"grp": grp, "fsdp": fsdp, "ctx": ctx},
        device_id_type=MESH,
    )


def greet(partners):
    barrier = pltpu.get_barrier_semaphore()
    for grp, fsdp, ctx in partners:
        pl.semaphore_signal(
            barrier, inc=1, device_id={"grp": grp, "fsdp": fsdp, "ctx": ctx}, device_id_type=MESH
        )
    pl.semaphore_wait(barrier, len(partners))


class Columns:
    split = True

    def __init__(self, core, shard, out):
        self.core, self.shard, self.out = core, shard, out
        self.rows, self.cols = shard.shape[0], out.shape[1] // 4

    def mine(self, j, quarter):
        to = self.core if j == 0 else 1 - self.core
        return self.shard.at[:, pl.ds(pl.multiple_of((2 * quarter + to) * self.cols, 128), self.cols)]

    def block(self, plane, j, quarter):
        owner = self.core if j == 0 else 1 - self.core
        start = pl.multiple_of((2 * plane + owner) * self.rows, 16)
        return self.out.at[pl.ds(start, self.rows), pl.ds(pl.multiple_of(quarter * self.cols, 128), self.cols)]


class Rows:
    split = False

    def __init__(self, core, shard, out):
        self.core, self.shard, self.out = core, shard, out
        self.rows = out.shape[0] // 32

    def mine(self, j, quarter):
        return self.shard.at[pl.ds(pl.multiple_of((2 * quarter + j) * self.rows, 16), self.rows), :]

    def block(self, plane, j, quarter):
        start = pl.multiple_of((8 * plane + 2 * quarter + j) * self.rows, 16)
        return self.out.at[pl.ds(start, self.rows), :]

    def own(self, plane):
        return self.out.at[pl.ds(pl.multiple_of(plane * 8 * self.rows, 16), 8 * self.rows), :]


class Gather:
    @staticmethod
    def semaphores(count):
        return [DMA((count, 4)), DMA((count, 4)), DMA((count, 4))] + [DMA((count, 3, 2))] * 2 + [DMA((count, 3, 2, 2))] * 2 + [DMA((count, 3, 2))] * 2

    def __init__(self, units, sems):
        self.units, self.sems = units, sems
        self.grp, self.plane, self.core = where_am_i()
        self.side = self.grp + 1 - 2 * lax.rem(self.grp, 2)
        self.up = lax.rem(self.grp + 2, 4)
        self.planes = [lax.rem(self.plane + s, 4) for s in (1, 2, 3)]
        self.origins = [lax.rem(self.plane + 4 - s, 4) for s in (1, 2, 3)]
        self.left = []

    def partners(self):
        grp, plane, core = self.grp, self.plane, self.core
        found = [(grp, z, c) for z in self.planes for c in (core, 1 - core)]
        return found + [(grp, plane, 1 - core), (self.side, plane, core), (self.up, plane, core)]

    def other(self, j):
        return self.core if j == 0 else 1 - self.core

    def send(self, src, dst, send, recv, grp, plane, core):
        copy = remote(src, dst, send, recv, grp, plane, core)
        copy.start()
        self.left.append(copy.wait_send)

    def got(self, here, send, recv):
        remote(here, here, send, recv, self.side, self.plane, self.core).wait_recv()

    def first(self, n):
        u = self.units[n]
        loc, near_s, near_r, z_s, z_r = self.sems[:5]
        for i, z in enumerate(self.planes):
            for j in range(2):
                if u.split:
                    dst = u.block(self.plane, 0, self.grp)
                    self.send(u.mine(j, self.grp), dst, z_s.at[n, i, j], z_r.at[n, i, j], self.grp, z, self.other(j))
                else:
                    dst = u.block(self.plane, j, self.grp)
                    self.send(u.mine(j, self.grp), dst, z_s.at[n, i, j], z_r.at[n, i, j], self.grp, z, self.core)
        if u.split:
            for q in range(4):
                dst = u.block(self.plane, 0, q)
                self.send(u.mine(1, q), dst, near_s.at[n, q], near_r.at[n, q], self.grp, self.plane, 1 - self.core)
                copy = pltpu.make_async_copy(u.mine(0, q), dst, loc.at[n, q])
                copy.start()
                self.left.append(copy.wait)
        else:
            copy = pltpu.make_async_copy(u.shard, u.own(self.plane), loc.at[n, 0])
            copy.start()
            self.left.append(copy.wait)

    def first_in(self, n):
        u = self.units[n]
        for i, z in enumerate(self.origins):
            for j in range(2):
                self.got(u.block(z, j, self.grp), self.sems[3].at[n, i, j], self.sems[4].at[n, i, j])

    def near_in(self, n):
        u = self.units[n]
        if u.split:
            for q in range(4):
                self.got(u.block(self.plane, 1, q), self.sems[1].at[n, q], self.sems[2].at[n, q])

    def second(self, n, here=False):
        u = self.units[n]
        z_s, z_r, xy_s, xy_r = self.sems[3:7]
        for i, z in enumerate(self.origins):
            for j in range(2):
                block = u.block(z, j, self.grp)
                if not here:
                    self.got(block, z_s.at[n, i, j], z_r.at[n, i, j])
                for t, to in enumerate((self.side, self.up)):
                    self.send(block, block, xy_s.at[n, i, j, t], xy_r.at[n, i, j, t], to, self.plane, self.core)

    def third(self, n):
        u = self.units[n]
        xy_s, xy_r, fw_s, fw_r = self.sems[5:9]
        for i, z in enumerate(self.origins):
            for t, (origin, to) in enumerate(((self.side, self.up), (self.up, self.side))):
                block = u.block(z, t, origin)
                self.got(block, xy_s.at[n, i, t, t], xy_r.at[n, i, t, t])
                self.send(block, block, fw_s.at[n, i, t], fw_r.at[n, i, t], to, self.plane, self.core)

    def last(self, n):
        u = self.units[n]
        xy_s, xy_r, fw_s, fw_r = self.sems[5:9]
        for i, z in enumerate(self.origins):
            for t, origin in enumerate((self.side, self.up)):
                self.got(u.block(z, 1 - t, origin), xy_s.at[n, i, 1 - t, t], xy_r.at[n, i, 1 - t, t])
            for t in range(2):
                self.got(u.block(z, t, 3 - self.grp), fw_s.at[n, i, t], fw_r.at[n, i, t])

    def sent_all(self, firsts, rest):
        loc, near_s, near_r, z_s, z_r, xy_s, xy_r, fw_s, fw_r = self.sems

        def out(block, send, recv):
            remote(block, block, send, recv, self.side, self.plane, self.core).wait_send()

        for n in firsts:
            u = self.units[n]
            for i in range(3):
                for j in range(2):
                    out(u.block(self.plane, j, self.grp), z_s.at[n, i, j], z_r.at[n, i, j])
            if u.split:
                for q in range(4):
                    out(u.block(self.plane, 0, q), near_s.at[n, q], near_r.at[n, q])
                    pltpu.make_async_copy(u.mine(0, q), u.block(self.plane, 0, q), loc.at[n, q]).wait()
            else:
                pltpu.make_async_copy(u.shard, u.own(self.plane), loc.at[n, 0]).wait()
        for n in rest:
            u = self.units[n]
            for i, z in enumerate(self.origins):
                for j in range(2):
                    for t in range(2):
                        out(u.block(z, j, self.grp), xy_s.at[n, i, j, t], xy_r.at[n, i, j, t])
                for t, origin in enumerate((self.side, self.up)):
                    out(u.block(z, t, origin), fw_s.at[n, i, t], fw_r.at[n, i, t])

    def drain(self):
        for wait in self.left:
            wait()
        self.left = []


def upright(row_ref):
    return jnp.broadcast_to(row_ref[...].astype(F32), (8, row_ref.shape[1])).T[:, :1]


def start_kernel(heads, kv_heads, x_ref, dy_ref, wq_ref, wk_ref, wv_ref, wo_ref, gate_ref, ga_ref, gf_ref,
                 pack_out, gate_out, x_out, dy_out, pack, gate, trade_s, trade_r, own_s, *sems):
    _, _, core = where_am_i()
    q_cols, kv_cols, span = heads * HEAD, kv_heads * HEAD, x_ref.shape[1]
    cols = pack.shape[1] // 8
    gain = upright(ga_ref)
    for k in range(2):
        parts = [(wq_ref[:, k * q_cols : (k + 1) * q_cols].astype(F32) * gain).astype(BF16)]
        parts += [(w[:, k * kv_cols : (k + 1) * kv_cols].astype(F32) * gain).astype(BF16) for w in (wk_ref, wv_ref)]
        row = jnp.concatenate(parts + [wo_ref[:, k * q_cols : (k + 1) * q_cols]], 1)
        for q in range(4):
            pack[:, (2 * q + k) * cols : (2 * q + k + 1) * cols] = row[:, q * cols : (q + 1) * cols]
    gather = Gather([Columns(core, pack, pack_out), Columns(core, gate, gate_out)], sems)
    greet(gather.partners())
    gather.first(0)
    gate[...] = (gate_ref[...].astype(F32) * upright(gf_ref)).astype(BF16)
    waits = []

    def trade(ref, out, which):
        for s in range(ref.shape[0]):
            def rows(owner):
                return out.at[pl.ds(pl.multiple_of((2 * s + owner) * span, 16), span), :]
            copy = remote(ref.at[s], rows(core), trade_s.at[which, s], trade_r.at[which, s], gather.grp, gather.plane, 1 - core)
            copy.start()
            gather.left.append(copy.wait_send)
            copy = pltpu.make_async_copy(ref.at[s], rows(core), own_s.at[which, s])
            copy.start()
            gather.left.append(copy.wait)
            waits.append((rows(1 - core), trade_s.at[which, s], trade_r.at[which, s]))

    trade(x_ref, x_out, 0)
    gather.second(0)
    gather.first(1)
    trade(dy_ref, dy_out, 1)
    gather.third(0)
    gather.last(0)
    gather.near_in(0)
    gather.near_in(1)
    for wait in waits:
        gather.got(*wait)
    gather.first_in(1)
    gather.drain()


def start(x, dy, wq, wk, wv, wo, gate, gain_attn, gain_ffn, heads, kv_heads):
    count, span, width = x.shape
    shard, hidden = gate.shape
    cols = 2 * (heads + kv_heads) * HEAD
    shape = jax.ShapeDtypeStruct
    return pl.pallas_call(
        functools.partial(start_kernel, heads, kv_heads),
        grid=(1,),
        in_specs=[pl.BlockSpec(a.shape, lambda i, n=a.ndim: (0,) * n) for a in (x, dy, wq, wk, wv, wo, gate, gain_attn, gain_ffn)],
        out_specs=(ANY,) * 4,
        out_shape=(
            shape((8 * shard, cols), BF16),
            shape((8 * shard, hidden // 2), BF16),
            shape((2 * count * span, width), BF16),
            shape((2 * count * span, width), BF16),
        ),
        scratch_shapes=[pltpu.VMEM((shard, 2 * cols), BF16), pltpu.VMEM((shard, hidden), BF16)]
        + [DMA((2, count))] * 3
        + Gather.semaphores(2),
        compiler_params=pltpu.CompilerParams(collective_id=0, has_side_effects=True, vmem_limit_bytes=62 * 2**20),
        name="start",
    )(x, dy, wq, wk, wv, wo, gate, gain_attn, gain_ffn)


def front_kernel(heads, kv_heads, blocks, prefix_ref, x_ref, own_ref, w_ref, up_ref, gf_ref, cos_ref, sin_ref, gate_in, down_ref,
                 n_ref, qt_out, kvt_out, kv_out, ot_out, lse_ref, wo_ref, x1_out, inv_ref, two_out, gate_out, up_out, down_out,
                 qt_ref, kvt_ref, kv_ref, ot_ref, x1_ref, flush_sem, ot_sem, x1_sem, up_s, wo_send, wo_recv, part_mine, part_send, part_recv, two_mine,
                 wo_sem, part_sem, two_sem, own_sem, *sems):
    step = pl.program_id(0)
    grp, plane, core = where_am_i()
    count = prefix_ref.shape[0]
    tiles = count * blocks
    groups = heads // kv_heads
    q_cols, kv_cols = heads * HEAD, kv_heads * HEAD
    width = x_ref.shape[1]
    half = blocks // 2
    gather = Gather([Columns(core, up_s, gate_out), Columns(core, up_s, up_out), Rows(core, down_ref, down_out)], sems)

    def at(when):
        return pl.when(step == when)

    def out_weight(owner):
        return w_ref[pl.ds(pl.multiple_of(owner * q_cols, 16), q_cols), q_cols + 2 * kv_cols :]

    def flush():
        pairs = ((qt_ref, qt_out), (kvt_ref, kvt_out), (kv_ref, kv_out))
        return [pltpu.make_async_copy(a, b, flush_sem.at[k]) for k, (a, b) in enumerate(pairs)]

    def ot_flush(turn):
        cols = pl.ds(pl.multiple_of(turn * BLOCK, BLOCK), BLOCK)
        return pltpu.make_async_copy(ot_ref.at[:, cols], ot_out.at[:, cols], ot_sem.at[turn])

    def x1_flush(slot):
        rows = pl.ds(pl.multiple_of(slot * BLOCK, BLOCK), BLOCK)
        return pltpu.make_async_copy(x1_ref.at[rows, :], x1_out.at[rows, :], x1_sem.at[slot])

    def wo_copy():
        return remote(wo_send, wo_recv, wo_sem.at[0], wo_sem.at[1], grp, plane, 1 - core)

    @at(0)
    def _():
        greet(gather.partners())
        gather.second(0, here=True)
        wo_send[...] = out_weight(1 - core)
        wo_copy().start()
        up_s[...] = (up_ref[...].astype(F32) * upright(gf_ref)).astype(BF16)
        gather.first(1)

    @at(tiles - 1)
    def _():
        wo_copy().wait()
        mine, other = out_weight(core), wo_recv[...]
        wo_ref[...] = jnp.concatenate([jnp.where(core == 0, mine, other), jnp.where(core == 0, other, mine)], 1)

    @at(tiles)
    def _():
        for copy in flush():
            copy.start()
        gather.first(2)
        gather.third(0)

    @at(tiles + 1)
    def _():
        gather.second(1)

    @at(tiles + 4)
    def _():
        gather.third(1)

    @at(tiles + 5)
    def _():
        gather.second(2)

    @pl.when(step < tiles)
    def _():
        x = x_ref[...].astype(F32)
        normed = (x * lax.rsqrt(jnp.mean(x * x, -1, keepdims=True) + epsilon)).astype(BF16)
        n_ref[...] = normed
        flat = dot(normed, w_ref[:, : q_cols + 2 * kv_cols])
        across = flat.T
        tokens = pl.ds(pl.multiple_of(step * BLOCK, BLOCK), BLOCK)
        here = pl.ds(pl.multiple_of(lax.rem(step, blocks) * BLOCK, BLOCK), BLOCK)
        cosine, sine = cos_ref[:, here], sin_ref[:, here]
        for h in range(heads):
            rows = turned(across[h * HEAD : (h + 1) * HEAD], cosine, sine, 1.0)
            qt_ref[h * HEAD : (h + 1) * HEAD, tokens] = (rows * TO_LOG2).astype(BF16)
        keys = [across[q_cols + h * HEAD : q_cols + (h + 1) * HEAD] for h in range(kv_heads)]
        keys = jnp.concatenate([turned(rows, cosine, sine, 1.0) for rows in keys], 0)
        kvt_ref[:kv_cols, tokens] = keys.astype(BF16)
        kvt_ref[kv_cols:, tokens] = across[q_cols + kv_cols :].astype(BF16)
        kv_ref[tokens, :kv_cols] = keys.T.astype(BF16)
        kv_ref[tokens, kv_cols:] = flat[:, q_cols + kv_cols :].astype(BF16)

    def rows_of(tile, owner):
        start = (tile // half) * blocks + owner * half + lax.rem(tile, half)
        return two_out.at[pl.ds(pl.multiple_of(start * BLOCK, BLOCK), BLOCK), :]

    def part_copy(slot):
        return remote(part_send.at[slot], part_recv.at[slot], part_sem.at[0, slot], part_sem.at[1, slot], grp, plane, 1 - core)

    def two_copy(slot):
        there = rows_of(slot, core)
        return remote(two_mine.at[slot], there, two_sem.at[0, slot], two_sem.at[1, slot], grp, plane, 1 - core)

    def two_keep(slot):
        return pltpu.make_async_copy(two_mine.at[slot], rows_of(slot, core), own_sem.at[slot])

    def finish(turn):
        block, s = lax.rem(turn, blocks), turn // blocks
        slot = s * half + lax.rem(block, half)

        @pl.when(block // half == core)
        def _():
            part_copy(slot).wait_recv()
            rows = pl.ds(pl.multiple_of(slot * BLOCK, BLOCK), BLOCK)
            middle = own_ref[rows, :].astype(F32) + part_mine[slot].astype(F32) + part_recv[slot].astype(F32)
            x1_ref[rows, :] = middle
            x1_flush(slot).start()
            inverse = lax.rsqrt(jnp.mean(middle * middle, -1, keepdims=True) + epsilon)
            inv_ref[rows, :] = inverse
            two_mine[slot] = (middle * inverse).astype(BF16)
            two_copy(slot).start()
            two_keep(slot).start()

    def run(block):
        n = reach(block)
        turn = step - tiles
        s = turn // blocks
        prefix = prefix_ref[s]
        base = pl.multiple_of(s * blocks * BLOCK, BLOCK)
        tokens = pl.ds(pl.multiple_of(turn * BLOCK, BLOCK), BLOCK)

        def score(h):
            kh = h // groups
            keys = kv_ref[pl.ds(base, n), kh * HEAD : (kh + 1) * HEAD]
            return scores_of(keys, qt_ref[h * HEAD : (h + 1) * HEAD, tokens], prefix, block)

        def mix(h, weights, total):
            kh = h // groups
            vt = kvt_ref[kv_cols + kh * HEAD : kv_cols + (kh + 1) * HEAD, pl.ds(base, n)]
            ot_ref[h * HEAD : (h + 1) * HEAD, tokens] = (dot(vt, weights) / total).astype(BF16)

        later, held = score(0), None
        for h in range(heads):
            scores = later
            if h + 1 < heads:
                later = score(h + 1)
            peak = jnp.max(scores, 0, keepdims=True)
            weights = jnp.exp2(scores - peak)
            total = jnp.sum(weights, 0, keepdims=True)
            lse_ref[h : h + 1, tokens] = peak + jnp.log2(total)
            if held:
                mix(*held)
            held = (h, weights.astype(BF16), total)
        mix(*held)
        ot_flush(turn).start()
        part = dot(ot_ref[:, tokens], wo_ref[...], TN).astype(BF16)
        slot = s * half + block % half

        @pl.when(core == block // half)
        def _():
            part_mine[slot] = part

        @pl.when(core != block // half)
        def _():
            part_send[slot] = part
            part_copy(slot).start()

    @pl.when(step > tiles)
    def _():
        finish(step - tiles - 1)

    for block in range(blocks):
        pl.when((step >= tiles) & (lax.rem(step, blocks) == block))(functools.partial(run, block))

    @at(2 * tiles - 1)
    def _():
        gather.third(2)
        finish(step - tiles)
        for n in range(3):
            gather.last(n)
        gather.near_in(1)
        for copy in flush():
            copy.wait()
        for turn in range(tiles):
            ot_flush(turn).wait()
        for slot in range(count * half):
            x1_flush(slot).wait()
            part_copy(slot).wait_send()
            two_copy(slot).wait_send()
            two_keep(slot).wait()
            there = rows_of(slot, 1 - core)
            remote(there, there, two_sem.at[0, slot], two_sem.at[1, slot], grp, plane, 1 - core).wait_recv()
        gather.sent_all((1, 2), (0, 1, 2))


def front(prefix, x, own, pack, gate_part, up, down, gain_ffn, cosine, sine, heads, kv_heads, length):
    tokens, width = x.shape
    count, blocks = tokens // length, length // BLOCK
    tiles = tokens // BLOCK
    slots = tiles // 2
    q_cols, kv_cols = heads * HEAD, kv_heads * HEAD
    shape = jax.ShapeDtypeStruct
    once = pl.Buffered(1)

    def fixed(*dims):
        return pl.BlockSpec(dims, lambda i: (0,) * len(dims), pipeline_mode=once)

    tile = pl.BlockSpec((BLOCK, width), lambda i: (jnp.minimum(i, tiles - 1), 0))
    return pl.pallas_call(
        functools.partial(front_kernel, heads, kv_heads, blocks),
        grid=(2 * tiles,),
        in_specs=[
            pl.BlockSpec(memory_space=pltpu.SMEM),
            tile,
            fixed(tokens // 2, width),
            fixed(*pack.shape),
            fixed(*up.shape),
            fixed(*gain_ffn.shape),
            fixed(*cosine.shape),
            fixed(*sine.shape),
            ANY,
            fixed(*down.shape),
        ],
        out_specs=(
            tile,
            ANY, ANY, ANY, ANY,
            fixed(heads, tokens),
            fixed(q_cols, width),
            ANY,
            fixed(tokens // 2, 1),
            ANY, ANY, ANY, ANY,
        ),
        out_shape=(
            shape((tokens, width), BF16),
            shape((q_cols, tokens), BF16),
            shape((2 * kv_cols, tokens), BF16),
            shape((tokens, 2 * kv_cols), BF16),
            shape((q_cols, tokens), BF16),
            shape((heads, tokens), F32),
            shape((q_cols, width), BF16),
            shape((tokens // 2, width), F32),
            shape((tokens // 2, 1), F32),
            shape((tokens, width), BF16),
            shape(gate_part.shape, BF16),
            shape(gate_part.shape, BF16),
            shape((4 * down.shape[0], width), BF16),
        ),
        input_output_aliases={8: 10},
        scratch_shapes=[
            pltpu.VMEM((q_cols, tokens), BF16),
            pltpu.VMEM((2 * kv_cols, tokens), BF16),
            pltpu.VMEM((tokens, 2 * kv_cols), BF16),
            pltpu.VMEM((q_cols, tokens), BF16),
            pltpu.VMEM((tokens // 2, width), F32),
            DMA((3,)),
            DMA((tiles,)),
            DMA((slots,)),
            pltpu.VMEM(up.shape, BF16),
            pltpu.VMEM((q_cols, q_cols), BF16),
            pltpu.VMEM((q_cols, q_cols), BF16),
        ]
        + [pltpu.VMEM((slots, BLOCK, width), BF16)] * 4
        + [DMA((2,)), DMA((2, slots)), DMA((2, slots)), DMA((slots,))]
        + Gather.semaphores(3),
        compiler_params=pltpu.CompilerParams(collective_id=1, has_side_effects=True, vmem_limit_bytes=60 * 2**20),
        cost_estimate=pl.CostEstimate(flops=2 * tokens * width * 1536, bytes_accessed=16 * tokens * width, transcendentals=0),
        name="front",
    )(prefix, x, own, pack, up, gain_ffn, cosine, sine, gate_part, down)


def feed_kernel(half, core_ref, n_ref, gate_ref, up_ref, down_ref, hidden_ref, by_up_ref, by_gate_ref, mine_ref, theirs_ref):
    n = n_ref[...]
    gate = dot(n, gate_ref[...])
    upward = dot(n, up_ref[...])
    sigma = 1.0 / (1.0 + jnp.exp(-gate))
    silu = gate * sigma
    hidden = (silu * upward).astype(BF16)
    hidden_ref[...] = hidden
    by_up_ref[...] = silu.astype(BF16)
    by_gate_ref[...] = (upward * sigma * (1.0 + gate - silu)).astype(BF16)
    part = dot(hidden, down_ref[...]).astype(BF16)
    own = lax.rem(pl.program_id(0) // half, 2) == core_ref[0]

    @pl.when(own)
    def _():
        mine_ref[...] = part

    @pl.when(jnp.logical_not(own))
    def _():
        theirs_ref[...] = part


def feed(core, n, gate, up, down, length):
    tokens, width = n.shape
    units = gate.shape[1]
    shape = jax.ShapeDtypeStruct
    once = pl.Buffered(1)
    half = length // BLOCK // 2
    tile = lambda cols: pl.BlockSpec((BLOCK, cols), lambda i, core: (i, 0))
    fixed = lambda a: pl.BlockSpec(a.shape, lambda i, core: (0, 0), pipeline_mode=once)

    def slot(i, owner):
        whole, rest = i // (2 * half), lax.rem(i, 2 * half)
        return whole * half + jnp.clip(rest - owner * half, 0, half - 1)

    mine = pl.BlockSpec((BLOCK, width), lambda i, core: (slot(i, core[0]), 0))
    theirs = pl.BlockSpec((BLOCK, width), lambda i, core: (slot(i, 1 - core[0]), 0))
    return pl.pallas_call(
        functools.partial(feed_kernel, half),
        grid_spec=pltpu.PrefetchScalarGridSpec(
            num_scalar_prefetch=1,
            grid=(tokens // BLOCK,),
            in_specs=[tile(width), fixed(gate), fixed(up), fixed(down)],
            out_specs=(tile(units), tile(units), tile(units), mine, theirs),
        ),
        out_shape=(shape((tokens, units), BF16),) * 3 + (shape((tokens // 2, width), BF16),) * 2,
        compiler_params=pltpu.CompilerParams(vmem_limit_bytes=62 * 2**20),
        cost_estimate=pl.CostEstimate(flops=6 * tokens * width * units, bytes_accessed=2 * tokens * (3 * units + 2 * width), transcendentals=tokens * units),
        name="feed",
    )(core, n, gate, up, down)


def finish_kernel(heads, kv_heads, pack_ref, gate_ref, up_ref, down_ref, wq_ref, wk_ref, wv_ref, wg_ref, wu_ref, ga_ref, gf_ref,
                  q_out, k_out, v_out, o_out, gate_out, up_out, down_out, ga_out, gf_out):
    q_cols, kv_cols = heads * HEAD, kv_heads * HEAD
    cols = pack_ref.shape[1] // 8
    gain = upright(ga_ref)
    total = jnp.zeros(gain.shape, F32)
    for k in range(2):
        row = jnp.concatenate([pack_ref[:, (2 * q + k) * cols : (2 * q + k + 1) * cols].astype(F32) for q in range(4)], 1)
        at = 0
        for w, out, size in ((wq_ref, q_out, q_cols), (wk_ref, k_out, kv_cols), (wv_ref, v_out, kv_cols)):
            part, here = row[:, at : at + size], slice(k * size, (k + 1) * size)
            total += jnp.sum(part * w[:, here].astype(F32), -1, keepdims=True)
            out[:, here] = part * gain
            at += size
        o_out[:, k * q_cols : (k + 1) * q_cols] = row[:, at:]
    ga_out[...] = jnp.broadcast_to(total, (total.shape[0], 8)).T[:1]
    gain = upright(gf_ref)
    total = jnp.zeros(gain.shape, F32)
    for ref, w, out in ((gate_ref, wg_ref, gate_out), (up_ref, wu_ref, up_out)):
        part = ref[...].astype(F32)
        total += jnp.sum(part * w[...].astype(F32), -1, keepdims=True)
        out[...] = part * gain
    gf_out[...] = jnp.broadcast_to(total, (total.shape[0], 8)).T[:1]
    down_out[...] = down_ref[...].astype(F32)


def finish(pack, gate, up, down, wq, wk, wv, wo, wg, wu, ga, gf, heads, kv_heads):
    shape = lambda a: jax.ShapeDtypeStruct(a.shape, F32)
    whole = lambda a: pl.BlockSpec(a.shape, lambda i: (0, 0))
    outs = (shape(wq), shape(wk), shape(wv), shape(wo), shape(wg), shape(wu), shape(down), shape(ga), shape(gf))
    return pl.pallas_call(
        functools.partial(finish_kernel, heads, kv_heads),
        grid=(1,),
        in_specs=[whole(a) for a in (pack, gate, up, down, wq, wk, wv, wg, wu, ga, gf)],
        out_specs=tuple(whole(a) for a in outs),
        out_shape=outs,
        compiler_params=pltpu.CompilerParams(vmem_limit_bytes=62 * 2**20),
        name="finish",
    )(pack, gate, up, down, wq, wk, wv, wg, wu, ga, gf)


def halves_of(rows, cols, split):
    return (rows // 8, cols // 4) if split else (rows // 32, cols)


class Summand:
    def __init__(self, core, ref, out, split, near=False):
        self.core, self.ref, self.out, self.split, self.near = core, ref, out, split, near
        self.rows, self.cols = halves_of(*ref.shape, split)

    def half(self, plane, quarter, path):
        if self.split:
            start = pl.multiple_of((2 * plane + path) * self.rows, 16)
            return self.ref.at[pl.ds(start, self.rows), pl.ds(pl.multiple_of(quarter * self.cols, 128), self.cols)]
        start = pl.multiple_of(((4 * plane + quarter) * 2 + path) * self.rows, 16)
        return self.ref.at[pl.ds(start, self.rows), :]

    def place(self, quarter, j, other):
        if self.split:
            return self.out.at[:, pl.ds(pl.multiple_of((2 * quarter + other) * self.cols, 128), self.cols)]
        return self.out.at[pl.ds(pl.multiple_of((2 * quarter + j) * self.rows, 16), self.rows), :]


class Reduce:
    @staticmethod
    def buffers(halves, near=(), begun=(), left=()):
        found = []
        for n, h in enumerate(halves):
            no_first, no_third = n in begun, n in left
            for lead, unused in (
                ((2, 4, 2), no_first or n in near),
                ((2, 4, 2), no_first),
                ((2, 4), no_first),
                ((3, 2), no_third),
                ((4, 2), False),
            ):
                found.append(pltpu.VMEM((1,) * len(lead) + (16, 128) if unused else lead + h, BF16))
        return found

    @staticmethod
    def semaphores(n):
        return [DMA((n, 2, 4, 2))] * 3 + [DMA((n, 2, 4))] * 2 + [DMA((n, 3))] * 2 + [DMA((n, 4, 2))] * 2

    def __init__(self, units, buffers, sems):
        self.units, self.sems = units, sems
        self.bufs = [buffers[5 * n : 5 * n + 5] for n in range(len(units))]
        self.grp, self.plane, self.core = where_am_i()
        gx, gy = lax.rem(self.grp, 2), self.grp // 2
        self.gx, self.gy = gx, gy
        side, up = self.grp + 1 - 2 * gx, lax.rem(self.grp + 2, 4)
        self.first_to, self.second_to, self.keep = (side, up), (up, side), (gy, gx)
        self.planes = [lax.rem(self.plane + s, 4) for s in (1, 2, 3)]
        self.origins = [lax.rem(self.plane + 4 - s, 4) for s in (1, 2, 3)]
        self.others = [lax.rem(self.grp + s, 4) for s in (1, 2, 3)]
        self.sources = [lax.rem(self.grp + 4 - s, 4) for s in (1, 2, 3)]

    def partners(self):
        grp, plane, core = self.grp, self.plane, self.core
        found = [(grp, z, core) for z in self.planes] + [(grp, plane, 1 - core)]
        return found + [(g, plane, c) for g in self.others for c in (core, 1 - core)]

    def quarter(self, path, i, own):
        if path == 0:
            return 2 * i + (self.gx if own else 1 - self.gx)
        return 2 * (self.gy if own else 1 - self.gy) + i

    def first_copy(self, n, path, z, i):
        _, s1, r1 = self.sems[:3]
        src = self.units[n].half(z, self.quarter(path, i, False), path)
        dst = self.bufs[n][1].at[path, z, i]
        return remote(src, dst, s1.at[n, path, z, i], r1.at[n, path, z, i], self.first_to[path], self.plane, self.core)

    def load_copy(self, n, path, z, i):
        src = self.units[n].half(z, self.quarter(path, i, True), path)
        return pltpu.make_async_copy(src, self.bufs[n][0].at[path, z, i], self.sems[0].at[n, path, z, i])

    def second_copy(self, n, path, z):
        _, got, second = self.bufs[n][:3]
        s2, r2 = self.sems[3:5]
        src = got.at[path, z, 1 - self.keep[path]]
        return remote(src, second.at[path, z], s2.at[n, path, z], r2.at[n, path, z], self.second_to[path], self.plane, self.core)

    def third_copy(self, n, i):
        third, fin = self.bufs[n][3:]
        s3, r3 = self.sems[5:7]
        return remote(fin.at[self.planes[i]], third.at[i], s3.at[n, i], r3.at[n, i], self.grp, self.planes[i], self.core)

    def fourth_copy(self, n, i, j, coming=False):
        u, fin = self.units[n], self.bufs[n][4]
        s4, r4 = self.sems[7:9]
        other = (self.core if j == 0 else 1 - self.core) if u.split else self.core
        grp = self.grp if i == 3 else (self.sources if coming else self.others)[i]
        if coming:
            src = dst = u.place(grp, j, other)
        else:
            src = fin.at[self.plane, other if u.split else j]
            dst = u.place(self.grp, j, self.core)
        if i == 3 and not (u.split and j == 1):
            return pltpu.make_async_copy(src, dst, s4.at[n, 3, j])
        return remote(src, dst, s4.at[n, i, j], r4.at[n, i, j], grp, self.plane, other)

    @staticmethod
    def each(planes=range(4)):
        return [(path, z, i) for z in planes for path in range(2) for i in range(2)]

    def a(self, n, planes=range(4)):
        for path, z, i in self.each(planes):
            self.first_copy(n, path, z, i).start()
            if not self.units[n].near:
                self.load_copy(n, path, z, i).start()

    def b(self, n, planes=range(4)):
        u, (acc, got) = self.units[n], self.bufs[n][:2]
        for z in planes:
            for path in range(2):
                for i in range(2):
                    self.first_copy(n, path, z, i).wait_recv()
                    if u.near:
                        own = u.half(z, self.quarter(path, i, True), path)[...]
                    else:
                        self.load_copy(n, path, z, i).wait()
                        own = acc[path, z, i]
                    got[path, z, i] = (own.astype(F32) + got[path, z, i].astype(F32)).astype(BF16)
                self.second_copy(n, path, z).start()

    def c(self, n, send=True):
        _, got, second, _, fin = self.bufs[n]
        for z in range(4):
            for path in range(2):
                self.second_copy(n, path, z).wait_recv()
                fin[z, path] = (got[path, z, self.keep[path]].astype(F32) + second[path, z].astype(F32)).astype(BF16)
            if send:
                self.third_to(n, z)

    def third_to(self, n, z):
        third, fin = self.bufs[n][3:]
        s3, r3 = self.sems[5:7]
        i = lax.rem(z + 7 - self.plane, 4)

        @pl.when(i != 3)
        def _():
            remote(fin.at[z], third.at[i], s3.at[n, i], r3.at[n, i], self.grp, z, self.core).start()

    def c2(self, n):
        for i in range(3):
            self.third_copy(n, i).start()

    def d(self, n):
        third, fin = self.bufs[n][3:]
        for i in range(3):
            self.third_copy(n, i).wait_recv()
        for j in range(2):
            total = fin[self.plane, j].astype(F32)
            for i in range(3):
                total += third[i, j].astype(F32)
            fin[self.plane, j] = total.astype(BF16)
        for j in range(2):
            for i in range(4):
                self.fourth_copy(n, i, j).start()

    def e1(self, n):
        for path, z, i in self.each():
            self.first_copy(n, path, z, i).wait_send()
        for z in range(4):
            for path in range(2):
                self.second_copy(n, path, z).wait_send()

    def e2(self, n):
        u = self.units[n]
        for i in range(3):
            self.third_copy(n, i).wait_send()
        for j in range(2):
            for i in range(4):
                if i == 3 and not (u.split and j == 1):
                    self.fourth_copy(n, i, j).wait()
                else:
                    self.fourth_copy(n, i, j).wait_send()
                    self.fourth_copy(n, i, j, coming=True).wait_recv()


class Trade:
    @staticmethod
    def buffers(slots, width):
        return [pltpu.VMEM((slots, BLOCK, width), BF16)] * 3

    @staticmethod
    def semaphores(slots):
        return [DMA((2, slots))]

    def __init__(self, bufs, sems, blocks):
        self.mine, self.out, self.come = bufs
        self.sem, self.half, self.blocks = sems[0], blocks // 2, blocks
        self.slots = self.mine.shape[0]
        self.grp, self.plane, self.core = where_am_i()

    def copy(self, slot):
        return remote(self.out.at[slot], self.come.at[slot], self.sem.at[0, slot], self.sem.at[1, slot], self.grp, self.plane, 1 - self.core)

    def where(self, turn):
        block = lax.rem(turn, self.blocks)
        return block // self.half, (turn // self.blocks) * self.half + lax.rem(block, self.half)

    def give(self, turn, part):
        owner, slot = self.where(turn)

        @pl.when(self.core == owner)
        def _():
            self.mine[slot] = part

        @pl.when(self.core != owner)
        def _():
            self.out[slot] = part
            self.copy(slot).start()

    def take(self, turn, close):
        owner, slot = self.where(turn)

        @pl.when(self.core == owner)
        def _():
            self.copy(slot).wait_recv()
            close(slot, self.mine[slot].astype(F32) + self.come[slot].astype(F32))

    def drain(self):
        for slot in range(self.slots):
            self.copy(slot).wait_send()

    def place(self, slot, owner):
        start = (slot // self.half) * self.blocks + owner * self.half + lax.rem(slot, self.half)
        return pl.ds(pl.multiple_of(start * BLOCK, BLOCK), BLOCK)

    def rows(self, ref, slot, owner):
        return ref.at[self.place(slot, owner), :]

    def columns(self, ref, slot, owner):
        return ref.at[:, self.place(slot, owner)]


WIDE = 2 * BLOCK


def feed_back_kernel(blocks, dy_ref, n_ref, gate_ref, up_ref, down_ref, inv_ref, by_up_ref, by_gate_ref, grad_ref,
                     g_up_ref, dx_out, r_down_out, begun_ref,
                     g_gate_ref, turned_n, d_gate, d_up, dx_mine, by_sem, dx_sem, keep_sem, *rest):
    step = pl.program_id(0)
    tiles = turned_n.shape[1] // BLOCK
    cuts = d_gate.shape[1] // WIDE
    second = tiles + 2 * cuts
    last = second + tiles - 1
    trade = Trade(rest[:3], rest[3:4], blocks)
    grp, plane, core = where_am_i()
    units = [Summand(core, grad_ref, r_down_out, False), Summand(core, g_gate_ref, None, True, near=True)]
    reduce = Reduce(units, list(rest[4:13]) + [begun_ref], rest[14:])

    def at(when):
        return pl.when(step == when)

    def tile_rows(tile):
        return pl.ds(pl.multiple_of(tile * BLOCK, BLOCK), BLOCK)

    def by_copies(tile):
        rows = tile_rows(tile)
        return [pltpu.make_async_copy(ref.at[rows, :], to.at[rows, :], by_sem.at[k, tile]) for k, (ref, to) in enumerate(((by_up_ref, d_up), (by_gate_ref, d_gate)))]

    @at(0)
    def _():
        for tile in range(tiles):
            for copy in by_copies(tile):
                copy.start()
        greet(reduce.partners())
        reduce.a(0)

    @at(tiles + 1)
    def _():
        reduce.b(0)

    @at(tiles + cuts)
    def _():
        reduce.a(1)

    @at(tiles + cuts + 1)
    def _():
        reduce.c(0)

    @at(second + 4)
    def _():
        reduce.b(1)
        reduce.d(0)

    @pl.when(step < tiles)
    def _():
        rows = tile_rows(step)
        dy = dy_ref[...]
        grad = dot(dy, down_ref[...], NT)
        for copy in by_copies(step):
            copy.wait()
        d_up[rows, :] = (grad * d_up[rows, :].astype(F32)).astype(BF16)
        d_gate[rows, :] = (grad * d_gate[rows, :].astype(F32)).astype(BF16)
        turned_n[:, rows] = n_ref[...].T
        owner, slot = trade.where(step)

        @pl.when(owner == core)
        def _():
            dx_mine[slot] = dy

    @pl.when((step >= tiles) & (step < tiles + cuts))
    def _():
        cols = pl.ds(pl.multiple_of((step - tiles) * WIDE, WIDE), WIDE)
        g_gate_ref[:, cols] = dot(turned_n[...], d_gate[:, cols]).astype(BF16)

    @pl.when((step >= tiles + cuts) & (step < second))
    def _():
        cols = pl.ds(pl.multiple_of((step - tiles - cuts) * WIDE, WIDE), WIDE)
        g_up_ref[...] = dot(turned_n[...], d_up[:, cols]).astype(BF16)

    def there(slot, owner):
        return trade.rows(dx_out, slot, owner)

    def dx_copy(slot):
        return remote(dx_mine.at[slot], there(slot, core), dx_sem.at[0, slot], dx_sem.at[1, slot], grp, plane, 1 - core)

    def dx_keep(slot):
        return pltpu.make_async_copy(dx_mine.at[slot], there(slot, core), keep_sem.at[slot])

    def close(slot, grad):
        rows = pl.ds(pl.multiple_of(slot * BLOCK, BLOCK), BLOCK)
        normed = trade.columns(turned_n, slot, core)[...].T.astype(F32)
        back = grad - normed * jnp.mean(grad * normed, -1, keepdims=True)
        dx_mine[slot] = (dx_mine[slot].astype(F32) + inv_ref[rows, :] * back).astype(BF16)
        dx_copy(slot).start()
        dx_keep(slot).start()

    @pl.when(step > second)
    def _():
        trade.take(step - second - 1, close)

    @pl.when(step >= second)
    def _():
        turn = step - second
        rows = tile_rows(turn)
        part = dot(d_gate[rows, :], gate_ref[...], NT) + dot(d_up[rows, :], up_ref[...], NT)
        trade.give(turn, part.astype(BF16))

    @at(last)
    def _():
        trade.take(tiles - 1, close)
        reduce.c(1, send=False)
        reduce.e1(0)
        reduce.e2(0)
        reduce.e1(1)
        trade.drain()
        for slot in range(trade.slots):
            dx_copy(slot).wait_send()
            dx_keep(slot).wait()
            here = there(slot, 1 - core)
            remote(here, here, dx_sem.at[0, slot], dx_sem.at[1, slot], grp, plane, 1 - core).wait_recv()


def feed_back(dy, by_up, by_gate, n, gate, up, down, inverse, grad_down, length):
    tokens, width = dy.shape
    units = gate.shape[1]
    blocks, tiles, cuts = length // BLOCK, tokens // BLOCK, units // WIDE
    slots = tiles // 2
    shape = jax.ShapeDtypeStruct
    once = pl.Buffered(1)
    early = lambda cols: pl.BlockSpec((BLOCK, cols), lambda i: (jnp.minimum(i, tiles - 1), 0))
    fixed = lambda a: pl.BlockSpec(a.shape, lambda i: (0,) * len(a.shape), pipeline_mode=once)
    cut = pl.BlockSpec((width, WIDE), lambda i: (0, jnp.clip(i - tiles - cuts, 0, cuts - 1)))
    g_gate = shape((width, units), BF16)
    halves = [halves_of(*grad_down.shape, False), halves_of(width, units, True)]
    begun = shape((4, 2) + halves[1], BF16)
    return pl.pallas_call(
        functools.partial(feed_back_kernel, blocks),
        grid=(2 * tiles + 2 * cuts,),
        in_specs=[early(width), early(width)] + [fixed(a) for a in (gate, up, down, inverse)] + [ANY] * 3,
        out_specs=(cut, ANY, ANY, fixed(begun)),
        out_shape=(
            g_gate,
            shape((tokens, width), BF16),
            shape((grad_down.shape[0] // 4, width), BF16),
            begun,
        ),
        scratch_shapes=[
            pltpu.VMEM(g_gate.shape, BF16),
            pltpu.VMEM((width, tokens), BF16),
            pltpu.VMEM((tokens, units), BF16),
            pltpu.VMEM((tokens, units), BF16),
            pltpu.VMEM((slots, BLOCK, width), BF16),
            DMA((2, tiles)),
            DMA((2, slots)),
            DMA((slots,)),
        ]
        + Trade.buffers(slots, width)
        + Trade.semaphores(slots)
        + Reduce.buffers(halves, near=(1,), left=(1,))
        + Reduce.semaphores(2),
        compiler_params=pltpu.CompilerParams(collective_id=3, has_side_effects=True, vmem_limit_bytes=62 * 2**20),
        name="feed_back",
    )(dy, n, gate, up, down, inverse, by_up, by_gate, grad_down)


def back_kernel(heads, kv_heads, blocks, prefix_ref, qt_ref, kv_ref, kt_ref, lse_ref, ot_ref, dx_ref, n_ref, own_in, wo_ref, w_in,
                cos_ref, sin_ref, begun_ref, g_up_ref,
                grad_out, r_pack_out, r_gate_out, r_up_out,
                dot_ref, dk_ref, dv_ref, dt, g_pack, g_wo, wo_send, wo_come, own_ref, w_ref, late_sem, wo_sem, *rest):
    step = pl.program_id(0)
    grp, plane, core = where_am_i()
    tokens, width = dx_ref.shape
    tiles, half, length = tokens // BLOCK, blocks // 2, blocks * BLOCK
    groups = heads // kv_heads
    q_cols, kv_cols = heads * HEAD, kv_heads * HEAD
    qkv = q_cols + 2 * kv_cols
    thirds = 3
    cut = width // thirds
    trade = Trade(rest[:3], rest[3:4], blocks)
    units = [Summand(core, g_up_ref, r_gate_out, True), Summand(core, g_up_ref, r_up_out, True), Summand(core, g_pack, r_pack_out, True, near=True)]
    reduce = Reduce(units, list(rest[4:8]) + [begun_ref] + list(rest[9:19]), rest[19:])
    turn = lax.rem(step, blocks)

    def at(when):
        return pl.when(step == when)

    def late():
        return [pltpu.make_async_copy(a, b, late_sem.at[k]) for k, (a, b) in enumerate(((own_in, own_ref), (w_in, w_ref)))]

    def wo_copy():
        return remote(wo_send, wo_come, wo_sem.at[0], wo_sem.at[1], grp, plane, 1 - core)

    @at(0)
    def _():
        for copy in late():
            copy.start()
        greet(reduce.partners())
        reduce.a(1)
        reduce.c2(0)

    for j in range(thirds):
        @at(1 + j)
        def _(j=j):
            g_wo[:, j * cut : (j + 1) * cut] = dot(ot_ref[...], dx_ref[:, j * cut : (j + 1) * cut]).astype(BF16)

    @at(1 + thirds)
    def _():
        low, high = g_wo[:, :q_cols], g_wo[:, q_cols:]
        wo_send[...] = jnp.where(core == 0, high, low)
        wo_copy().start()
        g_pack[pl.ds(pl.multiple_of(core * q_cols, 16), q_cols), qkv:] = jnp.where(core == 0, low, high)

    @at(5)
    def _():
        reduce.b(1)
        reduce.d(0)

    @at(tiles - 1)
    def _():
        reduce.c(1)

    @at(tiles)
    def _():
        for copy in late():
            copy.wait()
        wo_copy().wait()
        g_pack[pl.ds(pl.multiple_of((1 - core) * q_cols, 16), q_cols), qkv:] = wo_come[...]

    @at(tiles + 1)
    def _():
        reduce.a(2, (0,))

    @at(tiles + 2)
    def _():
        reduce.a(2, (1,))

    @at(tiles + thirds)
    def _():
        reduce.a(2, (2, 3))

    @pl.when((step < tiles) & (turn == 0))
    def _():
        dk_ref[...] = jnp.zeros_like(dk_ref)
        dv_ref[...] = jnp.zeros_like(dv_ref)

    @pl.when(step < tiles)
    def _():
        rows = pl.ds(pl.multiple_of(step * BLOCK, BLOCK), BLOCK)
        dot_ref[...] = dot(wo_ref[...], dx_ref[rows, :], NT).astype(BF16)

    def run(block):
        n = reach(block)
        prefix = prefix_ref[step // blocks]
        tokens_here = pl.ds(pl.multiple_of(step * BLOCK, BLOCK), BLOCK)
        here = pl.ds(block * BLOCK, BLOCK)
        cosine, sine = cos_ref[:, here], sin_ref[:, here]

        def score(h):
            kh = h // groups
            own = slice(h * HEAD, (h + 1) * HEAD)
            keys = kv_ref[:n, kh * HEAD : (kh + 1) * HEAD]
            values = kv_ref[:n, kv_cols + kh * HEAD : kv_cols + (kh + 1) * HEAD]
            return scores_of(keys, qt_ref[own, :], prefix, block), dot(values, dot_ref[own, :])

        later = score(0)
        for h in range(heads):
            kh = h // groups
            own = slice(h * HEAD, (h + 1) * HEAD)
            kt = kt_ref[kh * HEAD : (kh + 1) * HEAD, :n]
            query, grad = qt_ref[own, :], dot_ref[own, :]
            delta = jnp.sum(grad.astype(F32) * ot_ref[own, tokens_here].astype(F32), 0, keepdims=True)
            scores, grad_probs = later
            if h + 1 < heads:
                later = score(h + 1)
            probs = jnp.exp2(scores - lse_ref[h : h + 1, :])
            grad_scores = (probs * (grad_probs - delta)).astype(BF16)
            dv_ref[kh, :, :n] += dot(grad, probs.astype(BF16), NT)
            dk_ref[kh, :, :n] += dot(query, grad_scores, NT)
            grad_query = turned(dot(kt, grad_scores), cosine, sine, -1.0)
            dt[own, tokens_here] = (grad_query * (1.0 / math.sqrt(HEAD))).astype(BF16)

    for block in range(blocks):
        pl.when((step < tiles) & (turn == block))(functools.partial(run, block))

    @pl.when((step < tiles) & (turn == blocks - 1))
    def _():
        sequence = pl.ds(pl.multiple_of((step // blocks) * length, length), length)
        for kh in range(kv_heads):
            rows = turned(dk_ref[kh], cos_ref[...], sin_ref[...], -1.0) * math.log(2.0)
            dt[q_cols + kh * HEAD : q_cols + (kh + 1) * HEAD, sequence] = rows.astype(BF16)
            start = q_cols + kv_cols + kh * HEAD
            dt[start : start + HEAD, sequence] = dv_ref[kh].astype(BF16)

    for j in range(thirds):
        @at(tiles + j)
        def _(j=j):
            across = dot(dt[...], n_ref[...])
            g_pack[j * cut : (j + 1) * cut, :qkv] = across.T.astype(BF16)

    def close(slot, grad):
        rows = pl.ds(pl.multiple_of(slot * BLOCK, BLOCK), BLOCK)
        x = own_ref[rows, :].astype(F32)
        inverse = lax.rsqrt(jnp.mean(x * x, -1, keepdims=True) + epsilon)
        normed = x * inverse
        back = inverse * (grad - normed * jnp.mean(grad * normed, -1, keepdims=True))
        grad_out[rows, :] = (trade.rows(dx_ref, slot, core)[...].astype(F32) + back).astype(BF16)

    first = tiles + thirds

    @pl.when(step > first)
    def _():
        trade.take(step - first - 1, close)

    @pl.when(step >= first)
    def _():
        rows = pl.ds(pl.multiple_of((step - first) * BLOCK, BLOCK), BLOCK)
        part = dot(dt[:, rows].T, w_ref[:, :qkv], NT)
        trade.give(step - first, part.astype(BF16))

    @at(first)
    def _():
        reduce.d(1)

    @at(first + 3)
    def _():
        reduce.b(2, (0,))

    @at(first + 6)
    def _():
        reduce.b(2, (1,))

    @at(first + tiles - 1)
    def _():
        trade.take(tiles - 1, close)
        reduce.b(2, (2, 3))
        reduce.c(2)
        reduce.d(2)
        for n in range(3):
            reduce.e2(n)
        for n in (1, 2):
            reduce.e1(n)
        trade.drain()


def back(prefix, qt, kv, kvt, lse, ot, dx, n, own, wo, pack, cosine, sine, begun, g_up, heads, kv_heads, length):
    tokens, width = dx.shape
    count, blocks, tiles = tokens // length, length // BLOCK, tokens // BLOCK
    slots = tiles // 2
    q_cols, kv_cols = heads * HEAD, kv_heads * HEAD
    shape = jax.ShapeDtypeStruct
    once = pl.Buffered(1)
    fixed = lambda a: pl.BlockSpec(a.shape, lambda i: (0,) * a.ndim, pipeline_mode=once)
    early = lambda i: jnp.minimum(i, tiles - 1)
    shards = [shape((g.shape[0] // 8, g.shape[1] * 2), BF16) for g in (pack, g_up, g_up)]
    return pl.pallas_call(
        functools.partial(back_kernel, heads, kv_heads, blocks),
        grid=(2 * tiles + 3,),
        in_specs=[
            pl.BlockSpec(memory_space=pltpu.SMEM),
            pl.BlockSpec((q_cols, BLOCK), lambda i: (0, early(i))),
            pl.BlockSpec((length, 2 * kv_cols), lambda i: (early(i) // blocks, 0)),
            pl.BlockSpec((kv_cols, length), lambda i: (0, early(i) // blocks)),
            pl.BlockSpec((heads, BLOCK), lambda i: (0, early(i))),
        ]
        + [fixed(ot), fixed(dx), pl.BlockSpec((tokens, width // 3), lambda i: (0, jnp.clip(i - tiles, 0, 2)))]
        + [ANY, fixed(wo), ANY]
        + [fixed(a) for a in (cosine, sine, begun)]
        + [ANY],
        out_specs=(fixed(own), ANY, ANY, ANY),
        out_shape=[shape(own.shape, BF16)] + shards,
        scratch_shapes=[
            pltpu.VMEM((q_cols, BLOCK), BF16),
            pltpu.VMEM((kv_heads, HEAD, length), F32),
            pltpu.VMEM((kv_heads, HEAD, length), F32),
            pltpu.VMEM((q_cols + 2 * kv_cols, tokens), BF16),
            pltpu.VMEM(pack.shape, BF16),
            pltpu.VMEM(wo.shape, BF16),
            pltpu.VMEM((q_cols, q_cols), BF16),
            pltpu.VMEM((q_cols, q_cols), BF16),
            pltpu.VMEM(own.shape, BF16),
            pltpu.VMEM(pack.shape, BF16),
            DMA((2,)),
            DMA((2,)),
        ]
        + Trade.buffers(slots, width)
        + Trade.semaphores(slots)
        + Reduce.buffers([halves_of(*g.shape, True) for g in (g_up, g_up, pack)], near=(2,), begun=(0,))
        + Reduce.semaphores(3),
        compiler_params=pltpu.CompilerParams(collective_id=4, has_side_effects=True, vmem_limit_bytes=62 * 2**20),
        name="back",
    )(prefix, qt, kv, kvt, lse, ot, dx, n, own, wo, pack, cosine, sine, begun, g_up)


def tables(length):
    frequency = np.float32(10000.0) ** (-np.arange(HEAD // 2, dtype=np.float32) * np.float32(2.0) / np.float32(HEAD))
    angles = frequency[:, None] * np.arange(length, dtype=np.float32)[None, :]
    return jnp.asarray(np.cos(angles)), jnp.asarray(np.sin(angles))


def paired(
    activations_in,
    prefix_len,
    attn_gain,
    query_weight,
    key_weight,
    value_weight,
    out_weight,
    ffn_gain,
    gate_weight,
    up_weight,
    down_weight,
    cotangent,
):
    micro, seq_count, span, width = activations_in.shape
    count, length = micro * seq_count, 2 * span
    heads, kv_heads = HEADS // 2, KV_HEADS // 2

    own_x = activations_in.reshape(count, span, width)
    own_dy = cotangent.reshape(count, span, width)

    gain_attn, gain_ffn = attn_gain[None, :], ffn_gain[None, :]
    pack, gate_part, full_x, full_dy = start(
        own_x, own_dy, query_weight, key_weight, value_weight, out_weight, gate_weight, gain_attn, gain_ffn, heads, kv_heads
    )
    cosine, sine = tables(length)
    prefix = prefix_len.reshape(count)
    normed_one, qt, kvt, kv, ot, lse, w_out, middle, inverse, full_two, w_gate, w_up, w_down = front(
        prefix, full_x, own_x.reshape(count * span, width), pack, gate_part, up_weight, down_weight, gain_ffn, cosine, sine,
        heads, kv_heads, length,
    )
    core = lax.axis_index("ctx").astype(jnp.int32).reshape(1)
    hidden, by_up, by_gate, mine, theirs = feed(core, full_two, w_gate, w_up, w_down, length)
    result = middle + mine.astype(F32) + lax.ppermute(theirs, "ctx", [(0, 1), (1, 0)]).astype(F32)
    grad_down = dot(hidden, full_dy, TN).astype(BF16)
    grad_up, full_dx, r_down, begun = feed_back(
        full_dy, by_up, by_gate, full_two, w_gate, w_up, w_down, inverse, grad_down, length
    )
    grad_inputs, r_pack, r_gate, r_up = back(
        prefix, qt, kv, kvt, lse, ot, full_dx, normed_one, own_x.reshape(count * span, width), w_out, pack, cosine, sine,
        begun, grad_up, heads, kv_heads, length,
    )
    g_q, g_k, g_v, g_o, g_gate, g_up, g_down, g_ga, g_gf = finish(
        r_pack, r_gate, r_up, r_down, query_weight, key_weight, value_weight, out_weight, gate_weight, up_weight, gain_attn, gain_ffn,
        heads, kv_heads,
    )
    shape = activations_in.shape
    return (
        result.astype(BF16).reshape(shape),
        grad_inputs.reshape(shape),
        g_ga.reshape(-1),
        g_q,
        g_k,
        g_v,
        g_o,
        g_gf.reshape(-1),
        g_gate,
        g_up,
        g_down,
    )


def solution(mesh):
    small = dict(mesh.shape) == {"grp": 4, "fsdp": 4, "ctx": 2}

    return jax.shard_map(
        paired if small else local,
        mesh=mesh,
        in_specs=(
            P(None, ("grp", "fsdp"), "ctx", None),
            P(None, ("grp", "fsdp")),
            P(("fsdp", "ctx")),
            P(("fsdp", "ctx"), None),
            P(("fsdp", "ctx"), None),
            P(("fsdp", "ctx"), None),
            P(("fsdp", "ctx"), None),
            P(("fsdp", "ctx")),
            P(("fsdp", "ctx"), None),
            P(("fsdp", "ctx"), None),
            P(("fsdp", "ctx"), None),
            P(None, ("grp", "fsdp"), "ctx", None),
        ),
        out_specs=(
            P(None, ("grp", "fsdp"), "ctx", None),
            P(None, ("grp", "fsdp"), "ctx", None),
            P(("fsdp", "ctx")),
            P(("fsdp", "ctx"), None),
            P(("fsdp", "ctx"), None),
            P(("fsdp", "ctx"), None),
            P(("fsdp", "ctx"), None),
            P(("fsdp", "ctx")),
            P(("fsdp", "ctx"), None),
            P(("fsdp", "ctx"), None),
            P(("fsdp", "ctx"), None),
        ),
        check_vma=False,
    )
```
